32 devices in a mesh: groups: 2 (over y), rows: 4 (over z), frames: 2 (over x), heads: 2 (over core).
Axes of the slice: x: 2, y: 2, z: 4, core: 2. Of those that a mesh axis runs over, the one named last changes fastest.
Arguments:
- latents: bfloat16 [4, 512, 3072], P(('groups', 'frames'), 'rows'), parts along dimension 0
- w_qkv: bfloat16 [3072, 3, 3072], P('rows', None, ('frames', 'heads')), may hold values from -0.109375 to 0.109375
- w_out: bfloat16 [3072, 3072], P(('frames', 'heads'), 'rows'), may hold values from -0.109375 to 0.109375
- win_blocks: int32 [16, 4], P(('groups', 'rows')), parts along dimension 0, may hold values from 0 to 7, as said below
- win_counts: int32 [16], P(('groups', 'rows')), parts along dimension 0, may hold values from 1 to 4, as said below
- block_window: int32 [16], P(('groups', 'rows')), parts along dimension 0, may hold values from 0 to 7, as said below
Outputs:
- mixed: bfloat16 [4, 512, 3072], P(('groups', 'frames'), ('rows', 'heads')), parts along dimension 0
The draws below stay inside these ranges and needn't reach their ends.
There are 2 independent parts, one for each index of `groups`. The reference program is written for one: setup_inputs(seed, part) draws one part's arguments, and reference() takes and returns one part's arrays. A program takes and returns all parts, laid end to end along the dimension named above; an argument that names none is the same for every part. Nothing has to cross between parts.
Inputs may be any that keep to these rules, and one draw needn't show every extreme that they name: `win_blocks`: row w lists 4 different blocks; its first entry is w, and every entry c has c // 2 equal to w // 2 or one more or one less, counted cyclically modulo 8 // 2. `win_counts`: some window has 4 used entries. block_window[b] // 2 equals b // 2.
All inputs are finite; a program needn't handle non-finite values.
Results may differ from the reference program's by a relative error of at most 0.012.
The reference program's roundings to bfloat16 on the way count: a program that leaves them out, or rounds other values in their place, can miss the bound.
Values may be sent and summed in bfloat16 or wider, within the bound.
No kernel may reach another device: no remote copies, remote signals or barrier semaphores. Data moves between devices by JAX's collectives and lax.ppermute only.
A program may use at most 128 MiB of HBM per device.

```python
import math
import jax
import jax.numpy as jnp
from jax import lax

D = 3072
HEADS = 24
HD = 128
BS = 64
MAXB = 4
TOKF = 128
FRAMES = 2
S = 512
NBLK = 8
BLOCK = 128
HW = 3072
HG = 6
N_FRAMES = 2
N_HEADS = 2


def draw_latents(key, part):
    key = jax.random.fold_in(key, 1)
    key_a = jax.random.fold_in(key, 0)
    array_shape = (FRAMES, S, D)
    values = jnp.clip(jax.random.normal(key_a, array_shape, jnp.float32), -6.0, 6.0)
    return values.astype(jnp.bfloat16)


def draw_win_blocks(key, part):
    key = jax.random.fold_in(key, 2)
    per_shard = TOKF // BS
    window_ids = jnp.arange(NBLK, dtype=jnp.int32)
    key_list = jax.random.split(key, NBLK)
    orders = jax.vmap(lambda one_key: jax.random.permutation(one_key, 3 * per_shard - 1))(key_list)
    orders = orders[:, :MAXB - 1].astype(jnp.int32)
    home_pos = per_shard + window_ids % per_shard
    positions = jnp.where(orders < home_pos[:, None], orders, orders + 1)
    first_block = (window_ids // per_shard - 1) * per_shard
    others = (first_block[:, None] + positions + NBLK) % NBLK
    return jnp.concatenate([window_ids[:, None], others], axis=1).astype(jnp.int32)


def draw_win_counts(key, part):
    key = jax.random.fold_in(key, 3)
    key_a, key_b = jax.random.split(key, 2)
    counts = jax.random.randint(key_a, (NBLK,), 1, MAXB + 1, dtype=jnp.int32)
    full_at = jax.random.randint(key_b, (), 0, NBLK, dtype=jnp.int32)
    return jnp.where(jnp.arange(NBLK, dtype=jnp.int32) == full_at, MAXB, counts).astype(jnp.int32)


def draw_block_window(key, part):
    key = jax.random.fold_in(key, 4)
    per_shard = TOKF // BS
    picks = jax.random.randint(key, (NBLK,), 0, per_shard, dtype=jnp.int32)
    block_ids = jnp.arange(NBLK, dtype=jnp.int32)
    return (block_ids // per_shard * per_shard + picks).astype(jnp.int32)


def block_scale(own_key, extent, shards, smallest, top_value):
    level = 1.0
    for axis_at, shards_of in shards:
        steps = jax.random.uniform(jax.random.fold_in(jax.random.fold_in(own_key, 6), axis_at), (shards_of,), jnp.float32, smallest / len(shards), top_value / len(shards))
        level = level * jnp.repeat(jnp.exp(steps), extent[axis_at] // shards_of).reshape((-1,) + (1,) * (len(extent) - 1 - axis_at))
    return level


def bell_draw(own_key, extent, deviation, bound, shards=(), held_as=jnp.bfloat16):
    values = deviation * jax.random.normal(own_key, extent, jnp.float32)
    if shards:
        values = values * block_scale(own_key, extent, shards, -0.22, 0.18)
    return jnp.clip(values, -bound, bound).astype(held_as)


def setup_inputs(seed: int = 0, part: int = 0) -> dict:
    key_of = jax.random.split(jax.random.key(seed), 7)
    own_keys = jax.random.split(jax.random.fold_in(key_of[6], part), 7)
    latents = draw_latents(jax.random.fold_in(jax.random.fold_in(key_of[6], part), 71), part)
    w_qkv = bell_draw(key_of[1], (D, 3, HW), D ** -0.5, 0.109375, ((0, 4), (2, 4)))
    w_out = bell_draw(key_of[2], (HW, D), HW ** -0.5, 0.109375, ((0, 4), (1, 4)))
    win_blocks = draw_win_blocks(jax.random.fold_in(jax.random.fold_in(key_of[6], part), 71), part)
    win_counts = draw_win_counts(jax.random.fold_in(jax.random.fold_in(key_of[6], part), 71), part)
    block_window = draw_block_window(jax.random.fold_in(jax.random.fold_in(key_of[6], part), 71), part)
    return dict(latents=latents, w_qkv=w_qkv, w_out=w_out, win_blocks=win_blocks, win_counts=win_counts, block_window=block_window)


def reference(latents, w_qkv, w_out, win_blocks, win_counts, block_window):
    flat_tokens = latents.reshape(FRAMES * S, D)
    projected = jnp.dot(flat_tokens, w_qkv.reshape(D, 3 * HW), preferred_element_type=jnp.float32).astype(jnp.bfloat16)
    blocked = projected.reshape(FRAMES, NBLK, BS, 3, HW).transpose(1, 0, 2, 3, 4).reshape(NBLK, BLOCK, 3, HW)
    score_scale = 1.0 / math.sqrt(HD)

    def one_block(block_idx):
        window = block_window[block_idx]
        members = win_blocks[window]
        live_mask = jnp.repeat(jnp.arange(MAXB) < win_counts[window], BLOCK)
        query_rows = blocked[block_idx, :, 0].astype(jnp.float32).reshape(BLOCK, HEADS, HD)
        picked = blocked[members]
        key_rows = picked[:, :, 1].astype(jnp.float32).reshape(MAXB * BLOCK, HEADS, HD)
        value_rows = picked[:, :, 2].astype(jnp.float32).reshape(MAXB * BLOCK, HEADS, HD)
        scores = jnp.einsum('qhd,khd->hqk', query_rows, key_rows) * score_scale
        scores = jnp.where(live_mask[None, None, :], scores, -jnp.inf)
        row_max = lax.optimization_barrier(jnp.max(scores, axis=-1, keepdims=True))
        raised = jnp.exp(scores - row_max)
        weights = (raised / lax.optimization_barrier(jnp.sum(raised, axis=-1, keepdims=True))).astype(jnp.bfloat16)
        weights = lax.optimization_barrier(weights).astype(jnp.float32)
        blended = jnp.einsum('hqk,khd->qhd', weights, value_rows)
        return blended.reshape(BLOCK, HW).astype(jnp.bfloat16)
    attended = lax.map(one_block, jnp.arange(NBLK))
    ordered = attended.reshape(NBLK, FRAMES, BS, HW).transpose(1, 0, 2, 3).reshape(FRAMES * S, HW)
    group_count = N_FRAMES * N_HEADS
    grouped_attn = ordered.reshape(FRAMES * S, group_count, HG * HD).transpose(1, 0, 2)
    grouped_weight = w_out.reshape(group_count, HG * HD, D)

    def add_group(running, pair):
        partial_term = jnp.dot(pair[0], pair[1], preferred_element_type=jnp.float32).astype(jnp.bfloat16)
        partial_term = lax.optimization_barrier(partial_term)
        return (running + partial_term.astype(jnp.float32), None)
    running, _ = lax.scan(add_group, jnp.zeros((FRAMES * S, D), jnp.float32), (grouped_attn, grouped_weight))
    return running.astype(jnp.bfloat16).reshape(FRAMES, S, D)
```

```python
import math

import jax
import jax.numpy as jnp
from jax import lax
from jax.experimental import pallas as pl
from jax.experimental.pallas import tpu as pltpu
from jax.sharding import PartitionSpec as P

HD = 128
BS = 64
MAXB = 4
VMEM_BYTES = 48 * 1024 * 1024
EXP2_SCALE = math.log2(math.e) / math.sqrt(HD)


def with_halo(value, sides, width):
    for axis, dim in sides:
        peers, length = (lax.axis_size(axis), value.shape[dim])
        up = [(i, (i + 1) % peers) for i in range(peers)]
        down = [(j, i) for i, j in up]
        last = lax.slice_in_dim(value, length - width, length, axis=dim)
        first = lax.slice_in_dim(value, 0, width, axis=dim)
        before = lax.ppermute(last, axis, up)
        after = lax.ppermute(first, axis, down)
        value = jnp.concatenate([before, value, after], axis=dim)
    return value


def by_tokens(latents, w_qkv, w_out, win_blocks, win_counts, block_window):
    rows_n = lax.axis_size("rows")
    shard_idx = lax.axis_index("rows")
    frames = latents.shape[0] * lax.axis_size("frames")
    tok_frame = latents.shape[1]
    model_width = latents.shape[2]
    local_cols = w_qkv.shape[2]
    per_shard = tok_frame // BS
    block_total = per_shard * rows_n
    heads_here = local_cols // HD
    block_len = frames * BS
    score_scale = 1.0 / math.sqrt(HD)
    gathered = lax.all_gather(latents, "frames", axis=0, tiled=True)
    flat_tokens = gathered.reshape(frames * tok_frame, model_width)
    weight_rows = lax.all_gather(w_qkv, "rows", axis=0, tiled=True)
    projected = jnp.dot(
        flat_tokens,
        weight_rows.reshape(weight_rows.shape[0], 3 * local_cols),
        preferred_element_type=jnp.float32,
    ).astype(jnp.bfloat16)
    blocked = projected.reshape(frames, per_shard, BS, 3, local_cols).transpose(1, 0, 2, 3, 4)
    blocked = blocked.reshape(per_shard, block_len, 3, local_cols)
    queries = blocked[:, :, 0]
    keyvals = blocked[:, :, 1:]
    nearby = with_halo(keyvals, (("rows", 0),), per_shard)
    first_block = shard_idx * per_shard
    owners = block_window - first_block
    members = win_blocks[owners]
    lengths = win_counts[owners]
    positions = (members - first_block + per_shard + block_total) % block_total

    def attend(query_rows, picked, live_mask):
        key_count = picked.shape[0]
        key_blocks = nearby[picked]
        key_part = key_blocks[:, :, 0].reshape(key_count * block_len, heads_here, HD)
        value_part = key_blocks[:, :, 1].reshape(key_count * block_len, heads_here, HD)
        scores = (
            jnp.einsum(
                "qhd,khd->hqk",
                query_rows.reshape(block_len, heads_here, HD),
                key_part,
                preferred_element_type=jnp.float32,
            )
            * score_scale
        )
        scores = jnp.where(live_mask[None, None, :], scores, -jnp.inf)
        row_max = jnp.max(scores, axis=-1, keepdims=True)
        raised = jnp.exp(scores - row_max)
        weights = (raised / jnp.sum(raised, axis=-1, keepdims=True)).astype(jnp.bfloat16)
        blended = jnp.einsum(
            "hqk,khd->qhd", weights, value_part, preferred_element_type=jnp.float32
        )
        return blended.reshape(block_len, local_cols).astype(jnp.bfloat16)

    def one_block(block_item):
        query_rows, picked, length = block_item
        live_mask = jnp.repeat(jnp.arange(MAXB) < length, block_len)
        return attend(query_rows, picked, live_mask)

    attended = lax.map(one_block, (queries, positions, lengths))
    ordered = attended.reshape(per_shard, frames, BS, local_cols).transpose(1, 0, 2, 3)
    ordered = ordered.reshape(frames * tok_frame, local_cols)
    w_full = lax.all_gather(w_out, "rows", axis=1, tiled=True)
    group_count = lax.axis_size(("frames", "heads"))
    out_rows = frames * tok_frame // group_count
    summed = lax.psum_scatter(
        jnp.dot(ordered, w_full, preferred_element_type=jnp.float32).astype(jnp.bfloat16),
        ("frames", "heads"),
        scatter_dimension=0,
        tiled=True,
    )
    return summed.reshape(1, out_rows, model_width)


def swap(value, axis):
    return lax.ppermute(value, axis, [(0, 1), (1, 0)])


def call(kernel, out_shape, prefetch, operands, scratch=(), flops=0, read=0):
    return pl.pallas_call(
        kernel,
        out_shape=out_shape,
        grid_spec=pltpu.PrefetchScalarGridSpec(
            num_scalar_prefetch=len(prefetch),
            grid=(),
            in_specs=[pl.BlockSpec(memory_space=pltpu.VMEM)] * len(operands),
            out_specs=jax.tree.map(lambda _: pl.BlockSpec(memory_space=pltpu.VMEM), out_shape),
            scratch_shapes=scratch,
        ),
        compiler_params=pltpu.CompilerParams(vmem_limit_bytes=VMEM_BYTES),
        cost_estimate=pl.CostEstimate(flops=flops, bytes_accessed=read, transcendentals=0),
    )(*prefetch, *operands)


def project_part(tokens, chunk_ids, chunks, total):
    rows, depth, cols = tokens.shape[0], chunks[0].shape[1], chunks[0].shape[2]
    last = total is not None

    def kernel(ids_ref, tok_ref, *refs):
        w_refs = refs[: len(chunks)]
        rest = refs[len(chunks) :]
        for part in range(3):
            where = slice(part * cols, (part + 1) * cols)
            acc = rest[0][:, where] if last else None
            for i, w_ref in enumerate(w_refs):
                start = pl.multiple_of(ids_ref[i] * depth, depth)
                term = jnp.dot(
                    tok_ref[:, pl.ds(start, depth)], w_ref[part], preferred_element_type=jnp.float32
                )
                acc = term if acc is None else acc + term
            if not last:
                rest[0][:, where] = acc
            elif part == 0:
                rest[1][...] = acc.astype(jnp.bfloat16)
            else:
                rest[2][:, (part - 1) * cols : part * cols] = acc.astype(jnp.bfloat16)

    if last:
        out_shape = (
            jax.ShapeDtypeStruct((rows, cols), jnp.bfloat16),
            jax.ShapeDtypeStruct((rows, 2 * cols), jnp.bfloat16),
        )
    else:
        out_shape = jax.ShapeDtypeStruct((rows, 3 * cols), jnp.float32)
    operands = [tokens, *chunks] + ([total] if last else [])
    flops = 2 * rows * depth * len(chunks) * 3 * cols
    return call(kernel, out_shape, [chunk_ids], operands, flops=flops, read=flops // 200)


def attend_all(core, members, counts, queries, own, other, block_len):
    rows, cols = queries.shape
    blocks = rows // block_len

    def kernel(core_ref, members_ref, counts_ref, q_ref, own_ref, other_ref, out_ref, kv_ref):
        kv_ref[0] = own_ref[...].reshape(blocks, block_len, 2 * cols)
        kv_ref[1] = other_ref[...].reshape(blocks, block_len, 2 * cols)
        column = lax.broadcasted_iota(jnp.int32, (block_len, MAXB * block_len), 1)
        for b in range(blocks):
            live = column < counts_ref[b] * block_len
            listed = []
            for j in range(MAXB):
                member = members_ref[b * MAXB + j]
                side = (member + core_ref[0]) % 2
                listed.append(kv_ref[side, member // 2])
            q_rows = q_ref[b * block_len : (b + 1) * block_len, :]
            for h in range(cols // HD):
                at = slice(h * HD, (h + 1) * HD)
                at_v = slice(cols + h * HD, cols + (h + 1) * HD)
                keys = jnp.concatenate([block[:, at] for block in listed], axis=0)
                values = jnp.concatenate([block[:, at_v] for block in listed], axis=0)
                scores = lax.dot_general(
                    q_rows[:, at], keys, (((1,), (1,)), ((), ())), preferred_element_type=jnp.float32
                )
                scores = jnp.where(live, scores, -jnp.inf)
                raised = jnp.exp2((scores - jnp.max(scores, axis=-1, keepdims=True)) * EXP2_SCALE)
                weights = raised * (1.0 / jnp.sum(raised, axis=-1, keepdims=True))
                blended = jnp.dot(
                    weights.astype(jnp.bfloat16), values, preferred_element_type=jnp.float32
                )
                out_ref[b, :, at] = blended.astype(jnp.bfloat16)

    return call(
        kernel,
        jax.ShapeDtypeStruct((blocks, block_len, cols), jnp.bfloat16),
        [core, members, counts],
        [queries, own, other],
        scratch=[pltpu.VMEM((2, blocks, block_len, 2 * cols), jnp.bfloat16)],
        flops=4 * rows * MAXB * block_len * cols,
        read=8 * rows * cols,
    )


def mix(places, frame, attended, w_parts):
    _, block_len, depth = attended.shape
    peers, _, cols = w_parts[0].shape
    half = block_len // 2

    def kernel(places_ref, frame_ref, a_ref, w0, w1, w2, w3, keep_ref, send_ref, sum_ref):
        for r in range(peers):
            def term(refs, at):
                acc = None
                for i, ref in enumerate(refs):
                    part = jnp.dot(a_ref[places_ref[at + i]], ref[r], preferred_element_type=jnp.float32)
                    acc = part if acc is None else acc + part
                return acc.astype(jnp.bfloat16).astype(jnp.float32)

            sum_ref[...] = term((w0, w1), 0) + term((w2, w3), 2)
            mine = pl.multiple_of(frame_ref[0] * half, half)
            theirs = pl.multiple_of((1 - frame_ref[0]) * half, half)
            keep_ref[:, r * cols : (r + 1) * cols] = sum_ref[pl.ds(mine, half), :]
            send_ref[:, r * cols : (r + 1) * cols] = sum_ref[pl.ds(theirs, half), :].astype(jnp.bfloat16)

    shape = (half, peers * cols)
    return call(
        kernel,
        (jax.ShapeDtypeStruct(shape, jnp.float32), jax.ShapeDtypeStruct(shape, jnp.bfloat16)),
        [places, frame],
        [attended, *w_parts],
        scratch=[pltpu.VMEM((block_len, cols), jnp.float32)],
        flops=2 * block_len * depth * 4 * peers * cols,
        read=8 * depth * peers * cols,
    )


def by_heads(latents, w_qkv, w_out, win_blocks, win_counts, block_window):
    rows_n, heads_n = lax.axis_size("rows"), lax.axis_size("heads")
    group, row = lax.axis_index("groups"), lax.axis_index("rows")
    frame, core = lax.axis_index("frames"), lax.axis_index("heads")
    model_width = latents.shape[2]
    depth, _, local_cols = w_qkv.shape
    block_len = 2 * BS
    span = rows_n // heads_n
    cols = local_cols // span
    half = depth // 2

    tables = jnp.concatenate([win_blocks, win_counts[:, None], block_window[:, None]], axis=1)
    tables = lax.all_gather(tables, "rows", axis=0, tiled=True)
    windows = lax.dynamic_index_in_dim(
        tables[:, MAXB + 1].reshape(rows_n, heads_n), core, axis=1, keepdims=False
    )
    picked = tables[windows]
    members, counts = picked[:, :MAXB].reshape(-1), picked[:, MAXB]

    mine = lax.dynamic_slice_in_dim(latents[0], core * BS, BS, axis=0)
    tokens = lax.all_gather(mine, ("rows", "frames"), axis=0, tiled=True)

    w_half = lax.dynamic_slice_in_dim(w_qkv.transpose(1, 0, 2), group * half, half, axis=1)
    chunks, ids = [], []
    for k in range(span):
        pairs = [
            (r * heads_n + h, (h * span + (k + r) % span) * heads_n + r // span)
            for r in range(rows_n)
            for h in range(heads_n)
        ]
        piece = lax.dynamic_slice_in_dim(w_half, (k + row) % span * cols, cols, axis=2)
        here = lax.ppermute(piece, ("rows", "heads"), pairs)
        there = swap(here, "groups")
        chunks += [here, there]
        source = core * span + (row - k) % span
        ids += [2 * source + group, 2 * source + 1 - group]
    ids = jnp.stack(ids).astype(jnp.int32)
    other_ids = (ids + (1 - 2 * core) * 2 * span).astype(jnp.int32)
    total = project_part(tokens, ids, chunks, None)
    queries, keyvals = project_part(tokens, other_ids, [swap(c, "heads") for c in chunks], total)

    attended = attend_all(
        core.reshape(1), members, counts, queries, keyvals, swap(keyvals, "heads"), block_len
    )
    attended = lax.all_to_all(attended, "rows", 0, 0, tiled=True)

    out_half = lax.dynamic_slice_in_dim(w_out, group * cols, cols, axis=0)
    out_here = lax.all_gather(out_half, "rows", axis=0).reshape(rows_n, cols, w_out.shape[1])
    out_there = swap(out_here, "groups")
    first = core * span
    second = (1 - core) * span
    places = jnp.stack([first + group, first + 1 - group, second + group, second + 1 - group])
    keep, send = mix(
        places.astype(jnp.int32),
        frame.reshape(1),
        attended,
        [out_here, out_there, swap(out_here, "heads"), swap(out_there, "heads")],
    )
    out = keep + swap(send, "frames").astype(jnp.float32)
    return out.astype(jnp.bfloat16).reshape(1, BS, model_width)


def local(latents, w_qkv, w_out, win_blocks, win_counts, block_window):
    rows_n = lax.axis_size("rows")
    pairs = all(lax.axis_size(axis) == 2 for axis in ("groups", "frames", "heads"))
    heads_here = w_qkv.shape[2] // HD
    if pairs and rows_n == 4 and heads_here % 2 == 0 and latents.shape[:2] == (1, 2 * BS):
        plan = by_heads
    else:
        plan = by_tokens
    return plan(latents, w_qkv, w_out, win_blocks, win_counts, block_window)


def solution(mesh):
    in_specs = (
        P(("groups", "frames"), "rows", None),
        P("rows", None, ("frames", "heads")),
        P(("frames", "heads"), "rows"),
        P(("groups", "rows"), None),
        P(("groups", "rows")),
        P(("groups", "rows")),
    )
    out_specs = P(("groups", "frames"), ("rows", "heads"), None)
    return jax.shard_map(local, mesh=mesh, in_specs=in_specs, out_specs=out_specs, check_vma=False)
```

```python
import math

import jax
import jax.numpy as jnp
from jax import lax
from jax.experimental import pallas as pl
from jax.experimental.pallas import tpu as pltpu
from jax.sharding import PartitionSpec as P

HD = 128
BS = 64
MAXB = 4
VMEM_BYTES = 48 * 1024 * 1024
EXP2_SCALE = math.log2(math.e) / math.sqrt(HD)


def with_halo(value, sides, width):
    for axis, dim in sides:
        peers, length = (lax.axis_size(axis), value.shape[dim])
        up = [(i, (i + 1) % peers) for i in range(peers)]
        down = [(j, i) for i, j in up]
        last = lax.slice_in_dim(value, length - width, length, axis=dim)
        first = lax.slice_in_dim(value, 0, width, axis=dim)
        before = lax.ppermute(last, axis, up)
        after = lax.ppermute(first, axis, down)
        value = jnp.concatenate([before, value, after], axis=dim)
    return value


def by_tokens(latents, w_qkv, w_out, win_blocks, win_counts, block_window):
    rows_n = lax.axis_size("rows")
    shard_idx = lax.axis_index("rows")
    frames = latents.shape[0] * lax.axis_size("frames")
    tok_frame = latents.shape[1]
    model_width = latents.shape[2]
    local_cols = w_qkv.shape[2]
    per_shard = tok_frame // BS
    block_total = per_shard * rows_n
    heads_here = local_cols // HD
    block_len = frames * BS
    score_scale = 1.0 / math.sqrt(HD)
    gathered = lax.all_gather(latents, "frames", axis=0, tiled=True)
    flat_tokens = gathered.reshape(frames * tok_frame, model_width)
    weight_rows = lax.all_gather(w_qkv, "rows", axis=0, tiled=True)
    projected = jnp.dot(
        flat_tokens,
        weight_rows.reshape(weight_rows.shape[0], 3 * local_cols),
        preferred_element_type=jnp.float32,
    ).astype(jnp.bfloat16)
    blocked = projected.reshape(frames, per_shard, BS, 3, local_cols).transpose(1, 0, 2, 3, 4)
    blocked = blocked.reshape(per_shard, block_len, 3, local_cols)
    queries = blocked[:, :, 0]
    keyvals = blocked[:, :, 1:]
    nearby = with_halo(keyvals, (("rows", 0),), per_shard)
    first_block = shard_idx * per_shard
    owners = block_window - first_block
    members = win_blocks[owners]
    lengths = win_counts[owners]
    positions = (members - first_block + per_shard + block_total) % block_total

    def attend(query_rows, picked, live_mask):
        key_count = picked.shape[0]
        key_blocks = nearby[picked]
        key_part = key_blocks[:, :, 0].reshape(key_count * block_len, heads_here, HD)
        value_part = key_blocks[:, :, 1].reshape(key_count * block_len, heads_here, HD)
        scores = (
            jnp.einsum(
                "qhd,khd->hqk",
                query_rows.reshape(block_len, heads_here, HD),
                key_part,
                preferred_element_type=jnp.float32,
            )
            * score_scale
        )
        scores = jnp.where(live_mask[None, None, :], scores, -jnp.inf)
        row_max = jnp.max(scores, axis=-1, keepdims=True)
        raised = jnp.exp(scores - row_max)
        weights = (raised / jnp.sum(raised, axis=-1, keepdims=True)).astype(jnp.bfloat16)
        blended = jnp.einsum(
            "hqk,khd->qhd", weights, value_part, preferred_element_type=jnp.float32
        )
        return blended.reshape(block_len, local_cols).astype(jnp.bfloat16)

    def one_block(block_item):
        query_rows, picked, length = block_item
        live_mask = jnp.repeat(jnp.arange(MAXB) < length, block_len)
        return attend(query_rows, picked, live_mask)

    attended = lax.map(one_block, (queries, positions, lengths))
    ordered = attended.reshape(per_shard, frames, BS, local_cols).transpose(1, 0, 2, 3)
    ordered = ordered.reshape(frames * tok_frame, local_cols)
    w_full = lax.all_gather(w_out, "rows", axis=1, tiled=True)
    group_count = lax.axis_size(("frames", "heads"))
    out_rows = frames * tok_frame // group_count
    summed = lax.psum_scatter(
        jnp.dot(ordered, w_full, preferred_element_type=jnp.float32).astype(jnp.bfloat16),
        ("frames", "heads"),
        scatter_dimension=0,
        tiled=True,
    )
    return summed.reshape(1, out_rows, model_width)


def swap(value, axis):
    return lax.ppermute(value, axis, [(0, 1), (1, 0)])


def call(kernel, out_shape, prefetch, operands, scratch=(), flops=0, read=0):
    return pl.pallas_call(
        kernel,
        out_shape=out_shape,
        grid_spec=pltpu.PrefetchScalarGridSpec(
            num_scalar_prefetch=len(prefetch),
            grid=(),
            in_specs=[pl.BlockSpec(memory_space=pltpu.VMEM)] * len(operands),
            out_specs=jax.tree.map(lambda _: pl.BlockSpec(memory_space=pltpu.VMEM), out_shape),
            scratch_shapes=scratch,
        ),
        compiler_params=pltpu.CompilerParams(vmem_limit_bytes=VMEM_BYTES),
        cost_estimate=pl.CostEstimate(flops=flops, bytes_accessed=read, transcendentals=0),
    )(*prefetch, *operands)


def project(tokens, ids, chunks):
    peers, frames, count, width = tokens.shape
    _, depth, cols = chunks[0].shape
    rows = frames * count

    def kernel(ids_ref, core_ref, tok_ref, *refs):
        w_refs = refs[: len(chunks)]
        q_keep, kv_keep, q_send, kv_send, q_all = refs[len(chunks) :]
        for part in range(3):
            acc = None
            for i, w_ref in enumerate(w_refs):
                start = pl.multiple_of(ids_ref[i] * depth, depth)
                piece = tok_ref[0, :, :, pl.ds(start, depth)].reshape(rows, depth)
                term = jnp.dot(piece, w_ref[part], preferred_element_type=jnp.float32)
                acc = term if acc is None else acc + term
            if part == 0:
                q_all[...] = acc.reshape(frames, count, cols)
                own = pl.multiple_of(core_ref[0] * BS, BS)
                other = pl.multiple_of((1 - core_ref[0]) * BS, BS)
                q_keep[0] = q_all[:, pl.ds(own, BS), :].reshape(frames * BS, cols)
                q_send[0] = q_all[:, pl.ds(other, BS), :].reshape(frames * BS, cols).astype(jnp.bfloat16)
            else:
                where = slice((part - 1) * cols, part * cols)
                kv_keep[0, :, :, where] = acc.reshape(frames, count, cols)
                kv_send[0, :, :, where] = acc.reshape(frames, count, cols).astype(jnp.bfloat16)

    def at_row(*shape):
        return pl.BlockSpec((1, *shape), lambda i, *_: (i,) + (0,) * len(shape))

    def whole(shape):
        return pl.BlockSpec(shape, lambda i, *_: (0,) * len(shape))

    q_block, kv_block = (frames * BS, cols), (frames, count, 2 * cols)
    flops = 2 * peers * rows * width * 3 * cols
    return pl.pallas_call(
        kernel,
        out_shape=(
            jax.ShapeDtypeStruct((peers, *q_block), jnp.float32),
            jax.ShapeDtypeStruct((peers, *kv_block), jnp.float32),
            jax.ShapeDtypeStruct((peers, *q_block), jnp.bfloat16),
            jax.ShapeDtypeStruct((peers, *kv_block), jnp.bfloat16),
        ),
        grid_spec=pltpu.PrefetchScalarGridSpec(
            num_scalar_prefetch=2,
            grid=(peers,),
            in_specs=[at_row(frames, count, width)] + [whole(c.shape) for c in chunks],
            out_specs=(at_row(*q_block), at_row(*kv_block), at_row(*q_block), at_row(*kv_block)),
            scratch_shapes=[pltpu.VMEM((frames, count, cols), jnp.float32)],
        ),
        compiler_params=pltpu.CompilerParams(vmem_limit_bytes=VMEM_BYTES),
        cost_estimate=pl.CostEstimate(flops=flops, bytes_accessed=flops // 300, transcendentals=0),
    )(ids, lax.axis_index("heads").reshape(1), tokens, *chunks)


def attend_all(members, counts, queries, keyvals, other_queries, other_keyvals):
    blocks, block_len, cols = queries.shape
    frames, count = keyvals.shape[1:3]
    per_row = count // BS

    def kernel(members_ref, counts_ref, q_ref, kv_ref, q_more, kv_more, out_ref, q_sum, kv_sum):
        q_sum[...] = (q_ref[...] + q_more[...].astype(jnp.float32)).astype(jnp.bfloat16)
        for r in range(blocks):
            both = (kv_ref[r] + kv_more[r].astype(jnp.float32)).astype(jnp.bfloat16)
            for j in range(per_row):
                part = both[:, j * BS : (j + 1) * BS, :]
                kv_sum[r * per_row + j] = part.reshape(block_len, 2 * cols)
        column = lax.broadcasted_iota(jnp.int32, (block_len, MAXB * block_len), 1)
        for b in range(blocks):
            live = column < counts_ref[b] * block_len
            listed = [kv_sum.at[members_ref[b * MAXB + j]] for j in range(MAXB)]
            for h in range(cols // HD):
                at = slice(h * HD, (h + 1) * HD)
                at_v = slice(cols + h * HD, cols + (h + 1) * HD)
                keys = jnp.concatenate([block[:, at] for block in listed], axis=0)
                values = jnp.concatenate([block[:, at_v] for block in listed], axis=0)
                scores = lax.dot_general(
                    q_sum[b, :, at], keys, (((1,), (1,)), ((), ())), preferred_element_type=jnp.float32
                )
                scores = jnp.where(live, scores, -jnp.inf)
                raised = jnp.exp2((scores - jnp.max(scores, axis=-1, keepdims=True)) * EXP2_SCALE)
                weights = raised * (1.0 / jnp.sum(raised, axis=-1, keepdims=True))
                blended = jnp.dot(
                    weights.astype(jnp.bfloat16), values, preferred_element_type=jnp.float32
                )
                out_ref[b, :, at] = blended.astype(jnp.bfloat16)

    return call(
        kernel,
        jax.ShapeDtypeStruct((blocks, block_len, cols), jnp.bfloat16),
        [members, counts],
        [queries, keyvals, other_queries, other_keyvals],
        scratch=[
            pltpu.VMEM((blocks, block_len, cols), jnp.bfloat16),
            pltpu.VMEM((blocks * per_row, block_len, 2 * cols), jnp.bfloat16),
        ],
        flops=4 * blocks * block_len * MAXB * block_len * cols,
        read=16 * blocks * block_len * cols,
    )


def mix(places, frame, attended, w_parts):
    _, block_len, depth = attended.shape
    peers, _, cols = w_parts[0].shape
    half = block_len // 2

    def kernel(places_ref, frame_ref, a_ref, w0, w1, w2, w3, keep_ref, send_ref, sum_ref):
        for r in range(peers):
            def term(refs, at):
                acc = None
                for i, ref in enumerate(refs):
                    part = jnp.dot(a_ref[places_ref[at + i]], ref[r], preferred_element_type=jnp.float32)
                    acc = part if acc is None else acc + part
                return acc.astype(jnp.bfloat16).astype(jnp.float32)

            sum_ref[...] = term((w0, w1), 0) + term((w2, w3), 2)
            mine = pl.multiple_of(frame_ref[0] * half, half)
            theirs = pl.multiple_of((1 - frame_ref[0]) * half, half)
            keep_ref[:, r * cols : (r + 1) * cols] = sum_ref[pl.ds(mine, half), :]
            send_ref[:, r * cols : (r + 1) * cols] = sum_ref[pl.ds(theirs, half), :].astype(jnp.bfloat16)

    shape = (half, peers * cols)
    return call(
        kernel,
        (jax.ShapeDtypeStruct(shape, jnp.float32), jax.ShapeDtypeStruct(shape, jnp.bfloat16)),
        [places, frame],
        [attended, *w_parts],
        scratch=[pltpu.VMEM((block_len, cols), jnp.float32)],
        flops=2 * block_len * depth * 4 * peers * cols,
        read=8 * depth * peers * cols,
    )


def by_heads(latents, w_qkv, w_out, win_blocks, win_counts, block_window):
    rows_n, heads_n = lax.axis_size("rows"), lax.axis_size("heads")
    group, row = lax.axis_index("groups"), lax.axis_index("rows")
    frame, core = lax.axis_index("frames"), lax.axis_index("heads")
    _, count, model_width = latents.shape
    depth, _, local_cols = w_qkv.shape
    span = rows_n // heads_n
    cols = local_cols // span
    half = depth // 2

    w_half = lax.dynamic_slice_in_dim(w_qkv.transpose(1, 0, 2), group * half, half, axis=1)
    chunks, ids = [], []
    for k in range(span):
        pairs = [
            (r * heads_n + h, (h * span + (k + r) % span) * heads_n + r // span)
            for r in range(rows_n)
            for h in range(heads_n)
        ]
        piece = lax.dynamic_slice_in_dim(w_half, (k + row) % span * cols, cols, axis=2)
        here = lax.ppermute(piece, ("rows", "heads"), pairs)
        chunks += [here, swap(here, "groups")]
        source = (row - k) % span
        ids += [2 * source + group, 2 * source + 1 - group]

    mine = lax.dynamic_slice_in_dim(latents[0], core * span * depth, span * depth, axis=1)
    tokens = lax.all_gather(mine, ("rows", "frames"), axis=0)
    tokens = tokens.reshape(rows_n, 2, count, span * depth)

    tables = jnp.concatenate([win_blocks, win_counts[:, None], block_window[:, None]], axis=1)
    found = [tables]
    for step in range(1, rows_n):
        found.append(lax.ppermute(tables, "rows", [(r, (r + step) % rows_n) for r in range(rows_n)]))
    places = (row - jnp.arange(rows_n)) % rows_n
    tables = jnp.stack(found)[places].reshape(rows_n * heads_n, MAXB + 2)
    windows = lax.dynamic_index_in_dim(
        tables[:, MAXB + 1].reshape(rows_n, heads_n), core, axis=1, keepdims=False
    )
    picked = tables[windows]
    members, counts = picked[:, :MAXB].reshape(-1), picked[:, MAXB]

    partial = project(tokens, jnp.stack(ids).astype(jnp.int32), chunks)
    attended = attend_all(
        members, counts, *partial[:2], swap(partial[2], "heads"), swap(partial[3], "heads")
    )
    attended = lax.all_to_all(attended, "rows", 0, 0, tiled=True)

    out_half = lax.dynamic_slice_in_dim(w_out, group * cols, cols, axis=0)
    out_half, _, _ = lax.optimization_barrier((out_half, tokens, chunks[-2]))
    out_here = lax.all_gather(out_half, "rows", axis=0).reshape(rows_n, cols, w_out.shape[1])
    out_there = swap(out_here, "groups")
    first = core * span
    second = (1 - core) * span
    places = jnp.stack([first + group, first + 1 - group, second + group, second + 1 - group])
    keep, send = mix(
        places.astype(jnp.int32),
        frame.reshape(1),
        attended,
        [out_here, out_there, swap(out_here, "heads"), swap(out_there, "heads")],
    )
    out = keep + swap(send, "frames").astype(jnp.float32)
    return out.astype(jnp.bfloat16).reshape(1, BS, model_width)


def local(latents, w_qkv, w_out, win_blocks, win_counts, block_window):
    rows_n = lax.axis_size("rows")
    pairs = all(lax.axis_size(axis) == 2 for axis in ("groups", "frames", "heads"))
    heads_here = w_qkv.shape[2] // HD
    if pairs and rows_n == 4 and heads_here % 2 == 0 and latents.shape[:2] == (1, 2 * BS):
        plan = by_heads
    else:
        plan = by_tokens
    return plan(latents, w_qkv, w_out, win_blocks, win_counts, block_window)


def solution(mesh):
    in_specs = (
        P(("groups", "frames"), "rows", None),
        P("rows", None, ("frames", "heads")),
        P(("frames", "heads"), "rows"),
        P(("groups", "rows"), None),
        P(("groups", "rows")),
        P(("groups", "rows")),
    )
    out_specs = P(("groups", "frames"), ("rows", "heads"), None)
    return jax.shard_map(local, mesh=mesh, in_specs=in_specs, out_specs=out_specs, check_vma=False)
```

```python
import math

import jax
import jax.numpy as jnp
from jax import lax
from jax.experimental import pallas as pl
from jax.experimental.pallas import tpu as pltpu
from jax.sharding import PartitionSpec as P

HD = 128
BS = 64
MAXB = 4
VMEM_BYTES = 48 * 1024 * 1024
EXP2_SCALE = math.log2(math.e) / math.sqrt(HD)


def with_halo(value, sides, width):
    for axis, dim in sides:
        peers, length = (lax.axis_size(axis), value.shape[dim])
        up = [(i, (i + 1) % peers) for i in range(peers)]
        down = [(j, i) for i, j in up]
        last = lax.slice_in_dim(value, length - width, length, axis=dim)
        first = lax.slice_in_dim(value, 0, width, axis=dim)
        before = lax.ppermute(last, axis, up)
        after = lax.ppermute(first, axis, down)
        value = jnp.concatenate([before, value, after], axis=dim)
    return value


def by_tokens(latents, w_qkv, w_out, win_blocks, win_counts, block_window):
    rows_n = lax.axis_size("rows")
    shard_idx = lax.axis_index("rows")
    frames = latents.shape[0] * lax.axis_size("frames")
    tok_frame = latents.shape[1]
    model_width = latents.shape[2]
    local_cols = w_qkv.shape[2]
    per_shard = tok_frame // BS
    block_total = per_shard * rows_n
    heads_here = local_cols // HD
    block_len = frames * BS
    score_scale = 1.0 / math.sqrt(HD)
    gathered = lax.all_gather(latents, "frames", axis=0, tiled=True)
    flat_tokens = gathered.reshape(frames * tok_frame, model_width)
    weight_rows = lax.all_gather(w_qkv, "rows", axis=0, tiled=True)
    projected = jnp.dot(
        flat_tokens,
        weight_rows.reshape(weight_rows.shape[0], 3 * local_cols),
        preferred_element_type=jnp.float32,
    ).astype(jnp.bfloat16)
    blocked = projected.reshape(frames, per_shard, BS, 3, local_cols).transpose(1, 0, 2, 3, 4)
    blocked = blocked.reshape(per_shard, block_len, 3, local_cols)
    queries = blocked[:, :, 0]
    keyvals = blocked[:, :, 1:]
    nearby = with_halo(keyvals, (("rows", 0),), per_shard)
    first_block = shard_idx * per_shard
    owners = block_window - first_block
    members = win_blocks[owners]
    lengths = win_counts[owners]
    positions = (members - first_block + per_shard + block_total) % block_total

    def attend(query_rows, picked, live_mask):
        key_count = picked.shape[0]
        key_blocks = nearby[picked]
        key_part = key_blocks[:, :, 0].reshape(key_count * block_len, heads_here, HD)
        value_part = key_blocks[:, :, 1].reshape(key_count * block_len, heads_here, HD)
        scores = (
            jnp.einsum(
                "qhd,khd->hqk",
                query_rows.reshape(block_len, heads_here, HD),
                key_part,
                preferred_element_type=jnp.float32,
            )
            * score_scale
        )
        scores = jnp.where(live_mask[None, None, :], scores, -jnp.inf)
        row_max = jnp.max(scores, axis=-1, keepdims=True)
        raised = jnp.exp(scores - row_max)
        weights = (raised / jnp.sum(raised, axis=-1, keepdims=True)).astype(jnp.bfloat16)
        blended = jnp.einsum(
            "hqk,khd->qhd", weights, value_part, preferred_element_type=jnp.float32
        )
        return blended.reshape(block_len, local_cols).astype(jnp.bfloat16)

    def one_block(block_item):
        query_rows, picked, length = block_item
        live_mask = jnp.repeat(jnp.arange(MAXB) < length, block_len)
        return attend(query_rows, picked, live_mask)

    attended = lax.map(one_block, (queries, positions, lengths))
    ordered = attended.reshape(per_shard, frames, BS, local_cols).transpose(1, 0, 2, 3)
    ordered = ordered.reshape(frames * tok_frame, local_cols)
    w_full = lax.all_gather(w_out, "rows", axis=1, tiled=True)
    group_count = lax.axis_size(("frames", "heads"))
    out_rows = frames * tok_frame // group_count
    summed = lax.psum_scatter(
        jnp.dot(ordered, w_full, preferred_element_type=jnp.float32).astype(jnp.bfloat16),
        ("frames", "heads"),
        scatter_dimension=0,
        tiled=True,
    )
    return summed.reshape(1, out_rows, model_width)


def swap(value, axis, step=1):
    peers = lax.axis_size(axis)
    return lax.ppermute(value, axis, [(i, i ^ step) for i in range(peers)])


def after(value, *others):
    return lax.optimization_barrier((value, *others))[0]


def call(kernel, out_shape, prefetch, operands, scratch=(), flops=0, read=0):
    return pl.pallas_call(
        kernel,
        out_shape=out_shape,
        grid_spec=pltpu.PrefetchScalarGridSpec(
            num_scalar_prefetch=len(prefetch),
            grid=(),
            in_specs=[pl.BlockSpec(memory_space=pltpu.VMEM)] * len(operands),
            out_specs=jax.tree.map(lambda _: pl.BlockSpec(memory_space=pltpu.VMEM), out_shape),
            scratch_shapes=scratch,
        ),
        compiler_params=pltpu.CompilerParams(vmem_limit_bytes=VMEM_BYTES),
        cost_estimate=pl.CostEstimate(flops=flops, bytes_accessed=read, transcendentals=0),
    )(*prefetch, *operands)


def project(place, mine, theirs, chunks):
    peers, count, depth = mine[0].shape
    slices = len(mine)
    half, cols = chunks[0][0][0].shape
    flat = [w for of_round in chunks for of_part in of_round for w in of_part]

    def kernel(place_ref, *refs):
        row, group, frame, core = (place_ref[i] for i in range(4))
        x_refs, w_refs = refs[: 2 * slices], refs[2 * slices : 2 * slices + len(flat)]
        q_keep, kv_keep, send, x_all, q_all = refs[2 * slices + len(flat) :]
        for c in range(slices):
            x_all[c, frame] = x_refs[c][0]
            x_all[c, 1 - frame] = x_refs[slices + c][0]
        for part in range(3):
            acc = None
            for k in range(slices):
                at = (row + slices - k) % slices
                for g in range(2):
                    start = pl.multiple_of((group + g) % 2 * half, half)
                    piece = x_all[at, :, :, pl.ds(start, half)].reshape(2 * count, half)
                    w_ref = w_refs[(k * 3 + part) * 2 + g]
                    term = jnp.dot(piece, w_ref[...], preferred_element_type=jnp.float32)
                    acc = term if acc is None else acc + term
            if part == 0:
                q_all[...] = acc.reshape(2, count, cols)
                own = pl.multiple_of(core * BS, BS)
                other = pl.multiple_of((1 - core) * BS, BS)
                q_keep[0] = q_all[:, pl.ds(own, BS), :].reshape(2 * BS, cols)
                for f in range(2):
                    send[0, 2 * count :, f * cols : (f + 1) * cols] = q_all[f, pl.ds(other, BS), :].astype(
                        jnp.bfloat16
                    )
            else:
                where = slice((part - 1) * cols, part * cols)
                kv_keep[0, :, where] = acc
                send[0, : 2 * count, where] = acc.astype(jnp.bfloat16)

    def at_row(*shape):
        return pl.BlockSpec((1, *shape), lambda i, *_: (i,) + (0,) * len(shape))

    def whole(shape):
        return pl.BlockSpec(shape, lambda i, *_: (0,) * len(shape))

    shapes = ((2 * BS, cols), (2 * count, 2 * cols), (2 * count + BS, 2 * cols))
    flops = 2 * peers * 2 * count * slices * depth * 3 * cols
    return pl.pallas_call(
        kernel,
        out_shape=(
            jax.ShapeDtypeStruct((peers, *shapes[0]), jnp.float32),
            jax.ShapeDtypeStruct((peers, *shapes[1]), jnp.float32),
            jax.ShapeDtypeStruct((peers, *shapes[2]), jnp.bfloat16),
        ),
        grid_spec=pltpu.PrefetchScalarGridSpec(
            num_scalar_prefetch=1,
            grid=(peers,),
            in_specs=[at_row(count, depth)] * (2 * slices) + [whole(w.shape) for w in flat],
            out_specs=tuple(at_row(*shape) for shape in shapes),
            scratch_shapes=[
                pltpu.VMEM((slices, 2, count, depth), jnp.bfloat16),
                pltpu.VMEM((2, count, cols), jnp.float32),
            ],
        ),
        compiler_params=pltpu.CompilerParams(vmem_limit_bytes=VMEM_BYTES),
        cost_estimate=pl.CostEstimate(flops=flops, bytes_accessed=flops // 300, transcendentals=0),
    )(place, *mine, *theirs, *flat)


def attend_all(place, members, counts, queries, keyvals, more):
    blocks, block_len, cols = queries.shape
    rows = keyvals.shape[1]
    per_row = rows // block_len

    def kernel(place_ref, members_ref, counts_ref, q_ref, kv_ref, more_ref, same_ref, diff_ref, q_sum, kv_sum, out):
        for r in range(blocks):
            added = more_ref[r, rows:, :].astype(jnp.float32)
            added = jnp.concatenate([added[:, :cols], added[:, cols:]], axis=0)
            q_sum[r] = (q_ref[r] + added).astype(jnp.bfloat16)
            both = (kv_ref[r] + more_ref[r, :rows, :].astype(jnp.float32)).astype(jnp.bfloat16)
            both = both.reshape(2, rows // 2, 2 * cols)
            for j in range(per_row):
                part = both[:, j * BS : (j + 1) * BS, :]
                kv_sum[r * per_row + j] = part.reshape(block_len, 2 * cols)
        column = lax.broadcasted_iota(jnp.int32, (block_len, MAXB * block_len), 1)
        for b in range(blocks):
            live = column < counts_ref[b] * block_len
            listed = [kv_sum.at[members_ref[b * MAXB + j]] for j in range(MAXB)]
            for h in range(cols // HD):
                at = slice(h * HD, (h + 1) * HD)
                at_v = slice(cols + h * HD, cols + (h + 1) * HD)
                keys = jnp.concatenate([block[:, at] for block in listed], axis=0)
                values = jnp.concatenate([block[:, at_v] for block in listed], axis=0)
                scores = lax.dot_general(
                    q_sum[b, :, at], keys, (((1,), (1,)), ((), ())), preferred_element_type=jnp.float32
                )
                scores = jnp.where(live, scores, -jnp.inf)
                raised = jnp.exp2((scores - jnp.max(scores, axis=-1, keepdims=True)) * EXP2_SCALE)
                weights = raised * (1.0 / jnp.sum(raised, axis=-1, keepdims=True))
                blended = jnp.dot(
                    weights.astype(jnp.bfloat16), values, preferred_element_type=jnp.float32
                )
                out[(b + place_ref[0]) % 2, b // 2, :, at] = blended.astype(jnp.bfloat16)
        same_ref[...] = out[0]
        diff_ref[...] = out[1]

    half = jax.ShapeDtypeStruct((blocks // 2, block_len, cols), jnp.bfloat16)
    return call(
        kernel,
        (half, half),
        [place, members, counts],
        [queries, keyvals, more],
        scratch=[
            pltpu.VMEM((blocks, block_len, cols), jnp.bfloat16),
            pltpu.VMEM((blocks * per_row, block_len, 2 * cols), jnp.bfloat16),
            pltpu.VMEM((2, blocks // 2, block_len, cols), jnp.bfloat16),
        ],
        flops=4 * blocks * block_len * MAXB * block_len * cols,
        read=16 * blocks * block_len * cols,
    )


def mix(place, attended, w_parts):
    blocks, block_len, cols = attended[0].shape
    width = w_parts[0].shape[1]

    def kernel(place_ref, *refs):
        row, _, frame, core = (place_ref[i] for i in range(4))
        a_refs, w_refs = refs[:4], refs[4:8]
        keep, over_x, over_z, over_both, a_all, sums = refs[8:]
        for s in range(4):
            a_all[s] = a_refs[s][...].reshape(blocks * block_len, cols)

        def term(w_ref, side):
            first = a_all[(2 * side) ^ row]
            second = a_all[(2 * side + 1) ^ row]
            acc = jnp.dot(first, w_ref[:cols], preferred_element_type=jnp.float32)
            acc = acc + jnp.dot(second, w_ref[cols:], preferred_element_type=jnp.float32)
            return acc.astype(jnp.bfloat16).astype(jnp.float32)

        for c in range(2):
            total = term(w_refs[c], core) + term(w_refs[2 + c], 1 - core)
            sums[...] = total.reshape(blocks, 2, BS, width)
            at = (row + c) % 2
            keep[at] = sums[row // 2, frame]
            over_x[at] = sums[row // 2, 1 - frame].astype(jnp.bfloat16)
            over_z[at] = sums[1 - row // 2, frame].astype(jnp.bfloat16)
            over_both[at] = sums[1 - row // 2, 1 - frame].astype(jnp.bfloat16)

    shape = (2, BS, width)
    sent = jax.ShapeDtypeStruct(shape, jnp.bfloat16)
    return call(
        kernel,
        (jax.ShapeDtypeStruct(shape, jnp.float32), sent, sent, sent),
        [place],
        [*attended, *w_parts],
        scratch=[
            pltpu.VMEM((4, blocks * block_len, cols), jnp.bfloat16),
            pltpu.VMEM((blocks, 2, BS, width), jnp.float32),
        ],
        flops=2 * blocks * block_len * 4 * cols * 2 * width,
        read=16 * cols * width,
    )


def finish(place, keep, from_x, from_z, from_both):
    halves, rows, width = keep.shape

    def kernel(place_ref, keep_ref, x_ref, z_ref, both_ref, out_ref):
        pair = place_ref[0] // 2
        for c in range(halves):
            near = pl.multiple_of((pair * halves + c) * width, width)
            far = pl.multiple_of(((1 - pair) * halves + c) * width, width)
            out_ref[:, pl.ds(near, width)] = (keep_ref[c] + x_ref[c].astype(jnp.float32)).astype(jnp.bfloat16)
            out_ref[:, pl.ds(far, width)] = (
                z_ref[c].astype(jnp.float32) + both_ref[c].astype(jnp.float32)
            ).astype(jnp.bfloat16)

    return call(
        kernel,
        jax.ShapeDtypeStruct((rows, 2 * halves * width), jnp.bfloat16),
        [place],
        [keep, from_x, from_z, from_both],
        read=16 * rows * halves * width,
    )


def by_heads(latents, w_qkv, w_out, win_blocks, win_counts, block_window):
    rows_n, heads_n = lax.axis_size("rows"), lax.axis_size("heads")
    group, row = lax.axis_index("groups"), lax.axis_index("rows")
    frame, core = lax.axis_index("frames"), lax.axis_index("heads")
    depth, _, local_cols = w_qkv.shape
    span = rows_n // heads_n
    cols = local_cols // span
    half = depth // 2
    place = jnp.stack([row, group, frame, core]).astype(jnp.int32)

    gathered = []
    for c in range(span):
        slice_at = (core * span + c) * depth
        mine = lax.dynamic_slice_in_dim(latents[0], slice_at, depth, axis=1)
        gathered.append(lax.all_gather(mine, "rows", axis=0))

    tables = jnp.concatenate([win_blocks, win_counts[:, None], block_window[:, None]], axis=1)
    found = [tables] + [swap(tables, "rows", s) for s in range(1, rows_n)]
    tables = jnp.stack(found)[row ^ jnp.arange(rows_n)].reshape(rows_n * heads_n, MAXB + 2)
    windows = lax.dynamic_index_in_dim(
        tables[:, MAXB + 1].reshape(rows_n, heads_n), core, axis=1, keepdims=False
    )
    picked = tables[windows]
    members, counts = picked[:, :MAXB].reshape(-1), picked[:, MAXB]

    by_part = w_qkv.transpose(1, 0, 2)
    here = []
    for k in range(span):
        pairs = [
            (r * heads_n + h, (h * span + (k + r) % span) * heads_n + r // span)
            for r in range(rows_n)
            for h in range(heads_n)
        ]
        for part in range(3):
            piece = lax.dynamic_slice(
                by_part[part], (group * half, (k + row) % span * cols), (half, cols)
            )
            if len(here) >= 2:
                piece = after(piece, here[-2])
            if len(here) == 3 * span - 1:
                piece = after(piece, members, counts)
            here.append(lax.ppermute(piece, ("rows", "heads"), pairs))
    chunks = [
        [(here[3 * k + part], swap(here[3 * k + part], "groups")) for part in range(3)] for k in range(span)
    ]
    theirs = [swap(after(g, here[2 + 2 * c]), "frames") for c, g in enumerate(gathered)]

    queries, keyvals, send = project(place, gathered, theirs, chunks)
    same, diff = attend_all(place, members, counts, queries, keyvals, swap(send, "heads"))
    attended = [same] + [swap(same if s % 2 == 0 else diff, "rows", s) for s in range(1, rows_n)]

    across = swap(after(w_out, here[1]), "heads")
    beside = swap(after(w_out, here[-1]), "rows")
    keep, over_x, over_z, over_both = mix(
        place, attended, [w_out, beside, across, swap(beside, "heads")]
    )
    from_x = swap(over_x, "frames")
    from_z = swap(over_z, "rows", 2)
    from_both = lax.ppermute(
        over_both,
        ("rows", "frames"),
        [(2 * r + f, 2 * (r ^ 2) + 1 - f) for r in range(rows_n) for f in range(2)],
    )
    out = finish(place, keep, from_x, from_z, from_both)
    return out[None]


def local(latents, w_qkv, w_out, win_blocks, win_counts, block_window):
    rows_n = lax.axis_size("rows")
    pairs = all(lax.axis_size(axis) == 2 for axis in ("groups", "frames", "heads"))
    heads_here = w_qkv.shape[2] // HD
    if pairs and rows_n == 4 and heads_here % 2 == 0 and latents.shape[:2] == (1, 2 * BS):
        plan = by_heads
    else:
        plan = by_tokens
    return plan(latents, w_qkv, w_out, win_blocks, win_counts, block_window)


def solution(mesh):
    in_specs = (
        P(("groups", "frames"), "rows", None),
        P("rows", None, ("frames", "heads")),
        P(("frames", "heads"), "rows"),
        P(("groups", "rows"), None),
        P(("groups", "rows")),
        P(("groups", "rows")),
    )
    out_specs = P(("groups", "frames"), ("rows", "heads"), None)
    return jax.shard_map(local, mesh=mesh, in_specs=in_specs, out_specs=out_specs, check_vma=False)
```

```python
import math

import jax
import jax.numpy as jnp
from jax import lax
from jax.experimental import pallas as pl
from jax.experimental.pallas import tpu as pltpu
from jax.sharding import PartitionSpec as P

HD = 128
BS = 64
MAXB = 4
VMEM_BYTES = 24 * 1024 * 1024
EXP2_SCALE = math.log2(math.e) / math.sqrt(HD)


def with_halo(value, sides, width):
    for axis, dim in sides:
        peers, length = (lax.axis_size(axis), value.shape[dim])
        up = [(i, (i + 1) % peers) for i in range(peers)]
        down = [(j, i) for i, j in up]
        last = lax.slice_in_dim(value, length - width, length, axis=dim)
        first = lax.slice_in_dim(value, 0, width, axis=dim)
        before = lax.ppermute(last, axis, up)
        after = lax.ppermute(first, axis, down)
        value = jnp.concatenate([before, value, after], axis=dim)
    return value


def by_tokens(latents, w_qkv, w_out, win_blocks, win_counts, block_window):
    rows_n = lax.axis_size("rows")
    shard_idx = lax.axis_index("rows")
    frames = latents.shape[0] * lax.axis_size("frames")
    tok_frame = latents.shape[1]
    model_width = latents.shape[2]
    local_cols = w_qkv.shape[2]
    per_shard = tok_frame // BS
    block_total = per_shard * rows_n
    heads_here = local_cols // HD
    block_len = frames * BS
    score_scale = 1.0 / math.sqrt(HD)
    gathered = lax.all_gather(latents, "frames", axis=0, tiled=True)
    flat_tokens = gathered.reshape(frames * tok_frame, model_width)
    weight_rows = lax.all_gather(w_qkv, "rows", axis=0, tiled=True)
    projected = jnp.dot(
        flat_tokens,
        weight_rows.reshape(weight_rows.shape[0], 3 * local_cols),
        preferred_element_type=jnp.float32,
    ).astype(jnp.bfloat16)
    blocked = projected.reshape(frames, per_shard, BS, 3, local_cols).transpose(1, 0, 2, 3, 4)
    blocked = blocked.reshape(per_shard, block_len, 3, local_cols)
    queries = blocked[:, :, 0]
    keyvals = blocked[:, :, 1:]
    nearby = with_halo(keyvals, (("rows", 0),), per_shard)
    first_block = shard_idx * per_shard
    owners = block_window - first_block
    members = win_blocks[owners]
    lengths = win_counts[owners]
    positions = (members - first_block + per_shard + block_total) % block_total

    def attend(query_rows, picked, live_mask):
        key_count = picked.shape[0]
        key_blocks = nearby[picked]
        key_part = key_blocks[:, :, 0].reshape(key_count * block_len, heads_here, HD)
        value_part = key_blocks[:, :, 1].reshape(key_count * block_len, heads_here, HD)
        scores = (
            jnp.einsum(
                "qhd,khd->hqk",
                query_rows.reshape(block_len, heads_here, HD),
                key_part,
                preferred_element_type=jnp.float32,
            )
            * score_scale
        )
        scores = jnp.where(live_mask[None, None, :], scores, -jnp.inf)
        row_max = jnp.max(scores, axis=-1, keepdims=True)
        raised = jnp.exp(scores - row_max)
        weights = (raised / jnp.sum(raised, axis=-1, keepdims=True)).astype(jnp.bfloat16)
        blended = jnp.einsum(
            "hqk,khd->qhd", weights, value_part, preferred_element_type=jnp.float32
        )
        return blended.reshape(block_len, local_cols).astype(jnp.bfloat16)

    def one_block(block_item):
        query_rows, picked, length = block_item
        live_mask = jnp.repeat(jnp.arange(MAXB) < length, block_len)
        return attend(query_rows, picked, live_mask)

    attended = lax.map(one_block, (queries, positions, lengths))
    ordered = attended.reshape(per_shard, frames, BS, local_cols).transpose(1, 0, 2, 3)
    ordered = ordered.reshape(frames * tok_frame, local_cols)
    w_full = lax.all_gather(w_out, "rows", axis=1, tiled=True)
    group_count = lax.axis_size(("frames", "heads"))
    out_rows = frames * tok_frame // group_count
    summed = lax.psum_scatter(
        jnp.dot(ordered, w_full, preferred_element_type=jnp.float32).astype(jnp.bfloat16),
        ("frames", "heads"),
        scatter_dimension=0,
        tiled=True,
    )
    return summed.reshape(1, out_rows, model_width)


def swap(value, axis, step=1):
    peers = lax.axis_size(axis)
    return lax.ppermute(value, axis, [(i, i ^ step) for i in range(peers)])


def after(value, *others):
    return lax.optimization_barrier((value, *others))[0]


def call(kernel, out_shape, prefetch, operands, scratch=(), flops=0, read=0):
    return pl.pallas_call(
        kernel,
        out_shape=out_shape,
        grid_spec=pltpu.PrefetchScalarGridSpec(
            num_scalar_prefetch=len(prefetch),
            grid=(),
            in_specs=[pl.BlockSpec(memory_space=pltpu.VMEM)] * len(operands),
            out_specs=jax.tree.map(lambda _: pl.BlockSpec(memory_space=pltpu.VMEM), out_shape),
            scratch_shapes=scratch,
        ),
        compiler_params=pltpu.CompilerParams(vmem_limit_bytes=VMEM_BYTES),
        cost_estimate=pl.CostEstimate(flops=flops, bytes_accessed=read, transcendentals=0),
    )(*prefetch, *operands)


def assemble(place, mine, theirs):
    count, width = mine[0].shape
    rows = len(mine)

    def kernel(place_ref, *refs):
        row, frame = place_ref[0], place_ref[2]
        for s in range(rows):
            refs[-1][row ^ s, frame] = refs[s][...]
            refs[-1][row ^ s, 1 - frame] = refs[rows + s][...]

    return call(
        kernel,
        jax.ShapeDtypeStruct((rows, 2, count, width), jnp.bfloat16),
        [place],
        [*mine, *theirs],
        read=8 * rows * count * width,
    )


def project(place, tokens, chunks, only_own):
    rows, _, count, width = tokens.shape
    half, cols = chunks[0][0].shape
    slices = len(chunks)
    flat = [w for of_round in chunks for w in of_round]

    def kernel(place_ref, x_ref, *refs):
        row, group, core = place_ref[0], place_ref[1], place_ref[3]
        w_refs = refs[: len(flat)]
        keep, send = refs[len(flat) : len(flat) + 2]
        acc = None
        for k in range(slices):
            for g in range(2):
                at = (row + slices - k) % slices * (2 * half) + (group + g) % 2 * half
                piece = x_ref[:, :, :, pl.ds(pl.multiple_of(at, half), half)].reshape(-1, half)
                term = jnp.dot(piece, w_refs[2 * k + g][...], preferred_element_type=jnp.float32)
                acc = term if acc is None else acc + term
        if only_own:
            total = refs[-1]
            total[...] = acc.reshape(2 * rows, count, cols)
            own = pl.multiple_of(core * BS, BS)
            other = pl.multiple_of((1 - core) * BS, BS)
            keep[...] = total[:, pl.ds(own, BS), :].reshape(keep.shape)
            send[...] = total[:, pl.ds(other, BS), :].reshape(send.shape).astype(jnp.bfloat16)
        else:
            keep[...] = acc.reshape(keep.shape)
            send[...] = acc.reshape(send.shape).astype(jnp.bfloat16)

    shape = (rows, 2 * (BS if only_own else count), cols)
    flops = 4 * rows * count * width * cols
    return call(
        kernel,
        (jax.ShapeDtypeStruct(shape, jnp.float32), jax.ShapeDtypeStruct(shape, jnp.bfloat16)),
        [place],
        [tokens, *flat],
        scratch=[pltpu.VMEM((2 * rows, count, cols), jnp.float32)] if only_own else [],
        flops=flops,
        read=flops // 300,
    )


def by_block(out_ref, keep_ref, more_ref):
    rows, count, _ = keep_ref.shape
    per_row = count // (2 * BS)
    for r in range(rows):
        both = (keep_ref[r] + more_ref[r].astype(jnp.float32)).astype(jnp.bfloat16)
        both = both.reshape(2, count // 2, -1)
        for j in range(per_row):
            out_ref[r * per_row + j] = both[:, j * BS : (j + 1) * BS, :].reshape(2 * BS, -1)


def weigh(members, counts, queries, more_queries, keys, more_keys):
    blocks, block_len, cols = queries.shape
    per_row = keys.shape[1] // block_len
    heads = cols // HD

    def kernel(members_ref, counts_ref, q_ref, q_more, k_ref, k_more, out_ref, k_sum):
        by_block(k_sum, k_ref, k_more)
        column = lax.broadcasted_iota(jnp.int32, (block_len, MAXB * block_len), 1)
        for b in range(blocks):
            q_rows = (q_ref[b] + q_more[b].astype(jnp.float32)).astype(jnp.bfloat16)
            live = column < counts_ref[b] * block_len
            listed = [k_sum.at[members_ref[b * MAXB + j]] for j in range(MAXB)]
            for h in range(heads):
                at = slice(h * HD, (h + 1) * HD)
                of_head = jnp.concatenate([block[:, at] for block in listed], axis=0)
                scores = lax.dot_general(
                    q_rows[:, at], of_head, (((1,), (1,)), ((), ())), preferred_element_type=jnp.float32
                )
                scores = jnp.where(live, scores, -jnp.inf)
                raised = jnp.exp2((scores - jnp.max(scores, axis=-1, keepdims=True)) * EXP2_SCALE)
                weights = raised * (1.0 / jnp.sum(raised, axis=-1, keepdims=True))
                out_ref[b, h] = weights.astype(jnp.bfloat16)

    return call(
        kernel,
        jax.ShapeDtypeStruct((blocks, heads, block_len, MAXB * block_len), jnp.bfloat16),
        [members, counts],
        [queries, more_queries, keys, more_keys],
        scratch=[pltpu.VMEM((blocks * per_row, block_len, cols), jnp.bfloat16)],
        flops=2 * blocks * block_len * MAXB * block_len * cols,
        read=16 * blocks * block_len * cols,
    )


def blend(place, members, weights, values, more_values):
    blocks, heads, block_len, _ = weights.shape
    cols = values.shape[2]
    per_row = values.shape[1] // block_len

    def kernel(place_ref, members_ref, w_ref, v_ref, v_more, same_ref, diff_ref, v_sum, out):
        by_block(v_sum, v_ref, v_more)
        for b in range(blocks):
            listed = [v_sum.at[members_ref[b * MAXB + j]] for j in range(MAXB)]
            for h in range(heads):
                at = slice(h * HD, (h + 1) * HD)
                of_head = jnp.concatenate([block[:, at] for block in listed], axis=0)
                blended = jnp.dot(w_ref[b, h], of_head, preferred_element_type=jnp.float32)
                out[(b + place_ref[0]) % 2, b // 2, :, at] = blended.astype(jnp.bfloat16)
        same_ref[...] = out[0]
        diff_ref[...] = out[1]

    half = jax.ShapeDtypeStruct((blocks // 2, block_len, cols), jnp.bfloat16)
    return call(
        kernel,
        (half, half),
        [place, members],
        [weights, values, more_values],
        scratch=[
            pltpu.VMEM((blocks * per_row, block_len, cols), jnp.bfloat16),
            pltpu.VMEM((2, blocks // 2, block_len, cols), jnp.bfloat16),
        ],
        flops=2 * blocks * block_len * MAXB * block_len * cols,
        read=16 * blocks * block_len * cols,
    )


def mix(place, attended, w_parts):
    blocks, block_len, cols = attended[0].shape
    width = w_parts[0].shape[1]

    def kernel(place_ref, *refs):
        row, _, frame, core = (place_ref[i] for i in range(4))
        a_refs, w_refs = refs[:4], refs[4:8]
        keep, over_x, over_z, over_both, a_all, sums = refs[8:]
        for s in range(4):
            a_all[s] = a_refs[s][...].reshape(blocks * block_len, cols)

        def term(w_ref, side):
            first = a_all[(2 * side) ^ row]
            second = a_all[(2 * side + 1) ^ row]
            acc = jnp.dot(first, w_ref[:cols], preferred_element_type=jnp.float32)
            acc = acc + jnp.dot(second, w_ref[cols:], preferred_element_type=jnp.float32)
            return acc.astype(jnp.bfloat16).astype(jnp.float32)

        for c in range(2):
            total = term(w_refs[c], core) + term(w_refs[2 + c], 1 - core)
            sums[...] = total.reshape(blocks, 2, BS, width)
            at = (row + c) % 2
            keep[at] = sums[row // 2, frame]
            over_x[at] = sums[row // 2, 1 - frame].astype(jnp.bfloat16)
            over_z[at] = sums[1 - row // 2, frame].astype(jnp.bfloat16)
            over_both[at] = sums[1 - row // 2, 1 - frame].astype(jnp.bfloat16)

    shape = (2, BS, width)
    sent = jax.ShapeDtypeStruct(shape, jnp.bfloat16)
    return call(
        kernel,
        (jax.ShapeDtypeStruct(shape, jnp.float32), sent, sent, sent),
        [place],
        [*attended, *w_parts],
        scratch=[
            pltpu.VMEM((4, blocks * block_len, cols), jnp.bfloat16),
            pltpu.VMEM((blocks, 2, BS, width), jnp.float32),
        ],
        flops=2 * blocks * block_len * 4 * cols * 2 * width,
        read=16 * cols * width,
    )


def finish(place, keep, from_x, from_z, from_both):
    halves, rows, width = keep.shape

    def kernel(place_ref, keep_ref, x_ref, z_ref, both_ref, out_ref):
        pair = place_ref[0] // 2
        for c in range(halves):
            near = pl.multiple_of((pair * halves + c) * width, width)
            far = pl.multiple_of(((1 - pair) * halves + c) * width, width)
            out_ref[:, pl.ds(near, width)] = (keep_ref[c] + x_ref[c].astype(jnp.float32)).astype(jnp.bfloat16)
            out_ref[:, pl.ds(far, width)] = (
                z_ref[c].astype(jnp.float32) + both_ref[c].astype(jnp.float32)
            ).astype(jnp.bfloat16)

    return call(
        kernel,
        jax.ShapeDtypeStruct((rows, 2 * halves * width), jnp.bfloat16),
        [place],
        [keep, from_x, from_z, from_both],
        read=16 * rows * halves * width,
    )


def by_heads(latents, w_qkv, w_out, win_blocks, win_counts, block_window):
    rows_n, heads_n = lax.axis_size("rows"), lax.axis_size("heads")
    group, row = lax.axis_index("groups"), lax.axis_index("rows")
    frame, core = lax.axis_index("frames"), lax.axis_index("heads")
    depth, _, local_cols = w_qkv.shape
    span = rows_n // heads_n
    cols = local_cols // span
    half = depth // 2
    place = jnp.stack([row, group, frame, core]).astype(jnp.int32)

    mine = [lax.dynamic_slice_in_dim(latents[0], core * span * depth, span * depth, axis=1)]
    mine += [swap(mine[0], "rows", s) for s in range(1, rows_n)]
    theirs = [swap(x, "frames") for x in mine]
    tokens = assemble(place, mine, theirs)

    tables = jnp.concatenate([win_blocks, win_counts[:, None], block_window[:, None]], axis=1)
    tables = after(tables, mine[1])
    found = [tables] + [swap(tables, "rows", s) for s in range(1, rows_n)]
    tables = jnp.stack(found)[row ^ jnp.arange(rows_n)].reshape(rows_n * heads_n, MAXB + 2)
    windows = lax.dynamic_index_in_dim(
        tables[:, MAXB + 1].reshape(rows_n, heads_n), core, axis=1, keepdims=False
    )
    picked = tables[windows]
    members, counts = picked[:, :MAXB].reshape(-1), picked[:, MAXB]

    by_part = w_qkv.transpose(1, 0, 2)
    here = []
    for part in range(3):
        for k in range(span):
            pairs = [
                (r * heads_n + h, (h * span + (k + r) % span) * heads_n + r // span)
                for r in range(rows_n)
                for h in range(heads_n)
            ]
            piece = lax.dynamic_slice(
                by_part[part], (group * half, (k + row) % span * cols), (half, cols)
            )
            piece = after(piece, here[-2] if len(here) >= 2 else mine[1 + len(here)])
            if len(here) == 3:
                piece = after(piece, members, counts)
            here.append(lax.ppermute(piece, ("rows", "heads"), pairs))
    there = [swap(w, "groups") for w in here]

    partial, more = [], []
    for part in range(3):
        rounds = range(part * span, (part + 1) * span)
        keep, send = project(place, tokens, [(here[i], there[i]) for i in rounds], part == 0)
        partial.append(keep)
        more.append(swap(send, "heads"))
    weights = weigh(members, counts, partial[0], more[0], partial[1], more[1])
    same, diff = blend(place, members, weights, partial[2], more[2])
    attended = [same] + [swap(same if s % 2 == 0 else diff, "rows", s) for s in range(1, rows_n)]

    across = swap(after(w_out, here[1]), "heads")
    beside = swap(after(w_out, here[3]), "rows")
    keep, over_x, over_z, over_both = mix(
        place, attended, [w_out, beside, across, swap(beside, "heads")]
    )
    from_x = swap(over_x, "frames")
    from_z = swap(over_z, "rows", 2)
    from_both = lax.ppermute(
        over_both,
        ("rows", "frames"),
        [(2 * r + f, 2 * (r ^ 2) + 1 - f) for r in range(rows_n) for f in range(2)],
    )
    out = finish(place, keep, from_x, from_z, from_both)
    return out[None]


def local(latents, w_qkv, w_out, win_blocks, win_counts, block_window):
    rows_n = lax.axis_size("rows")
    pairs = all(lax.axis_size(axis) == 2 for axis in ("groups", "frames", "heads"))
    heads_here = w_qkv.shape[2] // HD
    if pairs and rows_n == 4 and heads_here % 2 == 0 and latents.shape[:2] == (1, 2 * BS):
        plan = by_heads
    else:
        plan = by_tokens
    return plan(latents, w_qkv, w_out, win_blocks, win_counts, block_window)


def solution(mesh):
    in_specs = (
        P(("groups", "frames"), "rows", None),
        P("rows", None, ("frames", "heads")),
        P(("frames", "heads"), "rows"),
        P(("groups", "rows"), None),
        P(("groups", "rows")),
        P(("groups", "rows")),
    )
    out_specs = P(("groups", "frames"), ("rows", "heads"), None)
    return jax.shard_map(local, mesh=mesh, in_specs=in_specs, out_specs=out_specs, check_vma=False)
```

```python
import math

import jax
import jax.numpy as jnp
from jax import lax
from jax.experimental import pallas as pl
from jax.experimental.pallas import tpu as pltpu
from jax.sharding import PartitionSpec as P

HD = 128
BS = 64
MAXB = 4
VMEM_BYTES = 24 * 1024 * 1024
EXP2_SCALE = math.log2(math.e) / math.sqrt(HD)


def with_halo(value, sides, width):
    for axis, dim in sides:
        peers, length = (lax.axis_size(axis), value.shape[dim])
        up = [(i, (i + 1) % peers) for i in range(peers)]
        down = [(j, i) for i, j in up]
        last = lax.slice_in_dim(value, length - width, length, axis=dim)
        first = lax.slice_in_dim(value, 0, width, axis=dim)
        before = lax.ppermute(last, axis, up)
        after = lax.ppermute(first, axis, down)
        value = jnp.concatenate([before, value, after], axis=dim)
    return value


def by_tokens(latents, w_qkv, w_out, win_blocks, win_counts, block_window):
    rows_n = lax.axis_size("rows")
    shard_idx = lax.axis_index("rows")
    frames = latents.shape[0] * lax.axis_size("frames")
    tok_frame = latents.shape[1]
    model_width = latents.shape[2]
    local_cols = w_qkv.shape[2]
    per_shard = tok_frame // BS
    block_total = per_shard * rows_n
    heads_here = local_cols // HD
    block_len = frames * BS
    score_scale = 1.0 / math.sqrt(HD)
    gathered = lax.all_gather(latents, "frames", axis=0, tiled=True)
    flat_tokens = gathered.reshape(frames * tok_frame, model_width)
    weight_rows = lax.all_gather(w_qkv, "rows", axis=0, tiled=True)
    projected = jnp.dot(
        flat_tokens,
        weight_rows.reshape(weight_rows.shape[0], 3 * local_cols),
        preferred_element_type=jnp.float32,
    ).astype(jnp.bfloat16)
    blocked = projected.reshape(frames, per_shard, BS, 3, local_cols).transpose(1, 0, 2, 3, 4)
    blocked = blocked.reshape(per_shard, block_len, 3, local_cols)
    queries = blocked[:, :, 0]
    keyvals = blocked[:, :, 1:]
    nearby = with_halo(keyvals, (("rows", 0),), per_shard)
    first_block = shard_idx * per_shard
    owners = block_window - first_block
    members = win_blocks[owners]
    lengths = win_counts[owners]
    positions = (members - first_block + per_shard + block_total) % block_total

    def attend(query_rows, picked, live_mask):
        key_count = picked.shape[0]
        key_blocks = nearby[picked]
        key_part = key_blocks[:, :, 0].reshape(key_count * block_len, heads_here, HD)
        value_part = key_blocks[:, :, 1].reshape(key_count * block_len, heads_here, HD)
        scores = (
            jnp.einsum(
                "qhd,khd->hqk",
                query_rows.reshape(block_len, heads_here, HD),
                key_part,
                preferred_element_type=jnp.float32,
            )
            * score_scale
        )
        scores = jnp.where(live_mask[None, None, :], scores, -jnp.inf)
        row_max = jnp.max(scores, axis=-1, keepdims=True)
        raised = jnp.exp(scores - row_max)
        weights = (raised / jnp.sum(raised, axis=-1, keepdims=True)).astype(jnp.bfloat16)
        blended = jnp.einsum(
            "hqk,khd->qhd", weights, value_part, preferred_element_type=jnp.float32
        )
        return blended.reshape(block_len, local_cols).astype(jnp.bfloat16)

    def one_block(block_item):
        query_rows, picked, length = block_item
        live_mask = jnp.repeat(jnp.arange(MAXB) < length, block_len)
        return attend(query_rows, picked, live_mask)

    attended = lax.map(one_block, (queries, positions, lengths))
    ordered = attended.reshape(per_shard, frames, BS, local_cols).transpose(1, 0, 2, 3)
    ordered = ordered.reshape(frames * tok_frame, local_cols)
    w_full = lax.all_gather(w_out, "rows", axis=1, tiled=True)
    group_count = lax.axis_size(("frames", "heads"))
    out_rows = frames * tok_frame // group_count
    summed = lax.psum_scatter(
        jnp.dot(ordered, w_full, preferred_element_type=jnp.float32).astype(jnp.bfloat16),
        ("frames", "heads"),
        scatter_dimension=0,
        tiled=True,
    )
    return summed.reshape(1, out_rows, model_width)


def swap(value, axis, step=1):
    peers = lax.axis_size(axis)
    return lax.ppermute(value, axis, [(i, i ^ step) for i in range(peers)])


def after(value, *others):
    return lax.optimization_barrier((value, *others))[0]


def call(kernel, out_shape, prefetch, operands, scratch=(), flops=0, read=0):
    return pl.pallas_call(
        kernel,
        out_shape=out_shape,
        grid_spec=pltpu.PrefetchScalarGridSpec(
            num_scalar_prefetch=len(prefetch),
            grid=(),
            in_specs=[pl.BlockSpec(memory_space=pltpu.VMEM)] * len(operands),
            out_specs=jax.tree.map(lambda _: pl.BlockSpec(memory_space=pltpu.VMEM), out_shape),
            scratch_shapes=scratch,
        ),
        compiler_params=pltpu.CompilerParams(vmem_limit_bytes=VMEM_BYTES),
        cost_estimate=pl.CostEstimate(flops=flops, bytes_accessed=read, transcendentals=0),
    )(*prefetch, *operands)


def assemble(place, mine, theirs):
    count, width = mine[0].shape
    rows = len(mine)

    def kernel(place_ref, *refs):
        row, frame = place_ref[0], place_ref[2]
        out_ref, sems = refs[2 * rows], refs[2 * rows + 1]
        copies = []
        for i in range(2 * rows):
            place_at = out_ref.at[row ^ (i % rows), (frame + i // rows) % 2]
            copies.append(pltpu.make_async_copy(refs[i], place_at, sems.at[i]))
            copies[-1].start()
        for copy in copies:
            copy.wait()

    return pl.pallas_call(
        kernel,
        out_shape=jax.ShapeDtypeStruct((rows, 2, count, width), jnp.bfloat16),
        grid_spec=pltpu.PrefetchScalarGridSpec(
            num_scalar_prefetch=1,
            grid=(),
            in_specs=[pl.BlockSpec(memory_space=pl.ANY)] * (2 * rows),
            out_specs=pl.BlockSpec(memory_space=pl.ANY),
            scratch_shapes=[pltpu.SemaphoreType.DMA((2 * rows,))],
        ),
        cost_estimate=pl.CostEstimate(flops=0, bytes_accessed=8 * rows * count * width, transcendentals=0),
    )(place, *mine, *theirs)


def project(place, tokens, chunks):
    rows, _, count, width = tokens.shape
    _, half, cols = chunks[0][0].shape
    slices = len(chunks)
    flat = [w for of_round in chunks for w in of_round]
    total_rows = rows * 2 * count

    def kernel(place_ref, x_ref, *refs):
        row, group, core = place_ref[0], place_ref[1], place_ref[3]
        w_refs = refs[: len(flat)]
        q_keep, kv_keep, send, total = refs[len(flat) :]
        acc = None
        for k in range(slices):
            for g in range(2):
                at = (row + slices - k) % slices * (2 * half) + (group + g) % 2 * half
                piece = x_ref[:, :, :, pl.ds(pl.multiple_of(at, half), half)].reshape(-1, half)
                w_ref = w_refs[2 * k + g]
                weight = jnp.concatenate([w_ref[part] for part in range(3)], axis=1)
                term = jnp.dot(piece, weight, preferred_element_type=jnp.float32)
                acc = term if acc is None else acc + term
        kv_part = acc[:, cols:].reshape(rows, 2 * count, 2 * cols)
        kv_keep[...] = kv_part
        send[:, : 2 * count, :] = kv_part.astype(jnp.bfloat16)
        total[...] = acc[:, :cols].reshape(rows, 2, count, cols)
        own = pl.multiple_of(core * BS, BS)
        other = pl.multiple_of((1 - core) * BS, BS)
        q_keep[...] = total[:, :, pl.ds(own, BS), :].reshape(q_keep.shape)
        for f in range(2):
            at = slice(f * cols, (f + 1) * cols)
            send[:, 2 * count :, at] = total[:, f, pl.ds(other, BS), :].astype(jnp.bfloat16)

    flops = 2 * total_rows * width * 3 * cols
    return call(
        kernel,
        (
            jax.ShapeDtypeStruct((rows, 2 * BS, cols), jnp.float32),
            jax.ShapeDtypeStruct((rows, 2 * count, 2 * cols), jnp.float32),
            jax.ShapeDtypeStruct((rows, 2 * count + BS, 2 * cols), jnp.bfloat16),
        ),
        [place],
        [tokens, *flat],
        scratch=[pltpu.VMEM((rows, 2, count, cols), jnp.float32)],
        flops=flops,
        read=flops // 300,
    )


def attend_all(place, members, counts, queries, keyvals, more):
    blocks, block_len, cols = queries.shape
    rows = keyvals.shape[1]
    per_row = rows // block_len

    def kernel(place_ref, members_ref, counts_ref, q_ref, kv_ref, more_ref, same_ref, diff_ref, q_sum, kv_sum, out):
        for r in range(blocks):
            added = more_ref[r, rows:, :].astype(jnp.float32)
            added = jnp.concatenate([added[:, :cols], added[:, cols:]], axis=0)
            q_sum[r] = (q_ref[r] + added).astype(jnp.bfloat16)
            both = (kv_ref[r] + more_ref[r, :rows, :].astype(jnp.float32)).astype(jnp.bfloat16)
            both = both.reshape(2, rows // 2, 2 * cols)
            for j in range(per_row):
                part = both[:, j * BS : (j + 1) * BS, :]
                kv_sum[r * per_row + j] = part.reshape(block_len, 2 * cols)
        column = lax.broadcasted_iota(jnp.int32, (block_len, MAXB * block_len), 1)
        for b in range(blocks):
            live = column < counts_ref[b] * block_len
            listed = [kv_sum.at[members_ref[b * MAXB + j]] for j in range(MAXB)]
            for h in range(cols // HD):
                at = slice(h * HD, (h + 1) * HD)
                at_v = slice(cols + h * HD, cols + (h + 1) * HD)
                keys = jnp.concatenate([block[:, at] for block in listed], axis=0)
                values = jnp.concatenate([block[:, at_v] for block in listed], axis=0)
                scores = lax.dot_general(
                    q_sum[b, :, at], keys, (((1,), (1,)), ((), ())), preferred_element_type=jnp.float32
                )
                scores = jnp.where(live, scores, -jnp.inf)
                raised = jnp.exp2((scores - jnp.max(scores, axis=-1, keepdims=True)) * EXP2_SCALE)
                weights = raised * (1.0 / jnp.sum(raised, axis=-1, keepdims=True))
                blended = jnp.dot(
                    weights.astype(jnp.bfloat16), values, preferred_element_type=jnp.float32
                )
                out[(b + place_ref[0]) % 2, b // 2, :, at] = blended.astype(jnp.bfloat16)
        same_ref[...] = out[0]
        diff_ref[...] = out[1]

    half = jax.ShapeDtypeStruct((blocks // 2, block_len, cols), jnp.bfloat16)
    return call(
        kernel,
        (half, half),
        [place, members, counts],
        [queries, keyvals, more],
        scratch=[
            pltpu.VMEM((blocks, block_len, cols), jnp.bfloat16),
            pltpu.VMEM((blocks * per_row, block_len, 2 * cols), jnp.bfloat16),
            pltpu.VMEM((2, blocks // 2, block_len, cols), jnp.bfloat16),
        ],
        flops=4 * blocks * block_len * MAXB * block_len * cols,
        read=16 * blocks * block_len * cols,
    )


def mix(place, attended, w_parts):
    blocks, block_len, _ = attended[0][0].shape
    widths = [a.shape[2] for a in attended[0]]
    cols, parts = sum(widths), len(widths)
    width = w_parts[0].shape[1]

    def kernel(place_ref, *refs):
        row, _, frame, core = (place_ref[i] for i in range(4))
        w_refs = refs[4 * parts : 4 * parts + 4]
        keep, over_x, over_z, over_both, a_all, sums = refs[4 * parts + 4 :]
        for s in range(4):
            for i, of_group in enumerate(widths):
                at = slice(sum(widths[:i]), sum(widths[: i + 1]))
                a_all[s, :, at] = refs[s * parts + i][...].reshape(blocks * block_len, of_group)

        def term(w_ref, side):
            first = a_all[(2 * side) ^ row]
            second = a_all[(2 * side + 1) ^ row]
            acc = jnp.dot(first, w_ref[:cols], preferred_element_type=jnp.float32)
            acc = acc + jnp.dot(second, w_ref[cols:], preferred_element_type=jnp.float32)
            return acc.astype(jnp.bfloat16).astype(jnp.float32)

        for c in range(2):
            total = term(w_refs[c], core) + term(w_refs[2 + c], 1 - core)
            sums[...] = total.reshape(blocks, 2, BS, width)
            at = (row + c) % 2
            keep[at] = sums[row // 2, frame]
            over_x[at] = sums[row // 2, 1 - frame].astype(jnp.bfloat16)
            over_z[at] = sums[1 - row // 2, frame].astype(jnp.bfloat16)
            over_both[at] = sums[1 - row // 2, 1 - frame].astype(jnp.bfloat16)

    shape = (2, BS, width)
    sent = jax.ShapeDtypeStruct(shape, jnp.bfloat16)
    return call(
        kernel,
        (jax.ShapeDtypeStruct(shape, jnp.float32), sent, sent, sent),
        [place],
        [*(a for of_row in attended for a in of_row), *w_parts],
        scratch=[
            pltpu.VMEM((4, blocks * block_len, cols), jnp.bfloat16),
            pltpu.VMEM((blocks, 2, BS, width), jnp.float32),
        ],
        flops=2 * blocks * block_len * 4 * cols * 2 * width,
        read=16 * cols * width,
    )


def finish(place, keep, from_x, from_z, from_both):
    halves, rows, width = keep.shape

    def kernel(place_ref, keep_ref, x_ref, z_ref, both_ref, out_ref):
        pair = place_ref[0] // 2
        for c in range(halves):
            near = pl.multiple_of((pair * halves + c) * width, width)
            far = pl.multiple_of(((1 - pair) * halves + c) * width, width)
            out_ref[:, pl.ds(near, width)] = (keep_ref[c] + x_ref[c].astype(jnp.float32)).astype(jnp.bfloat16)
            out_ref[:, pl.ds(far, width)] = (
                z_ref[c].astype(jnp.float32) + both_ref[c].astype(jnp.float32)
            ).astype(jnp.bfloat16)

    return call(
        kernel,
        jax.ShapeDtypeStruct((rows, 2 * halves * width), jnp.bfloat16),
        [place],
        [keep, from_x, from_z, from_both],
        read=16 * rows * halves * width,
    )


def by_heads(latents, w_qkv, w_out, win_blocks, win_counts, block_window):
    rows_n, heads_n = lax.axis_size("rows"), lax.axis_size("heads")
    group, row = lax.axis_index("groups"), lax.axis_index("rows")
    frame, core = lax.axis_index("frames"), lax.axis_index("heads")
    depth, _, local_cols = w_qkv.shape
    span = rows_n // heads_n
    cols = local_cols // span
    half = depth // 2
    place = jnp.stack([row, group, frame, core]).astype(jnp.int32)

    mine = [lax.dynamic_slice_in_dim(latents[0], core * span * depth, span * depth, axis=1)]
    mine += [swap(mine[0], "rows", s) for s in range(1, rows_n)]
    theirs = [swap(x, "frames") for x in mine]
    tokens = assemble(place, mine, theirs)

    tables = jnp.concatenate([win_blocks, win_counts[:, None], block_window[:, None]], axis=1)
    tables = after(tables, mine[1])
    found = [tables] + [swap(tables, "rows", s) for s in range(1, rows_n)]
    tables = jnp.stack(found)[row ^ jnp.arange(rows_n)].reshape(rows_n * heads_n, MAXB + 2)
    windows = lax.dynamic_index_in_dim(
        tables[:, MAXB + 1].reshape(rows_n, heads_n), core, axis=1, keepdims=False
    )
    picked = tables[windows]
    members, counts = picked[:, :MAXB].reshape(-1), picked[:, MAXB]

    across = swap(after(w_out, mine[1]), "heads")
    beside = swap(after(w_out, mine[3]), "rows")

    by_part = w_qkv.transpose(1, 0, 2)
    last = cols // (3 * HD) * HD
    waits = [[mine[1]], [mine[2]], [mine[3], theirs[0], members, counts], [theirs[1], across]]
    here, there = [], []
    for first, wide in ((0, cols - last), (cols - last, last)):
        for k in range(span):
            pairs = [
                (r * heads_n + h, (h * span + (k + r) % span) * heads_n + r // span)
                for r in range(rows_n)
                for h in range(heads_n)
            ]
            piece = lax.dynamic_slice(
                by_part, (0, group * half, (k + row) % span * cols + first), (3, half, wide)
            )
            piece = after(piece, *waits[len(here)], *here[-2:-1])
            here.append(lax.ppermute(piece, ("rows", "heads"), pairs))
    for i, piece in enumerate(here):
        there.append(swap(after(piece, tokens) if i == 2 else piece, "groups"))

    attended = [[] for _ in range(rows_n)]
    send = None
    for part in range(2):
        chunks = [[here[i], there[i]] for i in range(part * span, (part + 1) * span)]
        if part:
            chunks[-1][-1] = after(chunks[-1][-1], send)
        queries, keyvals, send = project(place, tokens, chunks)
        if part == 0:
            keyvals = after(keyvals, beside)
        else:
            keyvals = after(keyvals, attended[0][0])
        same, diff = attend_all(place, members, counts, queries, keyvals, swap(send, "heads"))
        for s in range(rows_n):
            attended[s].append(swap(same if s % 2 == 0 else diff, "rows", s) if s else same)

    keep, over_x, over_z, over_both = mix(
        place, attended, [w_out, beside, across, swap(beside, "heads")]
    )
    from_x = swap(over_x, "frames")
    from_z = swap(over_z, "rows", 2)
    from_both = lax.ppermute(
        over_both,
        ("rows", "frames"),
        [(2 * r + f, 2 * (r ^ 2) + 1 - f) for r in range(rows_n) for f in range(2)],
    )
    out = finish(place, keep, from_x, from_z, from_both)
    return out[None]


def local(latents, w_qkv, w_out, win_blocks, win_counts, block_window):
    rows_n = lax.axis_size("rows")
    pairs = all(lax.axis_size(axis) == 2 for axis in ("groups", "frames", "heads"))
    heads_here = w_qkv.shape[2] // HD
    if pairs and rows_n == 4 and heads_here % 2 == 0 and latents.shape[:2] == (1, 2 * BS):
        plan = by_heads
    else:
        plan = by_tokens
    return plan(latents, w_qkv, w_out, win_blocks, win_counts, block_window)


def solution(mesh):
    in_specs = (
        P(("groups", "frames"), "rows", None),
        P("rows", None, ("frames", "heads")),
        P(("frames", "heads"), "rows"),
        P(("groups", "rows"), None),
        P(("groups", "rows")),
        P(("groups", "rows")),
    )
    out_specs = P(("groups", "frames"), ("rows", "heads"), None)
    return jax.shard_map(local, mesh=mesh, in_specs=in_specs, out_specs=out_specs, check_vma=False)
```

```python
import math

import jax
import jax.numpy as jnp
from jax import lax
from jax.experimental import pallas as pl
from jax.experimental.pallas import tpu as pltpu
from jax.sharding import PartitionSpec as P

HD = 128
BS = 64
MAXB = 4
VMEM_BYTES = 24 * 1024 * 1024
WHOLE_VMEM_BYTES = 56 * 1024 * 1024
EXP2_SCALE = math.log2(math.e) / math.sqrt(HD)


def with_halo(value, sides, width):
    for axis, dim in sides:
        peers, length = (lax.axis_size(axis), value.shape[dim])
        up = [(i, (i + 1) % peers) for i in range(peers)]
        down = [(j, i) for i, j in up]
        last = lax.slice_in_dim(value, length - width, length, axis=dim)
        first = lax.slice_in_dim(value, 0, width, axis=dim)
        before = lax.ppermute(last, axis, up)
        after = lax.ppermute(first, axis, down)
        value = jnp.concatenate([before, value, after], axis=dim)
    return value


def by_tokens(latents, w_qkv, w_out, win_blocks, win_counts, block_window):
    rows_n = lax.axis_size("rows")
    shard_idx = lax.axis_index("rows")
    frames = latents.shape[0] * lax.axis_size("frames")
    tok_frame = latents.shape[1]
    model_width = latents.shape[2]
    local_cols = w_qkv.shape[2]
    per_shard = tok_frame // BS
    block_total = per_shard * rows_n
    heads_here = local_cols // HD
    block_len = frames * BS
    score_scale = 1.0 / math.sqrt(HD)
    gathered = lax.all_gather(latents, "frames", axis=0, tiled=True)
    flat_tokens = gathered.reshape(frames * tok_frame, model_width)
    weight_rows = lax.all_gather(w_qkv, "rows", axis=0, tiled=True)
    projected = jnp.dot(
        flat_tokens,
        weight_rows.reshape(weight_rows.shape[0], 3 * local_cols),
        preferred_element_type=jnp.float32,
    ).astype(jnp.bfloat16)
    blocked = projected.reshape(frames, per_shard, BS, 3, local_cols).transpose(1, 0, 2, 3, 4)
    blocked = blocked.reshape(per_shard, block_len, 3, local_cols)
    queries = blocked[:, :, 0]
    keyvals = blocked[:, :, 1:]
    nearby = with_halo(keyvals, (("rows", 0),), per_shard)
    first_block = shard_idx * per_shard
    owners = block_window - first_block
    members = win_blocks[owners]
    lengths = win_counts[owners]
    positions = (members - first_block + per_shard + block_total) % block_total

    def attend(query_rows, picked, live_mask):
        key_count = picked.shape[0]
        key_blocks = nearby[picked]
        key_part = key_blocks[:, :, 0].reshape(key_count * block_len, heads_here, HD)
        value_part = key_blocks[:, :, 1].reshape(key_count * block_len, heads_here, HD)
        scores = (
            jnp.einsum(
                "qhd,khd->hqk",
                query_rows.reshape(block_len, heads_here, HD),
                key_part,
                preferred_element_type=jnp.float32,
            )
            * score_scale
        )
        scores = jnp.where(live_mask[None, None, :], scores, -jnp.inf)
        row_max = jnp.max(scores, axis=-1, keepdims=True)
        raised = jnp.exp(scores - row_max)
        weights = (raised / jnp.sum(raised, axis=-1, keepdims=True)).astype(jnp.bfloat16)
        blended = jnp.einsum(
            "hqk,khd->qhd", weights, value_part, preferred_element_type=jnp.float32
        )
        return blended.reshape(block_len, local_cols).astype(jnp.bfloat16)

    def one_block(block_item):
        query_rows, picked, length = block_item
        live_mask = jnp.repeat(jnp.arange(MAXB) < length, block_len)
        return attend(query_rows, picked, live_mask)

    attended = lax.map(one_block, (queries, positions, lengths))
    ordered = attended.reshape(per_shard, frames, BS, local_cols).transpose(1, 0, 2, 3)
    ordered = ordered.reshape(frames * tok_frame, local_cols)
    w_full = lax.all_gather(w_out, "rows", axis=1, tiled=True)
    group_count = lax.axis_size(("frames", "heads"))
    out_rows = frames * tok_frame // group_count
    summed = lax.psum_scatter(
        jnp.dot(ordered, w_full, preferred_element_type=jnp.float32).astype(jnp.bfloat16),
        ("frames", "heads"),
        scatter_dimension=0,
        tiled=True,
    )
    return summed.reshape(1, out_rows, model_width)


def swap(value, axis, step=1):
    peers = lax.axis_size(axis)
    return lax.ppermute(value, axis, [(i, i ^ step) for i in range(peers)])


def after(value, *others):
    return lax.optimization_barrier((value, *others))[0]


def call(kernel, out_shape, prefetch, operands, scratch=(), flops=0, read=0, limit=VMEM_BYTES):
    return pl.pallas_call(
        kernel,
        out_shape=out_shape,
        grid_spec=pltpu.PrefetchScalarGridSpec(
            num_scalar_prefetch=len(prefetch),
            grid=(),
            in_specs=[pl.BlockSpec(memory_space=pltpu.VMEM)] * len(operands),
            out_specs=jax.tree.map(lambda _: pl.BlockSpec(memory_space=pltpu.VMEM), out_shape),
            scratch_shapes=scratch,
        ),
        compiler_params=pltpu.CompilerParams(vmem_limit_bytes=limit),
        cost_estimate=pl.CostEstimate(flops=flops, bytes_accessed=read, transcendentals=0),
    )(*prefetch, *operands)


def assemble(place, mine, theirs):
    count, width = mine[0].shape
    rows = len(mine)

    def kernel(place_ref, *refs):
        row, frame = place_ref[0], place_ref[2]
        for s in range(rows):
            refs[-1][row ^ s, frame] = refs[s][...]
            refs[-1][row ^ s, 1 - frame] = refs[rows + s][...]

    return call(
        kernel,
        jax.ShapeDtypeStruct((rows, 2, count, width), jnp.bfloat16),
        [place],
        [*mine, *theirs],
        read=8 * rows * count * width,
        limit=WHOLE_VMEM_BYTES,
    )


def project(place, tokens, chunks):
    rows, _, count, width = tokens.shape
    _, half, cols = chunks[0][0].shape
    slices = len(chunks)
    flat = [w for of_round in chunks for w in of_round]
    total_rows = rows * 2 * count

    def kernel(place_ref, x_ref, *refs):
        row, group, core = place_ref[0], place_ref[1], place_ref[3]
        w_refs = refs[: len(flat)]
        q_keep, kv_keep, send, total = refs[len(flat) :]
        acc = None
        for k in range(slices):
            for g in range(2):
                at = (row + slices - k) % slices * (2 * half) + (group + g) % 2 * half
                piece = x_ref[:, :, :, pl.ds(pl.multiple_of(at, half), half)].reshape(-1, half)
                w_ref = w_refs[2 * k + g]
                weight = jnp.concatenate([w_ref[part] for part in range(3)], axis=1)
                term = jnp.dot(piece, weight, preferred_element_type=jnp.float32)
                acc = term if acc is None else acc + term
        kv_part = acc[:, cols:].reshape(rows, 2 * count, 2 * cols)
        kv_keep[...] = kv_part
        send[:, : 2 * count, :] = kv_part.astype(jnp.bfloat16)
        total[...] = acc[:, :cols].reshape(rows, 2, count, cols)
        own = pl.multiple_of(core * BS, BS)
        other = pl.multiple_of((1 - core) * BS, BS)
        q_keep[...] = total[:, :, pl.ds(own, BS), :].reshape(q_keep.shape)
        for f in range(2):
            at = slice(f * cols, (f + 1) * cols)
            send[:, 2 * count :, at] = total[:, f, pl.ds(other, BS), :].astype(jnp.bfloat16)

    flops = 2 * total_rows * width * 3 * cols
    return call(
        kernel,
        (
            jax.ShapeDtypeStruct((rows, 2 * BS, cols), jnp.float32),
            jax.ShapeDtypeStruct((rows, 2 * count, 2 * cols), jnp.float32),
            jax.ShapeDtypeStruct((rows, 2 * count + BS, 2 * cols), jnp.bfloat16),
        ),
        [place],
        [tokens, *flat],
        scratch=[pltpu.VMEM((rows, 2, count, cols), jnp.float32)],
        flops=flops,
        read=flops // 300,
    )


def attend_all(place, members, counts, queries, keyvals, more):
    blocks, block_len, cols = queries.shape
    rows = keyvals.shape[1]
    per_row = rows // block_len

    def kernel(place_ref, members_ref, counts_ref, q_ref, kv_ref, more_ref, same_ref, diff_ref, q_sum, kv_sum, out):
        for r in range(blocks):
            added = more_ref[r, rows:, :].astype(jnp.float32)
            added = jnp.concatenate([added[:, :cols], added[:, cols:]], axis=0)
            q_sum[r] = (q_ref[r] + added).astype(jnp.bfloat16)
            both = (kv_ref[r] + more_ref[r, :rows, :].astype(jnp.float32)).astype(jnp.bfloat16)
            both = both.reshape(2, rows // 2, 2 * cols)
            for j in range(per_row):
                part = both[:, j * BS : (j + 1) * BS, :]
                kv_sum[r * per_row + j] = part.reshape(block_len, 2 * cols)
        column = lax.broadcasted_iota(jnp.int32, (block_len, MAXB * block_len), 1)
        for b in range(blocks):
            live = column < counts_ref[b] * block_len
            listed = [kv_sum.at[members_ref[b * MAXB + j]] for j in range(MAXB)]
            for h in range(cols // HD):
                at = slice(h * HD, (h + 1) * HD)
                at_v = slice(cols + h * HD, cols + (h + 1) * HD)
                keys = jnp.concatenate([block[:, at] for block in listed], axis=0)
                values = jnp.concatenate([block[:, at_v] for block in listed], axis=0)
                scores = lax.dot_general(
                    q_sum[b, :, at], keys, (((1,), (1,)), ((), ())), preferred_element_type=jnp.float32
                )
                scores = jnp.where(live, scores, -jnp.inf)
                raised = jnp.exp2((scores - jnp.max(scores, axis=-1, keepdims=True)) * EXP2_SCALE)
                weights = raised * (1.0 / jnp.sum(raised, axis=-1, keepdims=True))
                blended = jnp.dot(
                    weights.astype(jnp.bfloat16), values, preferred_element_type=jnp.float32
                )
                out[(b + place_ref[0]) % 2, b // 2, :, at] = blended.astype(jnp.bfloat16)
        same_ref[...] = out[0]
        diff_ref[...] = out[1]

    half = jax.ShapeDtypeStruct((blocks // 2, block_len, cols), jnp.bfloat16)
    return call(
        kernel,
        (half, half),
        [place, members, counts],
        [queries, keyvals, more],
        scratch=[
            pltpu.VMEM((blocks, block_len, cols), jnp.bfloat16),
            pltpu.VMEM((blocks * per_row, block_len, 2 * cols), jnp.bfloat16),
            pltpu.VMEM((2, blocks // 2, block_len, cols), jnp.bfloat16),
        ],
        flops=4 * blocks * block_len * MAXB * block_len * cols,
        read=16 * blocks * block_len * cols,
    )


def mix(place, attended, w_parts):
    blocks, block_len, _ = attended[0][0].shape
    widths = [a.shape[2] for a in attended[0]]
    cols, parts = sum(widths), len(widths)
    width = w_parts[0].shape[1]

    def kernel(place_ref, *refs):
        row, _, frame, core = (place_ref[i] for i in range(4))
        w_refs = refs[4 * parts : 4 * parts + 4]
        keep, over_x, over_z, over_both, a_all, sums = refs[4 * parts + 4 :]
        for s in range(4):
            for i, of_group in enumerate(widths):
                at = slice(sum(widths[:i]), sum(widths[: i + 1]))
                a_all[s, :, at] = refs[s * parts + i][...].reshape(blocks * block_len, of_group)

        def term(w_ref, side):
            first = a_all[(2 * side) ^ row]
            second = a_all[(2 * side + 1) ^ row]
            acc = jnp.dot(first, w_ref[:cols], preferred_element_type=jnp.float32)
            acc = acc + jnp.dot(second, w_ref[cols:], preferred_element_type=jnp.float32)
            return acc.astype(jnp.bfloat16).astype(jnp.float32)

        for c in range(2):
            total = term(w_refs[c], core) + term(w_refs[2 + c], 1 - core)
            sums[...] = total.reshape(blocks, 2, BS, width)
            at = (row + c) % 2
            keep[at] = sums[row // 2, frame]
            over_x[at] = sums[row // 2, 1 - frame].astype(jnp.bfloat16)
            over_z[at] = sums[1 - row // 2, frame].astype(jnp.bfloat16)
            over_both[at] = sums[1 - row // 2, 1 - frame].astype(jnp.bfloat16)

    shape = (2, BS, width)
    sent = jax.ShapeDtypeStruct(shape, jnp.bfloat16)
    return call(
        kernel,
        (jax.ShapeDtypeStruct(shape, jnp.float32), sent, sent, sent),
        [place],
        [*(a for of_row in attended for a in of_row), *w_parts],
        scratch=[
            pltpu.VMEM((4, blocks * block_len, cols), jnp.bfloat16),
            pltpu.VMEM((blocks, 2, BS, width), jnp.float32),
        ],
        flops=2 * blocks * block_len * 4 * cols * 2 * width,
        read=16 * cols * width,
    )


def finish(place, keep, from_x, from_z, from_both):
    halves, rows, width = keep.shape

    def kernel(place_ref, keep_ref, x_ref, z_ref, both_ref, out_ref):
        pair = place_ref[0] // 2
        for c in range(halves):
            near = pl.multiple_of((pair * halves + c) * width, width)
            far = pl.multiple_of(((1 - pair) * halves + c) * width, width)
            out_ref[:, pl.ds(near, width)] = (keep_ref[c] + x_ref[c].astype(jnp.float32)).astype(jnp.bfloat16)
            out_ref[:, pl.ds(far, width)] = (
                z_ref[c].astype(jnp.float32) + both_ref[c].astype(jnp.float32)
            ).astype(jnp.bfloat16)

    return call(
        kernel,
        jax.ShapeDtypeStruct((rows, 2 * halves * width), jnp.bfloat16),
        [place],
        [keep, from_x, from_z, from_both],
        read=16 * rows * halves * width,
    )


def by_heads(latents, w_qkv, w_out, win_blocks, win_counts, block_window):
    rows_n, heads_n = lax.axis_size("rows"), lax.axis_size("heads")
    group, row = lax.axis_index("groups"), lax.axis_index("rows")
    frame, core = lax.axis_index("frames"), lax.axis_index("heads")
    depth, _, local_cols = w_qkv.shape
    span = rows_n // heads_n
    cols = local_cols // span
    half = depth // 2
    place = jnp.stack([row, group, frame, core]).astype(jnp.int32)

    tables = jnp.concatenate([win_blocks, win_counts[:, None], block_window[:, None]], axis=1)
    found = [tables] + [swap(tables, "rows", s) for s in range(1, rows_n)]
    tables = jnp.stack(found)[row ^ jnp.arange(rows_n)].reshape(rows_n * heads_n, MAXB + 2)
    windows = lax.dynamic_index_in_dim(
        tables[:, MAXB + 1].reshape(rows_n, heads_n), core, axis=1, keepdims=False
    )
    picked = tables[windows]
    members, counts = picked[:, :MAXB].reshape(-1), picked[:, MAXB]

    mine = [lax.dynamic_slice_in_dim(latents[0], core * span * depth, span * depth, axis=1)]
    mine = [after(mine[0], members, counts)]
    mine += [swap(mine[0], "rows", s) for s in range(1, rows_n)]
    theirs = [swap(x, "frames") for x in mine]
    tokens = assemble(place, mine, theirs)

    across = swap(after(w_out, mine[1]), "heads")
    beside = swap(after(w_out, mine[3]), "rows")

    by_part = w_qkv.transpose(1, 0, 2)
    last = cols // (3 * HD) * HD
    waits = [[mine[1]], [mine[2]], [mine[3], theirs[0]], [theirs[1], across]]
    here, there = [], []
    for first, wide in ((0, cols - last), (cols - last, last)):
        for k in range(span):
            pairs = [
                (r * heads_n + h, (h * span + (k + r) % span) * heads_n + r // span)
                for r in range(rows_n)
                for h in range(heads_n)
            ]
            piece = lax.dynamic_slice(
                by_part, (0, group * half, (k + row) % span * cols + first), (3, half, wide)
            )
            piece = after(piece, *waits[len(here)], *here[-2:-1])
            here.append(lax.ppermute(piece, ("rows", "heads"), pairs))
    for i, piece in enumerate(here):
        there.append(swap(after(piece, tokens) if i == 2 else piece, "groups"))

    attended = [[] for _ in range(rows_n)]
    send = None
    for part in range(2):
        chunks = [[here[i], there[i]] for i in range(part * span, (part + 1) * span)]
        if part:
            chunks[-1][-1] = after(chunks[-1][-1], send)
        queries, keyvals, send = project(place, tokens, chunks)
        if part == 0:
            keyvals = after(keyvals, beside)
        else:
            keyvals = after(keyvals, attended[0][0])
        same, diff = attend_all(place, members, counts, queries, keyvals, swap(send, "heads"))
        for s in range(rows_n):
            attended[s].append(swap(same if s % 2 == 0 else diff, "rows", s) if s else same)

    keep, over_x, over_z, over_both = mix(
        place, attended, [w_out, beside, across, swap(beside, "heads")]
    )
    from_x = swap(over_x, "frames")
    from_z = swap(over_z, "rows", 2)
    from_both = lax.ppermute(
        over_both,
        ("rows", "frames"),
        [(2 * r + f, 2 * (r ^ 2) + 1 - f) for r in range(rows_n) for f in range(2)],
    )
    out = finish(place, keep, from_x, from_z, from_both)
    return out[None]


def local(latents, w_qkv, w_out, win_blocks, win_counts, block_window):
    rows_n = lax.axis_size("rows")
    pairs = all(lax.axis_size(axis) == 2 for axis in ("groups", "frames", "heads"))
    heads_here = w_qkv.shape[2] // HD
    if pairs and rows_n == 4 and heads_here % 2 == 0 and latents.shape[:2] == (1, 2 * BS):
        plan = by_heads
    else:
        plan = by_tokens
    return plan(latents, w_qkv, w_out, win_blocks, win_counts, block_window)


def solution(mesh):
    in_specs = (
        P(("groups", "frames"), "rows", None),
        P("rows", None, ("frames", "heads")),
        P(("frames", "heads"), "rows"),
        P(("groups", "rows"), None),
        P(("groups", "rows")),
        P(("groups", "rows")),
    )
    out_specs = P(("groups", "frames"), ("rows", "heads"), None)
    return jax.shard_map(local, mesh=mesh, in_specs=in_specs, out_specs=out_specs, check_vma=False)
```

```python
import math

import jax
import jax.numpy as jnp
from jax import lax
from jax.experimental import pallas as pl
from jax.experimental.pallas import tpu as pltpu
from jax.sharding import PartitionSpec as P

HD = 128
BS = 64
MAXB = 4
VMEM_BYTES = 24 * 1024 * 1024
WHOLE_VMEM_BYTES = 56 * 1024 * 1024
EXP2_SCALE = math.log2(math.e) / math.sqrt(HD)


def with_halo(value, sides, width):
    for axis, dim in sides:
        peers, length = (lax.axis_size(axis), value.shape[dim])
        up = [(i, (i + 1) % peers) for i in range(peers)]
        down = [(j, i) for i, j in up]
        last = lax.slice_in_dim(value, length - width, length, axis=dim)
        first = lax.slice_in_dim(value, 0, width, axis=dim)
        before = lax.ppermute(last, axis, up)
        after = lax.ppermute(first, axis, down)
        value = jnp.concatenate([before, value, after], axis=dim)
    return value


def by_tokens(latents, w_qkv, w_out, win_blocks, win_counts, block_window):
    rows_n = lax.axis_size("rows")
    shard_idx = lax.axis_index("rows")
    frames = latents.shape[0] * lax.axis_size("frames")
    tok_frame = latents.shape[1]
    model_width = latents.shape[2]
    local_cols = w_qkv.shape[2]
    per_shard = tok_frame // BS
    block_total = per_shard * rows_n
    heads_here = local_cols // HD
    block_len = frames * BS
    score_scale = 1.0 / math.sqrt(HD)
    gathered = lax.all_gather(latents, "frames", axis=0, tiled=True)
    flat_tokens = gathered.reshape(frames * tok_frame, model_width)
    weight_rows = lax.all_gather(w_qkv, "rows", axis=0, tiled=True)
    projected = jnp.dot(
        flat_tokens,
        weight_rows.reshape(weight_rows.shape[0], 3 * local_cols),
        preferred_element_type=jnp.float32,
    ).astype(jnp.bfloat16)
    blocked = projected.reshape(frames, per_shard, BS, 3, local_cols).transpose(1, 0, 2, 3, 4)
    blocked = blocked.reshape(per_shard, block_len, 3, local_cols)
    queries = blocked[:, :, 0]
    keyvals = blocked[:, :, 1:]
    nearby = with_halo(keyvals, (("rows", 0),), per_shard)
    first_block = shard_idx * per_shard
    owners = block_window - first_block
    members = win_blocks[owners]
    lengths = win_counts[owners]
    positions = (members - first_block + per_shard + block_total) % block_total

    def attend(query_rows, picked, live_mask):
        key_count = picked.shape[0]
        key_blocks = nearby[picked]
        key_part = key_blocks[:, :, 0].reshape(key_count * block_len, heads_here, HD)
        value_part = key_blocks[:, :, 1].reshape(key_count * block_len, heads_here, HD)
        scores = (
            jnp.einsum(
                "qhd,khd->hqk",
                query_rows.reshape(block_len, heads_here, HD),
                key_part,
                preferred_element_type=jnp.float32,
            )
            * score_scale
        )
        scores = jnp.where(live_mask[None, None, :], scores, -jnp.inf)
        row_max = jnp.max(scores, axis=-1, keepdims=True)
        raised = jnp.exp(scores - row_max)
        weights = (raised / jnp.sum(raised, axis=-1, keepdims=True)).astype(jnp.bfloat16)
        blended = jnp.einsum(
            "hqk,khd->qhd", weights, value_part, preferred_element_type=jnp.float32
        )
        return blended.reshape(block_len, local_cols).astype(jnp.bfloat16)

    def one_block(block_item):
        query_rows, picked, length = block_item
        live_mask = jnp.repeat(jnp.arange(MAXB) < length, block_len)
        return attend(query_rows, picked, live_mask)

    attended = lax.map(one_block, (queries, positions, lengths))
    ordered = attended.reshape(per_shard, frames, BS, local_cols).transpose(1, 0, 2, 3)
    ordered = ordered.reshape(frames * tok_frame, local_cols)
    w_full = lax.all_gather(w_out, "rows", axis=1, tiled=True)
    group_count = lax.axis_size(("frames", "heads"))
    out_rows = frames * tok_frame // group_count
    summed = lax.psum_scatter(
        jnp.dot(ordered, w_full, preferred_element_type=jnp.float32).astype(jnp.bfloat16),
        ("frames", "heads"),
        scatter_dimension=0,
        tiled=True,
    )
    return summed.reshape(1, out_rows, model_width)


def swap(value, axis, step=1):
    peers = lax.axis_size(axis)
    return lax.ppermute(value, axis, [(i, i ^ step) for i in range(peers)])


def after(value, *others):
    return lax.optimization_barrier((value, *others))[0]


def call(kernel, out_shape, prefetch, operands, scratch=(), flops=0, read=0, limit=VMEM_BYTES):
    return pl.pallas_call(
        kernel,
        out_shape=out_shape,
        grid_spec=pltpu.PrefetchScalarGridSpec(
            num_scalar_prefetch=len(prefetch),
            grid=(),
            in_specs=[pl.BlockSpec(memory_space=pltpu.VMEM)] * len(operands),
            out_specs=jax.tree.map(lambda _: pl.BlockSpec(memory_space=pltpu.VMEM), out_shape),
            scratch_shapes=scratch,
        ),
        compiler_params=pltpu.CompilerParams(vmem_limit_bytes=limit),
        cost_estimate=pl.CostEstimate(flops=flops, bytes_accessed=read, transcendentals=0),
    )(*prefetch, *operands)


def assemble(place, near, inward, outward):
    count, width = near[0][0].shape
    pieces = [x for pair in near + inward + outward for x in pair]

    def kernel(place_ref, *refs):
        row, frame = place_ref[0], place_ref[2]
        out_ref = refs[-1]

        def put(first, steps):
            for i, s in enumerate(steps):
                for f in range(2):
                    out_ref[row ^ s, (frame + f) % 2] = refs[2 * (first + i) + f][...]

        middle = (row == 1) | (row == 2)
        put(0, (0, 1))
        pl.when(middle)(lambda: put(2, (3, 2)))
        pl.when(jnp.logical_not(middle))(lambda: put(4, (2, 3)))

    return call(
        kernel,
        jax.ShapeDtypeStruct((4, 2, count, width), jnp.bfloat16),
        [place],
        pieces,
        read=40 * count * width,
        limit=WHOLE_VMEM_BYTES,
    )


def project(place, tokens, chunks):
    rows, _, count, width = tokens.shape
    _, half, cols = chunks[0][0].shape
    slices = len(chunks)
    flat = [w for of_round in chunks for w in of_round]
    total_rows = rows * 2 * count

    def kernel(place_ref, x_ref, *refs):
        row, group, core = place_ref[0], place_ref[1], place_ref[3]
        w_refs = refs[: len(flat)]
        q_keep, kv_keep, send, total = refs[len(flat) :]
        acc = None
        for k in range(slices):
            for g in range(2):
                at = (row + slices - k) % slices * (2 * half) + (group + g) % 2 * half
                piece = x_ref[:, :, :, pl.ds(pl.multiple_of(at, half), half)].reshape(-1, half)
                w_ref = w_refs[2 * k + g]
                weight = jnp.concatenate([w_ref[part] for part in range(3)], axis=1)
                term = jnp.dot(piece, weight, preferred_element_type=jnp.float32)
                acc = term if acc is None else acc + term
        kv_part = acc[:, cols:].reshape(rows, 2 * count, 2 * cols)
        kv_keep[...] = kv_part
        send[:, : 2 * count, :] = kv_part.astype(jnp.bfloat16)
        total[...] = acc[:, :cols].reshape(rows, 2, count, cols)
        own = pl.multiple_of(core * BS, BS)
        other = pl.multiple_of((1 - core) * BS, BS)
        q_keep[...] = total[:, :, pl.ds(own, BS), :].reshape(q_keep.shape)
        for f in range(2):
            at = slice(f * cols, (f + 1) * cols)
            send[:, 2 * count :, at] = total[:, f, pl.ds(other, BS), :].astype(jnp.bfloat16)

    flops = 2 * total_rows * width * 3 * cols
    return call(
        kernel,
        (
            jax.ShapeDtypeStruct((rows, 2 * BS, cols), jnp.float32),
            jax.ShapeDtypeStruct((rows, 2 * count, 2 * cols), jnp.float32),
            jax.ShapeDtypeStruct((rows, 2 * count + BS, 2 * cols), jnp.bfloat16),
        ),
        [place],
        [tokens, *flat],
        scratch=[pltpu.VMEM((rows, 2, count, cols), jnp.float32)],
        flops=flops,
        read=flops // 300,
    )


def attend_all(place, members, counts, queries, keyvals, more):
    blocks, block_len, cols = queries.shape
    rows = keyvals.shape[1]
    per_row = rows // block_len

    def kernel(place_ref, members_ref, counts_ref, q_ref, kv_ref, more_ref, same_ref, diff_ref, q_sum, kv_sum, out):
        for r in range(blocks):
            added = more_ref[r, rows:, :].astype(jnp.float32)
            added = jnp.concatenate([added[:, :cols], added[:, cols:]], axis=0)
            q_sum[r] = (q_ref[r] + added).astype(jnp.bfloat16)
            both = (kv_ref[r] + more_ref[r, :rows, :].astype(jnp.float32)).astype(jnp.bfloat16)
            both = both.reshape(2, rows // 2, 2 * cols)
            for j in range(per_row):
                part = both[:, j * BS : (j + 1) * BS, :]
                kv_sum[r * per_row + j] = part.reshape(block_len, 2 * cols)
        column = lax.broadcasted_iota(jnp.int32, (block_len, MAXB * block_len), 1)
        for b in range(blocks):
            live = column < counts_ref[b] * block_len
            listed = [kv_sum.at[members_ref[b * MAXB + j]] for j in range(MAXB)]
            for h in range(cols // HD):
                at = slice(h * HD, (h + 1) * HD)
                at_v = slice(cols + h * HD, cols + (h + 1) * HD)
                keys = jnp.concatenate([block[:, at] for block in listed], axis=0)
                values = jnp.concatenate([block[:, at_v] for block in listed], axis=0)
                scores = lax.dot_general(
                    q_sum[b, :, at], keys, (((1,), (1,)), ((), ())), preferred_element_type=jnp.float32
                )
                scores = jnp.where(live, scores, -jnp.inf)
                raised = jnp.exp2((scores - jnp.max(scores, axis=-1, keepdims=True)) * EXP2_SCALE)
                weights = raised * (1.0 / jnp.sum(raised, axis=-1, keepdims=True))
                blended = jnp.dot(
                    weights.astype(jnp.bfloat16), values, preferred_element_type=jnp.float32
                )
                out[(b + place_ref[0]) % 2, b // 2, :, at] = blended.astype(jnp.bfloat16)
        same_ref[...] = out[0]
        diff_ref[...] = out[1]

    half = jax.ShapeDtypeStruct((blocks // 2, block_len, cols), jnp.bfloat16)
    return call(
        kernel,
        (half, half),
        [place, members, counts],
        [queries, keyvals, more],
        scratch=[
            pltpu.VMEM((blocks, block_len, cols), jnp.bfloat16),
            pltpu.VMEM((blocks * per_row, block_len, 2 * cols), jnp.bfloat16),
            pltpu.VMEM((2, blocks // 2, block_len, cols), jnp.bfloat16),
        ],
        flops=4 * blocks * block_len * MAXB * block_len * cols,
        read=16 * blocks * block_len * cols,
    )


def mix(place, attended, w_parts):
    blocks, block_len, _ = attended[0][0].shape
    widths = [a.shape[2] for a in attended[0]]
    cols, parts = sum(widths), len(widths)
    width = w_parts[0].shape[1]

    def kernel(place_ref, *refs):
        row, _, frame, core = (place_ref[i] for i in range(4))
        w_refs = refs[4 * parts : 4 * parts + 4]
        keep, over_x, over_z, over_both, a_all, sums = refs[4 * parts + 4 :]
        for s in range(4):
            for i, of_group in enumerate(widths):
                at = slice(sum(widths[:i]), sum(widths[: i + 1]))
                a_all[s, :, at] = refs[s * parts + i][...].reshape(blocks * block_len, of_group)

        def term(w_ref, side):
            first = a_all[(2 * side) ^ row]
            second = a_all[(2 * side + 1) ^ row]
            acc = jnp.dot(first, w_ref[:cols], preferred_element_type=jnp.float32)
            acc = acc + jnp.dot(second, w_ref[cols:], preferred_element_type=jnp.float32)
            return acc.astype(jnp.bfloat16).astype(jnp.float32)

        for c in range(2):
            total = term(w_refs[c], core) + term(w_refs[2 + c], 1 - core)
            sums[...] = total.reshape(blocks, 2, BS, width)
            at = (row + c) % 2
            keep[at] = sums[row // 2, frame]
            over_x[at] = sums[row // 2, 1 - frame].astype(jnp.bfloat16)
            over_z[at] = sums[1 - row // 2, frame].astype(jnp.bfloat16)
            over_both[at] = sums[1 - row // 2, 1 - frame].astype(jnp.bfloat16)

    shape = (2, BS, width)
    sent = jax.ShapeDtypeStruct(shape, jnp.bfloat16)
    return call(
        kernel,
        (jax.ShapeDtypeStruct(shape, jnp.float32), sent, sent, sent),
        [place],
        [*(a for of_row in attended for a in of_row), *w_parts],
        scratch=[
            pltpu.VMEM((4, blocks * block_len, cols), jnp.bfloat16),
            pltpu.VMEM((blocks, 2, BS, width), jnp.float32),
        ],
        flops=2 * blocks * block_len * 4 * cols * 2 * width,
        read=16 * cols * width,
    )


def finish(place, keep, from_x, from_z, from_both):
    halves, rows, width = keep.shape

    def kernel(place_ref, keep_ref, x_ref, z_ref, both_ref, out_ref):
        pair = place_ref[0] // 2
        for c in range(halves):
            near = pl.multiple_of((pair * halves + c) * width, width)
            far = pl.multiple_of(((1 - pair) * halves + c) * width, width)
            out_ref[:, pl.ds(near, width)] = (keep_ref[c] + x_ref[c].astype(jnp.float32)).astype(jnp.bfloat16)
            out_ref[:, pl.ds(far, width)] = (
                z_ref[c].astype(jnp.float32) + both_ref[c].astype(jnp.float32)
            ).astype(jnp.bfloat16)

    return call(
        kernel,
        jax.ShapeDtypeStruct((rows, 2 * halves * width), jnp.bfloat16),
        [place],
        [keep, from_x, from_z, from_both],
        read=16 * rows * halves * width,
    )


def by_heads(latents, w_qkv, w_out, win_blocks, win_counts, block_window):
    rows_n, heads_n = lax.axis_size("rows"), lax.axis_size("heads")
    group, row = lax.axis_index("groups"), lax.axis_index("rows")
    frame, core = lax.axis_index("frames"), lax.axis_index("heads")
    depth, _, local_cols = w_qkv.shape
    span = rows_n // heads_n
    cols = local_cols // span
    half = depth // 2
    place = jnp.stack([row, group, frame, core]).astype(jnp.int32)

    mine = lax.dynamic_slice_in_dim(latents[0], core * span * depth, span * depth, axis=1)

    def over_frames(value, rows):
        pairs = [(2 * r + f, 2 * r + 1 - f) for r in rows for f in range(2)]
        return lax.ppermute(value, ("rows", "frames"), pairs)

    mine_x = swap(mine, "frames")
    beside_1 = swap(mine, "rows")
    in_1 = lax.ppermute(mine, "rows", [(1, 2), (2, 1)])
    beside_1x = swap(beside_1, "frames")
    in_2 = lax.ppermute(after(beside_1, in_1), "rows", [(1, 2), (2, 1)])
    out_1 = lax.ppermute(in_1, "rows", [(1, 0), (2, 3)])
    in_1x = over_frames(in_1, (1, 2))
    out_2 = lax.ppermute(in_2, "rows", [(1, 0), (2, 3)])
    in_2x = over_frames(in_2, (1, 2))
    out_1x = over_frames(out_1, (0, 3))
    out_2x = over_frames(out_2, (0, 3))
    tokens = assemble(
        place,
        [(mine, mine_x), (beside_1, beside_1x)],
        [(in_1, in_1x), (in_2, in_2x)],
        [(out_1, out_1x), (out_2, out_2x)],
    )

    by_part = w_qkv.transpose(1, 0, 2)
    last = cols // (3 * HD) * HD
    waits = [[beside_1, in_1, mine_x], [in_2, beside_1x], [out_1, in_1x], [out_2, in_2x, out_1x]]
    here, there = [], []
    for first, wide in ((0, cols - last), (cols - last, last)):
        for k in range(span):
            pairs = [
                (r * heads_n + h, (h * span + (k + r) % span) * heads_n + r // span)
                for r in range(rows_n)
                for h in range(heads_n)
            ]
            piece = lax.dynamic_slice(
                by_part, (0, group * half, (k + row) % span * cols + first), (3, half, wide)
            )
            piece = after(piece, *waits[len(here)], *here[-2:-1], *there[-3:-2])
            here.append(lax.ppermute(piece, ("rows", "heads"), pairs))
            there.append(swap(here[-1], "groups"))
    across = swap(after(w_out, here[0]), "heads")
    beside = swap(after(w_out, here[1]), "rows")

    tables = jnp.concatenate([win_blocks, win_counts[:, None], block_window[:, None]], axis=1)
    tables = after(tables, here[0])
    found = [tables] + [swap(tables, "rows", s) for s in range(1, rows_n)]
    tables = jnp.stack(found)[row ^ jnp.arange(rows_n)].reshape(rows_n * heads_n, MAXB + 2)
    windows = lax.dynamic_index_in_dim(
        tables[:, MAXB + 1].reshape(rows_n, heads_n), core, axis=1, keepdims=False
    )
    picked = tables[windows]
    members, counts = picked[:, :MAXB].reshape(-1), picked[:, MAXB]

    attended = [[] for _ in range(rows_n)]
    send = None
    for part in range(2):
        chunks = [[here[i], there[i]] for i in range(part * span, (part + 1) * span)]
        if part:
            chunks[-1][-1] = after(chunks[-1][-1], send)
        else:
            chunks[-1][-1] = after(chunks[-1][-1], there[2], members, counts)
        queries, keyvals, send = project(place, tokens, chunks)
        if part:
            keyvals = after(keyvals, attended[0][0], beside)
        same, diff = attend_all(place, members, counts, queries, keyvals, swap(send, "heads"))
        for s in range(rows_n):
            attended[s].append(swap(same if s % 2 == 0 else diff, "rows", s) if s else same)

    keep, over_x, over_z, over_both = mix(
        place, attended, [w_out, beside, across, swap(beside, "heads")]
    )
    from_x = swap(over_x, "frames")
    from_z = swap(over_z, "rows", 2)
    from_both = lax.ppermute(
        over_both,
        ("rows", "frames"),
        [(2 * r + f, 2 * (r ^ 2) + 1 - f) for r in range(rows_n) for f in range(2)],
    )
    out = finish(place, keep, from_x, from_z, from_both)
    return out[None]


def local(latents, w_qkv, w_out, win_blocks, win_counts, block_window):
    rows_n = lax.axis_size("rows")
    pairs = all(lax.axis_size(axis) == 2 for axis in ("groups", "frames", "heads"))
    heads_here = w_qkv.shape[2] // HD
    if pairs and rows_n == 4 and heads_here % 2 == 0 and latents.shape[:2] == (1, 2 * BS):
        plan = by_heads
    else:
        plan = by_tokens
    return plan(latents, w_qkv, w_out, win_blocks, win_counts, block_window)


def solution(mesh):
    in_specs = (
        P(("groups", "frames"), "rows", None),
        P("rows", None, ("frames", "heads")),
        P(("frames", "heads"), "rows"),
        P(("groups", "rows"), None),
        P(("groups", "rows")),
        P(("groups", "rows")),
    )
    out_specs = P(("groups", "frames"), ("rows", "heads"), None)
    return jax.shard_map(local, mesh=mesh, in_specs=in_specs, out_specs=out_specs, check_vma=False)
```

```python
import math

import jax
import jax.numpy as jnp
from jax import lax
from jax.experimental import pallas as pl
from jax.experimental.pallas import tpu as pltpu
from jax.sharding import PartitionSpec as P

HD = 128
BS = 64
MAXB = 4
VMEM_BYTES = 24 * 1024 * 1024
WHOLE_VMEM_BYTES = 56 * 1024 * 1024
EXP2_SCALE = math.log2(math.e) / math.sqrt(HD)


def with_halo(value, sides, width):
    for axis, dim in sides:
        peers, length = (lax.axis_size(axis), value.shape[dim])
        up = [(i, (i + 1) % peers) for i in range(peers)]
        down = [(j, i) for i, j in up]
        last = lax.slice_in_dim(value, length - width, length, axis=dim)
        first = lax.slice_in_dim(value, 0, width, axis=dim)
        before = lax.ppermute(last, axis, up)
        after = lax.ppermute(first, axis, down)
        value = jnp.concatenate([before, value, after], axis=dim)
    return value


def by_tokens(latents, w_qkv, w_out, win_blocks, win_counts, block_window):
    rows_n = lax.axis_size("rows")
    shard_idx = lax.axis_index("rows")
    frames = latents.shape[0] * lax.axis_size("frames")
    tok_frame = latents.shape[1]
    model_width = latents.shape[2]
    local_cols = w_qkv.shape[2]
    per_shard = tok_frame // BS
    block_total = per_shard * rows_n
    heads_here = local_cols // HD
    block_len = frames * BS
    score_scale = 1.0 / math.sqrt(HD)
    gathered = lax.all_gather(latents, "frames", axis=0, tiled=True)
    flat_tokens = gathered.reshape(frames * tok_frame, model_width)
    weight_rows = lax.all_gather(w_qkv, "rows", axis=0, tiled=True)
    projected = jnp.dot(
        flat_tokens,
        weight_rows.reshape(weight_rows.shape[0], 3 * local_cols),
        preferred_element_type=jnp.float32,
    ).astype(jnp.bfloat16)
    blocked = projected.reshape(frames, per_shard, BS, 3, local_cols).transpose(1, 0, 2, 3, 4)
    blocked = blocked.reshape(per_shard, block_len, 3, local_cols)
    queries = blocked[:, :, 0]
    keyvals = blocked[:, :, 1:]
    nearby = with_halo(keyvals, (("rows", 0),), per_shard)
    first_block = shard_idx * per_shard
    owners = block_window - first_block
    members = win_blocks[owners]
    lengths = win_counts[owners]
    positions = (members - first_block + per_shard + block_total) % block_total

    def attend(query_rows, picked, live_mask):
        key_count = picked.shape[0]
        key_blocks = nearby[picked]
        key_part = key_blocks[:, :, 0].reshape(key_count * block_len, heads_here, HD)
        value_part = key_blocks[:, :, 1].reshape(key_count * block_len, heads_here, HD)
        scores = (
            jnp.einsum(
                "qhd,khd->hqk",
                query_rows.reshape(block_len, heads_here, HD),
                key_part,
                preferred_element_type=jnp.float32,
            )
            * score_scale
        )
        scores = jnp.where(live_mask[None, None, :], scores, -jnp.inf)
        row_max = jnp.max(scores, axis=-1, keepdims=True)
        raised = jnp.exp(scores - row_max)
        weights = (raised / jnp.sum(raised, axis=-1, keepdims=True)).astype(jnp.bfloat16)
        blended = jnp.einsum(
            "hqk,khd->qhd", weights, value_part, preferred_element_type=jnp.float32
        )
        return blended.reshape(block_len, local_cols).astype(jnp.bfloat16)

    def one_block(block_item):
        query_rows, picked, length = block_item
        live_mask = jnp.repeat(jnp.arange(MAXB) < length, block_len)
        return attend(query_rows, picked, live_mask)

    attended = lax.map(one_block, (queries, positions, lengths))
    ordered = attended.reshape(per_shard, frames, BS, local_cols).transpose(1, 0, 2, 3)
    ordered = ordered.reshape(frames * tok_frame, local_cols)
    w_full = lax.all_gather(w_out, "rows", axis=1, tiled=True)
    group_count = lax.axis_size(("frames", "heads"))
    out_rows = frames * tok_frame // group_count
    summed = lax.psum_scatter(
        jnp.dot(ordered, w_full, preferred_element_type=jnp.float32).astype(jnp.bfloat16),
        ("frames", "heads"),
        scatter_dimension=0,
        tiled=True,
    )
    return summed.reshape(1, out_rows, model_width)


def swap(value, axis, step=1):
    peers = lax.axis_size(axis)
    return lax.ppermute(value, axis, [(i, i ^ step) for i in range(peers)])


def settle(*values):
    return lax.optimization_barrier(values)


def call(kernel, out_shape, prefetch, operands, scratch=(), flops=0, read=0, limit=VMEM_BYTES):
    return pl.pallas_call(
        kernel,
        out_shape=out_shape,
        grid_spec=pltpu.PrefetchScalarGridSpec(
            num_scalar_prefetch=len(prefetch),
            grid=(),
            in_specs=[pl.BlockSpec(memory_space=pltpu.VMEM)] * len(operands),
            out_specs=jax.tree.map(lambda _: pl.BlockSpec(memory_space=pltpu.VMEM), out_shape),
            scratch_shapes=scratch,
        ),
        compiler_params=pltpu.CompilerParams(vmem_limit_bytes=limit),
        cost_estimate=pl.CostEstimate(flops=flops, bytes_accessed=read, transcendentals=0),
    )(*prefetch, *operands)


def assemble(place, near, inward, outward):
    count, width = near[0][0].shape
    pieces = [x for pair in near + inward + outward for x in pair]

    def kernel(place_ref, *refs):
        row, frame = place_ref[0], place_ref[2]
        out_ref = refs[-1]

        def put(first, steps):
            for i, s in enumerate(steps):
                for f in range(2):
                    out_ref[row ^ s, (frame + f) % 2] = refs[2 * (first + i) + f][...]

        middle = (row == 1) | (row == 2)
        put(0, (0, 1))
        pl.when(middle)(lambda: put(2, (3, 2)))
        pl.when(jnp.logical_not(middle))(lambda: put(4, (2, 3)))

    return call(
        kernel,
        jax.ShapeDtypeStruct((4, 2, count, width), jnp.bfloat16),
        [place],
        pieces,
        read=40 * count * width,
        limit=WHOLE_VMEM_BYTES,
    )


def project(place, tokens, chunks):
    rows, _, count, width = tokens.shape
    half, cols = chunks[0][0][0].shape[1], len(chunks) * HD
    slices = len(chunks[0])
    flat = [w for of_head in chunks for of_round in of_head for w in of_round]
    total_rows = rows * 2 * count

    def kernel(place_ref, x_ref, *refs):
        row, group, core = place_ref[0], place_ref[1], place_ref[3]
        w_refs = refs[: len(flat)]
        q_keep, kv_keep, send, total = refs[len(flat) :]
        acc = None
        for k in range(slices):
            for g in range(2):
                at = (row + slices - k) % slices * (2 * half) + (group + g) % 2 * half
                piece = x_ref[:, :, :, pl.ds(pl.multiple_of(at, half), half)].reshape(-1, half)
                of_heads = w_refs[2 * k + g :: 2 * slices]
                weight = jnp.concatenate([w_ref[part] for part in range(3) for w_ref in of_heads], axis=1)
                term = jnp.dot(piece, weight, preferred_element_type=jnp.float32)
                acc = term if acc is None else acc + term
        kv_part = acc[:, cols:].reshape(rows, 2 * count, 2 * cols)
        kv_keep[...] = kv_part
        send[:, : 2 * count, :] = kv_part.astype(jnp.bfloat16)
        total[...] = acc[:, :cols].reshape(rows, 2, count, cols)
        own = pl.multiple_of(core * BS, BS)
        other = pl.multiple_of((1 - core) * BS, BS)
        q_keep[...] = total[:, :, pl.ds(own, BS), :].reshape(q_keep.shape)
        for f in range(2):
            at = slice(f * cols, (f + 1) * cols)
            send[:, 2 * count :, at] = total[:, f, pl.ds(other, BS), :].astype(jnp.bfloat16)

    flops = 2 * total_rows * width * 3 * cols
    return call(
        kernel,
        (
            jax.ShapeDtypeStruct((rows, 2 * BS, cols), jnp.float32),
            jax.ShapeDtypeStruct((rows, 2 * count, 2 * cols), jnp.float32),
            jax.ShapeDtypeStruct((rows, 2 * count + BS, 2 * cols), jnp.bfloat16),
        ),
        [place],
        [tokens, *flat],
        scratch=[pltpu.VMEM((rows, 2, count, cols), jnp.float32)],
        flops=flops,
        read=flops // 300,
    )


def attend_all(place, members, counts, queries, keyvals, more, earlier=()):
    blocks, block_len, cols = queries.shape
    first = earlier[0].shape[2] if earlier else 0
    rows = keyvals.shape[1]
    per_row = rows // block_len

    def kernel(place_ref, members_ref, counts_ref, q_ref, kv_ref, more_ref, *refs):
        same_ref, diff_ref, q_sum, kv_sum, out = refs[len(earlier) :]
        for r in range(blocks):
            added = more_ref[r, rows:, :].astype(jnp.float32)
            added = jnp.concatenate([added[:, :cols], added[:, cols:]], axis=0)
            q_sum[r] = (q_ref[r] + added).astype(jnp.bfloat16)
            both = (kv_ref[r] + more_ref[r, :rows, :].astype(jnp.float32)).astype(jnp.bfloat16)
            both = both.reshape(2, rows // 2, 2 * cols)
            for j in range(per_row):
                part = both[:, j * BS : (j + 1) * BS, :]
                kv_sum[r * per_row + j] = part.reshape(block_len, 2 * cols)
        column = lax.broadcasted_iota(jnp.int32, (block_len, MAXB * block_len), 1)
        for b in range(blocks):
            live = column < counts_ref[b] * block_len
            listed = [kv_sum.at[members_ref[b * MAXB + j]] for j in range(MAXB)]
            for h in range(cols // HD):
                at = slice(h * HD, (h + 1) * HD)
                at_v = slice(cols + h * HD, cols + (h + 1) * HD)
                keys = jnp.concatenate([block[:, at] for block in listed], axis=0)
                values = jnp.concatenate([block[:, at_v] for block in listed], axis=0)
                scores = lax.dot_general(
                    q_sum[b, :, at], keys, (((1,), (1,)), ((), ())), preferred_element_type=jnp.float32
                )
                scores = jnp.where(live, scores, -jnp.inf)
                raised = jnp.exp2((scores - jnp.max(scores, axis=-1, keepdims=True)) * EXP2_SCALE)
                weights = raised * (1.0 / jnp.sum(raised, axis=-1, keepdims=True))
                blended = jnp.dot(
                    weights.astype(jnp.bfloat16), values, preferred_element_type=jnp.float32
                )
                out[(b + place_ref[0]) % 2, b // 2, :, at] = blended.astype(jnp.bfloat16)
        for i, out_ref in enumerate((same_ref, diff_ref)):
            if earlier:
                out_ref[:, :, :first] = refs[i][...]
            out_ref[:, :, first:] = out[i]

    half = jax.ShapeDtypeStruct((blocks // 2, block_len, first + cols), jnp.bfloat16)
    return call(
        kernel,
        (half, half),
        [place, members, counts],
        [queries, keyvals, more, *earlier],
        scratch=[
            pltpu.VMEM((blocks, block_len, cols), jnp.bfloat16),
            pltpu.VMEM((blocks * per_row, block_len, 2 * cols), jnp.bfloat16),
            pltpu.VMEM((2, blocks // 2, block_len, cols), jnp.bfloat16),
        ],
        flops=4 * blocks * block_len * MAXB * block_len * cols,
        read=16 * blocks * block_len * cols,
    )


def mix(place, attended, w_parts):
    blocks, block_len, cols = attended[0].shape
    width = w_parts[0].shape[1]

    def kernel(place_ref, *refs):
        row, _, frame, core = (place_ref[i] for i in range(4))
        w_refs = refs[4:12]
        keep, over_x, over_z, over_both, a_all, sums = refs[12:]
        for s in range(4):
            a_all[s] = refs[s][...].reshape(blocks * block_len, cols)

        def term(first, side):
            acc = jnp.dot(a_all[(2 * side) ^ row], w_refs[first][...], preferred_element_type=jnp.float32)
            acc = acc + jnp.dot(
                a_all[(2 * side + 1) ^ row], w_refs[first + 1][...], preferred_element_type=jnp.float32
            )
            return acc.astype(jnp.bfloat16).astype(jnp.float32)

        for c in range(2):
            total = term(2 * c, core) + term(4 + 2 * c, 1 - core)
            sums[...] = total.reshape(blocks, 2, BS, width)
            at = (row + c) % 2
            keep[at] = sums[row // 2, frame]
            over_x[at] = sums[row // 2, 1 - frame].astype(jnp.bfloat16)
            over_z[at] = sums[1 - row // 2, frame].astype(jnp.bfloat16)
            over_both[at] = sums[1 - row // 2, 1 - frame].astype(jnp.bfloat16)

    shape = (2, BS, width)
    sent = jax.ShapeDtypeStruct(shape, jnp.bfloat16)
    return call(
        kernel,
        (jax.ShapeDtypeStruct(shape, jnp.float32), sent, sent, sent),
        [place],
        [*attended, *w_parts],
        scratch=[
            pltpu.VMEM((4, blocks * block_len, cols), jnp.bfloat16),
            pltpu.VMEM((blocks, 2, BS, width), jnp.float32),
        ],
        flops=2 * blocks * block_len * 4 * cols * 2 * width,
        read=16 * cols * width,
    )


def finish(place, keep, from_x, from_z, from_both):
    halves, rows, width = keep.shape

    def kernel(place_ref, keep_ref, x_ref, z_ref, both_ref, out_ref):
        pair = place_ref[0] // 2
        for c in range(halves):
            near = pl.multiple_of((pair * halves + c) * width, width)
            far = pl.multiple_of(((1 - pair) * halves + c) * width, width)
            out_ref[:, pl.ds(near, width)] = (keep_ref[c] + x_ref[c].astype(jnp.float32)).astype(jnp.bfloat16)
            out_ref[:, pl.ds(far, width)] = (
                z_ref[c].astype(jnp.float32) + both_ref[c].astype(jnp.float32)
            ).astype(jnp.bfloat16)

    return call(
        kernel,
        jax.ShapeDtypeStruct((rows, 2 * halves * width), jnp.bfloat16),
        [place],
        [keep, from_x, from_z, from_both],
        read=16 * rows * halves * width,
    )


def by_heads(latents, w_qkv, w_out, win_blocks, win_counts, block_window):
    rows_n, heads_n = lax.axis_size("rows"), lax.axis_size("heads")
    group, row = lax.axis_index("groups"), lax.axis_index("rows")
    frame, core = lax.axis_index("frames"), lax.axis_index("heads")
    depth, _, local_cols = w_qkv.shape
    span = rows_n // heads_n
    cols = local_cols // span
    half = depth // 2
    place = jnp.stack([row, group, frame, core]).astype(jnp.int32)

    def over_frames(value, rows):
        pairs = [(2 * r + f, 2 * r + 1 - f) for r in rows for f in range(2)]
        return lax.ppermute(value, ("rows", "frames"), pairs)

    def inward(value):
        return lax.ppermute(value, "rows", [(1, 2), (2, 1)])

    def outward(value):
        return lax.ppermute(value, "rows", [(1, 0), (2, 3)])

    def piece(weights, i):
        at = (0, group * half, (i % span + row) % span * cols + i // span * HD)
        return lax.dynamic_slice(weights.transpose(1, 0, 2), at, (3, half, HD))

    def reshard(value, i):
        pairs = [
            (r * heads_n + h, (h * span + (i % span + r) % span) * heads_n + r // span)
            for r in range(rows_n)
            for h in range(heads_n)
        ]
        return lax.ppermute(value, ("rows", "heads"), pairs)

    here, there = {}, {}
    mine = lax.dynamic_slice_in_dim(latents[0], core * span * depth, span * depth, axis=1)
    here[0] = reshard(piece(w_qkv, 0), 0)
    mine_x = swap(mine, "frames")
    near = swap(mine, "rows")
    in_1 = inward(mine)
    ready = piece(w_qkv, 1)
    here, mine_x, near, in_1, ready, w_qkv, w_out = settle(here, mine_x, near, in_1, ready, w_qkv, w_out)

    here[1] = reshard(ready, 1)
    there[0] = swap(here[0], "groups")
    near_x = swap(near, "frames")
    in_1x = over_frames(in_1, (1, 2))
    in_2 = inward(near)
    out_1 = outward(in_1)
    ready = [piece(w_qkv, 2), piece(w_qkv, 3)]
    here, there, near_x, in_1x, in_2, out_1, ready, w_qkv, w_out = settle(
        here, there, near_x, in_1x, in_2, out_1, ready, w_qkv, w_out
    )

    here[2], here[3] = reshard(ready[0], 2), reshard(ready[1], 3)
    there[1] = swap(here[1], "groups")
    in_2x = over_frames(in_2, (1, 2))
    out_2 = outward(in_2)
    out_1x = over_frames(out_1, (0, 3))
    across = swap(w_out, "heads")
    ready = [piece(w_qkv, 4), piece(w_qkv, 5)]
    here, there, in_2x, out_2, out_1x, across, ready, w_qkv, w_out = settle(
        here, there, in_2x, out_2, out_1x, across, ready, w_qkv, w_out
    )

    here[4], here[5] = reshard(ready[0], 4), reshard(ready[1], 5)
    there[2], there[3] = swap(here[2], "groups"), swap(here[3], "groups")
    out_2x = over_frames(out_2, (0, 3))
    upper, lower = w_out[:cols], w_out[cols:]
    tables = jnp.concatenate([win_blocks, win_counts[:, None], block_window[:, None]], axis=1)
    here, there, out_2x, upper, lower, w_out, tables = settle(here, there, out_2x, upper, lower, w_out, tables)

    there[4], there[5] = swap(here[4], "groups"), swap(here[5], "groups")
    beside_upper = swap(upper, "rows")
    found = [tables] + [swap(tables, "rows", s) for s in range(1, rows_n)]
    tables = jnp.stack(found)[row ^ jnp.arange(rows_n)].reshape(rows_n * heads_n, MAXB + 2)
    windows = lax.dynamic_index_in_dim(
        tables[:, MAXB + 1].reshape(rows_n, heads_n), core, axis=1, keepdims=False
    )
    picked = tables[windows]
    members, counts = picked[:, :MAXB].reshape(-1), picked[:, MAXB]
    tokens = assemble(
        place, [(mine, mine_x), (near, near_x)], [(in_1, in_1x), (in_2, in_2x)], [(out_1, out_1x), (out_2, out_2x)]
    )
    heads = len(here) // span
    chunks = [[(here[h * span + k], there[h * span + k]) for k in range(span)] for h in range(heads)]
    first = project(place, tokens, chunks[:-1])
    beside_upper, tokens, first, chunks, members, counts, lower = settle(
        beside_upper, tokens, first, chunks, members, counts, lower
    )

    beside_lower = swap(lower, "rows")
    first_more = swap(first[2], "heads")
    second = project(place, tokens, chunks[-1:])
    second_more = swap(second[2], "heads")
    attended = attend_all(place, members, counts, *first[:2], first_more)
    attended, second, second_more, beside_upper, beside_lower = settle(
        attended, second, second_more, beside_upper, beside_lower
    )

    same, diff = attend_all(place, members, counts, *second[:2], second_more, attended)
    attended = [same] + [swap(same if s % 2 == 0 else diff, "rows", s) for s in range(1, rows_n)]
    beside = [beside_upper, beside_lower]
    beside_across = [swap(part, "heads") for part in beside]
    keep, over_x, over_z, over_both = mix(
        place, attended, [upper, lower, *beside, across[:cols], across[cols:], *beside_across]
    )
    from_x = swap(over_x, "frames")
    from_z = swap(over_z, "rows", 2)
    from_both = lax.ppermute(
        over_both,
        ("rows", "frames"),
        [(2 * r + f, 2 * (r ^ 2) + 1 - f) for r in range(rows_n) for f in range(2)],
    )
    out = finish(place, keep, from_x, from_z, from_both)
    return out[None]


def local(latents, w_qkv, w_out, win_blocks, win_counts, block_window):
    rows_n = lax.axis_size("rows")
    pairs = all(lax.axis_size(axis) == 2 for axis in ("groups", "frames", "heads"))
    heads_here = w_qkv.shape[2] // HD
    if pairs and rows_n == 4 and heads_here == 6 and latents.shape[:2] == (1, 2 * BS):
        plan = by_heads
    else:
        plan = by_tokens
    return plan(latents, w_qkv, w_out, win_blocks, win_counts, block_window)


def solution(mesh):
    in_specs = (
        P(("groups", "frames"), "rows", None),
        P("rows", None, ("frames", "heads")),
        P(("frames", "heads"), "rows"),
        P(("groups", "rows"), None),
        P(("groups", "rows")),
        P(("groups", "rows")),
    )
    out_specs = P(("groups", "frames"), ("rows", "heads"), None)
    return jax.shard_map(local, mesh=mesh, in_specs=in_specs, out_specs=out_specs, check_vma=False)
```

```python
import math

import jax
import jax.numpy as jnp
from jax import lax
from jax.experimental import pallas as pl
from jax.experimental.pallas import tpu as pltpu
from jax.sharding import PartitionSpec as P

HD = 128
BS = 64
MAXB = 4
VMEM_BYTES = 24 * 1024 * 1024
WHOLE_VMEM_BYTES = 56 * 1024 * 1024
EXP2_SCALE = math.log2(math.e) / math.sqrt(HD)


def with_halo(value, sides, width):
    for axis, dim in sides:
        peers, length = (lax.axis_size(axis), value.shape[dim])
        up = [(i, (i + 1) % peers) for i in range(peers)]
        down = [(j, i) for i, j in up]
        last = lax.slice_in_dim(value, length - width, length, axis=dim)
        first = lax.slice_in_dim(value, 0, width, axis=dim)
        before = lax.ppermute(last, axis, up)
        after = lax.ppermute(first, axis, down)
        value = jnp.concatenate([before, value, after], axis=dim)
    return value


def by_tokens(latents, w_qkv, w_out, win_blocks, win_counts, block_window):
    rows_n = lax.axis_size("rows")
    shard_idx = lax.axis_index("rows")
    frames = latents.shape[0] * lax.axis_size("frames")
    tok_frame = latents.shape[1]
    model_width = latents.shape[2]
    local_cols = w_qkv.shape[2]
    per_shard = tok_frame // BS
    block_total = per_shard * rows_n
    heads_here = local_cols // HD
    block_len = frames * BS
    score_scale = 1.0 / math.sqrt(HD)
    gathered = lax.all_gather(latents, "frames", axis=0, tiled=True)
    flat_tokens = gathered.reshape(frames * tok_frame, model_width)
    weight_rows = lax.all_gather(w_qkv, "rows", axis=0, tiled=True)
    projected = jnp.dot(
        flat_tokens,
        weight_rows.reshape(weight_rows.shape[0], 3 * local_cols),
        preferred_element_type=jnp.float32,
    ).astype(jnp.bfloat16)
    blocked = projected.reshape(frames, per_shard, BS, 3, local_cols).transpose(1, 0, 2, 3, 4)
    blocked = blocked.reshape(per_shard, block_len, 3, local_cols)
    queries = blocked[:, :, 0]
    keyvals = blocked[:, :, 1:]
    nearby = with_halo(keyvals, (("rows", 0),), per_shard)
    first_block = shard_idx * per_shard
    owners = block_window - first_block
    members = win_blocks[owners]
    lengths = win_counts[owners]
    positions = (members - first_block + per_shard + block_total) % block_total

    def attend(query_rows, picked, live_mask):
        key_count = picked.shape[0]
        key_blocks = nearby[picked]
        key_part = key_blocks[:, :, 0].reshape(key_count * block_len, heads_here, HD)
        value_part = key_blocks[:, :, 1].reshape(key_count * block_len, heads_here, HD)
        scores = (
            jnp.einsum(
                "qhd,khd->hqk",
                query_rows.reshape(block_len, heads_here, HD),
                key_part,
                preferred_element_type=jnp.float32,
            )
            * score_scale
        )
        scores = jnp.where(live_mask[None, None, :], scores, -jnp.inf)
        row_max = jnp.max(scores, axis=-1, keepdims=True)
        raised = jnp.exp(scores - row_max)
        weights = (raised / jnp.sum(raised, axis=-1, keepdims=True)).astype(jnp.bfloat16)
        blended = jnp.einsum(
            "hqk,khd->qhd", weights, value_part, preferred_element_type=jnp.float32
        )
        return blended.reshape(block_len, local_cols).astype(jnp.bfloat16)

    def one_block(block_item):
        query_rows, picked, length = block_item
        live_mask = jnp.repeat(jnp.arange(MAXB) < length, block_len)
        return attend(query_rows, picked, live_mask)

    attended = lax.map(one_block, (queries, positions, lengths))
    ordered = attended.reshape(per_shard, frames, BS, local_cols).transpose(1, 0, 2, 3)
    ordered = ordered.reshape(frames * tok_frame, local_cols)
    w_full = lax.all_gather(w_out, "rows", axis=1, tiled=True)
    group_count = lax.axis_size(("frames", "heads"))
    out_rows = frames * tok_frame // group_count
    summed = lax.psum_scatter(
        jnp.dot(ordered, w_full, preferred_element_type=jnp.float32).astype(jnp.bfloat16),
        ("frames", "heads"),
        scatter_dimension=0,
        tiled=True,
    )
    return summed.reshape(1, out_rows, model_width)


def swap(value, axis, step=1):
    peers = lax.axis_size(axis)
    return lax.ppermute(value, axis, [(i, i ^ step) for i in range(peers)])


def after(value, *others):
    return lax.optimization_barrier((value, *others))[0]


def call(kernel, out_shape, prefetch, operands, scratch=(), flops=0, read=0, limit=VMEM_BYTES):
    return pl.pallas_call(
        kernel,
        out_shape=out_shape,
        grid_spec=pltpu.PrefetchScalarGridSpec(
            num_scalar_prefetch=len(prefetch),
            grid=(),
            in_specs=[pl.BlockSpec(memory_space=pltpu.VMEM)] * len(operands),
            out_specs=jax.tree.map(lambda _: pl.BlockSpec(memory_space=pltpu.VMEM), out_shape),
            scratch_shapes=scratch,
        ),
        compiler_params=pltpu.CompilerParams(vmem_limit_bytes=limit),
        cost_estimate=pl.CostEstimate(flops=flops, bytes_accessed=read, transcendentals=0),
    )(*prefetch, *operands)


def assemble(place, near, inward, outward):
    count, width = near[0][0].shape
    pieces = [x for pair in near + inward + outward for x in pair]

    def kernel(place_ref, *refs):
        row, frame = place_ref[0], place_ref[2]
        out_ref = refs[-1]

        def put(first, steps):
            for i, s in enumerate(steps):
                for f in range(2):
                    out_ref[row ^ s, (frame + f) % 2] = refs[2 * (first + i) + f][...]

        middle = (row == 1) | (row == 2)
        put(0, (0, 1))
        pl.when(middle)(lambda: put(2, (3, 2)))
        pl.when(jnp.logical_not(middle))(lambda: put(4, (2, 3)))

    return call(
        kernel,
        jax.ShapeDtypeStruct((4, 2, count, width), jnp.bfloat16),
        [place],
        pieces,
        read=40 * count * width,
        limit=WHOLE_VMEM_BYTES,
    )


def project(place, tokens, chunks):
    rows, _, count, width = tokens.shape
    _, half, cols = chunks[0][0].shape
    slices = len(chunks)
    flat = [w for of_round in chunks for w in of_round]
    total_rows = rows * 2 * count

    def kernel(place_ref, x_ref, *refs):
        row, group, core = place_ref[0], place_ref[1], place_ref[3]
        w_refs = refs[: len(flat)]
        q_keep, kv_keep, send, total = refs[len(flat) :]
        acc = None
        for k in range(slices):
            for g in range(2):
                at = (row + slices - k) % slices * (2 * half) + (group + g) % 2 * half
                piece = x_ref[:, :, :, pl.ds(pl.multiple_of(at, half), half)].reshape(-1, half)
                w_ref = w_refs[2 * k + g]
                weight = jnp.concatenate([w_ref[part] for part in range(3)], axis=1)
                term = jnp.dot(piece, weight, preferred_element_type=jnp.float32)
                acc = term if acc is None else acc + term
        kv_part = acc[:, cols:].reshape(rows, 2 * count, 2 * cols)
        kv_keep[...] = kv_part
        send[:, : 2 * count, :] = kv_part.astype(jnp.bfloat16)
        total[...] = acc[:, :cols].reshape(rows, 2, count, cols)
        own = pl.multiple_of(core * BS, BS)
        other = pl.multiple_of((1 - core) * BS, BS)
        q_keep[...] = total[:, :, pl.ds(own, BS), :].reshape(q_keep.shape)
        for f in range(2):
            at = slice(f * cols, (f + 1) * cols)
            send[:, 2 * count :, at] = total[:, f, pl.ds(other, BS), :].astype(jnp.bfloat16)

    flops = 2 * total_rows * width * 3 * cols
    return call(
        kernel,
        (
            jax.ShapeDtypeStruct((rows, 2 * BS, cols), jnp.float32),
            jax.ShapeDtypeStruct((rows, 2 * count, 2 * cols), jnp.float32),
            jax.ShapeDtypeStruct((rows, 2 * count + BS, 2 * cols), jnp.bfloat16),
        ),
        [place],
        [tokens, *flat],
        scratch=[pltpu.VMEM((rows, 2, count, cols), jnp.float32)],
        flops=flops,
        read=flops // 300,
    )


def attend_all(place, members, counts, queries, keyvals, more, earlier=()):
    blocks, block_len, cols = queries.shape
    first = earlier[0].shape[2] if earlier else 0
    rows = keyvals.shape[1]
    per_row = rows // block_len

    def kernel(place_ref, members_ref, counts_ref, q_ref, kv_ref, more_ref, *refs):
        same_ref, diff_ref, q_sum, kv_sum, out = refs[len(earlier) :]
        for r in range(blocks):
            added = more_ref[r, rows:, :].astype(jnp.float32)
            added = jnp.concatenate([added[:, :cols], added[:, cols:]], axis=0)
            q_sum[r] = (q_ref[r] + added).astype(jnp.bfloat16)
            both = (kv_ref[r] + more_ref[r, :rows, :].astype(jnp.float32)).astype(jnp.bfloat16)
            both = both.reshape(2, rows // 2, 2 * cols)
            for j in range(per_row):
                part = both[:, j * BS : (j + 1) * BS, :]
                kv_sum[r * per_row + j] = part.reshape(block_len, 2 * cols)
        column = lax.broadcasted_iota(jnp.int32, (block_len, MAXB * block_len), 1)
        for b in range(blocks):
            live = column < counts_ref[b] * block_len
            listed = [kv_sum.at[members_ref[b * MAXB + j]] for j in range(MAXB)]
            for h in range(cols // HD):
                at = slice(h * HD, (h + 1) * HD)
                at_v = slice(cols + h * HD, cols + (h + 1) * HD)
                keys = jnp.concatenate([block[:, at] for block in listed], axis=0)
                values = jnp.concatenate([block[:, at_v] for block in listed], axis=0)
                scores = lax.dot_general(
                    q_sum[b, :, at], keys, (((1,), (1,)), ((), ())), preferred_element_type=jnp.float32
                )
                scores = jnp.where(live, scores, -jnp.inf)
                raised = jnp.exp2((scores - jnp.max(scores, axis=-1, keepdims=True)) * EXP2_SCALE)
                weights = raised * (1.0 / jnp.sum(raised, axis=-1, keepdims=True))
                blended = jnp.dot(
                    weights.astype(jnp.bfloat16), values, preferred_element_type=jnp.float32
                )
                out[(b + place_ref[0]) % 2, b // 2, :, at] = blended.astype(jnp.bfloat16)
        for i, out_ref in enumerate((same_ref, diff_ref)):
            if earlier:
                out_ref[:, :, :first] = refs[i][...]
            out_ref[:, :, first:] = out[i]

    half = jax.ShapeDtypeStruct((blocks // 2, block_len, first + cols), jnp.bfloat16)
    return call(
        kernel,
        (half, half),
        [place, members, counts],
        [queries, keyvals, more, *earlier],
        scratch=[
            pltpu.VMEM((blocks, block_len, cols), jnp.bfloat16),
            pltpu.VMEM((blocks * per_row, block_len, 2 * cols), jnp.bfloat16),
            pltpu.VMEM((2, blocks // 2, block_len, cols), jnp.bfloat16),
        ],
        flops=4 * blocks * block_len * MAXB * block_len * cols,
        read=16 * blocks * block_len * cols,
    )


def mix(place, attended, w_parts):
    blocks, block_len, cols = attended[0].shape
    width = w_parts[0].shape[1]

    def kernel(place_ref, *refs):
        row, group, frame, core = (place_ref[i] for i in range(4))
        w_refs = refs[4:12]
        keep, over_x, over_z, over_both, a_all, sums = refs[12:]
        for s in range(4):
            a_all[s] = refs[s][...].reshape(blocks * block_len, cols)

        def term(c, first, side):
            acc = None
            for i in range(2):
                at = 2 * side + (i if c == 0 else (i + group) % 2)
                part = jnp.dot(a_all[at ^ row], w_refs[first + i][...], preferred_element_type=jnp.float32)
                acc = part if acc is None else acc + part
            return acc.astype(jnp.bfloat16).astype(jnp.float32)

        for c in range(2):
            total = term(c, 2 * c, core) + term(c, 4 + 2 * c, 1 - core)
            sums[...] = total.reshape(blocks, 2, BS, width)
            at = (row + c) % 2
            keep[at] = sums[row // 2, frame]
            over_x[at] = sums[row // 2, 1 - frame].astype(jnp.bfloat16)
            over_z[at] = sums[1 - row // 2, frame].astype(jnp.bfloat16)
            over_both[at] = sums[1 - row // 2, 1 - frame].astype(jnp.bfloat16)

    shape = (2, BS, width)
    sent = jax.ShapeDtypeStruct(shape, jnp.bfloat16)
    return call(
        kernel,
        (jax.ShapeDtypeStruct(shape, jnp.float32), sent, sent, sent),
        [place],
        [*attended, *w_parts],
        scratch=[
            pltpu.VMEM((4, blocks * block_len, cols), jnp.bfloat16),
            pltpu.VMEM((blocks, 2, BS, width), jnp.float32),
        ],
        flops=2 * blocks * block_len * 4 * cols * 2 * width,
        read=16 * cols * width,
    )


def finish(place, keep, from_x, from_z, from_both):
    halves, rows, width = keep.shape

    def kernel(place_ref, keep_ref, x_ref, z_ref, both_ref, out_ref):
        pair = place_ref[0] // 2
        for c in range(halves):
            near = pl.multiple_of((pair * halves + c) * width, width)
            far = pl.multiple_of(((1 - pair) * halves + c) * width, width)
            out_ref[:, pl.ds(near, width)] = (keep_ref[c] + x_ref[c].astype(jnp.float32)).astype(jnp.bfloat16)
            out_ref[:, pl.ds(far, width)] = (
                z_ref[c].astype(jnp.float32) + both_ref[c].astype(jnp.float32)
            ).astype(jnp.bfloat16)

    return call(
        kernel,
        jax.ShapeDtypeStruct((rows, 2 * halves * width), jnp.bfloat16),
        [place],
        [keep, from_x, from_z, from_both],
        read=16 * rows * halves * width,
    )


def by_heads(latents, w_qkv, w_out, win_blocks, win_counts, block_window):
    rows_n, heads_n = lax.axis_size("rows"), lax.axis_size("heads")
    group, row = lax.axis_index("groups"), lax.axis_index("rows")
    frame, core = lax.axis_index("frames"), lax.axis_index("heads")
    depth, _, local_cols = w_qkv.shape
    span = rows_n // heads_n
    cols = local_cols // span
    half = depth // 2
    place = jnp.stack([row, group, frame, core]).astype(jnp.int32)

    def over_frames(value, rows):
        pairs = [(2 * r + f, 2 * r + 1 - f) for r in rows for f in range(2)]
        return lax.ppermute(value, ("rows", "frames"), pairs)

    def inward(value):
        return lax.ppermute(value, "rows", [(1, 2), (2, 1)])

    def outward(value):
        return lax.ppermute(value, "rows", [(1, 0), (2, 3)])

    last = cols // (3 * HD) * HD

    def reshard(i, *others):
        k = i % span
        at, wide = (0, cols - last) if i < span else (cols - last, last)
        value = lax.dynamic_slice(
            w_qkv.transpose(1, 0, 2), (0, group * half, (k + row) % span * cols + at), (3, half, wide)
        )
        pairs = [
            (r * heads_n + h, (h * span + (k + r) % span) * heads_n + r // span)
            for r in range(rows_n)
            for h in range(heads_n)
        ]
        return lax.ppermute(after(value, *others) if others else value, ("rows", "heads"), pairs)

    mine = lax.dynamic_slice_in_dim(latents[0], core * span * depth, span * depth, axis=1)
    in_1, near, mine_x = inward(mine), swap(mine, "rows"), swap(mine, "frames")
    here, there = [reshard(0)], []
    near_x = swap(near, "frames")
    out_1, in_1x = outward(in_1), over_frames(in_1, (1, 2))
    here.append(reshard(1, in_1, near))
    there.append(swap(here[0], "groups"))
    across = swap(after(w_out, near), "heads")
    in_2 = inward(after(near, here[0]))
    out_1x = over_frames(out_1, (0, 3))
    here.append(reshard(2, here[1], there[0], mine_x, near_x, in_1x, out_1, across))
    there.append(swap(here[1], "groups"))
    out_2, in_2x = outward(in_2), over_frames(in_2, (1, 2))
    here.append(reshard(3, here[1], there[1], in_2, in_2x, out_1x))
    there += [swap(here[2], "groups"), swap(here[3], "groups")]
    out_2x = over_frames(out_2, (0, 3))
    tokens = assemble(
        place, [(mine, mine_x), (near, near_x)], [(in_1, in_1x), (in_2, in_2x)], [(out_1, out_1x), (out_2, out_2x)]
    )

    tables = jnp.concatenate([win_blocks, win_counts[:, None], block_window[:, None]], axis=1)
    tables = after(tables, there[2])
    found = [tables] + [swap(tables, "rows", s) for s in range(1, rows_n)]
    tables = jnp.stack(found)[row ^ jnp.arange(rows_n)].reshape(rows_n * heads_n, MAXB + 2)
    windows = lax.dynamic_index_in_dim(
        tables[:, MAXB + 1].reshape(rows_n, heads_n), core, axis=1, keepdims=False
    )
    picked = tables[windows]
    members, counts = picked[:, :MAXB].reshape(-1), picked[:, MAXB]

    out_half = lax.dynamic_slice_in_dim(w_out, group * cols, cols, axis=0)
    beside = [swap(after(out_half, here[2]), "rows")]
    beside.append(swap(beside[0], "groups"))

    chunks = [(here[0], there[0]), (here[1], after(there[1], there[2], there[3], members, counts))]
    first = project(place, tokens, chunks)
    first_more = swap(first[2], "heads")
    second = project(place, tokens, [(here[2], there[2]), (here[3], after(there[3], first[2], beside[0]))])
    second_more = swap(second[2], "heads")
    attended = attend_all(place, members, counts, *first[:2], first_more)
    same, diff = attend_all(place, members, counts, *second[:2], second_more, attended)
    attended = [same] + [swap(same if s % 2 == 0 else diff, "rows", s) for s in range(1, rows_n)]
    halves = [w_out[:cols], w_out[cols:], *beside]
    beside_across = [swap(part, "heads") for part in (beside[0], after(beside[1], attended[1]))]
    keep, over_x, over_z, over_both = mix(
        place, attended, [*halves, across[:cols], across[cols:], *beside_across]
    )
    from_x = swap(over_x, "frames")
    from_z = swap(over_z, "rows", 2)
    from_both = lax.ppermute(
        over_both,
        ("rows", "frames"),
        [(2 * r + f, 2 * (r ^ 2) + 1 - f) for r in range(rows_n) for f in range(2)],
    )
    out = finish(place, keep, from_x, from_z, from_both)
    return out[None]


def local(latents, w_qkv, w_out, win_blocks, win_counts, block_window):
    rows_n = lax.axis_size("rows")
    pairs = all(lax.axis_size(axis) == 2 for axis in ("groups", "frames", "heads"))
    heads_here = w_qkv.shape[2] // HD
    if pairs and rows_n == 4 and heads_here == 6 and latents.shape[:2] == (1, 2 * BS):
        plan = by_heads
    else:
        plan = by_tokens
    return plan(latents, w_qkv, w_out, win_blocks, win_counts, block_window)


def solution(mesh):
    in_specs = (
        P(("groups", "frames"), "rows", None),
        P("rows", None, ("frames", "heads")),
        P(("frames", "heads"), "rows"),
        P(("groups", "rows"), None),
        P(("groups", "rows")),
        P(("groups", "rows")),
    )
    out_specs = P(("groups", "frames"), ("rows", "heads"), None)
    return jax.shard_map(local, mesh=mesh, in_specs=in_specs, out_specs=out_specs, check_vma=False)
```

```python
import math

import jax
import jax.numpy as jnp
from jax import lax
from jax.experimental import pallas as pl
from jax.experimental.pallas import tpu as pltpu
from jax.sharding import PartitionSpec as P

HD = 128
BS = 64
MAXB = 4
VMEM_BYTES = 24 * 1024 * 1024
WHOLE_VMEM_BYTES = 56 * 1024 * 1024
EXP2_SCALE = math.log2(math.e) / math.sqrt(HD)


def with_halo(value, sides, width):
    for axis, dim in sides:
        peers, length = (lax.axis_size(axis), value.shape[dim])
        up = [(i, (i + 1) % peers) for i in range(peers)]
        down = [(j, i) for i, j in up]
        last = lax.slice_in_dim(value, length - width, length, axis=dim)
        first = lax.slice_in_dim(value, 0, width, axis=dim)
        before = lax.ppermute(last, axis, up)
        after = lax.ppermute(first, axis, down)
        value = jnp.concatenate([before, value, after], axis=dim)
    return value


def by_tokens(latents, w_qkv, w_out, win_blocks, win_counts, block_window):
    rows_n = lax.axis_size("rows")
    shard_idx = lax.axis_index("rows")
    frames = latents.shape[0] * lax.axis_size("frames")
    tok_frame = latents.shape[1]
    model_width = latents.shape[2]
    local_cols = w_qkv.shape[2]
    per_shard = tok_frame // BS
    block_total = per_shard * rows_n
    heads_here = local_cols // HD
    block_len = frames * BS
    score_scale = 1.0 / math.sqrt(HD)
    gathered = lax.all_gather(latents, "frames", axis=0, tiled=True)
    flat_tokens = gathered.reshape(frames * tok_frame, model_width)
    weight_rows = lax.all_gather(w_qkv, "rows", axis=0, tiled=True)
    projected = jnp.dot(
        flat_tokens,
        weight_rows.reshape(weight_rows.shape[0], 3 * local_cols),
        preferred_element_type=jnp.float32,
    ).astype(jnp.bfloat16)
    blocked = projected.reshape(frames, per_shard, BS, 3, local_cols).transpose(1, 0, 2, 3, 4)
    blocked = blocked.reshape(per_shard, block_len, 3, local_cols)
    queries = blocked[:, :, 0]
    keyvals = blocked[:, :, 1:]
    nearby = with_halo(keyvals, (("rows", 0),), per_shard)
    first_block = shard_idx * per_shard
    owners = block_window - first_block
    members = win_blocks[owners]
    lengths = win_counts[owners]
    positions = (members - first_block + per_shard + block_total) % block_total

    def attend(query_rows, picked, live_mask):
        key_count = picked.shape[0]
        key_blocks = nearby[picked]
        key_part = key_blocks[:, :, 0].reshape(key_count * block_len, heads_here, HD)
        value_part = key_blocks[:, :, 1].reshape(key_count * block_len, heads_here, HD)
        scores = (
            jnp.einsum(
                "qhd,khd->hqk",
                query_rows.reshape(block_len, heads_here, HD),
                key_part,
                preferred_element_type=jnp.float32,
            )
            * score_scale
        )
        scores = jnp.where(live_mask[None, None, :], scores, -jnp.inf)
        row_max = jnp.max(scores, axis=-1, keepdims=True)
        raised = jnp.exp(scores - row_max)
        weights = (raised / jnp.sum(raised, axis=-1, keepdims=True)).astype(jnp.bfloat16)
        blended = jnp.einsum(
            "hqk,khd->qhd", weights, value_part, preferred_element_type=jnp.float32
        )
        return blended.reshape(block_len, local_cols).astype(jnp.bfloat16)

    def one_block(block_item):
        query_rows, picked, length = block_item
        live_mask = jnp.repeat(jnp.arange(MAXB) < length, block_len)
        return attend(query_rows, picked, live_mask)

    attended = lax.map(one_block, (queries, positions, lengths))
    ordered = attended.reshape(per_shard, frames, BS, local_cols).transpose(1, 0, 2, 3)
    ordered = ordered.reshape(frames * tok_frame, local_cols)
    w_full = lax.all_gather(w_out, "rows", axis=1, tiled=True)
    group_count = lax.axis_size(("frames", "heads"))
    out_rows = frames * tok_frame // group_count
    summed = lax.psum_scatter(
        jnp.dot(ordered, w_full, preferred_element_type=jnp.float32).astype(jnp.bfloat16),
        ("frames", "heads"),
        scatter_dimension=0,
        tiled=True,
    )
    return summed.reshape(1, out_rows, model_width)


def swap(value, axis, step=1):
    peers = lax.axis_size(axis)
    return lax.ppermute(value, axis, [(i, i ^ step) for i in range(peers)])


def after(value, *others):
    return lax.optimization_barrier((value, *others))[0]


def call(kernel, out_shape, prefetch, operands, scratch=(), flops=0, read=0, limit=VMEM_BYTES):
    return pl.pallas_call(
        kernel,
        out_shape=out_shape,
        grid_spec=pltpu.PrefetchScalarGridSpec(
            num_scalar_prefetch=len(prefetch),
            grid=(),
            in_specs=[pl.BlockSpec(memory_space=pltpu.VMEM)] * len(operands),
            out_specs=jax.tree.map(lambda _: pl.BlockSpec(memory_space=pltpu.VMEM), out_shape),
            scratch_shapes=scratch,
        ),
        compiler_params=pltpu.CompilerParams(vmem_limit_bytes=limit),
        cost_estimate=pl.CostEstimate(flops=flops, bytes_accessed=read, transcendentals=0),
    )(*prefetch, *operands)


def assemble(place, mine, theirs, count):
    width, rows = mine[0].shape[1], len(mine)

    def kernel(place_ref, *refs):
        row, frame = place_ref[0], place_ref[2]
        for s in range(rows):
            refs[-1][row ^ s, frame] = refs[s][:count]
            refs[-1][row ^ s, 1 - frame] = refs[rows + s][:count]

    return call(
        kernel,
        jax.ShapeDtypeStruct((rows, 2, count, width), jnp.bfloat16),
        [place],
        [*mine, *theirs],
        read=8 * rows * count * width,
        limit=WHOLE_VMEM_BYTES,
    )


def project(place, tokens, chunks):
    rows, _, count, width = tokens.shape
    _, half, cols = chunks[0][0].shape
    slices = len(chunks)
    flat = [w for of_round in chunks for w in of_round]
    total_rows = rows * 2 * count

    def kernel(place_ref, x_ref, *refs):
        row, group, core = place_ref[0], place_ref[1], place_ref[3]
        w_refs = refs[: len(flat)]
        q_keep, kv_keep, send, total = refs[len(flat) :]
        acc = None
        for k in range(slices):
            for g in range(2):
                at = (row + slices - k) % slices * (2 * half) + (group + g) % 2 * half
                piece = x_ref[:, :, :, pl.ds(pl.multiple_of(at, half), half)].reshape(-1, half)
                w_ref = w_refs[2 * k + g]
                weight = jnp.concatenate([w_ref[part] for part in range(3)], axis=1)
                term = jnp.dot(piece, weight, preferred_element_type=jnp.float32)
                acc = term if acc is None else acc + term
        kv_part = acc[:, cols:].reshape(rows, 2 * count, 2 * cols)
        kv_keep[...] = kv_part
        send[:, : 2 * count, :] = kv_part.astype(jnp.bfloat16)
        total[...] = acc[:, :cols].reshape(rows, 2, count, cols)
        own = pl.multiple_of(core * BS, BS)
        other = pl.multiple_of((1 - core) * BS, BS)
        q_keep[...] = total[:, :, pl.ds(own, BS), :].reshape(q_keep.shape)
        for f in range(2):
            at = slice(f * cols, (f + 1) * cols)
            send[:, 2 * count :, at] = total[:, f, pl.ds(other, BS), :].astype(jnp.bfloat16)

    flops = 2 * total_rows * width * 3 * cols
    return call(
        kernel,
        (
            jax.ShapeDtypeStruct((rows, 2 * BS, cols), jnp.float32),
            jax.ShapeDtypeStruct((rows, 2 * count, 2 * cols), jnp.float32),
            jax.ShapeDtypeStruct((rows, 2 * count + BS, 2 * cols), jnp.bfloat16),
        ),
        [place],
        [tokens, *flat],
        scratch=[pltpu.VMEM((rows, 2, count, cols), jnp.float32)],
        flops=8 * flops,
        read=flops // 300,
        limit=WHOLE_VMEM_BYTES,
    )


def attend_all(place, members, counts, queries, keyvals, more, earlier=()):
    blocks, block_len, cols = queries.shape
    first = earlier[0].shape[2] if earlier else 0
    rows = keyvals.shape[1]
    per_row = rows // block_len

    def kernel(place_ref, members_ref, counts_ref, q_ref, kv_ref, more_ref, *refs):
        same_ref, diff_ref, q_sum, kv_sum, out = refs[len(earlier) :]
        for r in range(blocks):
            added = more_ref[r, rows:, :].astype(jnp.float32)
            added = jnp.concatenate([added[:, :cols], added[:, cols:]], axis=0)
            q_sum[r] = (q_ref[r] + added).astype(jnp.bfloat16)
            both = (kv_ref[r] + more_ref[r, :rows, :].astype(jnp.float32)).astype(jnp.bfloat16)
            both = both.reshape(2, rows // 2, 2 * cols)
            for j in range(per_row):
                part = both[:, j * BS : (j + 1) * BS, :]
                kv_sum[r * per_row + j] = part.reshape(block_len, 2 * cols)
        column = lax.broadcasted_iota(jnp.int32, (block_len, MAXB * block_len), 1)
        for b in range(blocks):
            live = column < counts_ref[b] * block_len
            listed = [kv_sum.at[members_ref[b * MAXB + j]] for j in range(MAXB)]
            for h in range(cols // HD):
                at = slice(h * HD, (h + 1) * HD)
                at_v = slice(cols + h * HD, cols + (h + 1) * HD)
                keys = jnp.concatenate([block[:, at] for block in listed], axis=0)
                values = jnp.concatenate([block[:, at_v] for block in listed], axis=0)
                scores = lax.dot_general(
                    q_sum[b, :, at], keys, (((1,), (1,)), ((), ())), preferred_element_type=jnp.float32
                )
                scores = jnp.where(live, scores, -jnp.inf)
                raised = jnp.exp2((scores - jnp.max(scores, axis=-1, keepdims=True)) * EXP2_SCALE)
                weights = raised * (1.0 / jnp.sum(raised, axis=-1, keepdims=True))
                blended = jnp.dot(
                    weights.astype(jnp.bfloat16), values, preferred_element_type=jnp.float32
                )
                out[(b + place_ref[0]) % 2, b // 2, :, at] = blended.astype(jnp.bfloat16)
        for i, out_ref in enumerate((same_ref, diff_ref)):
            if earlier:
                out_ref[:, :, :first] = refs[i][...]
            out_ref[:, :, first:] = out[i]

    half = jax.ShapeDtypeStruct((blocks // 2, block_len, first + cols), jnp.bfloat16)
    return call(
        kernel,
        (half, half),
        [place, members, counts],
        [queries, keyvals, more, *earlier],
        scratch=[
            pltpu.VMEM((blocks, block_len, cols), jnp.bfloat16),
            pltpu.VMEM((blocks * per_row, block_len, 2 * cols), jnp.bfloat16),
            pltpu.VMEM((2, blocks // 2, block_len, cols), jnp.bfloat16),
        ],
        flops=4 * blocks * block_len * MAXB * block_len * cols,
        read=16 * blocks * block_len * cols,
        limit=WHOLE_VMEM_BYTES,
    )


def mix(place, attended, w_parts):
    blocks, block_len, cols = attended[0].shape
    width = w_parts[0].shape[1]

    def kernel(place_ref, *refs):
        row, group, frame, core = (place_ref[i] for i in range(4))
        w_refs = refs[4:12]
        keep, over_x, over_z, over_both, a_all, sums = refs[12:]
        for s in range(4):
            a_all[s] = refs[s][...].reshape(blocks * block_len, cols)

        def term(c, first, side):
            acc = None
            for i in range(2):
                at = 2 * side + (i if c == 0 else (i + group) % 2)
                part = jnp.dot(a_all[at ^ row], w_refs[first + i][...], preferred_element_type=jnp.float32)
                acc = part if acc is None else acc + part
            return acc.astype(jnp.bfloat16).astype(jnp.float32)

        for c in range(2):
            total = term(c, 2 * c, core) + term(c, 4 + 2 * c, 1 - core)
            sums[...] = total.reshape(blocks, 2, BS, width)
            at = (row + c) % 2
            keep[at] = sums[row // 2, frame]
            over_x[at] = sums[row // 2, 1 - frame].astype(jnp.bfloat16)
            over_z[at] = sums[1 - row // 2, frame].astype(jnp.bfloat16)
            over_both[at] = sums[1 - row // 2, 1 - frame].astype(jnp.bfloat16)

    shape = (2, BS, width)
    sent = jax.ShapeDtypeStruct(shape, jnp.bfloat16)
    return call(
        kernel,
        (jax.ShapeDtypeStruct(shape, jnp.float32), sent, sent, sent),
        [place],
        [*attended, *w_parts],
        scratch=[
            pltpu.VMEM((4, blocks * block_len, cols), jnp.bfloat16),
            pltpu.VMEM((blocks, 2, BS, width), jnp.float32),
        ],
        flops=2 * blocks * block_len * 4 * cols * 2 * width,
        read=16 * cols * width,
    )


def finish(place, keep, from_x, from_z, from_both):
    halves, rows, width = keep.shape

    def kernel(place_ref, keep_ref, x_ref, z_ref, both_ref, out_ref):
        pair = place_ref[0] // 2
        for c in range(halves):
            near = pl.multiple_of((pair * halves + c) * width, width)
            far = pl.multiple_of(((1 - pair) * halves + c) * width, width)
            out_ref[:, pl.ds(near, width)] = (keep_ref[c] + x_ref[c].astype(jnp.float32)).astype(jnp.bfloat16)
            out_ref[:, pl.ds(far, width)] = (
                z_ref[c].astype(jnp.float32) + both_ref[c].astype(jnp.float32)
            ).astype(jnp.bfloat16)

    return call(
        kernel,
        jax.ShapeDtypeStruct((rows, 2 * halves * width), jnp.bfloat16),
        [place],
        [keep, from_x, from_z, from_both],
        read=16 * rows * halves * width,
    )


def by_heads(latents, w_qkv, w_out, win_blocks, win_counts, block_window):
    rows_n, heads_n = lax.axis_size("rows"), lax.axis_size("heads")
    group, row = lax.axis_index("groups"), lax.axis_index("rows")
    frame, core = lax.axis_index("frames"), lax.axis_index("heads")
    count = latents.shape[1]
    depth, _, local_cols = w_qkv.shape
    span = rows_n // heads_n
    cols = local_cols // span
    half = depth // 2
    place = jnp.stack([row, group, frame, core]).astype(jnp.int32)

    last = cols // (3 * HD) * HD

    def reshard(i, *others):
        k = i % span
        at, wide = (0, cols - last) if i < span else (cols - last, last)
        value = lax.dynamic_slice(
            w_qkv.transpose(1, 0, 2), (0, group * half, (k + row) % span * cols + at), (3, half, wide)
        )
        pairs = [
            (r * heads_n + h, (h * span + (k + r) % span) * heads_n + r // span)
            for r in range(rows_n)
            for h in range(heads_n)
        ]
        return lax.ppermute(after(value, *others) if others else value, ("rows", "heads"), pairs)

    tables = jnp.concatenate([win_blocks, win_counts[:, None], block_window[:, None]], axis=1)
    tables = jnp.pad(tables, ((0, 6), (0, span * depth - MAXB - 2))).astype(latents.dtype)
    mine = lax.dynamic_slice_in_dim(latents[0], core * span * depth, span * depth, axis=1)
    mine = jnp.concatenate([mine, tables], axis=0)

    near, mine_x = swap(mine, "rows"), swap(mine, "frames")
    here, there = [reshard(0)], []
    near_x = swap(near, "frames")
    across = swap(after(w_out, near), "heads")
    here.append(reshard(1, near, mine_x))
    there.append(swap(here[0], "groups"))
    far_2 = swap(after(mine, here[0]), "rows", 2)
    there.append(swap(here[1], "groups"))
    far_3 = swap(after(mine, here[1], near_x), "rows", 3)
    far_2x = swap(far_2, "frames")
    out_half = lax.dynamic_slice_in_dim(w_out, group * cols, cols, axis=0)
    beside = [swap(after(out_half, here[0]), "rows")]
    beside.append(swap(beside[0], "groups"))
    here.append(reshard(2, far_2, there[0], there[1], across, beside[0]))
    far_3x = swap(far_3, "frames")
    here.append(reshard(3, far_3, far_2x, beside[1]))
    there += [swap(here[2], "groups"), swap(here[3], "groups")]
    pieces = [mine, near, far_2, far_3]
    tokens = assemble(place, pieces, [mine_x, near_x, far_2x, far_3x], count)

    found = jnp.stack([x[count : count + heads_n, : MAXB + 2] for x in pieces]).astype(jnp.int32)
    tables = found[row ^ jnp.arange(rows_n)].reshape(rows_n * heads_n, MAXB + 2)
    windows = lax.dynamic_index_in_dim(
        tables[:, MAXB + 1].reshape(rows_n, heads_n), core, axis=1, keepdims=False
    )
    picked = tables[windows]
    members, counts = picked[:, :MAXB].reshape(-1), picked[:, MAXB]

    chunks = [(here[0], there[0]), (here[1], after(there[1], there[2], here[3]))]
    first = project(place, tokens, chunks)
    first_more = swap(first[2], "heads")
    second = project(place, tokens, [(here[2], there[2]), (here[3], after(there[3], first[2]))])
    second_more = swap(second[2], "heads")
    attended = attend_all(place, members, counts, *first[:2], first_more)
    same, diff = attend_all(place, members, counts, *second[:2], second_more, attended)
    attended = [same] + [swap(same if s % 2 == 0 else diff, "rows", s) for s in range(1, rows_n)]
    halves = [w_out[:cols], w_out[cols:], *beside]
    beside_across = [swap(part, "heads") for part in beside]
    keep, over_x, over_z, over_both = mix(
        place, attended, [*halves, across[:cols], across[cols:], *beside_across]
    )
    from_x = swap(over_x, "frames")
    from_z = swap(over_z, "rows", 2)
    from_both = lax.ppermute(
        over_both,
        ("rows", "frames"),
        [(2 * r + f, 2 * (r ^ 2) + 1 - f) for r in range(rows_n) for f in range(2)],
    )
    out = finish(place, keep, from_x, from_z, from_both)
    return out[None]


def local(latents, w_qkv, w_out, win_blocks, win_counts, block_window):
    rows_n = lax.axis_size("rows")
    pairs = all(lax.axis_size(axis) == 2 for axis in ("groups", "frames", "heads"))
    heads_here = w_qkv.shape[2] // HD
    if pairs and rows_n == 4 and heads_here == 6 and latents.shape[:2] == (1, 2 * BS):
        plan = by_heads
    else:
        plan = by_tokens
    return plan(latents, w_qkv, w_out, win_blocks, win_counts, block_window)


def solution(mesh):
    in_specs = (
        P(("groups", "frames"), "rows", None),
        P("rows", None, ("frames", "heads")),
        P(("frames", "heads"), "rows"),
        P(("groups", "rows"), None),
        P(("groups", "rows")),
        P(("groups", "rows")),
    )
    out_specs = P(("groups", "frames"), ("rows", "heads"), None)
    return jax.shard_map(local, mesh=mesh, in_specs=in_specs, out_specs=out_specs, check_vma=False)
```

```python
import math

import jax
import jax.numpy as jnp
from jax import lax
from jax.experimental import pallas as pl
from jax.experimental.pallas import tpu as pltpu
from jax.sharding import PartitionSpec as P

HD = 128
BS = 64
MAXB = 4
VMEM_BYTES = 24 * 1024 * 1024
WHOLE_VMEM_BYTES = 56 * 1024 * 1024
EXP2_SCALE = math.log2(math.e) / math.sqrt(HD)


def with_halo(value, sides, width):
    for axis, dim in sides:
        peers, length = (lax.axis_size(axis), value.shape[dim])
        up = [(i, (i + 1) % peers) for i in range(peers)]
        down = [(j, i) for i, j in up]
        last = lax.slice_in_dim(value, length - width, length, axis=dim)
        first = lax.slice_in_dim(value, 0, width, axis=dim)
        before = lax.ppermute(last, axis, up)
        after = lax.ppermute(first, axis, down)
        value = jnp.concatenate([before, value, after], axis=dim)
    return value


def by_tokens(latents, w_qkv, w_out, win_blocks, win_counts, block_window):
    rows_n = lax.axis_size("rows")
    shard_idx = lax.axis_index("rows")
    frames = latents.shape[0] * lax.axis_size("frames")
    tok_frame = latents.shape[1]
    model_width = latents.shape[2]
    local_cols = w_qkv.shape[2]
    per_shard = tok_frame // BS
    block_total = per_shard * rows_n
    heads_here = local_cols // HD
    block_len = frames * BS
    score_scale = 1.0 / math.sqrt(HD)
    gathered = lax.all_gather(latents, "frames", axis=0, tiled=True)
    flat_tokens = gathered.reshape(frames * tok_frame, model_width)
    weight_rows = lax.all_gather(w_qkv, "rows", axis=0, tiled=True)
    projected = jnp.dot(
        flat_tokens,
        weight_rows.reshape(weight_rows.shape[0], 3 * local_cols),
        preferred_element_type=jnp.float32,
    ).astype(jnp.bfloat16)
    blocked = projected.reshape(frames, per_shard, BS, 3, local_cols).transpose(1, 0, 2, 3, 4)
    blocked = blocked.reshape(per_shard, block_len, 3, local_cols)
    queries = blocked[:, :, 0]
    keyvals = blocked[:, :, 1:]
    nearby = with_halo(keyvals, (("rows", 0),), per_shard)
    first_block = shard_idx * per_shard
    owners = block_window - first_block
    members = win_blocks[owners]
    lengths = win_counts[owners]
    positions = (members - first_block + per_shard + block_total) % block_total

    def attend(query_rows, picked, live_mask):
        key_count = picked.shape[0]
        key_blocks = nearby[picked]
        key_part = key_blocks[:, :, 0].reshape(key_count * block_len, heads_here, HD)
        value_part = key_blocks[:, :, 1].reshape(key_count * block_len, heads_here, HD)
        scores = (
            jnp.einsum(
                "qhd,khd->hqk",
                query_rows.reshape(block_len, heads_here, HD),
                key_part,
                preferred_element_type=jnp.float32,
            )
            * score_scale
        )
        scores = jnp.where(live_mask[None, None, :], scores, -jnp.inf)
        row_max = jnp.max(scores, axis=-1, keepdims=True)
        raised = jnp.exp(scores - row_max)
        weights = (raised / jnp.sum(raised, axis=-1, keepdims=True)).astype(jnp.bfloat16)
        blended = jnp.einsum(
            "hqk,khd->qhd", weights, value_part, preferred_element_type=jnp.float32
        )
        return blended.reshape(block_len, local_cols).astype(jnp.bfloat16)

    def one_block(block_item):
        query_rows, picked, length = block_item
        live_mask = jnp.repeat(jnp.arange(MAXB) < length, block_len)
        return attend(query_rows, picked, live_mask)

    attended = lax.map(one_block, (queries, positions, lengths))
    ordered = attended.reshape(per_shard, frames, BS, local_cols).transpose(1, 0, 2, 3)
    ordered = ordered.reshape(frames * tok_frame, local_cols)
    w_full = lax.all_gather(w_out, "rows", axis=1, tiled=True)
    group_count = lax.axis_size(("frames", "heads"))
    out_rows = frames * tok_frame // group_count
    summed = lax.psum_scatter(
        jnp.dot(ordered, w_full, preferred_element_type=jnp.float32).astype(jnp.bfloat16),
        ("frames", "heads"),
        scatter_dimension=0,
        tiled=True,
    )
    return summed.reshape(1, out_rows, model_width)


def swap(value, axis, step=1):
    peers = lax.axis_size(axis)
    return lax.ppermute(value, axis, [(i, i ^ step) for i in range(peers)])


def after(value, *others):
    return lax.optimization_barrier((value, *others))[0]


def call(kernel, out_shape, prefetch, operands, scratch=(), flops=0, read=0, limit=VMEM_BYTES):
    return pl.pallas_call(
        kernel,
        out_shape=out_shape,
        grid_spec=pltpu.PrefetchScalarGridSpec(
            num_scalar_prefetch=len(prefetch),
            grid=(),
            in_specs=[pl.BlockSpec(memory_space=pltpu.VMEM)] * len(operands),
            out_specs=jax.tree.map(lambda _: pl.BlockSpec(memory_space=pltpu.VMEM), out_shape),
            scratch_shapes=scratch,
        ),
        compiler_params=pltpu.CompilerParams(vmem_limit_bytes=limit),
        cost_estimate=pl.CostEstimate(flops=flops, bytes_accessed=read, transcendentals=0),
    )(*prefetch, *operands)


def assemble(place, near, inward, outward):
    count, width = near[0][0].shape
    pieces = [x for pair in near + inward + outward for x in pair]

    def kernel(place_ref, *refs):
        row, frame = place_ref[0], place_ref[2]
        out_ref = refs[-1]

        def put(first, steps):
            for i, s in enumerate(steps):
                for f in range(2):
                    out_ref[row ^ s, (frame + f) % 2] = refs[2 * (first + i) + f][...]

        middle = (row == 1) | (row == 2)
        put(0, (0, 1))
        pl.when(middle)(lambda: put(2, (3, 2)))
        pl.when(jnp.logical_not(middle))(lambda: put(4, (2, 3)))

    return call(
        kernel,
        jax.ShapeDtypeStruct((4, 2, count, width), jnp.bfloat16),
        [place],
        pieces,
        read=40 * count * width,
        limit=WHOLE_VMEM_BYTES,
    )


def project(place, tokens, chunks):
    rows, _, count, width = tokens.shape
    _, half, cols = chunks[0][0].shape
    slices = len(chunks)
    flat = [w for of_round in chunks for w in of_round]
    total_rows = rows * 2 * count

    def kernel(place_ref, x_ref, *refs):
        row, group, core = place_ref[0], place_ref[1], place_ref[3]
        w_refs = refs[: len(flat)]
        q_keep, kv_keep, send, total = refs[len(flat) :]
        acc = None
        for k in range(slices):
            for g in range(2):
                at = (row + slices - k) % slices * (2 * half) + (group + g) % 2 * half
                piece = x_ref[:, :, :, pl.ds(pl.multiple_of(at, half), half)].reshape(-1, half)
                w_ref = w_refs[2 * k + g]
                weight = jnp.concatenate([w_ref[part] for part in range(3)], axis=1)
                term = jnp.dot(piece, weight, preferred_element_type=jnp.float32)
                acc = term if acc is None else acc + term
        kv_part = acc[:, cols:].reshape(rows, 2 * count, 2 * cols)
        kv_keep[...] = kv_part
        send[:, : 2 * count, :] = kv_part.astype(jnp.bfloat16)
        total[...] = acc[:, :cols].reshape(rows, 2, count, cols)
        own = pl.multiple_of(core * BS, BS)
        other = pl.multiple_of((1 - core) * BS, BS)
        q_keep[...] = total[:, :, pl.ds(own, BS), :].reshape(q_keep.shape)
        for f in range(2):
            at = slice(f * cols, (f + 1) * cols)
            send[:, 2 * count :, at] = total[:, f, pl.ds(other, BS), :].astype(jnp.bfloat16)

    flops = 2 * total_rows * width * 3 * cols
    return call(
        kernel,
        (
            jax.ShapeDtypeStruct((rows, 2 * BS, cols), jnp.float32),
            jax.ShapeDtypeStruct((rows, 2 * count, 2 * cols), jnp.float32),
            jax.ShapeDtypeStruct((rows, 2 * count + BS, 2 * cols), jnp.bfloat16),
        ),
        [place],
        [tokens, *flat],
        scratch=[pltpu.VMEM((rows, 2, count, cols), jnp.float32)],
        flops=8 * flops,
        read=flops // 300,
    )


def attend_all(place, members, counts, queries, keyvals, more, earlier=()):
    blocks, block_len, cols = queries.shape
    first = earlier[0].shape[2] if earlier else 0
    rows = keyvals.shape[1]
    per_row = rows // block_len

    def kernel(place_ref, members_ref, counts_ref, q_ref, kv_ref, more_ref, *refs):
        same_ref, diff_ref, q_sum, kv_sum, out = refs[len(earlier) :]
        for r in range(blocks):
            added = more_ref[r, rows:, :].astype(jnp.float32)
            added = jnp.concatenate([added[:, :cols], added[:, cols:]], axis=0)
            q_sum[r] = (q_ref[r] + added).astype(jnp.bfloat16)
            both = (kv_ref[r] + more_ref[r, :rows, :].astype(jnp.float32)).astype(jnp.bfloat16)
            both = both.reshape(2, rows // 2, 2 * cols)
            for j in range(per_row):
                part = both[:, j * BS : (j + 1) * BS, :]
                kv_sum[r * per_row + j] = part.reshape(block_len, 2 * cols)
        column = lax.broadcasted_iota(jnp.int32, (block_len, MAXB * block_len), 1)
        for b in range(blocks):
            live = column < counts_ref[b] * block_len
            listed = [kv_sum.at[members_ref[b * MAXB + j]] for j in range(MAXB)]
            for h in range(cols // HD):
                at = slice(h * HD, (h + 1) * HD)
                at_v = slice(cols + h * HD, cols + (h + 1) * HD)
                keys = jnp.concatenate([block[:, at] for block in listed], axis=0)
                values = jnp.concatenate([block[:, at_v] for block in listed], axis=0)
                scores = lax.dot_general(
                    q_sum[b, :, at], keys, (((1,), (1,)), ((), ())), preferred_element_type=jnp.float32
                )
                scores = jnp.where(live, scores, -jnp.inf)
                raised = jnp.exp2((scores - jnp.max(scores, axis=-1, keepdims=True)) * EXP2_SCALE)
                weights = raised * (1.0 / jnp.sum(raised, axis=-1, keepdims=True))
                blended = jnp.dot(
                    weights.astype(jnp.bfloat16), values, preferred_element_type=jnp.float32
                )
                out[(b + place_ref[0]) % 2, b // 2, :, at] = blended.astype(jnp.bfloat16)
        for i, out_ref in enumerate((same_ref, diff_ref)):
            if earlier:
                out_ref[:, :, :first] = refs[i][...]
            out_ref[:, :, first:] = out[i]

    half = jax.ShapeDtypeStruct((blocks // 2, block_len, first + cols), jnp.bfloat16)
    return call(
        kernel,
        (half, half),
        [place, members, counts],
        [queries, keyvals, more, *earlier],
        scratch=[
            pltpu.VMEM((blocks, block_len, cols), jnp.bfloat16),
            pltpu.VMEM((blocks * per_row, block_len, 2 * cols), jnp.bfloat16),
            pltpu.VMEM((2, blocks // 2, block_len, cols), jnp.bfloat16),
        ],
        flops=4 * blocks * block_len * MAXB * block_len * cols,
        read=16 * blocks * block_len * cols,
    )


def mix(place, attended, w_parts):
    blocks, block_len, cols = attended[0].shape
    width = w_parts[0].shape[1]

    def kernel(place_ref, *refs):
        row, group, frame, core = (place_ref[i] for i in range(4))
        w_refs = refs[4:12]
        keep, over_x, over_z, over_both, a_all, sums = refs[12:]
        for s in range(4):
            a_all[s] = refs[s][...].reshape(blocks * block_len, cols)

        def term(c, first, side):
            acc = None
            for i in range(2):
                at = 2 * side + (i if c == 0 else (i + group) % 2)
                part = jnp.dot(a_all[at ^ row], w_refs[first + i][...], preferred_element_type=jnp.float32)
                acc = part if acc is None else acc + part
            return acc.astype(jnp.bfloat16).astype(jnp.float32)

        for c in range(2):
            total = term(c, 2 * c, core) + term(c, 4 + 2 * c, 1 - core)
            sums[...] = total.reshape(blocks, 2, BS, width)
            at = (row + c) % 2
            keep[at] = sums[row // 2, frame]
            over_x[at] = sums[row // 2, 1 - frame].astype(jnp.bfloat16)
            over_z[at] = sums[1 - row // 2, frame].astype(jnp.bfloat16)
            over_both[at] = sums[1 - row // 2, 1 - frame].astype(jnp.bfloat16)

    shape = (2, BS, width)
    sent = jax.ShapeDtypeStruct(shape, jnp.bfloat16)
    return call(
        kernel,
        (jax.ShapeDtypeStruct(shape, jnp.float32), sent, sent, sent),
        [place],
        [*attended, *w_parts],
        scratch=[
            pltpu.VMEM((4, blocks * block_len, cols), jnp.bfloat16),
            pltpu.VMEM((blocks, 2, BS, width), jnp.float32),
        ],
        flops=2 * blocks * block_len * 4 * cols * 2 * width,
        read=16 * cols * width,
    )


def finish(place, keep, from_x, from_z, from_both):
    halves, rows, width = keep.shape

    def kernel(place_ref, keep_ref, x_ref, z_ref, both_ref, out_ref):
        pair = place_ref[0] // 2
        for c in range(halves):
            near = pl.multiple_of((pair * halves + c) * width, width)
            far = pl.multiple_of(((1 - pair) * halves + c) * width, width)
            out_ref[:, pl.ds(near, width)] = (keep_ref[c] + x_ref[c].astype(jnp.float32)).astype(jnp.bfloat16)
            out_ref[:, pl.ds(far, width)] = (
                z_ref[c].astype(jnp.float32) + both_ref[c].astype(jnp.float32)
            ).astype(jnp.bfloat16)

    return call(
        kernel,
        jax.ShapeDtypeStruct((rows, 2 * halves * width), jnp.bfloat16),
        [place],
        [keep, from_x, from_z, from_both],
        read=16 * rows * halves * width,
    )


def by_heads(latents, w_qkv, w_out, win_blocks, win_counts, block_window):
    rows_n, heads_n = lax.axis_size("rows"), lax.axis_size("heads")
    group, row = lax.axis_index("groups"), lax.axis_index("rows")
    frame, core = lax.axis_index("frames"), lax.axis_index("heads")
    depth, _, local_cols = w_qkv.shape
    span = rows_n // heads_n
    cols = local_cols // span
    half = depth // 2
    place = jnp.stack([row, group, frame, core]).astype(jnp.int32)

    def over_frames(value, rows):
        pairs = [(2 * r + f, 2 * r + 1 - f) for r in rows for f in range(2)]
        return lax.ppermute(value, ("rows", "frames"), pairs)

    def inward(value):
        return lax.ppermute(value, "rows", [(1, 2), (2, 1)])

    def outward(value):
        return lax.ppermute(value, "rows", [(1, 0), (2, 3)])

    last = cols // (3 * HD) * HD

    def reshard(i, *others):
        k = i % span
        at, wide = (0, cols - last) if i < span else (cols - last, last)
        value = lax.dynamic_slice(
            w_qkv.transpose(1, 0, 2), (0, group * half, (k + row) % span * cols + at), (3, half, wide)
        )
        pairs = [
            (r * heads_n + h, (h * span + (k + r) % span) * heads_n + r // span)
            for r in range(rows_n)
            for h in range(heads_n)
        ]
        return lax.ppermute(after(value, *others) if others else value, ("rows", "heads"), pairs)

    mine = lax.dynamic_slice_in_dim(latents[0], core * span * depth, span * depth, axis=1)
    in_1, near, mine_x = inward(mine), swap(mine, "rows"), swap(mine, "frames")
    here, there = [reshard(0)], []
    here.append(reshard(1, in_1, near, mine_x))
    in_2 = inward(after(near, in_1))
    near_x = swap(near, "frames")
    out_1, in_1x = outward(after(in_1, near_x)), over_frames(in_1, (1, 2))
    across = swap(after(w_out, near), "heads")
    there.append(swap(here[0], "groups"))
    here.append(reshard(2, in_2, out_1, near_x, in_1x, there[0], across))
    there.append(swap(here[1], "groups"))
    out_2, in_2x = outward(after(in_2, there[0])), over_frames(in_2, (1, 2))
    out_1x = over_frames(out_1, (0, 3))
    here.append(reshard(3, here[1], in_2x, out_1x))
    there += [swap(after(here[2], there[1]), "groups"), swap(here[3], "groups")]
    out_2x = over_frames(out_2, (0, 3))
    tokens = assemble(
        place, [(mine, mine_x), (near, near_x)], [(in_1, in_1x), (in_2, in_2x)], [(out_1, out_1x), (out_2, out_2x)]
    )

    tables = jnp.concatenate([win_blocks, win_counts[:, None], block_window[:, None]], axis=1)
    tables = after(tables, there[2])
    found = [tables] + [swap(tables, "rows", s) for s in range(1, rows_n)]
    tables = jnp.stack(found)[row ^ jnp.arange(rows_n)].reshape(rows_n * heads_n, MAXB + 2)
    windows = lax.dynamic_index_in_dim(
        tables[:, MAXB + 1].reshape(rows_n, heads_n), core, axis=1, keepdims=False
    )
    picked = tables[windows]
    members, counts = picked[:, :MAXB].reshape(-1), picked[:, MAXB]

    out_half = lax.dynamic_slice_in_dim(w_out, group * cols, cols, axis=0)
    beside = [swap(after(out_half, members, counts), "rows")]
    beside.append(swap(beside[0], "groups"))

    chunks = [(here[0], there[0]), (here[1], after(there[1], there[2]))]
    first = project(place, tokens, chunks)
    first_more = swap(first[2], "heads")
    second = project(place, tokens, [(here[2], there[2]), (here[3], after(there[3], first[2], beside[0]))])
    second_more = swap(second[2], "heads")
    attended = attend_all(place, members, counts, *first[:2], first_more)
    same, diff = attend_all(place, members, counts, *second[:2], second_more, attended)
    attended = [same] + [swap(same if s % 2 == 0 else diff, "rows", s) for s in range(1, rows_n)]
    halves = [w_out[:cols], w_out[cols:], *beside]
    beside_across = [swap(part, "heads") for part in (beside[0], after(beside[1], *attended[1:]))]
    keep, over_x, over_z, over_both = mix(
        place, attended, [*halves, across[:cols], across[cols:], *beside_across]
    )
    from_x = swap(over_x, "frames")
    from_z = swap(over_z, "rows", 2)
    from_both = lax.ppermute(
        over_both,
        ("rows", "frames"),
        [(2 * r + f, 2 * (r ^ 2) + 1 - f) for r in range(rows_n) for f in range(2)],
    )
    out = finish(place, keep, from_x, from_z, from_both)
    return out[None]


def local(latents, w_qkv, w_out, win_blocks, win_counts, block_window):
    rows_n = lax.axis_size("rows")
    pairs = all(lax.axis_size(axis) == 2 for axis in ("groups", "frames", "heads"))
    heads_here = w_qkv.shape[2] // HD
    if pairs and rows_n == 4 and heads_here == 6 and latents.shape[:2] == (1, 2 * BS):
        plan = by_heads
    else:
        plan = by_tokens
    return plan(latents, w_qkv, w_out, win_blocks, win_counts, block_window)


def solution(mesh):
    in_specs = (
        P(("groups", "frames"), "rows", None),
        P("rows", None, ("frames", "heads")),
        P(("frames", "heads"), "rows"),
        P(("groups", "rows"), None),
        P(("groups", "rows")),
        P(("groups", "rows")),
    )
    out_specs = P(("groups", "frames"), ("rows", "heads"), None)
    return jax.shard_map(local, mesh=mesh, in_specs=in_specs, out_specs=out_specs, check_vma=False)
```

```python
import math

import jax
import jax.numpy as jnp
from jax import lax
from jax.experimental import pallas as pl
from jax.experimental.pallas import tpu as pltpu
from jax.sharding import PartitionSpec as P

HD = 128
BS = 64
MAXB = 4
VMEM_BYTES = 24 * 1024 * 1024
WHOLE_VMEM_BYTES = 56 * 1024 * 1024
EXP2_SCALE = math.log2(math.e) / math.sqrt(HD)


def with_halo(value, sides, width):
    for axis, dim in sides:
        peers, length = (lax.axis_size(axis), value.shape[dim])
        up = [(i, (i + 1) % peers) for i in range(peers)]
        down = [(j, i) for i, j in up]
        last = lax.slice_in_dim(value, length - width, length, axis=dim)
        first = lax.slice_in_dim(value, 0, width, axis=dim)
        before = lax.ppermute(last, axis, up)
        after = lax.ppermute(first, axis, down)
        value = jnp.concatenate([before, value, after], axis=dim)
    return value


def by_tokens(latents, w_qkv, w_out, win_blocks, win_counts, block_window):
    rows_n = lax.axis_size("rows")
    shard_idx = lax.axis_index("rows")
    frames = latents.shape[0] * lax.axis_size("frames")
    tok_frame = latents.shape[1]
    model_width = latents.shape[2]
    local_cols = w_qkv.shape[2]
    per_shard = tok_frame // BS
    block_total = per_shard * rows_n
    heads_here = local_cols // HD
    block_len = frames * BS
    score_scale = 1.0 / math.sqrt(HD)
    gathered = lax.all_gather(latents, "frames", axis=0, tiled=True)
    flat_tokens = gathered.reshape(frames * tok_frame, model_width)
    weight_rows = lax.all_gather(w_qkv, "rows", axis=0, tiled=True)
    projected = jnp.dot(
        flat_tokens,
        weight_rows.reshape(weight_rows.shape[0], 3 * local_cols),
        preferred_element_type=jnp.float32,
    ).astype(jnp.bfloat16)
    blocked = projected.reshape(frames, per_shard, BS, 3, local_cols).transpose(1, 0, 2, 3, 4)
    blocked = blocked.reshape(per_shard, block_len, 3, local_cols)
    queries = blocked[:, :, 0]
    keyvals = blocked[:, :, 1:]
    nearby = with_halo(keyvals, (("rows", 0),), per_shard)
    first_block = shard_idx * per_shard
    owners = block_window - first_block
    members = win_blocks[owners]
    lengths = win_counts[owners]
    positions = (members - first_block + per_shard + block_total) % block_total

    def attend(query_rows, picked, live_mask):
        key_count = picked.shape[0]
        key_blocks = nearby[picked]
        key_part = key_blocks[:, :, 0].reshape(key_count * block_len, heads_here, HD)
        value_part = key_blocks[:, :, 1].reshape(key_count * block_len, heads_here, HD)
        scores = (
            jnp.einsum(
                "qhd,khd->hqk",
                query_rows.reshape(block_len, heads_here, HD),
                key_part,
                preferred_element_type=jnp.float32,
            )
            * score_scale
        )
        scores = jnp.where(live_mask[None, None, :], scores, -jnp.inf)
        row_max = jnp.max(scores, axis=-1, keepdims=True)
        raised = jnp.exp(scores - row_max)
        weights = (raised / jnp.sum(raised, axis=-1, keepdims=True)).astype(jnp.bfloat16)
        blended = jnp.einsum(
            "hqk,khd->qhd", weights, value_part, preferred_element_type=jnp.float32
        )
        return blended.reshape(block_len, local_cols).astype(jnp.bfloat16)

    def one_block(block_item):
        query_rows, picked, length = block_item
        live_mask = jnp.repeat(jnp.arange(MAXB) < length, block_len)
        return attend(query_rows, picked, live_mask)

    attended = lax.map(one_block, (queries, positions, lengths))
    ordered = attended.reshape(per_shard, frames, BS, local_cols).transpose(1, 0, 2, 3)
    ordered = ordered.reshape(frames * tok_frame, local_cols)
    w_full = lax.all_gather(w_out, "rows", axis=1, tiled=True)
    group_count = lax.axis_size(("frames", "heads"))
    out_rows = frames * tok_frame // group_count
    summed = lax.psum_scatter(
        jnp.dot(ordered, w_full, preferred_element_type=jnp.float32).astype(jnp.bfloat16),
        ("frames", "heads"),
        scatter_dimension=0,
        tiled=True,
    )
    return summed.reshape(1, out_rows, model_width)


def swap(value, axis, step=1):
    peers = lax.axis_size(axis)
    return lax.ppermute(value, axis, [(i, i ^ step) for i in range(peers)])


def after(value, *others):
    return lax.optimization_barrier((value, *others))[0]


def call(kernel, out_shape, prefetch, operands, scratch=(), flops=0, read=0, limit=VMEM_BYTES):
    return pl.pallas_call(
        kernel,
        out_shape=out_shape,
        grid_spec=pltpu.PrefetchScalarGridSpec(
            num_scalar_prefetch=len(prefetch),
            grid=(),
            in_specs=[pl.BlockSpec(memory_space=pltpu.VMEM)] * len(operands),
            out_specs=jax.tree.map(lambda _: pl.BlockSpec(memory_space=pltpu.VMEM), out_shape),
            scratch_shapes=scratch,
        ),
        compiler_params=pltpu.CompilerParams(vmem_limit_bytes=limit),
        cost_estimate=pl.CostEstimate(flops=flops, bytes_accessed=read, transcendentals=0),
    )(*prefetch, *operands)


def project(place, mine, theirs, chunks):
    rows, (count, width) = len(mine), mine[0].shape
    _, half, cols = chunks[0][0].shape
    slices = len(chunks)
    flat = [w for of_round in chunks for w in of_round]

    def kernel(place_ref, *refs):
        row, group, frame, core = (place_ref[i] for i in range(4))
        x_refs, w_refs = refs[: 2 * rows], refs[2 * rows : 2 * rows + len(flat)]
        q_keep, kv_keep, send, x_all, total, sems = refs[2 * rows + len(flat) :]
        copies = []
        for i, x_ref in enumerate(x_refs):
            to = x_all.at[row ^ (i % rows), (frame + i // rows) % 2]
            copies.append(pltpu.make_async_copy(x_ref, to, sems.at[i]))
            copies[-1].start()
        for copy in copies:
            copy.wait()
        acc = None
        for k in range(slices):
            for g in range(2):
                at = (row + slices - k) % slices * (2 * half) + (group + g) % 2 * half
                piece = x_all[:, :, :, pl.ds(pl.multiple_of(at, half), half)].reshape(-1, half)
                w_ref = w_refs[2 * k + g]
                weight = jnp.concatenate([w_ref[part] for part in range(3)], axis=1)
                term = jnp.dot(piece, weight, preferred_element_type=jnp.float32)
                acc = term if acc is None else acc + term
        kv_part = acc[:, cols:].reshape(rows, 2 * count, 2 * cols)
        kv_keep[...] = kv_part
        send[:, : 2 * count, :] = kv_part.astype(jnp.bfloat16)
        total[...] = acc[:, :cols].reshape(rows, 2, count, cols)
        own = pl.multiple_of(core * BS, BS)
        other = pl.multiple_of((1 - core) * BS, BS)
        q_keep[...] = total[:, :, pl.ds(own, BS), :].reshape(q_keep.shape)
        for f in range(2):
            at = slice(f * cols, (f + 1) * cols)
            send[:, 2 * count :, at] = total[:, f, pl.ds(other, BS), :].astype(jnp.bfloat16)

    vmem, anywhere = pl.BlockSpec(memory_space=pltpu.VMEM), pl.BlockSpec(memory_space=pl.ANY)
    flops = 2 * rows * 2 * count * width * 3 * cols
    return pl.pallas_call(
        kernel,
        out_shape=(
            jax.ShapeDtypeStruct((rows, 2 * BS, cols), jnp.float32),
            jax.ShapeDtypeStruct((rows, 2 * count, 2 * cols), jnp.float32),
            jax.ShapeDtypeStruct((rows, 2 * count + BS, 2 * cols), jnp.bfloat16),
        ),
        grid_spec=pltpu.PrefetchScalarGridSpec(
            num_scalar_prefetch=1,
            grid=(),
            in_specs=[anywhere] * (2 * rows) + [vmem] * len(flat),
            out_specs=(vmem, vmem, vmem),
            scratch_shapes=[
                pltpu.VMEM((rows, 2, count, width), jnp.bfloat16),
                pltpu.VMEM((rows, 2, count, cols), jnp.float32),
                pltpu.SemaphoreType.DMA((2 * rows,)),
            ],
        ),
        compiler_params=pltpu.CompilerParams(vmem_limit_bytes=VMEM_BYTES),
        cost_estimate=pl.CostEstimate(flops=8 * flops, bytes_accessed=flops // 300, transcendentals=0),
    )(place, *mine, *theirs, *flat)


def attend_all(place, members, counts, queries, keyvals, more, earlier=()):
    blocks, block_len, cols = queries.shape
    first = earlier[0].shape[2] if earlier else 0
    rows = keyvals.shape[1]
    per_row = rows // block_len

    def kernel(place_ref, members_ref, counts_ref, q_ref, kv_ref, more_ref, *refs):
        same_ref, diff_ref, q_sum, kv_sum, out = refs[len(earlier) :]
        for r in range(blocks):
            added = more_ref[r, rows:, :].astype(jnp.float32)
            added = jnp.concatenate([added[:, :cols], added[:, cols:]], axis=0)
            q_sum[r] = (q_ref[r] + added).astype(jnp.bfloat16)
            both = (kv_ref[r] + more_ref[r, :rows, :].astype(jnp.float32)).astype(jnp.bfloat16)
            both = both.reshape(2, rows // 2, 2 * cols)
            for j in range(per_row):
                part = both[:, j * BS : (j + 1) * BS, :]
                kv_sum[r * per_row + j] = part.reshape(block_len, 2 * cols)
        column = lax.broadcasted_iota(jnp.int32, (block_len, MAXB * block_len), 1)
        for b in range(blocks):
            live = column < counts_ref[b] * block_len
            listed = [kv_sum.at[members_ref[b * MAXB + j]] for j in range(MAXB)]
            for h in range(cols // HD):
                at = slice(h * HD, (h + 1) * HD)
                at_v = slice(cols + h * HD, cols + (h + 1) * HD)
                keys = jnp.concatenate([block[:, at] for block in listed], axis=0)
                values = jnp.concatenate([block[:, at_v] for block in listed], axis=0)
                scores = lax.dot_general(
                    q_sum[b, :, at], keys, (((1,), (1,)), ((), ())), preferred_element_type=jnp.float32
                )
                scores = jnp.where(live, scores, -jnp.inf)
                raised = jnp.exp2((scores - jnp.max(scores, axis=-1, keepdims=True)) * EXP2_SCALE)
                weights = raised * (1.0 / jnp.sum(raised, axis=-1, keepdims=True))
                blended = jnp.dot(
                    weights.astype(jnp.bfloat16), values, preferred_element_type=jnp.float32
                )
                out[(b + place_ref[0]) % 2, b // 2, :, at] = blended.astype(jnp.bfloat16)
        for i, out_ref in enumerate((same_ref, diff_ref)):
            if earlier:
                out_ref[:, :, :first] = refs[i][...]
            out_ref[:, :, first:] = out[i]

    half = jax.ShapeDtypeStruct((blocks // 2, block_len, first + cols), jnp.bfloat16)
    return call(
        kernel,
        (half, half),
        [place, members, counts],
        [queries, keyvals, more, *earlier],
        scratch=[
            pltpu.VMEM((blocks, block_len, cols), jnp.bfloat16),
            pltpu.VMEM((blocks * per_row, block_len, 2 * cols), jnp.bfloat16),
            pltpu.VMEM((2, blocks // 2, block_len, cols), jnp.bfloat16),
        ],
        flops=4 * blocks * block_len * MAXB * block_len * cols,
        read=16 * blocks * block_len * cols,
    )


def mix(place, attended, w_parts):
    blocks, block_len, cols = attended[0].shape
    width = w_parts[0].shape[1]

    def kernel(place_ref, *refs):
        row, group, frame, core = (place_ref[i] for i in range(4))
        w_refs = refs[4:12]
        keep, over_x, over_z, over_both, a_all, sums = refs[12:]
        for s in range(4):
            a_all[s] = refs[s][...].reshape(blocks * block_len, cols)

        def term(c, first, side):
            acc = None
            for i in range(2):
                at = 2 * side + (i if c == 0 else (i + group) % 2)
                part = jnp.dot(a_all[at ^ row], w_refs[first + i][...], preferred_element_type=jnp.float32)
                acc = part if acc is None else acc + part
            return acc.astype(jnp.bfloat16).astype(jnp.float32)

        for c in range(2):
            total = term(c, 2 * c, core) + term(c, 4 + 2 * c, 1 - core)
            sums[...] = total.reshape(blocks, 2, BS, width)
            at = (row + c) % 2
            keep[at] = sums[row // 2, frame]
            over_x[at] = sums[row // 2, 1 - frame].astype(jnp.bfloat16)
            over_z[at] = sums[1 - row // 2, frame].astype(jnp.bfloat16)
            over_both[at] = sums[1 - row // 2, 1 - frame].astype(jnp.bfloat16)

    shape = (2, BS, width)
    sent = jax.ShapeDtypeStruct(shape, jnp.bfloat16)
    return call(
        kernel,
        (jax.ShapeDtypeStruct(shape, jnp.float32), sent, sent, sent),
        [place],
        [*attended, *w_parts],
        scratch=[
            pltpu.VMEM((4, blocks * block_len, cols), jnp.bfloat16),
            pltpu.VMEM((blocks, 2, BS, width), jnp.float32),
        ],
        flops=2 * blocks * block_len * 4 * cols * 2 * width,
        read=16 * cols * width,
    )


def finish(place, keep, from_x, from_z, from_both):
    halves, rows, width = keep.shape

    def kernel(place_ref, keep_ref, x_ref, z_ref, both_ref, out_ref):
        pair = place_ref[0] // 2
        for c in range(halves):
            near = pl.multiple_of((pair * halves + c) * width, width)
            far = pl.multiple_of(((1 - pair) * halves + c) * width, width)
            out_ref[:, pl.ds(near, width)] = (keep_ref[c] + x_ref[c].astype(jnp.float32)).astype(jnp.bfloat16)
            out_ref[:, pl.ds(far, width)] = (
                z_ref[c].astype(jnp.float32) + both_ref[c].astype(jnp.float32)
            ).astype(jnp.bfloat16)

    return call(
        kernel,
        jax.ShapeDtypeStruct((rows, 2 * halves * width), jnp.bfloat16),
        [place],
        [keep, from_x, from_z, from_both],
        read=16 * rows * halves * width,
    )


def by_heads(latents, w_qkv, w_out, win_blocks, win_counts, block_window):
    rows_n, heads_n = lax.axis_size("rows"), lax.axis_size("heads")
    group, row = lax.axis_index("groups"), lax.axis_index("rows")
    frame, core = lax.axis_index("frames"), lax.axis_index("heads")
    depth, _, local_cols = w_qkv.shape
    span = rows_n // heads_n
    cols = local_cols // span
    half = depth // 2
    place = jnp.stack([row, group, frame, core]).astype(jnp.int32)

    last = cols // (3 * HD) * HD

    def reshard(i, *others):
        k = i % span
        at, wide = (0, cols - last) if i < span else (cols - last, last)
        value = lax.dynamic_slice(
            w_qkv.transpose(1, 0, 2), (0, group * half, (k + row) % span * cols + at), (3, half, wide)
        )
        pairs = [
            (r * heads_n + h, (h * span + (k + r) % span) * heads_n + r // span)
            for r in range(rows_n)
            for h in range(heads_n)
        ]
        return lax.ppermute(after(value, *others) if others else value, ("rows", "heads"), pairs)

    tables = jnp.concatenate([win_blocks, win_counts[:, None], block_window[:, None]], axis=1)
    found = [tables] + [swap(tables, "rows", s) for s in range(1, rows_n)]
    tables = jnp.stack(found)[row ^ jnp.arange(rows_n)].reshape(rows_n * heads_n, MAXB + 2)
    windows = lax.dynamic_index_in_dim(
        tables[:, MAXB + 1].reshape(rows_n, heads_n), core, axis=1, keepdims=False
    )
    picked = tables[windows]
    members, counts = picked[:, :MAXB].reshape(-1), picked[:, MAXB]

    mine = lax.dynamic_slice_in_dim(latents[0], core * span * depth, span * depth, axis=1)
    near, mine_x = swap(mine, "rows"), swap(mine, "frames")
    here, there = [reshard(0)], []
    far_2 = swap(after(mine, members, counts), "rows", 2)
    here.append(reshard(1, near, mine_x, here[0]))
    near_x = swap(near, "frames")
    across = swap(after(w_out, near), "heads")
    there.append(swap(here[0], "groups"))
    far_3 = swap(after(mine, here[0], near_x), "rows", 3)
    here.append(reshard(2, far_2, across))
    far_2x = swap(far_2, "frames")
    here.append(reshard(3, here[1], there[0], far_2x))
    there.append(swap(here[1], "groups"))
    far_3x = swap(far_3, "frames")
    there += [swap(here[2], "groups"), swap(here[3], "groups")]

    out_half = lax.dynamic_slice_in_dim(w_out, group * cols, cols, axis=0)
    beside = [swap(after(out_half, here[3]), "rows")]

    pieces = [mine, near, far_2, far_3], [mine_x, near_x, far_2x, far_3x]
    first = project(place, *pieces, [(here[0], there[0]), (here[1], after(there[1], there[2]))])
    first_more = swap(first[2], "heads")
    second = project(place, *pieces, [(here[2], there[2]), (here[3], after(there[3], first[2]))])
    second_more = swap(second[2], "heads")
    attended = attend_all(place, members, counts, first[0], after(first[1], beside[0]), first_more)
    beside.append(swap(after(beside[0], attended[0]), "groups"))
    same, diff = attend_all(place, members, counts, *second[:2], second_more, attended)
    attended = [same] + [swap(same if s % 2 == 0 else diff, "rows", s) for s in range(1, rows_n)]
    halves = [w_out[:cols], w_out[cols:], *beside]
    beside_across = [swap(part, "heads") for part in (beside[0], after(beside[1], *attended[1:]))]
    keep, over_x, over_z, over_both = mix(
        place, attended, [*halves, across[:cols], across[cols:], *beside_across]
    )
    from_x = swap(over_x, "frames")
    from_z = swap(over_z, "rows", 2)
    from_both = lax.ppermute(
        over_both,
        ("rows", "frames"),
        [(2 * r + f, 2 * (r ^ 2) + 1 - f) for r in range(rows_n) for f in range(2)],
    )
    out = finish(place, keep, from_x, from_z, from_both)
    return out[None]


def local(latents, w_qkv, w_out, win_blocks, win_counts, block_window):
    rows_n = lax.axis_size("rows")
    pairs = all(lax.axis_size(axis) == 2 for axis in ("groups", "frames", "heads"))
    heads_here = w_qkv.shape[2] // HD
    if pairs and rows_n == 4 and heads_here == 6 and latents.shape[:2] == (1, 2 * BS):
        plan = by_heads
    else:
        plan = by_tokens
    return plan(latents, w_qkv, w_out, win_blocks, win_counts, block_window)


def solution(mesh):
    in_specs = (
        P(("groups", "frames"), "rows", None),
        P("rows", None, ("frames", "heads")),
        P(("frames", "heads"), "rows"),
        P(("groups", "rows"), None),
        P(("groups", "rows")),
        P(("groups", "rows")),
    )
    out_specs = P(("groups", "frames"), ("rows", "heads"), None)
    return jax.shard_map(local, mesh=mesh, in_specs=in_specs, out_specs=out_specs, check_vma=False)
```

```python
import math

import jax
import jax.numpy as jnp
from jax import lax
from jax.experimental import pallas as pl
from jax.experimental.pallas import tpu as pltpu
from jax.sharding import PartitionSpec as P

HD = 128
BS = 64
MAXB = 4
VMEM_BYTES = 24 * 1024 * 1024
WHOLE_VMEM_BYTES = 56 * 1024 * 1024
EXP2_SCALE = math.log2(math.e) / math.sqrt(HD)


def with_halo(value, sides, width):
    for axis, dim in sides:
        peers, length = (lax.axis_size(axis), value.shape[dim])
        up = [(i, (i + 1) % peers) for i in range(peers)]
        down = [(j, i) for i, j in up]
        last = lax.slice_in_dim(value, length - width, length, axis=dim)
        first = lax.slice_in_dim(value, 0, width, axis=dim)
        before = lax.ppermute(last, axis, up)
        after = lax.ppermute(first, axis, down)
        value = jnp.concatenate([before, value, after], axis=dim)
    return value


def by_tokens(latents, w_qkv, w_out, win_blocks, win_counts, block_window):
    rows_n = lax.axis_size("rows")
    shard_idx = lax.axis_index("rows")
    frames = latents.shape[0] * lax.axis_size("frames")
    tok_frame = latents.shape[1]
    model_width = latents.shape[2]
    local_cols = w_qkv.shape[2]
    per_shard = tok_frame // BS
    block_total = per_shard * rows_n
    heads_here = local_cols // HD
    block_len = frames * BS
    score_scale = 1.0 / math.sqrt(HD)
    gathered = lax.all_gather(latents, "frames", axis=0, tiled=True)
    flat_tokens = gathered.reshape(frames * tok_frame, model_width)
    weight_rows = lax.all_gather(w_qkv, "rows", axis=0, tiled=True)
    projected = jnp.dot(
        flat_tokens,
        weight_rows.reshape(weight_rows.shape[0], 3 * local_cols),
        preferred_element_type=jnp.float32,
    ).astype(jnp.bfloat16)
    blocked = projected.reshape(frames, per_shard, BS, 3, local_cols).transpose(1, 0, 2, 3, 4)
    blocked = blocked.reshape(per_shard, block_len, 3, local_cols)
    queries = blocked[:, :, 0]
    keyvals = blocked[:, :, 1:]
    nearby = with_halo(keyvals, (("rows", 0),), per_shard)
    first_block = shard_idx * per_shard
    owners = block_window - first_block
    members = win_blocks[owners]
    lengths = win_counts[owners]
    positions = (members - first_block + per_shard + block_total) % block_total

    def attend(query_rows, picked, live_mask):
        key_count = picked.shape[0]
        key_blocks = nearby[picked]
        key_part = key_blocks[:, :, 0].reshape(key_count * block_len, heads_here, HD)
        value_part = key_blocks[:, :, 1].reshape(key_count * block_len, heads_here, HD)
        scores = (
            jnp.einsum(
                "qhd,khd->hqk",
                query_rows.reshape(block_len, heads_here, HD),
                key_part,
                preferred_element_type=jnp.float32,
            )
            * score_scale
        )
        scores = jnp.where(live_mask[None, None, :], scores, -jnp.inf)
        row_max = jnp.max(scores, axis=-1, keepdims=True)
        raised = jnp.exp(scores - row_max)
        weights = (raised / jnp.sum(raised, axis=-1, keepdims=True)).astype(jnp.bfloat16)
        blended = jnp.einsum(
            "hqk,khd->qhd", weights, value_part, preferred_element_type=jnp.float32
        )
        return blended.reshape(block_len, local_cols).astype(jnp.bfloat16)

    def one_block(block_item):
        query_rows, picked, length = block_item
        live_mask = jnp.repeat(jnp.arange(MAXB) < length, block_len)
        return attend(query_rows, picked, live_mask)

    attended = lax.map(one_block, (queries, positions, lengths))
    ordered = attended.reshape(per_shard, frames, BS, local_cols).transpose(1, 0, 2, 3)
    ordered = ordered.reshape(frames * tok_frame, local_cols)
    w_full = lax.all_gather(w_out, "rows", axis=1, tiled=True)
    group_count = lax.axis_size(("frames", "heads"))
    out_rows = frames * tok_frame // group_count
    summed = lax.psum_scatter(
        jnp.dot(ordered, w_full, preferred_element_type=jnp.float32).astype(jnp.bfloat16),
        ("frames", "heads"),
        scatter_dimension=0,
        tiled=True,
    )
    return summed.reshape(1, out_rows, model_width)


def swap(value, axis, step=1):
    peers = lax.axis_size(axis)
    return lax.ppermute(value, axis, [(i, i ^ step) for i in range(peers)])


def after(value, *others):
    return lax.optimization_barrier((value, *others))[0]


def call(kernel, out_shape, prefetch, operands, scratch=(), flops=0, read=0, limit=VMEM_BYTES):
    return pl.pallas_call(
        kernel,
        out_shape=out_shape,
        grid_spec=pltpu.PrefetchScalarGridSpec(
            num_scalar_prefetch=len(prefetch),
            grid=(),
            in_specs=[pl.BlockSpec(memory_space=pltpu.VMEM)] * len(operands),
            out_specs=jax.tree.map(lambda _: pl.BlockSpec(memory_space=pltpu.VMEM), out_shape),
            scratch_shapes=scratch,
        ),
        compiler_params=pltpu.CompilerParams(vmem_limit_bytes=limit),
        cost_estimate=pl.CostEstimate(flops=flops, bytes_accessed=read, transcendentals=0),
    )(*prefetch, *operands)


def project(place, tokens, chunks):
    rows, _, count, width = tokens.shape
    _, half, cols = chunks[0][0].shape
    slices = len(chunks)
    flat = [w for of_round in chunks for w in of_round]
    total_rows = rows * 2 * count

    def kernel(place_ref, x_ref, *refs):
        row, group, core = place_ref[0], place_ref[1], place_ref[3]
        w_refs = refs[: len(flat)]
        q_keep, kv_keep, send, total = refs[len(flat) :]
        acc = None
        for k in range(slices):
            for g in range(2):
                at = (row + slices - k) % slices * (2 * half) + (group + g) % 2 * half
                piece = x_ref[:, :, :, pl.ds(pl.multiple_of(at, half), half)].reshape(-1, half)
                w_ref = w_refs[2 * k + g]
                weight = jnp.concatenate([w_ref[part] for part in range(3)], axis=1)
                term = jnp.dot(piece, weight, preferred_element_type=jnp.float32)
                acc = term if acc is None else acc + term
        kv_part = acc[:, cols:].reshape(rows, 2 * count, 2 * cols)
        kv_keep[...] = kv_part
        send[:, : 2 * count, :] = kv_part.astype(jnp.bfloat16)
        total[...] = acc[:, :cols].reshape(rows, 2, count, cols)
        own = pl.multiple_of(core * BS, BS)
        other = pl.multiple_of((1 - core) * BS, BS)
        q_keep[...] = total[:, :, pl.ds(own, BS), :].reshape(q_keep.shape)
        for f in range(2):
            at = slice(f * cols, (f + 1) * cols)
            send[:, 2 * count :, at] = total[:, f, pl.ds(other, BS), :].astype(jnp.bfloat16)

    flops = 2 * total_rows * width * 3 * cols
    return call(
        kernel,
        (
            jax.ShapeDtypeStruct((rows, 2 * BS, cols), jnp.float32),
            jax.ShapeDtypeStruct((rows, 2 * count, 2 * cols), jnp.float32),
            jax.ShapeDtypeStruct((rows, 2 * count + BS, 2 * cols), jnp.bfloat16),
        ),
        [place],
        [tokens, *flat],
        scratch=[pltpu.VMEM((rows, 2, count, cols), jnp.float32)],
        flops=8 * flops,
        read=flops // 300,
    )


def attend_all(place, members, counts, queries, keyvals, more, earlier=()):
    blocks, block_len, cols = queries.shape
    first = earlier[0].shape[2] if earlier else 0
    rows = keyvals.shape[1]
    per_row = rows // block_len

    def kernel(place_ref, members_ref, counts_ref, q_ref, kv_ref, more_ref, *refs):
        same_ref, diff_ref, q_sum, kv_sum, out = refs[len(earlier) :]
        for r in range(blocks):
            added = more_ref[r, rows:, :].astype(jnp.float32)
            added = jnp.concatenate([added[:, :cols], added[:, cols:]], axis=0)
            q_sum[r] = (q_ref[r] + added).astype(jnp.bfloat16)
            both = (kv_ref[r] + more_ref[r, :rows, :].astype(jnp.float32)).astype(jnp.bfloat16)
            both = both.reshape(2, rows // 2, 2 * cols)
            for j in range(per_row):
                part = both[:, j * BS : (j + 1) * BS, :]
                kv_sum[r * per_row + j] = part.reshape(block_len, 2 * cols)
        column = lax.broadcasted_iota(jnp.int32, (block_len, MAXB * block_len), 1)
        for b in range(blocks):
            live = column < counts_ref[b] * block_len
            listed = [kv_sum.at[members_ref[b * MAXB + j]] for j in range(MAXB)]
            for h in range(cols // HD):
                at = slice(h * HD, (h + 1) * HD)
                at_v = slice(cols + h * HD, cols + (h + 1) * HD)
                keys = jnp.concatenate([block[:, at] for block in listed], axis=0)
                values = jnp.concatenate([block[:, at_v] for block in listed], axis=0)
                scores = lax.dot_general(
                    q_sum[b, :, at], keys, (((1,), (1,)), ((), ())), preferred_element_type=jnp.float32
                )
                scores = jnp.where(live, scores, -jnp.inf)
                raised = jnp.exp2((scores - jnp.max(scores, axis=-1, keepdims=True)) * EXP2_SCALE)
                weights = raised * (1.0 / jnp.sum(raised, axis=-1, keepdims=True))
                blended = jnp.dot(
                    weights.astype(jnp.bfloat16), values, preferred_element_type=jnp.float32
                )
                out[(b + place_ref[0]) % 2, b // 2, :, at] = blended.astype(jnp.bfloat16)
        for i, out_ref in enumerate((same_ref, diff_ref)):
            if earlier:
                out_ref[:, :, :first] = refs[i][...]
            out_ref[:, :, first:] = out[i]

    half = jax.ShapeDtypeStruct((blocks // 2, block_len, first + cols), jnp.bfloat16)
    return call(
        kernel,
        (half, half),
        [place, members, counts],
        [queries, keyvals, more, *earlier],
        scratch=[
            pltpu.VMEM((blocks, block_len, cols), jnp.bfloat16),
            pltpu.VMEM((blocks * per_row, block_len, 2 * cols), jnp.bfloat16),
            pltpu.VMEM((2, blocks // 2, block_len, cols), jnp.bfloat16),
        ],
        flops=4 * blocks * block_len * MAXB * block_len * cols,
        read=16 * blocks * block_len * cols,
    )


def mix(place, attended, w_parts):
    blocks, block_len, cols = attended[0].shape
    width = w_parts[0].shape[1]

    def kernel(place_ref, *refs):
        row, group, frame, core = (place_ref[i] for i in range(4))
        w_refs = refs[4:12]
        keep, over_x, over_z, over_both, a_all, sums = refs[12:]
        for s in range(4):
            a_all[s] = refs[s][...].reshape(blocks * block_len, cols)

        def term(c, first, side):
            acc = None
            for i in range(2):
                at = 2 * side + (i if c == 0 else (i + group) % 2)
                part = jnp.dot(a_all[at ^ row], w_refs[first + i][...], preferred_element_type=jnp.float32)
                acc = part if acc is None else acc + part
            return acc.astype(jnp.bfloat16).astype(jnp.float32)

        for c in range(2):
            total = term(c, 2 * c, core) + term(c, 4 + 2 * c, 1 - core)
            sums[...] = total.reshape(blocks, 2, BS, width)
            at = (row + c) % 2
            keep[at] = sums[row // 2, frame]
            over_x[at] = sums[row // 2, 1 - frame].astype(jnp.bfloat16)
            over_z[at] = sums[1 - row // 2, frame].astype(jnp.bfloat16)
            over_both[at] = sums[1 - row // 2, 1 - frame].astype(jnp.bfloat16)

    shape = (2, BS, width)
    sent = jax.ShapeDtypeStruct(shape, jnp.bfloat16)
    return call(
        kernel,
        (jax.ShapeDtypeStruct(shape, jnp.float32), sent, sent, sent),
        [place],
        [*attended, *w_parts],
        scratch=[
            pltpu.VMEM((4, blocks * block_len, cols), jnp.bfloat16),
            pltpu.VMEM((blocks, 2, BS, width), jnp.float32),
        ],
        flops=2 * blocks * block_len * 4 * cols * 2 * width,
        read=16 * cols * width,
    )


def finish(place, keep, from_x, from_z, from_both):
    halves, rows, width = keep.shape

    def kernel(place_ref, keep_ref, x_ref, z_ref, both_ref, out_ref):
        pair = place_ref[0] // 2
        for c in range(halves):
            near = pl.multiple_of((pair * halves + c) * width, width)
            far = pl.multiple_of(((1 - pair) * halves + c) * width, width)
            out_ref[:, pl.ds(near, width)] = (keep_ref[c] + x_ref[c].astype(jnp.float32)).astype(jnp.bfloat16)
            out_ref[:, pl.ds(far, width)] = (
                z_ref[c].astype(jnp.float32) + both_ref[c].astype(jnp.float32)
            ).astype(jnp.bfloat16)

    return call(
        kernel,
        jax.ShapeDtypeStruct((rows, 2 * halves * width), jnp.bfloat16),
        [place],
        [keep, from_x, from_z, from_both],
        read=16 * rows * halves * width,
    )


def by_heads(latents, w_qkv, w_out, win_blocks, win_counts, block_window):
    rows_n, heads_n = lax.axis_size("rows"), lax.axis_size("heads")
    group, row = lax.axis_index("groups"), lax.axis_index("rows")
    frame, core = lax.axis_index("frames"), lax.axis_index("heads")
    count = latents.shape[1]
    depth, _, local_cols = w_qkv.shape
    span = rows_n // heads_n
    cols = local_cols // span
    half = depth // 2
    place = jnp.stack([row, group, frame, core]).astype(jnp.int32)

    last = cols // (3 * HD) * HD

    def reshard(i, *others):
        k = i % span
        at, wide = (0, cols - last) if i < span else (cols - last, last)
        value = lax.dynamic_slice(
            w_qkv.transpose(1, 0, 2), (0, group * half, (k + row) % span * cols + at), (3, half, wide)
        )
        pairs = [
            (r * heads_n + h, (h * span + (k + r) % span) * heads_n + r // span)
            for r in range(rows_n)
            for h in range(heads_n)
        ]
        return lax.ppermute(after(value, *others) if others else value, ("rows", "heads"), pairs)

    mine = lax.dynamic_slice_in_dim(latents[0], core * span * depth, span * depth, axis=1)
    tokens = lax.all_gather(mine, ("rows", "frames"), axis=0).reshape(rows_n, 2, count, span * depth)

    tables = jnp.concatenate([win_blocks, win_counts[:, None], block_window[:, None]], axis=1)
    found = [tables] + [swap(tables, "rows", s) for s in range(1, rows_n)]
    tables = jnp.stack(found)[row ^ jnp.arange(rows_n)].reshape(rows_n * heads_n, MAXB + 2)
    windows = lax.dynamic_index_in_dim(
        tables[:, MAXB + 1].reshape(rows_n, heads_n), core, axis=1, keepdims=False
    )
    picked = tables[windows]
    members, counts = picked[:, :MAXB].reshape(-1), picked[:, MAXB]

    here, there = [reshard(0), reshard(1)], []
    there += [swap(here[0], "groups"), swap(here[1], "groups")]
    across = swap(w_out, "heads")
    here.append(reshard(2, here[0], here[1], members, counts))
    here.append(reshard(3, there[0], across))
    there += [swap(here[2], "groups"), swap(here[3], "groups")]
    out_half = lax.dynamic_slice_in_dim(w_out, group * cols, cols, axis=0)
    beside = [swap(after(out_half, here[2]), "rows")]
    beside.append(swap(beside[0], "groups"))
    beside_across = [swap(part, "heads") for part in beside]

    tokens = after(tokens, *there, *beside, *beside_across)
    first = project(place, tokens, [(here[0], there[0]), (here[1], there[1])])
    first_more = swap(first[2], "heads")
    second = project(place, tokens, [(here[2], there[2]), (here[3], after(there[3], first[2]))])
    second_more = swap(second[2], "heads")
    attended = attend_all(place, members, counts, *first[:2], first_more)
    same, diff = attend_all(place, members, counts, *second[:2], second_more, attended)
    attended = [same] + [swap(same if s % 2 == 0 else diff, "rows", s) for s in range(1, rows_n)]
    halves = [w_out[:cols], w_out[cols:], *beside]
    keep, over_x, over_z, over_both = mix(
        place, attended, [*halves, across[:cols], across[cols:], *beside_across]
    )
    from_x = swap(over_x, "frames")
    from_z = swap(over_z, "rows", 2)
    from_both = lax.ppermute(
        over_both,
        ("rows", "frames"),
        [(2 * r + f, 2 * (r ^ 2) + 1 - f) for r in range(rows_n) for f in range(2)],
    )
    out = finish(place, keep, from_x, from_z, from_both)
    return out[None]


def local(latents, w_qkv, w_out, win_blocks, win_counts, block_window):
    rows_n = lax.axis_size("rows")
    pairs = all(lax.axis_size(axis) == 2 for axis in ("groups", "frames", "heads"))
    heads_here = w_qkv.shape[2] // HD
    if pairs and rows_n == 4 and heads_here == 6 and latents.shape[:2] == (1, 2 * BS):
        plan = by_heads
    else:
        plan = by_tokens
    return plan(latents, w_qkv, w_out, win_blocks, win_counts, block_window)


def solution(mesh):
    in_specs = (
        P(("groups", "frames"), "rows", None),
        P("rows", None, ("frames", "heads")),
        P(("frames", "heads"), "rows"),
        P(("groups", "rows"), None),
        P(("groups", "rows")),
        P(("groups", "rows")),
    )
    out_specs = P(("groups", "frames"), ("rows", "heads"), None)
    return jax.shard_map(local, mesh=mesh, in_specs=in_specs, out_specs=out_specs, check_vma=False)
```

```python
import math

import jax
import jax.numpy as jnp
from jax import lax
from jax.experimental import pallas as pl
from jax.experimental.pallas import tpu as pltpu
from jax.sharding import PartitionSpec as P

HD = 128
BS = 64
MAXB = 4
VMEM_BYTES = 24 * 1024 * 1024
WHOLE_VMEM_BYTES = 56 * 1024 * 1024
EXP2_SCALE = math.log2(math.e) / math.sqrt(HD)


def with_halo(value, sides, width):
    for axis, dim in sides:
        peers, length = (lax.axis_size(axis), value.shape[dim])
        up = [(i, (i + 1) % peers) for i in range(peers)]
        down = [(j, i) for i, j in up]
        last = lax.slice_in_dim(value, length - width, length, axis=dim)
        first = lax.slice_in_dim(value, 0, width, axis=dim)
        before = lax.ppermute(last, axis, up)
        after = lax.ppermute(first, axis, down)
        value = jnp.concatenate([before, value, after], axis=dim)
    return value


def by_tokens(latents, w_qkv, w_out, win_blocks, win_counts, block_window):
    rows_n = lax.axis_size("rows")
    shard_idx = lax.axis_index("rows")
    frames = latents.shape[0] * lax.axis_size("frames")
    tok_frame = latents.shape[1]
    model_width = latents.shape[2]
    local_cols = w_qkv.shape[2]
    per_shard = tok_frame // BS
    block_total = per_shard * rows_n
    heads_here = local_cols // HD
    block_len = frames * BS
    score_scale = 1.0 / math.sqrt(HD)
    gathered = lax.all_gather(latents, "frames", axis=0, tiled=True)
    flat_tokens = gathered.reshape(frames * tok_frame, model_width)
    weight_rows = lax.all_gather(w_qkv, "rows", axis=0, tiled=True)
    projected = jnp.dot(
        flat_tokens,
        weight_rows.reshape(weight_rows.shape[0], 3 * local_cols),
        preferred_element_type=jnp.float32,
    ).astype(jnp.bfloat16)
    blocked = projected.reshape(frames, per_shard, BS, 3, local_cols).transpose(1, 0, 2, 3, 4)
    blocked = blocked.reshape(per_shard, block_len, 3, local_cols)
    queries = blocked[:, :, 0]
    keyvals = blocked[:, :, 1:]
    nearby = with_halo(keyvals, (("rows", 0),), per_shard)
    first_block = shard_idx * per_shard
    owners = block_window - first_block
    members = win_blocks[owners]
    lengths = win_counts[owners]
    positions = (members - first_block + per_shard + block_total) % block_total

    def attend(query_rows, picked, live_mask):
        key_count = picked.shape[0]
        key_blocks = nearby[picked]
        key_part = key_blocks[:, :, 0].reshape(key_count * block_len, heads_here, HD)
        value_part = key_blocks[:, :, 1].reshape(key_count * block_len, heads_here, HD)
        scores = (
            jnp.einsum(
                "qhd,khd->hqk",
                query_rows.reshape(block_len, heads_here, HD),
                key_part,
                preferred_element_type=jnp.float32,
            )
            * score_scale
        )
        scores = jnp.where(live_mask[None, None, :], scores, -jnp.inf)
        row_max = jnp.max(scores, axis=-1, keepdims=True)
        raised = jnp.exp(scores - row_max)
        weights = (raised / jnp.sum(raised, axis=-1, keepdims=True)).astype(jnp.bfloat16)
        blended = jnp.einsum(
            "hqk,khd->qhd", weights, value_part, preferred_element_type=jnp.float32
        )
        return blended.reshape(block_len, local_cols).astype(jnp.bfloat16)

    def one_block(block_item):
        query_rows, picked, length = block_item
        live_mask = jnp.repeat(jnp.arange(MAXB) < length, block_len)
        return attend(query_rows, picked, live_mask)

    attended = lax.map(one_block, (queries, positions, lengths))
    ordered = attended.reshape(per_shard, frames, BS, local_cols).transpose(1, 0, 2, 3)
    ordered = ordered.reshape(frames * tok_frame, local_cols)
    w_full = lax.all_gather(w_out, "rows", axis=1, tiled=True)
    group_count = lax.axis_size(("frames", "heads"))
    out_rows = frames * tok_frame // group_count
    summed = lax.psum_scatter(
        jnp.dot(ordered, w_full, preferred_element_type=jnp.float32).astype(jnp.bfloat16),
        ("frames", "heads"),
        scatter_dimension=0,
        tiled=True,
    )
    return summed.reshape(1, out_rows, model_width)


def swap(value, axis, step=1):
    peers = lax.axis_size(axis)
    return lax.ppermute(value, axis, [(i, i ^ step) for i in range(peers)])


def after(value, *others):
    return lax.optimization_barrier((value, *others))[0]


def call(kernel, out_shape, prefetch, operands, scratch=(), flops=0, read=0, limit=VMEM_BYTES):
    return pl.pallas_call(
        kernel,
        out_shape=out_shape,
        grid_spec=pltpu.PrefetchScalarGridSpec(
            num_scalar_prefetch=len(prefetch),
            grid=(),
            in_specs=[pl.BlockSpec(memory_space=pltpu.VMEM)] * len(operands),
            out_specs=jax.tree.map(lambda _: pl.BlockSpec(memory_space=pltpu.VMEM), out_shape),
            scratch_shapes=scratch,
        ),
        compiler_params=pltpu.CompilerParams(vmem_limit_bytes=limit),
        cost_estimate=pl.CostEstimate(flops=flops, bytes_accessed=read, transcendentals=0),
    )(*prefetch, *operands)


def project(place, mine, theirs, chunks):
    rows, (count, width) = len(mine), theirs[0].shape
    _, half, cols = chunks[0][0].shape
    slices = len(chunks)
    flat = [w for of_round in chunks for w in of_round]

    def kernel(place_ref, *refs):
        row, group, frame, core = (place_ref[i] for i in range(4))
        x_refs, w_refs = refs[: 2 * rows], refs[2 * rows : 2 * rows + len(flat)]
        q_keep, kv_keep, send, x_all, w_all, total, sems = refs[2 * rows + len(flat) :]
        copies = []
        for i, x_ref in enumerate(x_refs):
            to = x_all.at[row ^ (i % rows), (frame + i // rows) % 2]
            copies.append(pltpu.make_async_copy(x_ref.at[pl.ds(0, count)], to, sems.at[i]))
            copies[-1].start()
        for k in range(slices):
            for g in range(2):
                at = (row + slices - k) % slices * (2 * half) + (group + g) % 2 * half
                for part in range(3):
                    into = w_all.at[pl.ds(pl.multiple_of(at, half), half), part * cols : (part + 1) * cols]
                    into[...] = w_refs[2 * k + g][part]
        for copy in copies:
            copy.wait()
        acc = jnp.dot(x_all[...].reshape(-1, width), w_all[...], preferred_element_type=jnp.float32)
        kv_part = acc[:, cols:].reshape(rows, 2 * count, 2 * cols)
        kv_keep[...] = kv_part
        send[:, : 2 * count, :] = kv_part.astype(jnp.bfloat16)
        total[...] = acc[:, :cols].reshape(rows, 2, count, cols)
        own = pl.multiple_of(core * BS, BS)
        other = pl.multiple_of((1 - core) * BS, BS)
        q_keep[...] = total[:, :, pl.ds(own, BS), :].reshape(q_keep.shape)
        for f in range(2):
            at = slice(f * cols, (f + 1) * cols)
            send[:, 2 * count :, at] = total[:, f, pl.ds(other, BS), :].astype(jnp.bfloat16)

    vmem, hbm = pl.BlockSpec(memory_space=pltpu.VMEM), pl.BlockSpec(memory_space=pltpu.HBM)
    flops = 2 * rows * 2 * count * width * 3 * cols
    return pl.pallas_call(
        kernel,
        out_shape=(
            jax.ShapeDtypeStruct((rows, 2 * BS, cols), jnp.float32),
            jax.ShapeDtypeStruct((rows, 2 * count, 2 * cols), jnp.float32),
            jax.ShapeDtypeStruct((rows, 2 * count + BS, 2 * cols), jnp.bfloat16),
        ),
        grid_spec=pltpu.PrefetchScalarGridSpec(
            num_scalar_prefetch=1,
            grid=(),
            in_specs=[hbm] * (2 * rows) + [vmem] * len(flat),
            out_specs=(vmem, vmem, vmem),
            scratch_shapes=[
                pltpu.VMEM((rows, 2, count, width), jnp.bfloat16),
                pltpu.VMEM((width, 3 * cols), jnp.bfloat16),
                pltpu.VMEM((rows, 2, count, cols), jnp.float32),
                pltpu.SemaphoreType.DMA((2 * rows,)),
            ],
        ),
        compiler_params=pltpu.CompilerParams(vmem_limit_bytes=VMEM_BYTES),
        cost_estimate=pl.CostEstimate(flops=8 * flops, bytes_accessed=flops // 300, transcendentals=0),
    )(place, *mine, *theirs, *flat)


def attend_all(place, members, counts, queries, keyvals, more, earlier=()):
    blocks, block_len, cols = queries.shape
    first = earlier[0].shape[2] if earlier else 0
    rows = keyvals.shape[1]
    per_row = rows // block_len

    def kernel(place_ref, members_ref, counts_ref, q_ref, kv_ref, more_ref, *refs):
        same_ref, diff_ref, q_sum, kv_sum, out = refs[len(earlier) :]
        for r in range(blocks):
            added = more_ref[r, rows:, :].astype(jnp.float32)
            added = jnp.concatenate([added[:, :cols], added[:, cols:]], axis=0)
            q_sum[r] = (q_ref[r] + added).astype(jnp.bfloat16)
            both = (kv_ref[r] + more_ref[r, :rows, :].astype(jnp.float32)).astype(jnp.bfloat16)
            both = both.reshape(2, rows // 2, 2 * cols)
            for j in range(per_row):
                part = both[:, j * BS : (j + 1) * BS, :]
                kv_sum[r * per_row + j] = part.reshape(block_len, 2 * cols)
        column = lax.broadcasted_iota(jnp.int32, (block_len, MAXB * block_len), 1)
        for b in range(blocks):
            live = column < counts_ref[b] * block_len
            listed = [kv_sum.at[members_ref[b * MAXB + j]] for j in range(MAXB)]
            for h in range(cols // HD):
                at = slice(h * HD, (h + 1) * HD)
                at_v = slice(cols + h * HD, cols + (h + 1) * HD)
                keys = jnp.concatenate([block[:, at] for block in listed], axis=0)
                values = jnp.concatenate([block[:, at_v] for block in listed], axis=0)
                scores = lax.dot_general(
                    q_sum[b, :, at], keys, (((1,), (1,)), ((), ())), preferred_element_type=jnp.float32
                )
                scores = jnp.where(live, scores, -jnp.inf)
                raised = jnp.exp2((scores - jnp.max(scores, axis=-1, keepdims=True)) * EXP2_SCALE)
                weights = raised * (1.0 / jnp.sum(raised, axis=-1, keepdims=True))
                blended = jnp.dot(
                    weights.astype(jnp.bfloat16), values, preferred_element_type=jnp.float32
                )
                out[(b + place_ref[0]) % 2, b // 2, :, at] = blended.astype(jnp.bfloat16)
        for i, out_ref in enumerate((same_ref, diff_ref)):
            if earlier:
                out_ref[:, :, :first] = refs[i][...]
            out_ref[:, :, first:] = out[i]

    half = jax.ShapeDtypeStruct((blocks // 2, block_len, first + cols), jnp.bfloat16)
    return call(
        kernel,
        (half, half),
        [place, members, counts],
        [queries, keyvals, more, *earlier],
        scratch=[
            pltpu.VMEM((blocks, block_len, cols), jnp.bfloat16),
            pltpu.VMEM((blocks * per_row, block_len, 2 * cols), jnp.bfloat16),
            pltpu.VMEM((2, blocks // 2, block_len, cols), jnp.bfloat16),
        ],
        flops=4 * blocks * block_len * MAXB * block_len * cols,
        read=16 * blocks * block_len * cols,
    )


def mix(place, attended, w_own, w_across, beside, beside_across):
    blocks, block_len, cols = attended[0].shape
    width = w_own.shape[1]

    def kernel(place_ref, *refs):
        row, group, frame, core = (place_ref[i] for i in range(4))
        w_refs = refs[4:10]
        near_keep, near_send, far_keep, far_send, a_all, sums = refs[10:]
        for s in range(4):
            a_all[s] = refs[s][...].reshape(blocks * block_len, cols)

        def term(c, other):
            side = 1 - core if other else core
            acc = None
            for i in range(2):
                if c == 0:
                    weight, half = w_refs[other][i * cols : (i + 1) * cols, :], i
                else:
                    weight, half = w_refs[2 + 2 * other + i][...], (i + group) % 2
                part = jnp.dot(a_all[(2 * side + half) ^ row], weight, preferred_element_type=jnp.float32)
                acc = part if acc is None else acc + part
            return acc.astype(jnp.bfloat16).astype(jnp.float32)

        for c in range(2):
            sums[...] = (term(c, 0) + term(c, 1)).reshape(blocks, 2, BS, width)
            at = (row + c) % 2
            near_keep[at] = sums[row // 2, frame]
            near_send[at] = sums[row // 2, 1 - frame].astype(jnp.bfloat16)
            far_keep[at] = sums[1 - row // 2, frame]
            far_send[at] = sums[1 - row // 2, 1 - frame].astype(jnp.bfloat16)

    kept = jax.ShapeDtypeStruct((2, BS, width), jnp.float32)
    sent = jax.ShapeDtypeStruct((2, BS, width), jnp.bfloat16)
    return call(
        kernel,
        (kept, sent, kept, sent),
        [place],
        [*attended, w_own, w_across, *beside, *beside_across],
        scratch=[
            pltpu.VMEM((4, blocks * block_len, cols), jnp.bfloat16),
            pltpu.VMEM((blocks, 2, BS, width), jnp.float32),
        ],
        flops=2 * blocks * block_len * 4 * cols * 2 * width,
        read=16 * cols * width,
    )


def finish(place, near_keep, near_more, far):
    halves, rows, width = near_keep.shape

    def kernel(place_ref, keep_ref, more_ref, far_ref, out_ref):
        pair = place_ref[0] // 2
        for c in range(halves):
            here = pl.multiple_of((pair * halves + c) * width, width)
            there = pl.multiple_of(((1 - pair) * halves + c) * width, width)
            out_ref[:, pl.ds(here, width)] = (keep_ref[c] + more_ref[c].astype(jnp.float32)).astype(jnp.bfloat16)
            out_ref[:, pl.ds(there, width)] = far_ref[c]

    return call(
        kernel,
        jax.ShapeDtypeStruct((rows, 2 * halves * width), jnp.bfloat16),
        [place],
        [near_keep, near_more, far],
        read=12 * rows * halves * width,
    )


def by_heads(latents, w_qkv, w_out, win_blocks, win_counts, block_window):
    rows_n, heads_n = lax.axis_size("rows"), lax.axis_size("heads")
    group, row = lax.axis_index("groups"), lax.axis_index("rows")
    frame, core = lax.axis_index("frames"), lax.axis_index("heads")
    count = latents.shape[1]
    depth, _, local_cols = w_qkv.shape
    span = rows_n // heads_n
    cols = local_cols // span
    half = depth // 2
    place = jnp.stack([row, group, frame, core]).astype(jnp.int32)

    last = cols // (3 * HD) * HD

    def reshard(i, *others):
        k = i % span
        at, wide = (0, cols - last) if i < span else (cols - last, last)
        value = lax.dynamic_slice(
            w_qkv.transpose(1, 0, 2), (0, group * half, (k + row) % span * cols + at), (3, half, wide)
        )
        pairs = [
            (r * heads_n + h, (h * span + (k + r) % span) * heads_n + r // span)
            for r in range(rows_n)
            for h in range(heads_n)
        ]
        return lax.ppermute(after(value, *others) if others else value, ("rows", "heads"), pairs)

    mine = lax.dynamic_slice_in_dim(latents[0], core * span * depth, span * depth, axis=1)
    mine_x = swap(mine, "frames")
    here, there = [reshard(0)], []
    tables = jnp.concatenate([win_blocks, win_counts[:, None], block_window[:, None]], axis=1)
    tables = jnp.pad(tables, ((0, 8 - heads_n), (0, span * depth - MAXB - 2))).astype(mine.dtype)
    joined = jnp.concatenate([mine, tables], axis=0)
    near = swap(joined, "rows")
    near_x = swap(near, "frames")
    across = swap(after(w_out, near), "heads")
    there.append(swap(here[0], "groups"))
    here.append(reshard(1, near, mine_x, here[0]))
    far_2 = swap(after(joined, here[0]), "rows", 2)
    there.append(swap(here[1], "groups"))
    far_2x = swap(far_2, "frames")
    far_3 = swap(after(joined, far_2), "rows", 3)
    here.append(reshard(2, far_2, near_x, there[0], across))
    out_half = lax.dynamic_slice_in_dim(w_out, group * cols, cols, axis=0)
    beside = [swap(after(out_half, far_2), "rows")]
    here.append(reshard(3, here[1]))
    far_3x = swap(after(far_3, here[2], there[1]), "frames")
    there += [swap(here[2], "groups"), swap(after(here[3], beside[0]), "groups")]

    found = jnp.stack([x[count : count + heads_n, : MAXB + 2] for x in (joined, near, far_2, far_3)])
    tables = found.astype(jnp.int32)[row ^ jnp.arange(rows_n)].reshape(rows_n * heads_n, MAXB + 2)
    windows = lax.dynamic_index_in_dim(
        tables[:, MAXB + 1].reshape(rows_n, heads_n), core, axis=1, keepdims=False
    )
    picked = tables[windows]
    members, counts = picked[:, :MAXB].reshape(-1), picked[:, MAXB]

    pieces = [joined, near, far_2, far_3], [mine_x, near_x, far_2x, far_3x]
    first = project(place, *pieces, [(here[0], there[0]), (here[1], after(there[1], there[2], members, counts))])
    beside.append(swap(after(beside[0], first[2]), "groups"))
    first_more = swap(first[2], "heads")
    second = project(place, *pieces, [(here[2], there[2]), (here[3], after(there[3], first[2]))])
    second_more = swap(second[2], "heads")
    attended = attend_all(place, members, counts, *first[:2], first_more)
    same, diff = attend_all(place, members, counts, *second[:2], second_more, attended)
    attended = [same] + [swap(same if s % 2 == 0 else diff, "rows", s) for s in range(1, rows_n)]
    beside_across = [swap(part, "heads") for part in (beside[0], after(beside[1], *attended[1:]))]
    near_keep, near_send, far_keep, far_send = mix(place, attended, w_out, across, beside, beside_across)
    far_more = swap(far_send, "frames")
    far = swap((far_keep + far_more.astype(jnp.float32)).astype(jnp.bfloat16), "rows", 2)
    near_more = swap(after(near_send, far_more), "frames")
    return finish(place, near_keep, near_more, far)[None]


def local(latents, w_qkv, w_out, win_blocks, win_counts, block_window):
    rows_n = lax.axis_size("rows")
    pairs = all(lax.axis_size(axis) == 2 for axis in ("groups", "frames", "heads"))
    heads_here = w_qkv.shape[2] // HD
    if pairs and rows_n == 4 and heads_here == 6 and latents.shape[:2] == (1, 2 * BS):
        plan = by_heads
    else:
        plan = by_tokens
    return plan(latents, w_qkv, w_out, win_blocks, win_counts, block_window)


def solution(mesh):
    in_specs = (
        P(("groups", "frames"), "rows", None),
        P("rows", None, ("frames", "heads")),
        P(("frames", "heads"), "rows"),
        P(("groups", "rows"), None),
        P(("groups", "rows")),
        P(("groups", "rows")),
    )
    out_specs = P(("groups", "frames"), ("rows", "heads"), None)
    return jax.shard_map(local, mesh=mesh, in_specs=in_specs, out_specs=out_specs, check_vma=False)
```

```python
import math

import jax
import jax.numpy as jnp
from jax import lax
from jax.experimental import pallas as pl
from jax.experimental.pallas import tpu as pltpu
from jax.sharding import PartitionSpec as P

HD = 128
BS = 64
MAXB = 4
VMEM_BYTES = 24 * 1024 * 1024
WHOLE_VMEM_BYTES = 56 * 1024 * 1024
EXP2_SCALE = math.log2(math.e) / math.sqrt(HD)


def with_halo(value, sides, width):
    for axis, dim in sides:
        peers, length = (lax.axis_size(axis), value.shape[dim])
        up = [(i, (i + 1) % peers) for i in range(peers)]
        down = [(j, i) for i, j in up]
        last = lax.slice_in_dim(value, length - width, length, axis=dim)
        first = lax.slice_in_dim(value, 0, width, axis=dim)
        before = lax.ppermute(last, axis, up)
        after = lax.ppermute(first, axis, down)
        value = jnp.concatenate([before, value, after], axis=dim)
    return value


def by_tokens(latents, w_qkv, w_out, win_blocks, win_counts, block_window):
    rows_n = lax.axis_size("rows")
    shard_idx = lax.axis_index("rows")
    frames = latents.shape[0] * lax.axis_size("frames")
    tok_frame = latents.shape[1]
    model_width = latents.shape[2]
    local_cols = w_qkv.shape[2]
    per_shard = tok_frame // BS
    block_total = per_shard * rows_n
    heads_here = local_cols // HD
    block_len = frames * BS
    score_scale = 1.0 / math.sqrt(HD)
    gathered = lax.all_gather(latents, "frames", axis=0, tiled=True)
    flat_tokens = gathered.reshape(frames * tok_frame, model_width)
    weight_rows = lax.all_gather(w_qkv, "rows", axis=0, tiled=True)
    projected = jnp.dot(
        flat_tokens,
        weight_rows.reshape(weight_rows.shape[0], 3 * local_cols),
        preferred_element_type=jnp.float32,
    ).astype(jnp.bfloat16)
    blocked = projected.reshape(frames, per_shard, BS, 3, local_cols).transpose(1, 0, 2, 3, 4)
    blocked = blocked.reshape(per_shard, block_len, 3, local_cols)
    queries = blocked[:, :, 0]
    keyvals = blocked[:, :, 1:]
    nearby = with_halo(keyvals, (("rows", 0),), per_shard)
    first_block = shard_idx * per_shard
    owners = block_window - first_block
    members = win_blocks[owners]
    lengths = win_counts[owners]
    positions = (members - first_block + per_shard + block_total) % block_total

    def attend(query_rows, picked, live_mask):
        key_count = picked.shape[0]
        key_blocks = nearby[picked]
        key_part = key_blocks[:, :, 0].reshape(key_count * block_len, heads_here, HD)
        value_part = key_blocks[:, :, 1].reshape(key_count * block_len, heads_here, HD)
        scores = (
            jnp.einsum(
                "qhd,khd->hqk",
                query_rows.reshape(block_len, heads_here, HD),
                key_part,
                preferred_element_type=jnp.float32,
            )
            * score_scale
        )
        scores = jnp.where(live_mask[None, None, :], scores, -jnp.inf)
        row_max = jnp.max(scores, axis=-1, keepdims=True)
        raised = jnp.exp(scores - row_max)
        weights = (raised / jnp.sum(raised, axis=-1, keepdims=True)).astype(jnp.bfloat16)
        blended = jnp.einsum(
            "hqk,khd->qhd", weights, value_part, preferred_element_type=jnp.float32
        )
        return blended.reshape(block_len, local_cols).astype(jnp.bfloat16)

    def one_block(block_item):
        query_rows, picked, length = block_item
        live_mask = jnp.repeat(jnp.arange(MAXB) < length, block_len)
        return attend(query_rows, picked, live_mask)

    attended = lax.map(one_block, (queries, positions, lengths))
    ordered = attended.reshape(per_shard, frames, BS, local_cols).transpose(1, 0, 2, 3)
    ordered = ordered.reshape(frames * tok_frame, local_cols)
    w_full = lax.all_gather(w_out, "rows", axis=1, tiled=True)
    group_count = lax.axis_size(("frames", "heads"))
    out_rows = frames * tok_frame // group_count
    summed = lax.psum_scatter(
        jnp.dot(ordered, w_full, preferred_element_type=jnp.float32).astype(jnp.bfloat16),
        ("frames", "heads"),
        scatter_dimension=0,
        tiled=True,
    )
    return summed.reshape(1, out_rows, model_width)


def swap(value, axis, step=1):
    peers = lax.axis_size(axis)
    return lax.ppermute(value, axis, [(i, i ^ step) for i in range(peers)])


def after(value, *others):
    return lax.optimization_barrier((value, *others))[0]


def call(kernel, out_shape, prefetch, operands, scratch=(), flops=0, read=0, limit=VMEM_BYTES):
    return pl.pallas_call(
        kernel,
        out_shape=out_shape,
        grid_spec=pltpu.PrefetchScalarGridSpec(
            num_scalar_prefetch=len(prefetch),
            grid=(),
            in_specs=[pl.BlockSpec(memory_space=pltpu.VMEM)] * len(operands),
            out_specs=jax.tree.map(lambda _: pl.BlockSpec(memory_space=pltpu.VMEM), out_shape),
            scratch_shapes=scratch,
        ),
        compiler_params=pltpu.CompilerParams(vmem_limit_bytes=limit),
        cost_estimate=pl.CostEstimate(flops=flops, bytes_accessed=read, transcendentals=0),
    )(*prefetch, *operands)


def project(place, mine, theirs, chunks):
    rows, (count, width) = len(mine) - 1, theirs[0].shape
    _, half, cols = chunks[0][0].shape
    slices = len(chunks)
    flat = [w for of_round in chunks for w in of_round]
    fetched = 2 * len(mine) + len(flat)

    def kernel(place_ref, *refs):
        row, group, frame, core = (place_ref[i] for i in range(4))
        w_refs = refs[2 * len(mine) : fetched]
        q_keep, kv_keep, send, x_all, w_all, total, sems = refs[fetched:]
        middle = (row == 1) | (row == 2)
        copies = []
        for k in range(slices):
            for g in range(2):
                at = pl.multiple_of((row + slices - k) % slices * (2 * half) + (group + g) % 2 * half, half)
                for part in range(3):
                    into = w_all.at[pl.ds(at, half), part * cols : (part + 1) * cols]
                    copy = pltpu.make_async_copy(w_refs[2 * k + g].at[part], into, sems.at[len(copies)])
                    copy.start()
                    copies.append(copy)
        for f in range(2):
            x_refs = refs[f * len(mine) : (f + 1) * len(mine)]
            for s in range(rows):
                to, sem = x_all.at[row ^ s, (frame + f) % 2], sems.at[len(copies)]
                copy = pltpu.make_async_copy(x_refs[s].at[pl.ds(0, count)], to, sem)
                copies.append(copy)
                if s < rows - 1:
                    copy.start()
                else:
                    other = pltpu.make_async_copy(x_refs[rows].at[pl.ds(0, count)], to, sem)
                    pl.when(middle)(copy.start)
                    pl.when(jnp.logical_not(middle))(other.start)
        for copy in copies:
            copy.wait()
        acc = jnp.dot(x_all[...].reshape(-1, width), w_all[...], preferred_element_type=jnp.float32)
        kv_part = acc[:, cols:].reshape(rows, 2 * count, 2 * cols)
        kv_keep[...] = kv_part
        send[:, : 2 * count, :] = kv_part.astype(jnp.bfloat16)
        total[...] = acc[:, :cols].reshape(rows, 2, count, cols)
        own = pl.multiple_of(core * BS, BS)
        other = pl.multiple_of((1 - core) * BS, BS)
        q_keep[...] = total[:, :, pl.ds(own, BS), :].reshape(q_keep.shape)
        for f in range(2):
            at = slice(f * cols, (f + 1) * cols)
            send[:, 2 * count :, at] = total[:, f, pl.ds(other, BS), :].astype(jnp.bfloat16)

    vmem, hbm = pl.BlockSpec(memory_space=pltpu.VMEM), pl.BlockSpec(memory_space=pltpu.HBM)
    flops = 2 * rows * 2 * count * width * 3 * cols
    return pl.pallas_call(
        kernel,
        out_shape=(
            jax.ShapeDtypeStruct((rows, 2 * BS, cols), jnp.float32),
            jax.ShapeDtypeStruct((rows, 2 * count, 2 * cols), jnp.float32),
            jax.ShapeDtypeStruct((rows, 2 * count + BS, 2 * cols), jnp.bfloat16),
        ),
        grid_spec=pltpu.PrefetchScalarGridSpec(
            num_scalar_prefetch=1,
            grid=(),
            in_specs=[hbm] * fetched,
            out_specs=(vmem, vmem, vmem),
            scratch_shapes=[
                pltpu.VMEM((rows, 2, count, width), jnp.bfloat16),
                pltpu.VMEM((width, 3 * cols), jnp.bfloat16),
                pltpu.VMEM((rows, 2, count, cols), jnp.float32),
                pltpu.SemaphoreType.DMA((2 * rows + 3 * len(flat),)),
            ],
        ),
        compiler_params=pltpu.CompilerParams(vmem_limit_bytes=VMEM_BYTES),
        cost_estimate=pl.CostEstimate(flops=8 * flops, bytes_accessed=flops // 300, transcendentals=0),
    )(place, *mine, *theirs, *flat)


def attend_all(place, members, counts, queries, keyvals, more, earlier=()):
    blocks, block_len, cols = queries.shape
    first = earlier[0].shape[2] if earlier else 0
    rows = keyvals.shape[1]
    per_row = rows // block_len

    def kernel(place_ref, members_ref, counts_ref, q_ref, kv_ref, more_ref, *refs):
        same_ref, diff_ref, q_sum, kv_sum, out = refs[len(earlier) :]
        for r in range(blocks):
            added = more_ref[r, rows:, :].astype(jnp.float32)
            added = jnp.concatenate([added[:, :cols], added[:, cols:]], axis=0)
            q_sum[r] = (q_ref[r] + added).astype(jnp.bfloat16)
            both = (kv_ref[r] + more_ref[r, :rows, :].astype(jnp.float32)).astype(jnp.bfloat16)
            both = both.reshape(2, rows // 2, 2 * cols)
            for j in range(per_row):
                part = both[:, j * BS : (j + 1) * BS, :]
                kv_sum[r * per_row + j] = part.reshape(block_len, 2 * cols)
        column = lax.broadcasted_iota(jnp.int32, (block_len, MAXB * block_len), 1)
        for b in range(blocks):
            live = column < counts_ref[b] * block_len
            listed = [kv_sum.at[members_ref[b * MAXB + j]] for j in range(MAXB)]
            for h in range(cols // HD):
                at = slice(h * HD, (h + 1) * HD)
                at_v = slice(cols + h * HD, cols + (h + 1) * HD)
                keys = jnp.concatenate([block[:, at] for block in listed], axis=0)
                values = jnp.concatenate([block[:, at_v] for block in listed], axis=0)
                scores = lax.dot_general(
                    q_sum[b, :, at], keys, (((1,), (1,)), ((), ())), preferred_element_type=jnp.float32
                )
                scores = jnp.where(live, scores, -jnp.inf)
                raised = jnp.exp2((scores - jnp.max(scores, axis=-1, keepdims=True)) * EXP2_SCALE)
                weights = raised * (1.0 / jnp.sum(raised, axis=-1, keepdims=True))
                blended = jnp.dot(
                    weights.astype(jnp.bfloat16), values, preferred_element_type=jnp.float32
                )
                out[(b + place_ref[0]) % 2, b // 2, :, at] = blended.astype(jnp.bfloat16)
        for i, out_ref in enumerate((same_ref, diff_ref)):
            if earlier:
                out_ref[:, :, :first] = refs[i][...]
            out_ref[:, :, first:] = out[i]

    half = jax.ShapeDtypeStruct((blocks // 2, block_len, first + cols), jnp.bfloat16)
    return call(
        kernel,
        (half, half),
        [place, members, counts],
        [queries, keyvals, more, *earlier],
        scratch=[
            pltpu.VMEM((blocks, block_len, cols), jnp.bfloat16),
            pltpu.VMEM((blocks * per_row, block_len, 2 * cols), jnp.bfloat16),
            pltpu.VMEM((2, blocks // 2, block_len, cols), jnp.bfloat16),
        ],
        flops=4 * blocks * block_len * MAXB * block_len * cols,
        read=16 * blocks * block_len * cols,
    )


def mix(place, attended, w_own, w_across, beside, beside_across):
    blocks, block_len, cols = attended[0].shape
    width = w_own.shape[1]

    def kernel(place_ref, *refs):
        row, group, frame, core = (place_ref[i] for i in range(4))
        w_refs = refs[4:10]
        near_keep, near_send, far_keep, far_send, a_all, sums = refs[10:]
        for s in range(4):
            a_all[s] = refs[s][...].reshape(blocks * block_len, cols)

        def term(c, other):
            side = 1 - core if other else core
            acc = None
            for i in range(2):
                if c == 0:
                    weight, half = w_refs[other][i * cols : (i + 1) * cols, :], i
                else:
                    weight, half = w_refs[2 + 2 * other + i][...], (i + group) % 2
                part = jnp.dot(a_all[(2 * side + half) ^ row], weight, preferred_element_type=jnp.float32)
                acc = part if acc is None else acc + part
            return acc.astype(jnp.bfloat16).astype(jnp.float32)

        for c in range(2):
            sums[...] = (term(c, 0) + term(c, 1)).reshape(blocks, 2, BS, width)
            at = (row + c) % 2
            near_keep[at] = sums[row // 2, frame]
            near_send[at] = sums[row // 2, 1 - frame].astype(jnp.bfloat16)
            far_keep[at] = sums[1 - row // 2, frame]
            far_send[at] = sums[1 - row // 2, 1 - frame].astype(jnp.bfloat16)

    kept = jax.ShapeDtypeStruct((2, BS, width), jnp.float32)
    sent = jax.ShapeDtypeStruct((2, BS, width), jnp.bfloat16)
    return call(
        kernel,
        (kept, sent, kept, sent),
        [place],
        [*attended, w_own, w_across, *beside, *beside_across],
        scratch=[
            pltpu.VMEM((4, blocks * block_len, cols), jnp.bfloat16),
            pltpu.VMEM((blocks, 2, BS, width), jnp.float32),
        ],
        flops=2 * blocks * block_len * 4 * cols * 2 * width,
        read=16 * cols * width,
    )


def finish(place, near_keep, near_more, far):
    halves, rows, width = near_keep.shape

    def kernel(place_ref, keep_ref, more_ref, far_ref, out_ref):
        pair = place_ref[0] // 2
        for c in range(halves):
            here = pl.multiple_of((pair * halves + c) * width, width)
            there = pl.multiple_of(((1 - pair) * halves + c) * width, width)
            out_ref[:, pl.ds(here, width)] = (keep_ref[c] + more_ref[c].astype(jnp.float32)).astype(jnp.bfloat16)
            out_ref[:, pl.ds(there, width)] = far_ref[c]

    return call(
        kernel,
        jax.ShapeDtypeStruct((rows, 2 * halves * width), jnp.bfloat16),
        [place],
        [near_keep, near_more, far],
        read=12 * rows * halves * width,
    )


def by_heads(latents, w_qkv, w_out, win_blocks, win_counts, block_window):
    rows_n, heads_n = lax.axis_size("rows"), lax.axis_size("heads")
    group, row = lax.axis_index("groups"), lax.axis_index("rows")
    frame, core = lax.axis_index("frames"), lax.axis_index("heads")
    count = latents.shape[1]
    depth, _, local_cols = w_qkv.shape
    span = rows_n // heads_n
    cols = local_cols // span
    half = depth // 2
    place = jnp.stack([row, group, frame, core]).astype(jnp.int32)

    def over_frames(value, rows):
        pairs = [(2 * r + f, 2 * r + 1 - f) for r in rows for f in range(2)]
        return lax.ppermute(value, ("rows", "frames"), pairs)

    last = cols // (3 * HD) * HD

    def reshard(i, *others):
        k = i % span
        at, wide = (0, cols - last) if i < span else (cols - last, last)
        value = lax.dynamic_slice(
            w_qkv.transpose(1, 0, 2), (0, group * half, (k + row) % span * cols + at), (3, half, wide)
        )
        pairs = [
            (r * heads_n + h, (h * span + (k + r) % span) * heads_n + r // span)
            for r in range(rows_n)
            for h in range(heads_n)
        ]
        return lax.ppermute(after(value, *others) if others else value, ("rows", "heads"), pairs)

    mine = lax.dynamic_slice_in_dim(latents[0], core * span * depth, span * depth, axis=1)
    mine_x = swap(mine, "frames")
    here, there = [reshard(0)], []
    tables = jnp.concatenate([win_blocks, win_counts[:, None], block_window[:, None]], axis=1)
    tables = jnp.pad(tables, ((0, 8 - heads_n), (0, span * depth - MAXB - 2))).astype(mine.dtype)
    joined = jnp.concatenate([mine, tables], axis=0)
    in_3 = lax.ppermute(joined, "rows", [(1, 2), (2, 1)])
    near = swap(joined, "rows")
    near_x = swap(near, "frames")
    across = swap(after(w_out, near), "heads")
    there.append(swap(here[0], "groups"))
    in_3x = over_frames(after(in_3, there[0]), (1, 2))
    here.append(reshard(1, near, mine_x, in_3, here[0]))
    far_2 = swap(after(joined, near), "rows", 2)
    there.append(swap(here[1], "groups"))
    far_2x = swap(far_2, "frames")
    out_3 = lax.ppermute(far_2, "rows", [(1, 0), (2, 3)])
    here.append(reshard(2, far_2, near_x, in_3x, there[0], across))
    out_half = lax.dynamic_slice_in_dim(w_out, group * cols, cols, axis=0)
    beside = [swap(after(out_half, far_2), "rows")]
    here.append(reshard(3, here[1]))
    out_3x = over_frames(after(out_3, there[1]), (0, 3))
    there += [swap(here[2], "groups"), swap(after(here[3], beside[0]), "groups")]

    extra = jnp.where((row == 1) | (row == 2), in_3[count:], out_3[count:])
    found = [joined[count:], near[count:], far_2[count:], extra]
    found = jnp.stack([x[:heads_n, : MAXB + 2] for x in found])
    tables = found.astype(jnp.int32)[row ^ jnp.arange(rows_n)].reshape(rows_n * heads_n, MAXB + 2)
    windows = lax.dynamic_index_in_dim(
        tables[:, MAXB + 1].reshape(rows_n, heads_n), core, axis=1, keepdims=False
    )
    picked = tables[windows]
    members, counts = picked[:, :MAXB].reshape(-1), picked[:, MAXB]

    pieces = [joined, near, far_2, in_3, out_3], [mine_x, near_x, far_2x, in_3x, out_3x]
    first = project(place, *pieces, [(here[0], there[0]), (here[1], after(there[1], there[2], members, counts))])
    beside.append(swap(after(beside[0], first[2]), "groups"))
    first_more = swap(first[2], "heads")
    second = project(place, *pieces, [(here[2], there[2]), (here[3], after(there[3], first[2]))])
    second_more = swap(second[2], "heads")
    attended = attend_all(place, members, counts, *first[:2], first_more)
    same, diff = attend_all(place, members, counts, *second[:2], second_more, attended)
    attended = [same] + [swap(same if s % 2 == 0 else diff, "rows", s) for s in range(1, rows_n)]
    beside_across = [swap(part, "heads") for part in (beside[0], after(beside[1], *attended[1:]))]
    near_keep, near_send, far_keep, far_send = mix(place, attended, w_out, across, beside, beside_across)
    far_more = swap(far_send, "frames")
    far = swap((far_keep + far_more.astype(jnp.float32)).astype(jnp.bfloat16), "rows", 2)
    near_more = swap(after(near_send, far_more), "frames")
    return finish(place, near_keep, near_more, far)[None]


def local(latents, w_qkv, w_out, win_blocks, win_counts, block_window):
    rows_n = lax.axis_size("rows")
    pairs = all(lax.axis_size(axis) == 2 for axis in ("groups", "frames", "heads"))
    heads_here = w_qkv.shape[2] // HD
    if pairs and rows_n == 4 and heads_here == 6 and latents.shape[:2] == (1, 2 * BS):
        plan = by_heads
    else:
        plan = by_tokens
    return plan(latents, w_qkv, w_out, win_blocks, win_counts, block_window)


def solution(mesh):
    in_specs = (
        P(("groups", "frames"), "rows", None),
        P("rows", None, ("frames", "heads")),
        P(("frames", "heads"), "rows"),
        P(("groups", "rows"), None),
        P(("groups", "rows")),
        P(("groups", "rows")),
    )
    out_specs = P(("groups", "frames"), ("rows", "heads"), None)
    return jax.shard_map(local, mesh=mesh, in_specs=in_specs, out_specs=out_specs, check_vma=False)
```

```python
import math

import jax
import jax.numpy as jnp
from jax import lax
from jax.experimental import pallas as pl
from jax.experimental.pallas import tpu as pltpu
from jax.sharding import PartitionSpec as P

HD = 128
BS = 64
MAXB = 4
VMEM_BYTES = 24 * 1024 * 1024
WHOLE_VMEM_BYTES = 56 * 1024 * 1024
EXP2_SCALE = math.log2(math.e) / math.sqrt(HD)


def with_halo(value, sides, width):
    for axis, dim in sides:
        peers, length = (lax.axis_size(axis), value.shape[dim])
        up = [(i, (i + 1) % peers) for i in range(peers)]
        down = [(j, i) for i, j in up]
        last = lax.slice_in_dim(value, length - width, length, axis=dim)
        first = lax.slice_in_dim(value, 0, width, axis=dim)
        before = lax.ppermute(last, axis, up)
        after = lax.ppermute(first, axis, down)
        value = jnp.concatenate([before, value, after], axis=dim)
    return value


def by_tokens(latents, w_qkv, w_out, win_blocks, win_counts, block_window):
    rows_n = lax.axis_size("rows")
    shard_idx = lax.axis_index("rows")
    frames = latents.shape[0] * lax.axis_size("frames")
    tok_frame = latents.shape[1]
    model_width = latents.shape[2]
    local_cols = w_qkv.shape[2]
    per_shard = tok_frame // BS
    block_total = per_shard * rows_n
    heads_here = local_cols // HD
    block_len = frames * BS
    score_scale = 1.0 / math.sqrt(HD)
    gathered = lax.all_gather(latents, "frames", axis=0, tiled=True)
    flat_tokens = gathered.reshape(frames * tok_frame, model_width)
    weight_rows = lax.all_gather(w_qkv, "rows", axis=0, tiled=True)
    projected = jnp.dot(
        flat_tokens,
        weight_rows.reshape(weight_rows.shape[0], 3 * local_cols),
        preferred_element_type=jnp.float32,
    ).astype(jnp.bfloat16)
    blocked = projected.reshape(frames, per_shard, BS, 3, local_cols).transpose(1, 0, 2, 3, 4)
    blocked = blocked.reshape(per_shard, block_len, 3, local_cols)
    queries = blocked[:, :, 0]
    keyvals = blocked[:, :, 1:]
    nearby = with_halo(keyvals, (("rows", 0),), per_shard)
    first_block = shard_idx * per_shard
    owners = block_window - first_block
    members = win_blocks[owners]
    lengths = win_counts[owners]
    positions = (members - first_block + per_shard + block_total) % block_total

    def attend(query_rows, picked, live_mask):
        key_count = picked.shape[0]
        key_blocks = nearby[picked]
        key_part = key_blocks[:, :, 0].reshape(key_count * block_len, heads_here, HD)
        value_part = key_blocks[:, :, 1].reshape(key_count * block_len, heads_here, HD)
        scores = (
            jnp.einsum(
                "qhd,khd->hqk",
                query_rows.reshape(block_len, heads_here, HD),
                key_part,
                preferred_element_type=jnp.float32,
            )
            * score_scale
        )
        scores = jnp.where(live_mask[None, None, :], scores, -jnp.inf)
        row_max = jnp.max(scores, axis=-1, keepdims=True)
        raised = jnp.exp(scores - row_max)
        weights = (raised / jnp.sum(raised, axis=-1, keepdims=True)).astype(jnp.bfloat16)
        blended = jnp.einsum(
            "hqk,khd->qhd", weights, value_part, preferred_element_type=jnp.float32
        )
        return blended.reshape(block_len, local_cols).astype(jnp.bfloat16)

    def one_block(block_item):
        query_rows, picked, length = block_item
        live_mask = jnp.repeat(jnp.arange(MAXB) < length, block_len)
        return attend(query_rows, picked, live_mask)

    attended = lax.map(one_block, (queries, positions, lengths))
    ordered = attended.reshape(per_shard, frames, BS, local_cols).transpose(1, 0, 2, 3)
    ordered = ordered.reshape(frames * tok_frame, local_cols)
    w_full = lax.all_gather(w_out, "rows", axis=1, tiled=True)
    group_count = lax.axis_size(("frames", "heads"))
    out_rows = frames * tok_frame // group_count
    summed = lax.psum_scatter(
        jnp.dot(ordered, w_full, preferred_element_type=jnp.float32).astype(jnp.bfloat16),
        ("frames", "heads"),
        scatter_dimension=0,
        tiled=True,
    )
    return summed.reshape(1, out_rows, model_width)


def swap(value, axis, step=1):
    peers = lax.axis_size(axis)
    return lax.ppermute(value, axis, [(i, i ^ step) for i in range(peers)])


def after(value, *others):
    return lax.optimization_barrier((value, *others))[0]


def call(kernel, out_shape, prefetch, operands, scratch=(), flops=0, read=0, limit=VMEM_BYTES):
    return pl.pallas_call(
        kernel,
        out_shape=out_shape,
        grid_spec=pltpu.PrefetchScalarGridSpec(
            num_scalar_prefetch=len(prefetch),
            grid=(),
            in_specs=[pl.BlockSpec(memory_space=pltpu.VMEM)] * len(operands),
            out_specs=jax.tree.map(lambda _: pl.BlockSpec(memory_space=pltpu.VMEM), out_shape),
            scratch_shapes=scratch,
        ),
        compiler_params=pltpu.CompilerParams(vmem_limit_bytes=limit),
        cost_estimate=pl.CostEstimate(flops=flops, bytes_accessed=read, transcendentals=0),
    )(*prefetch, *operands)


def project(place, mine, theirs, chunks, first, cols):
    rows, (count, width) = len(mine), theirs[0].shape
    half = chunks[0][0].shape[1]
    slices = len(chunks)
    flat = [w for of_round in chunks for w in of_round]
    fetched = 2 * rows + len(flat)

    def kernel(place_ref, *refs):
        row, group, frame, core = (place_ref[i] for i in range(4))
        w_refs = refs[2 * rows : fetched]
        q_keep, kv_keep, send, x_all, w_all, total, sems = refs[fetched:]
        copies = []
        for k in range(slices):
            for g in range(2):
                at = pl.multiple_of((row + slices - k) % slices * (2 * half) + (group + g) % 2 * half, half)
                for part in range(3):
                    source = w_refs[2 * k + g].at[part, :, first : first + cols]
                    into = w_all.at[pl.ds(at, half), part * cols : (part + 1) * cols]
                    copies.append(pltpu.make_async_copy(source, into, sems.at[len(copies)]))
        for i in range(2 * rows):
            to = x_all.at[row ^ (i % rows), (frame + i // rows) % 2]
            copies.append(pltpu.make_async_copy(refs[i].at[pl.ds(0, count)], to, sems.at[len(copies)]))
        for copy in copies:
            copy.start()
        for copy in copies:
            copy.wait()
        acc = jnp.dot(x_all[...].reshape(-1, width), w_all[...], preferred_element_type=jnp.float32)
        kv_part = acc[:, cols:].reshape(rows, 2 * count, 2 * cols)
        kv_keep[...] = kv_part
        send[:, : 2 * count, :] = kv_part.astype(jnp.bfloat16)
        total[...] = acc[:, :cols].reshape(rows, 2, count, cols)
        own = pl.multiple_of(core * BS, BS)
        other = pl.multiple_of((1 - core) * BS, BS)
        q_keep[...] = total[:, :, pl.ds(own, BS), :].reshape(q_keep.shape)
        for f in range(2):
            at = slice(f * cols, (f + 1) * cols)
            send[:, 2 * count :, at] = total[:, f, pl.ds(other, BS), :].astype(jnp.bfloat16)

    vmem, hbm = pl.BlockSpec(memory_space=pltpu.VMEM), pl.BlockSpec(memory_space=pltpu.HBM)
    flops = 2 * rows * 2 * count * width * 3 * cols
    return pl.pallas_call(
        kernel,
        out_shape=(
            jax.ShapeDtypeStruct((rows, 2 * BS, cols), jnp.float32),
            jax.ShapeDtypeStruct((rows, 2 * count, 2 * cols), jnp.float32),
            jax.ShapeDtypeStruct((rows, 2 * count + BS, 2 * cols), jnp.bfloat16),
        ),
        grid_spec=pltpu.PrefetchScalarGridSpec(
            num_scalar_prefetch=1,
            grid=(),
            in_specs=[hbm] * fetched,
            out_specs=(vmem, vmem, vmem),
            scratch_shapes=[
                pltpu.VMEM((rows, 2, count, width), jnp.bfloat16),
                pltpu.VMEM((width, 3 * cols), jnp.bfloat16),
                pltpu.VMEM((rows, 2, count, cols), jnp.float32),
                pltpu.SemaphoreType.DMA((2 * rows + 3 * len(flat),)),
            ],
        ),
        compiler_params=pltpu.CompilerParams(vmem_limit_bytes=VMEM_BYTES),
        cost_estimate=pl.CostEstimate(flops=8 * flops, bytes_accessed=flops // 300, transcendentals=0),
    )(place, *mine, *theirs, *flat)


def attend_all(place, members, counts, queries, keyvals, more, earlier=()):
    blocks, block_len, cols = queries.shape
    first = earlier[0].shape[2] if earlier else 0
    rows = keyvals.shape[1]
    per_row = rows // block_len

    def kernel(place_ref, members_ref, counts_ref, q_ref, kv_ref, more_ref, *refs):
        same_ref, diff_ref, q_sum, kv_sum, out = refs[len(earlier) :]
        for r in range(blocks):
            added = more_ref[r, rows:, :].astype(jnp.float32)
            added = jnp.concatenate([added[:, :cols], added[:, cols:]], axis=0)
            q_sum[r] = (q_ref[r] + added).astype(jnp.bfloat16)
            both = (kv_ref[r] + more_ref[r, :rows, :].astype(jnp.float32)).astype(jnp.bfloat16)
            both = both.reshape(2, rows // 2, 2 * cols)
            for j in range(per_row):
                part = both[:, j * BS : (j + 1) * BS, :]
                kv_sum[r * per_row + j] = part.reshape(block_len, 2 * cols)
        column = lax.broadcasted_iota(jnp.int32, (block_len, MAXB * block_len), 1)
        for b in range(blocks):
            live = column < counts_ref[b] * block_len
            listed = [kv_sum.at[members_ref[b * MAXB + j]] for j in range(MAXB)]
            for h in range(cols // HD):
                at = slice(h * HD, (h + 1) * HD)
                at_v = slice(cols + h * HD, cols + (h + 1) * HD)
                keys = jnp.concatenate([block[:, at] for block in listed], axis=0)
                values = jnp.concatenate([block[:, at_v] for block in listed], axis=0)
                scores = lax.dot_general(
                    q_sum[b, :, at], keys, (((1,), (1,)), ((), ())), preferred_element_type=jnp.float32
                )
                scores = jnp.where(live, scores, -jnp.inf)
                raised = jnp.exp2((scores - jnp.max(scores, axis=-1, keepdims=True)) * EXP2_SCALE)
                weights = raised * (1.0 / jnp.sum(raised, axis=-1, keepdims=True))
                blended = jnp.dot(
                    weights.astype(jnp.bfloat16), values, preferred_element_type=jnp.float32
                )
                out[(b + place_ref[0]) % 2, b // 2, :, at] = blended.astype(jnp.bfloat16)
        for i, out_ref in enumerate((same_ref, diff_ref)):
            if earlier:
                out_ref[:, :, :first] = refs[i][...]
            out_ref[:, :, first:] = out[i]

    half = jax.ShapeDtypeStruct((blocks // 2, block_len, first + cols), jnp.bfloat16)
    return call(
        kernel,
        (half, half),
        [place, members, counts],
        [queries, keyvals, more, *earlier],
        scratch=[
            pltpu.VMEM((blocks, block_len, cols), jnp.bfloat16),
            pltpu.VMEM((blocks * per_row, block_len, 2 * cols), jnp.bfloat16),
            pltpu.VMEM((2, blocks // 2, block_len, cols), jnp.bfloat16),
        ],
        flops=4 * blocks * block_len * MAXB * block_len * cols,
        read=16 * blocks * block_len * cols,
    )


def mix(place, attended, w_own, w_across, beside, beside_across):
    blocks, block_len, cols = attended[0].shape
    width = w_own.shape[1]

    def kernel(place_ref, *refs):
        row, group, frame, core = (place_ref[i] for i in range(4))
        w_refs = refs[4:10]
        near_keep, near_send, far_keep, far_send, a_all, sums = refs[10:]
        for s in range(4):
            a_all[s] = refs[s][...].reshape(blocks * block_len, cols)

        def term(c, other):
            side = 1 - core if other else core
            acc = None
            for i in range(2):
                if c == 0:
                    weight, half = w_refs[other][i * cols : (i + 1) * cols, :], i
                else:
                    weight, half = w_refs[2 + 2 * other + i][...], (i + group) % 2
                part = jnp.dot(a_all[(2 * side + half) ^ row], weight, preferred_element_type=jnp.float32)
                acc = part if acc is None else acc + part
            return acc.astype(jnp.bfloat16).astype(jnp.float32)

        for c in range(2):
            sums[...] = (term(c, 0) + term(c, 1)).reshape(blocks, 2, BS, width)
            at = (row + c) % 2
            near_keep[at] = sums[row // 2, frame]
            near_send[at] = sums[row // 2, 1 - frame].astype(jnp.bfloat16)
            far_keep[at] = sums[1 - row // 2, frame]
            far_send[at] = sums[1 - row // 2, 1 - frame].astype(jnp.bfloat16)

    kept = jax.ShapeDtypeStruct((2, BS, width), jnp.float32)
    sent = jax.ShapeDtypeStruct((2, BS, width), jnp.bfloat16)
    return call(
        kernel,
        (kept, sent, kept, sent),
        [place],
        [*attended, w_own, w_across, *beside, *beside_across],
        scratch=[
            pltpu.VMEM((4, blocks * block_len, cols), jnp.bfloat16),
            pltpu.VMEM((blocks, 2, BS, width), jnp.float32),
        ],
        flops=2 * blocks * block_len * 4 * cols * 2 * width,
        read=16 * cols * width,
    )


def finish(place, near_keep, near_more, far):
    halves, rows, width = near_keep.shape

    def kernel(place_ref, keep_ref, more_ref, far_ref, out_ref):
        pair = place_ref[0] // 2
        for c in range(halves):
            here = pl.multiple_of((pair * halves + c) * width, width)
            there = pl.multiple_of(((1 - pair) * halves + c) * width, width)
            out_ref[:, pl.ds(here, width)] = (keep_ref[c] + more_ref[c].astype(jnp.float32)).astype(jnp.bfloat16)
            out_ref[:, pl.ds(there, width)] = far_ref[c]

    return call(
        kernel,
        jax.ShapeDtypeStruct((rows, 2 * halves * width), jnp.bfloat16),
        [place],
        [near_keep, near_more, far],
        read=12 * rows * halves * width,
    )


def by_heads(latents, w_qkv, w_out, win_blocks, win_counts, block_window):
    rows_n, heads_n = lax.axis_size("rows"), lax.axis_size("heads")
    group, row = lax.axis_index("groups"), lax.axis_index("rows")
    frame, core = lax.axis_index("frames"), lax.axis_index("heads")
    count = latents.shape[1]
    depth, _, local_cols = w_qkv.shape
    span = rows_n // heads_n
    cols = local_cols // span
    half = depth // 2
    place = jnp.stack([row, group, frame, core]).astype(jnp.int32)

    def reshard(k, *others):
        value = lax.dynamic_slice(
            w_qkv.transpose(1, 0, 2), (0, group * half, (k + row) % span * cols), (3, half, cols)
        )
        pairs = [
            (r * heads_n + h, (h * span + (k + r) % span) * heads_n + r // span)
            for r in range(rows_n)
            for h in range(heads_n)
        ]
        return lax.ppermute(after(value, *others) if others else value, ("rows", "heads"), pairs)

    mine = lax.dynamic_slice_in_dim(latents[0], core * span * depth, span * depth, axis=1)
    mine_x = swap(mine, "frames")
    here, there = [reshard(0)], []
    tables = jnp.concatenate([win_blocks, win_counts[:, None], block_window[:, None]], axis=1)
    tables = jnp.pad(tables, ((0, 8 - heads_n), (0, span * depth - MAXB - 2))).astype(mine.dtype)
    joined = jnp.concatenate([mine, tables], axis=0)
    near = swap(joined, "rows")
    near_x = swap(near, "frames")
    across = swap(after(w_out, near), "heads")
    there.append(swap(here[0], "groups"))
    here.append(reshard(1, near, mine_x, here[0]))
    far_2 = swap(after(joined, here[0]), "rows", 2)
    out_half = lax.dynamic_slice_in_dim(w_out, group * cols, cols, axis=0)
    beside = [swap(after(out_half, here[0]), "rows")]
    there.append(swap(here[1], "groups"))
    far_2x = swap(far_2, "frames")
    far_3 = swap(after(joined, far_2, near_x, there[0], across), "rows", 3)
    far_3x = swap(far_3, "frames")

    found = jnp.stack([x[count : count + heads_n, : MAXB + 2] for x in (joined, near, far_2, far_3)])
    tables = found.astype(jnp.int32)[row ^ jnp.arange(rows_n)].reshape(rows_n * heads_n, MAXB + 2)
    windows = lax.dynamic_index_in_dim(
        tables[:, MAXB + 1].reshape(rows_n, heads_n), core, axis=1, keepdims=False
    )
    picked = tables[windows]
    members, counts = picked[:, :MAXB].reshape(-1), picked[:, MAXB]

    pieces = [joined, near, far_2, far_3], [mine_x, near_x, far_2x, far_3x]
    chunks = [(here[0], there[0]), (here[1], after(there[1], members, counts, beside[0]))]
    last = cols // (3 * HD) * HD
    first = project(place, *pieces, chunks, 0, cols - last)
    first_more = swap(first[2], "heads")
    beside.append(swap(after(beside[0], there[1]), "groups"))
    chunks[1] = (here[1], after(there[1], first[2]))
    second = project(place, *pieces, chunks, cols - last, last)
    second_more = swap(second[2], "heads")
    attended = attend_all(place, members, counts, *first[:2], first_more)
    same, diff = attend_all(place, members, counts, *second[:2], second_more, attended)
    attended = [same] + [swap(same if s % 2 == 0 else diff, "rows", s) for s in range(1, rows_n)]
    beside_across = [swap(part, "heads") for part in (beside[0], after(beside[1], same))]
    near_keep, near_send, far_keep, far_send = mix(place, attended, w_out, across, beside, beside_across)
    far_more = swap(far_send, "frames")
    far = swap((far_keep + far_more.astype(jnp.float32)).astype(jnp.bfloat16), "rows", 2)
    near_more = swap(after(near_send, far_more), "frames")
    return finish(place, near_keep, near_more, far)[None]


def local(latents, w_qkv, w_out, win_blocks, win_counts, block_window):
    rows_n = lax.axis_size("rows")
    pairs = all(lax.axis_size(axis) == 2 for axis in ("groups", "frames", "heads"))
    heads_here = w_qkv.shape[2] // HD
    if pairs and rows_n == 4 and heads_here == 6 and latents.shape[:2] == (1, 2 * BS):
        plan = by_heads
    else:
        plan = by_tokens
    return plan(latents, w_qkv, w_out, win_blocks, win_counts, block_window)


def solution(mesh):
    in_specs = (
        P(("groups", "frames"), "rows", None),
        P("rows", None, ("frames", "heads")),
        P(("frames", "heads"), "rows"),
        P(("groups", "rows"), None),
        P(("groups", "rows")),
        P(("groups", "rows")),
    )
    out_specs = P(("groups", "frames"), ("rows", "heads"), None)
    return jax.shard_map(local, mesh=mesh, in_specs=in_specs, out_specs=out_specs, check_vma=False)
```

```python
import math

import jax
import jax.numpy as jnp
from jax import lax
from jax.experimental import pallas as pl
from jax.experimental.pallas import tpu as pltpu
from jax.sharding import PartitionSpec as P

HD = 128
BS = 64
MAXB = 4
VMEM_BYTES = 24 * 1024 * 1024
WHOLE_VMEM_BYTES = 56 * 1024 * 1024
EXP2_SCALE = math.log2(math.e) / math.sqrt(HD)


def with_halo(value, sides, width):
    for axis, dim in sides:
        peers, length = (lax.axis_size(axis), value.shape[dim])
        up = [(i, (i + 1) % peers) for i in range(peers)]
        down = [(j, i) for i, j in up]
        last = lax.slice_in_dim(value, length - width, length, axis=dim)
        first = lax.slice_in_dim(value, 0, width, axis=dim)
        before = lax.ppermute(last, axis, up)
        after = lax.ppermute(first, axis, down)
        value = jnp.concatenate([before, value, after], axis=dim)
    return value


def by_tokens(latents, w_qkv, w_out, win_blocks, win_counts, block_window):
    rows_n = lax.axis_size("rows")
    shard_idx = lax.axis_index("rows")
    frames = latents.shape[0] * lax.axis_size("frames")
    tok_frame = latents.shape[1]
    model_width = latents.shape[2]
    local_cols = w_qkv.shape[2]
    per_shard = tok_frame // BS
    block_total = per_shard * rows_n
    heads_here = local_cols // HD
    block_len = frames * BS
    score_scale = 1.0 / math.sqrt(HD)
    gathered = lax.all_gather(latents, "frames", axis=0, tiled=True)
    flat_tokens = gathered.reshape(frames * tok_frame, model_width)
    weight_rows = lax.all_gather(w_qkv, "rows", axis=0, tiled=True)
    projected = jnp.dot(
        flat_tokens,
        weight_rows.reshape(weight_rows.shape[0], 3 * local_cols),
        preferred_element_type=jnp.float32,
    ).astype(jnp.bfloat16)
    blocked = projected.reshape(frames, per_shard, BS, 3, local_cols).transpose(1, 0, 2, 3, 4)
    blocked = blocked.reshape(per_shard, block_len, 3, local_cols)
    queries = blocked[:, :, 0]
    keyvals = blocked[:, :, 1:]
    nearby = with_halo(keyvals, (("rows", 0),), per_shard)
    first_block = shard_idx * per_shard
    owners = block_window - first_block
    members = win_blocks[owners]
    lengths = win_counts[owners]
    positions = (members - first_block + per_shard + block_total) % block_total

    def attend(query_rows, picked, live_mask):
        key_count = picked.shape[0]
        key_blocks = nearby[picked]
        key_part = key_blocks[:, :, 0].reshape(key_count * block_len, heads_here, HD)
        value_part = key_blocks[:, :, 1].reshape(key_count * block_len, heads_here, HD)
        scores = (
            jnp.einsum(
                "qhd,khd->hqk",
                query_rows.reshape(block_len, heads_here, HD),
                key_part,
                preferred_element_type=jnp.float32,
            )
            * score_scale
        )
        scores = jnp.where(live_mask[None, None, :], scores, -jnp.inf)
        row_max = jnp.max(scores, axis=-1, keepdims=True)
        raised = jnp.exp(scores - row_max)
        weights = (raised / jnp.sum(raised, axis=-1, keepdims=True)).astype(jnp.bfloat16)
        blended = jnp.einsum(
            "hqk,khd->qhd", weights, value_part, preferred_element_type=jnp.float32
        )
        return blended.reshape(block_len, local_cols).astype(jnp.bfloat16)

    def one_block(block_item):
        query_rows, picked, length = block_item
        live_mask = jnp.repeat(jnp.arange(MAXB) < length, block_len)
        return attend(query_rows, picked, live_mask)

    attended = lax.map(one_block, (queries, positions, lengths))
    ordered = attended.reshape(per_shard, frames, BS, local_cols).transpose(1, 0, 2, 3)
    ordered = ordered.reshape(frames * tok_frame, local_cols)
    w_full = lax.all_gather(w_out, "rows", axis=1, tiled=True)
    group_count = lax.axis_size(("frames", "heads"))
    out_rows = frames * tok_frame // group_count
    summed = lax.psum_scatter(
        jnp.dot(ordered, w_full, preferred_element_type=jnp.float32).astype(jnp.bfloat16),
        ("frames", "heads"),
        scatter_dimension=0,
        tiled=True,
    )
    return summed.reshape(1, out_rows, model_width)


def swap(value, axis, step=1):
    peers = lax.axis_size(axis)
    return lax.ppermute(value, axis, [(i, i ^ step) for i in range(peers)])


def after(value, *others):
    return lax.optimization_barrier((value, *others))[0]


def call(kernel, out_shape, prefetch, operands, scratch=(), flops=0, read=0, limit=VMEM_BYTES):
    return pl.pallas_call(
        kernel,
        out_shape=out_shape,
        grid_spec=pltpu.PrefetchScalarGridSpec(
            num_scalar_prefetch=len(prefetch),
            grid=(),
            in_specs=[pl.BlockSpec(memory_space=pltpu.VMEM)] * len(operands),
            out_specs=jax.tree.map(lambda _: pl.BlockSpec(memory_space=pltpu.VMEM), out_shape),
            scratch_shapes=scratch,
        ),
        compiler_params=pltpu.CompilerParams(vmem_limit_bytes=limit),
        cost_estimate=pl.CostEstimate(flops=flops, bytes_accessed=read, transcendentals=0),
    )(*prefetch, *operands)


def project(place, mine, theirs, chunks, first, cols):
    rows, (count, width) = len(mine), theirs[0].shape
    half = chunks[0][0].shape[1]
    slices = len(chunks)
    flat = [w for of_round in chunks for w in of_round]
    fetched = 2 * rows + len(flat)

    def kernel(place_ref, *refs):
        row, group, frame, core = (place_ref[i] for i in range(4))
        w_refs = refs[2 * rows : fetched]
        q_keep, kv_keep, send, x_all, w_all, total, sems = refs[fetched:]
        copies = []
        for k in range(slices):
            for g in range(2):
                at = pl.multiple_of((row + slices - k) % slices * (2 * half) + (group + g) % 2 * half, half)
                for part in range(3):
                    source = w_refs[2 * k + g].at[part, :, first : first + cols]
                    into = w_all.at[pl.ds(at, half), part * cols : (part + 1) * cols]
                    copies.append(pltpu.make_async_copy(source, into, sems.at[len(copies)]))
        for i in range(2 * rows):
            to = x_all.at[row ^ (i % rows), (frame + i // rows) % 2]
            copies.append(pltpu.make_async_copy(refs[i].at[pl.ds(0, count)], to, sems.at[len(copies)]))
        for copy in copies:
            copy.start()
        for copy in copies:
            copy.wait()
        acc = jnp.dot(x_all[...].reshape(-1, width), w_all[...], preferred_element_type=jnp.float32)
        kv_part = acc[:, cols:].reshape(rows, 2 * count, 2 * cols)
        kv_keep[...] = kv_part
        send[:, : 2 * count, :] = kv_part.astype(jnp.bfloat16)
        total[...] = acc[:, :cols].reshape(rows, 2, count, cols)
        own = pl.multiple_of(core * BS, BS)
        other = pl.multiple_of((1 - core) * BS, BS)
        q_keep[...] = total[:, :, pl.ds(own, BS), :].reshape(q_keep.shape)
        for f in range(2):
            at = slice(f * cols, (f + 1) * cols)
            send[:, 2 * count :, at] = total[:, f, pl.ds(other, BS), :].astype(jnp.bfloat16)

    vmem, hbm = pl.BlockSpec(memory_space=pltpu.VMEM), pl.BlockSpec(memory_space=pltpu.HBM)
    flops = 2 * rows * 2 * count * width * 3 * cols
    return pl.pallas_call(
        kernel,
        out_shape=(
            jax.ShapeDtypeStruct((rows, 2 * BS, cols), jnp.float32),
            jax.ShapeDtypeStruct((rows, 2 * count, 2 * cols), jnp.float32),
            jax.ShapeDtypeStruct((rows, 2 * count + BS, 2 * cols), jnp.bfloat16),
        ),
        grid_spec=pltpu.PrefetchScalarGridSpec(
            num_scalar_prefetch=1,
            grid=(),
            in_specs=[hbm] * fetched,
            out_specs=(vmem, vmem, vmem),
            scratch_shapes=[
                pltpu.VMEM((rows, 2, count, width), jnp.bfloat16),
                pltpu.VMEM((width, 3 * cols), jnp.bfloat16),
                pltpu.VMEM((rows, 2, count, cols), jnp.float32),
                pltpu.SemaphoreType.DMA((2 * rows + 3 * len(flat),)),
            ],
        ),
        compiler_params=pltpu.CompilerParams(vmem_limit_bytes=VMEM_BYTES),
        cost_estimate=pl.CostEstimate(flops=8 * flops, bytes_accessed=flops // 300, transcendentals=0),
    )(place, *mine, *theirs, *flat)


def attend_all(place, members, counts, queries, keyvals, more, earlier=()):
    blocks, block_len, cols = queries.shape
    first = earlier[0].shape[2] if earlier else 0
    rows = keyvals.shape[1]
    per_row = rows // block_len

    def kernel(place_ref, members_ref, counts_ref, q_ref, kv_ref, more_ref, *refs):
        same_ref, diff_ref, q_sum, kv_sum, out = refs[len(earlier) :]
        for r in range(blocks):
            added = more_ref[r, rows:, :].astype(jnp.float32)
            added = jnp.concatenate([added[:, :cols], added[:, cols:]], axis=0)
            q_sum[r] = (q_ref[r] + added).astype(jnp.bfloat16)
            both = (kv_ref[r] + more_ref[r, :rows, :].astype(jnp.float32)).astype(jnp.bfloat16)
            both = both.reshape(2, rows // 2, 2 * cols)
            for j in range(per_row):
                part = both[:, j * BS : (j + 1) * BS, :]
                kv_sum[r * per_row + j] = part.reshape(block_len, 2 * cols)
        column = lax.broadcasted_iota(jnp.int32, (block_len, MAXB * block_len), 1)
        for b in range(blocks):
            live = column < counts_ref[b] * block_len
            listed = [kv_sum.at[members_ref[b * MAXB + j]] for j in range(MAXB)]
            for h in range(cols // HD):
                at = slice(h * HD, (h + 1) * HD)
                at_v = slice(cols + h * HD, cols + (h + 1) * HD)
                keys = jnp.concatenate([block[:, at] for block in listed], axis=0)
                values = jnp.concatenate([block[:, at_v] for block in listed], axis=0)
                scores = lax.dot_general(
                    q_sum[b, :, at], keys, (((1,), (1,)), ((), ())), preferred_element_type=jnp.float32
                )
                scores = jnp.where(live, scores, -jnp.inf)
                raised = jnp.exp2((scores - jnp.max(scores, axis=-1, keepdims=True)) * EXP2_SCALE)
                weights = raised * (1.0 / jnp.sum(raised, axis=-1, keepdims=True))
                blended = jnp.dot(
                    weights.astype(jnp.bfloat16), values, preferred_element_type=jnp.float32
                )
                out[(b + place_ref[0]) % 2, b // 2, :, at] = blended.astype(jnp.bfloat16)
        for i, out_ref in enumerate((same_ref, diff_ref)):
            if earlier:
                out_ref[:, :, :first] = refs[i][...]
            out_ref[:, :, first:] = out[i]

    half = jax.ShapeDtypeStruct((blocks // 2, block_len, first + cols), jnp.bfloat16)
    return call(
        kernel,
        (half, half),
        [place, members, counts],
        [queries, keyvals, more, *earlier],
        scratch=[
            pltpu.VMEM((blocks, block_len, cols), jnp.bfloat16),
            pltpu.VMEM((blocks * per_row, block_len, 2 * cols), jnp.bfloat16),
            pltpu.VMEM((2, blocks // 2, block_len, cols), jnp.bfloat16),
        ],
        flops=4 * blocks * block_len * MAXB * block_len * cols,
        read=16 * blocks * block_len * cols,
    )


def mix(place, attended, w_own, w_across, beside, beside_across):
    blocks, block_len, cols = attended[0].shape
    width = w_own.shape[1]

    def kernel(place_ref, *refs):
        row, group, frame, core = (place_ref[i] for i in range(4))
        w_refs = refs[4:10]
        near_keep, near_send, far_keep, far_send, a_all, sums = refs[10:]
        for s in range(4):
            a_all[s] = refs[s][...].reshape(blocks * block_len, cols)

        def term(c, other):
            side = 1 - core if other else core
            acc = None
            for i in range(2):
                if c == 0:
                    weight, half = w_refs[other][i * cols : (i + 1) * cols, :], i
                else:
                    weight, half = w_refs[2 + 2 * other + i][...], (i + group) % 2
                part = jnp.dot(a_all[(2 * side + half) ^ row], weight, preferred_element_type=jnp.float32)
                acc = part if acc is None else acc + part
            return acc.astype(jnp.bfloat16).astype(jnp.float32)

        for c in range(2):
            sums[...] = (term(c, 0) + term(c, 1)).reshape(blocks, 2, BS, width)
            at = (row + c) % 2
            near_keep[at] = sums[row // 2, frame]
            near_send[at] = sums[row // 2, 1 - frame].astype(jnp.bfloat16)
            far_keep[at] = sums[1 - row // 2, frame]
            far_send[at] = sums[1 - row // 2, 1 - frame].astype(jnp.bfloat16)

    kept = jax.ShapeDtypeStruct((2, BS, width), jnp.float32)
    sent = jax.ShapeDtypeStruct((2, BS, width), jnp.bfloat16)
    return call(
        kernel,
        (kept, sent, kept, sent),
        [place],
        [*attended, w_own, w_across, *beside, *beside_across],
        scratch=[
            pltpu.VMEM((4, blocks * block_len, cols), jnp.bfloat16),
            pltpu.VMEM((blocks, 2, BS, width), jnp.float32),
        ],
        flops=2 * blocks * block_len * 4 * cols * 2 * width,
        read=16 * cols * width,
    )


def finish(place, near_keep, near_more, far):
    halves, rows, width = near_keep.shape

    def kernel(place_ref, keep_ref, more_ref, far_ref, out_ref):
        pair = place_ref[0] // 2
        for c in range(halves):
            here = pl.multiple_of((pair * halves + c) * width, width)
            there = pl.multiple_of(((1 - pair) * halves + c) * width, width)
            out_ref[:, pl.ds(here, width)] = (keep_ref[c] + more_ref[c].astype(jnp.float32)).astype(jnp.bfloat16)
            out_ref[:, pl.ds(there, width)] = far_ref[c]

    return call(
        kernel,
        jax.ShapeDtypeStruct((rows, 2 * halves * width), jnp.bfloat16),
        [place],
        [near_keep, near_more, far],
        read=12 * rows * halves * width,
    )


def by_heads(latents, w_qkv, w_out, win_blocks, win_counts, block_window):
    rows_n, heads_n = lax.axis_size("rows"), lax.axis_size("heads")
    group, row = lax.axis_index("groups"), lax.axis_index("rows")
    frame, core = lax.axis_index("frames"), lax.axis_index("heads")
    count = latents.shape[1]
    depth, _, local_cols = w_qkv.shape
    span = rows_n // heads_n
    cols = local_cols // span
    half = depth // 2
    place = jnp.stack([row, group, frame, core]).astype(jnp.int32)

    def reshard(k, *others):
        value = lax.dynamic_slice(
            w_qkv.transpose(1, 0, 2), (0, group * half, (k + row) % span * cols), (3, half, cols)
        )
        pairs = [
            (r * heads_n + h, (h * span + (k + r) % span) * heads_n + r // span)
            for r in range(rows_n)
            for h in range(heads_n)
        ]
        return lax.ppermute(after(value, *others) if others else value, ("rows", "heads"), pairs)

    mine = lax.dynamic_slice_in_dim(latents[0], core * span * depth, span * depth, axis=1)
    mine_x = swap(mine, "frames")
    here, there = [reshard(0)], []
    tables = jnp.concatenate([win_blocks, win_counts[:, None], block_window[:, None]], axis=1)
    tables = jnp.pad(tables, ((0, 8 - heads_n), (0, span * depth - MAXB - 2))).astype(mine.dtype)
    joined = jnp.concatenate([mine, tables], axis=0)
    near = swap(joined, "rows")
    near_x = swap(near, "frames")
    across = swap(after(w_out, near), "heads")
    there.append(swap(here[0], "groups"))
    here.append(reshard(1, near))
    far_2 = swap(after(joined, near, mine_x), "rows", 2)
    out_half = lax.dynamic_slice_in_dim(w_out, group * cols, cols, axis=0)
    beside = [swap(after(out_half, here[0]), "rows")]
    there.append(swap(after(here[1], beside[0], there[0]), "groups"))
    far_2x = swap(after(far_2, near_x), "frames")
    far_3 = swap(after(joined, far_2, across), "rows", 3)
    far_3x = swap(far_3, "frames")

    found = jnp.stack([x[count : count + heads_n, : MAXB + 2] for x in (joined, near, far_2, far_3)])
    tables = found.astype(jnp.int32)[row ^ jnp.arange(rows_n)].reshape(rows_n * heads_n, MAXB + 2)
    windows = lax.dynamic_index_in_dim(
        tables[:, MAXB + 1].reshape(rows_n, heads_n), core, axis=1, keepdims=False
    )
    picked = tables[windows]
    members, counts = picked[:, :MAXB].reshape(-1), picked[:, MAXB]

    pieces = [joined, near, far_2, far_3], [mine_x, near_x, far_2x, far_3x]
    chunks = [(here[0], there[0]), (here[1], after(there[1], members, counts))]
    last = cols // (3 * HD) * HD
    first = project(place, *pieces, chunks, 0, cols - last)
    first_more = swap(first[2], "heads")
    beside.append(swap(after(beside[0], there[1]), "groups"))
    chunks[1] = (here[1], after(there[1], first[2]))
    second = project(place, *pieces, chunks, cols - last, last)
    second_more = swap(second[2], "heads")
    attended = attend_all(place, members, counts, *first[:2], first_more)
    beside_across = [swap(part, "heads") for part in (beside[0], after(beside[1], attended[0]))]
    same, diff = attend_all(place, members, counts, *second[:2], second_more, attended)
    attended = [same] + [swap(same if s % 2 == 0 else diff, "rows", s) for s in range(1, rows_n)]
    near_keep, near_send, far_keep, far_send = mix(place, attended, w_out, across, beside, beside_across)
    far_more = swap(far_send, "frames")
    far = swap((far_keep + far_more.astype(jnp.float32)).astype(jnp.bfloat16), "rows", 2)
    near_more = swap(after(near_send, far_more), "frames")
    return finish(place, near_keep, near_more, far)[None]


def local(latents, w_qkv, w_out, win_blocks, win_counts, block_window):
    rows_n = lax.axis_size("rows")
    pairs = all(lax.axis_size(axis) == 2 for axis in ("groups", "frames", "heads"))
    heads_here = w_qkv.shape[2] // HD
    if pairs and rows_n == 4 and heads_here == 6 and latents.shape[:2] == (1, 2 * BS):
        plan = by_heads
    else:
        plan = by_tokens
    return plan(latents, w_qkv, w_out, win_blocks, win_counts, block_window)


def solution(mesh):
    in_specs = (
        P(("groups", "frames"), "rows", None),
        P("rows", None, ("frames", "heads")),
        P(("frames", "heads"), "rows"),
        P(("groups", "rows"), None),
        P(("groups", "rows")),
        P(("groups", "rows")),
    )
    out_specs = P(("groups", "frames"), ("rows", "heads"), None)
    return jax.shard_map(local, mesh=mesh, in_specs=in_specs, out_specs=out_specs, check_vma=False)
```

```python
import math

import jax
import jax.numpy as jnp
from jax import lax
from jax.experimental import pallas as pl
from jax.experimental.pallas import tpu as pltpu
from jax.sharding import PartitionSpec as P

HD = 128
BS = 64
MAXB = 4
VMEM_BYTES = 24 * 1024 * 1024
WHOLE_VMEM_BYTES = 56 * 1024 * 1024
EXP2_SCALE = math.log2(math.e) / math.sqrt(HD)


def with_halo(value, sides, width):
    for axis, dim in sides:
        peers, length = (lax.axis_size(axis), value.shape[dim])
        up = [(i, (i + 1) % peers) for i in range(peers)]
        down = [(j, i) for i, j in up]
        last = lax.slice_in_dim(value, length - width, length, axis=dim)
        first = lax.slice_in_dim(value, 0, width, axis=dim)
        before = lax.ppermute(last, axis, up)
        after = lax.ppermute(first, axis, down)
        value = jnp.concatenate([before, value, after], axis=dim)
    return value


def by_tokens(latents, w_qkv, w_out, win_blocks, win_counts, block_window):
    rows_n = lax.axis_size("rows")
    shard_idx = lax.axis_index("rows")
    frames = latents.shape[0] * lax.axis_size("frames")
    tok_frame = latents.shape[1]
    model_width = latents.shape[2]
    local_cols = w_qkv.shape[2]
    per_shard = tok_frame // BS
    block_total = per_shard * rows_n
    heads_here = local_cols // HD
    block_len = frames * BS
    score_scale = 1.0 / math.sqrt(HD)
    gathered = lax.all_gather(latents, "frames", axis=0, tiled=True)
    flat_tokens = gathered.reshape(frames * tok_frame, model_width)
    weight_rows = lax.all_gather(w_qkv, "rows", axis=0, tiled=True)
    projected = jnp.dot(
        flat_tokens,
        weight_rows.reshape(weight_rows.shape[0], 3 * local_cols),
        preferred_element_type=jnp.float32,
    ).astype(jnp.bfloat16)
    blocked = projected.reshape(frames, per_shard, BS, 3, local_cols).transpose(1, 0, 2, 3, 4)
    blocked = blocked.reshape(per_shard, block_len, 3, local_cols)
    queries = blocked[:, :, 0]
    keyvals = blocked[:, :, 1:]
    nearby = with_halo(keyvals, (("rows", 0),), per_shard)
    first_block = shard_idx * per_shard
    owners = block_window - first_block
    members = win_blocks[owners]
    lengths = win_counts[owners]
    positions = (members - first_block + per_shard + block_total) % block_total

    def attend(query_rows, picked, live_mask):
        key_count = picked.shape[0]
        key_blocks = nearby[picked]
        key_part = key_blocks[:, :, 0].reshape(key_count * block_len, heads_here, HD)
        value_part = key_blocks[:, :, 1].reshape(key_count * block_len, heads_here, HD)
        scores = (
            jnp.einsum(
                "qhd,khd->hqk",
                query_rows.reshape(block_len, heads_here, HD),
                key_part,
                preferred_element_type=jnp.float32,
            )
            * score_scale
        )
        scores = jnp.where(live_mask[None, None, :], scores, -jnp.inf)
        row_max = jnp.max(scores, axis=-1, keepdims=True)
        raised = jnp.exp(scores - row_max)
        weights = (raised / jnp.sum(raised, axis=-1, keepdims=True)).astype(jnp.bfloat16)
        blended = jnp.einsum(
            "hqk,khd->qhd", weights, value_part, preferred_element_type=jnp.float32
        )
        return blended.reshape(block_len, local_cols).astype(jnp.bfloat16)

    def one_block(block_item):
        query_rows, picked, length = block_item
        live_mask = jnp.repeat(jnp.arange(MAXB) < length, block_len)
        return attend(query_rows, picked, live_mask)

    attended = lax.map(one_block, (queries, positions, lengths))
    ordered = attended.reshape(per_shard, frames, BS, local_cols).transpose(1, 0, 2, 3)
    ordered = ordered.reshape(frames * tok_frame, local_cols)
    w_full = lax.all_gather(w_out, "rows", axis=1, tiled=True)
    group_count = lax.axis_size(("frames", "heads"))
    out_rows = frames * tok_frame // group_count
    summed = lax.psum_scatter(
        jnp.dot(ordered, w_full, preferred_element_type=jnp.float32).astype(jnp.bfloat16),
        ("frames", "heads"),
        scatter_dimension=0,
        tiled=True,
    )
    return summed.reshape(1, out_rows, model_width)


def swap(value, axis, step=1):
    peers = lax.axis_size(axis)
    return lax.ppermute(value, axis, [(i, i ^ step) for i in range(peers)])


def after(value, *others):
    return lax.optimization_barrier((value, *others))[0]


def call(kernel, out_shape, prefetch, operands, scratch=(), flops=0, read=0, limit=VMEM_BYTES):
    return pl.pallas_call(
        kernel,
        out_shape=out_shape,
        grid_spec=pltpu.PrefetchScalarGridSpec(
            num_scalar_prefetch=len(prefetch),
            grid=(),
            in_specs=[pl.BlockSpec(memory_space=pltpu.VMEM)] * len(operands),
            out_specs=jax.tree.map(lambda _: pl.BlockSpec(memory_space=pltpu.VMEM), out_shape),
            scratch_shapes=scratch,
        ),
        compiler_params=pltpu.CompilerParams(vmem_limit_bytes=limit),
        cost_estimate=pl.CostEstimate(flops=flops, bytes_accessed=read, transcendentals=0),
    )(*prefetch, *operands)


def project(place, mine, theirs, chunks, first, cols, weight):
    rows, (count, width) = len(mine) - 1, theirs[0].shape
    half = chunks[0][0].shape[1]
    slices = len(chunks)
    flat = [w for of_round in chunks for w in of_round]
    fetched = 2 * len(mine) + len(flat)

    def kernel(place_ref, *refs):
        row, group, frame, core = (place_ref[i] for i in range(4))
        w_refs = refs[2 * len(mine) : fetched]
        q_keep, kv_keep, send, x_all, w_all, total, sems = refs[fetched:]
        copies = []
        for k in range(slices):
            for g in range(2):
                at = pl.multiple_of((row + slices - k) % slices * (2 * half) + (group + g) % 2 * half, half)
                for part in range(3):
                    source = w_refs[2 * k + g].at[part, :, first : first + cols]
                    into = w_all.at[pl.ds(at, half), part * cols : (part + 1) * cols]
                    copies.append(pltpu.make_async_copy(source, into, sems.at[len(copies)]))
        for copy in copies:
            copy.start()
        middle = (row == 1) | (row == 2)
        for f in range(2):
            x_refs = refs[f * len(mine) : (f + 1) * len(mine)]
            for s in range(rows):
                to, sem = x_all.at[row ^ s, (frame + f) % 2], sems.at[len(copies)]
                copies.append(pltpu.make_async_copy(x_refs[s].at[pl.ds(0, count)], to, sem))
                if s < rows - 1:
                    copies[-1].start()
                else:
                    other = pltpu.make_async_copy(x_refs[rows].at[pl.ds(0, count)], to, sem)
                    pl.when(middle)(copies[-1].start)
                    pl.when(jnp.logical_not(middle))(other.start)
        for copy in copies:
            copy.wait()
        acc = jnp.dot(x_all[...].reshape(-1, width), w_all[...], preferred_element_type=jnp.float32)
        kv_part = acc[:, cols:].reshape(rows, 2 * count, 2 * cols)
        kv_keep[...] = kv_part
        send[:, : 2 * count, :] = kv_part.astype(jnp.bfloat16)
        total[...] = acc[:, :cols].reshape(rows, 2, count, cols)
        own = pl.multiple_of(core * BS, BS)
        other = pl.multiple_of((1 - core) * BS, BS)
        q_keep[...] = total[:, :, pl.ds(own, BS), :].reshape(q_keep.shape)
        for f in range(2):
            at = slice(f * cols, (f + 1) * cols)
            send[:, 2 * count :, at] = total[:, f, pl.ds(other, BS), :].astype(jnp.bfloat16)

    vmem, hbm = pl.BlockSpec(memory_space=pltpu.VMEM), pl.BlockSpec(memory_space=pltpu.HBM)
    flops = 2 * rows * 2 * count * width * 3 * cols
    return pl.pallas_call(
        kernel,
        out_shape=(
            jax.ShapeDtypeStruct((rows, 2 * BS, cols), jnp.float32),
            jax.ShapeDtypeStruct((rows, 2 * count, 2 * cols), jnp.float32),
            jax.ShapeDtypeStruct((rows, 2 * count + BS, 2 * cols), jnp.bfloat16),
        ),
        grid_spec=pltpu.PrefetchScalarGridSpec(
            num_scalar_prefetch=1,
            grid=(),
            in_specs=[hbm] * fetched,
            out_specs=(vmem, vmem, vmem),
            scratch_shapes=[
                pltpu.VMEM((rows, 2, count, width), jnp.bfloat16),
                pltpu.VMEM((width, 3 * cols), jnp.bfloat16),
                pltpu.VMEM((rows, 2, count, cols), jnp.float32),
                pltpu.SemaphoreType.DMA((2 * rows + 3 * len(flat),)),
            ],
        ),
        compiler_params=pltpu.CompilerParams(vmem_limit_bytes=VMEM_BYTES),
        cost_estimate=pl.CostEstimate(flops=weight * flops, bytes_accessed=flops // 300, transcendentals=0),
    )(place, *mine, *theirs, *flat)


def attend_all(place, members, counts, queries, keyvals, more, earlier=()):
    blocks, block_len, cols = queries.shape
    first = earlier[0].shape[2] if earlier else 0
    rows = keyvals.shape[1]
    per_row = rows // block_len

    def kernel(place_ref, members_ref, counts_ref, q_ref, kv_ref, more_ref, *refs):
        same_ref, diff_ref, q_sum, kv_sum, out = refs[len(earlier) :]
        for r in range(blocks):
            added = more_ref[r, rows:, :].astype(jnp.float32)
            added = jnp.concatenate([added[:, :cols], added[:, cols:]], axis=0)
            q_sum[r] = (q_ref[r] + added).astype(jnp.bfloat16)
            both = (kv_ref[r] + more_ref[r, :rows, :].astype(jnp.float32)).astype(jnp.bfloat16)
            both = both.reshape(2, rows // 2, 2 * cols)
            for j in range(per_row):
                part = both[:, j * BS : (j + 1) * BS, :]
                kv_sum[r * per_row + j] = part.reshape(block_len, 2 * cols)
        column = lax.broadcasted_iota(jnp.int32, (block_len, MAXB * block_len), 1)
        for b in range(blocks):
            live = column < counts_ref[b] * block_len
            listed = [kv_sum.at[members_ref[b * MAXB + j]] for j in range(MAXB)]
            for h in range(cols // HD):
                at = slice(h * HD, (h + 1) * HD)
                at_v = slice(cols + h * HD, cols + (h + 1) * HD)
                keys = jnp.concatenate([block[:, at] for block in listed], axis=0)
                values = jnp.concatenate([block[:, at_v] for block in listed], axis=0)
                scores = lax.dot_general(
                    q_sum[b, :, at], keys, (((1,), (1,)), ((), ())), preferred_element_type=jnp.float32
                )
                scores = jnp.where(live, scores, -jnp.inf)
                raised = jnp.exp2((scores - jnp.max(scores, axis=-1, keepdims=True)) * EXP2_SCALE)
                weights = raised * (1.0 / jnp.sum(raised, axis=-1, keepdims=True))
                blended = jnp.dot(
                    weights.astype(jnp.bfloat16), values, preferred_element_type=jnp.float32
                )
                out[(b + place_ref[0]) % 2, b // 2, :, at] = blended.astype(jnp.bfloat16)
        for i, out_ref in enumerate((same_ref, diff_ref)):
            if earlier:
                out_ref[:, :, :first] = refs[i][...]
            out_ref[:, :, first:] = out[i]

    half = jax.ShapeDtypeStruct((blocks // 2, block_len, first + cols), jnp.bfloat16)
    return call(
        kernel,
        (half, half),
        [place, members, counts],
        [queries, keyvals, more, *earlier],
        scratch=[
            pltpu.VMEM((blocks, block_len, cols), jnp.bfloat16),
            pltpu.VMEM((blocks * per_row, block_len, 2 * cols), jnp.bfloat16),
            pltpu.VMEM((2, blocks // 2, block_len, cols), jnp.bfloat16),
        ],
        flops=4 * blocks * block_len * MAXB * block_len * cols,
        read=16 * blocks * block_len * cols,
    )


def mix(place, attended, w_own, w_across, beside, beside_across):
    blocks, block_len, cols = attended[0].shape
    width = w_own.shape[1]

    def kernel(place_ref, *refs):
        row, group, frame, core = (place_ref[i] for i in range(4))
        w_refs = refs[4:10]
        near_keep, near_send, far_keep, far_send, a_all, sums = refs[10:]
        for s in range(4):
            a_all[s] = refs[s][...].reshape(blocks * block_len, cols)

        def term(c, other):
            side = 1 - core if other else core
            acc = None
            for i in range(2):
                if c == 0:
                    weight, half = w_refs[other][i * cols : (i + 1) * cols, :], i
                else:
                    weight, half = w_refs[2 + 2 * other + i][...], (i + group) % 2
                part = jnp.dot(a_all[(2 * side + half) ^ row], weight, preferred_element_type=jnp.float32)
                acc = part if acc is None else acc + part
            return acc.astype(jnp.bfloat16).astype(jnp.float32)

        for c in range(2):
            sums[...] = (term(c, 0) + term(c, 1)).reshape(blocks, 2, BS, width)
            at = (row + c) % 2
            near_keep[at] = sums[row // 2, frame]
            near_send[at] = sums[row // 2, 1 - frame].astype(jnp.bfloat16)
            far_keep[at] = sums[1 - row // 2, frame]
            far_send[at] = sums[1 - row // 2, 1 - frame].astype(jnp.bfloat16)

    kept = jax.ShapeDtypeStruct((2, BS, width), jnp.float32)
    sent = jax.ShapeDtypeStruct((2, BS, width), jnp.bfloat16)
    return call(
        kernel,
        (kept, sent, kept, sent),
        [place],
        [*attended, w_own, w_across, *beside, *beside_across],
        scratch=[
            pltpu.VMEM((4, blocks * block_len, cols), jnp.bfloat16),
            pltpu.VMEM((blocks, 2, BS, width), jnp.float32),
        ],
        flops=2 * blocks * block_len * 4 * cols * 2 * width,
        read=16 * cols * width,
    )


def finish(place, near_keep, near_more, far):
    halves, rows, width = near_keep.shape

    def kernel(place_ref, keep_ref, more_ref, far_ref, out_ref):
        pair = place_ref[0] // 2
        for c in range(halves):
            here = pl.multiple_of((pair * halves + c) * width, width)
            there = pl.multiple_of(((1 - pair) * halves + c) * width, width)
            out_ref[:, pl.ds(here, width)] = (keep_ref[c] + more_ref[c].astype(jnp.float32)).astype(jnp.bfloat16)
            out_ref[:, pl.ds(there, width)] = far_ref[c]

    return call(
        kernel,
        jax.ShapeDtypeStruct((rows, 2 * halves * width), jnp.bfloat16),
        [place],
        [near_keep, near_more, far],
        read=12 * rows * halves * width,
    )


def by_heads(latents, w_qkv, w_out, win_blocks, win_counts, block_window):
    rows_n, heads_n = lax.axis_size("rows"), lax.axis_size("heads")
    group, row = lax.axis_index("groups"), lax.axis_index("rows")
    frame, core = lax.axis_index("frames"), lax.axis_index("heads")
    count = latents.shape[1]
    depth, _, local_cols = w_qkv.shape
    span = rows_n // heads_n
    cols = local_cols // span
    half = depth // 2
    place = jnp.stack([row, group, frame, core]).astype(jnp.int32)

    def over_frames(value, rows):
        pairs = [(2 * r + f, 2 * r + 1 - f) for r in rows for f in range(2)]
        return lax.ppermute(value, ("rows", "frames"), pairs)

    def reshard(k, *others):
        value = lax.dynamic_slice(
            w_qkv.transpose(1, 0, 2), (0, group * half, (k + row) % span * cols), (3, half, cols)
        )
        pairs = [
            (r * heads_n + h, (h * span + (k + r) % span) * heads_n + r // span)
            for r in range(rows_n)
            for h in range(heads_n)
        ]
        return lax.ppermute(after(value, *others) if others else value, ("rows", "heads"), pairs)

    mine = lax.dynamic_slice_in_dim(latents[0], core * span * depth, span * depth, axis=1)
    mine_x = swap(mine, "frames")
    here, there = [reshard(0)], []
    tables = jnp.concatenate([win_blocks, win_counts[:, None], block_window[:, None]], axis=1)
    tables = jnp.pad(tables, ((0, 8 - heads_n), (0, span * depth - MAXB - 2))).astype(mine.dtype)
    joined = jnp.concatenate([mine, tables], axis=0)
    near = swap(joined, "rows")
    in_3 = lax.ppermute(joined, "rows", [(1, 2), (2, 1)])
    near_x = swap(near, "frames")
    across = swap(after(w_out, near), "heads")
    there.append(swap(here[0], "groups"))
    here.append(reshard(1, near))
    far_2 = swap(after(joined, near, mine_x, near_x), "rows", 2)
    out_half = lax.dynamic_slice_in_dim(w_out, group * cols, cols, axis=0)
    beside = [swap(after(out_half, here[0]), "rows")]
    in_3x = over_frames(in_3, (1, 2))
    there.append(swap(after(here[1], beside[0], there[0], across), "groups"))
    far_2x = swap(after(far_2, in_3x), "frames")
    out_3 = lax.ppermute(far_2, "rows", [(1, 0), (2, 3)])
    out_3x = over_frames(out_3, (0, 3))

    extra = jnp.where((row == 1) | (row == 2), in_3[count:], out_3[count:])
    found = [joined[count:], near[count:], far_2[count:], extra]
    found = jnp.stack([x[:heads_n, : MAXB + 2] for x in found])
    tables = found.astype(jnp.int32)[row ^ jnp.arange(rows_n)].reshape(rows_n * heads_n, MAXB + 2)
    windows = lax.dynamic_index_in_dim(
        tables[:, MAXB + 1].reshape(rows_n, heads_n), core, axis=1, keepdims=False
    )
    picked = tables[windows]
    members, counts = picked[:, :MAXB].reshape(-1), picked[:, MAXB]

    pieces = [joined, near, far_2, in_3, out_3], [mine_x, near_x, far_2x, in_3x, out_3x]
    chunks = [(here[0], there[0]), (here[1], after(there[1], members, counts))]
    last = cols // (3 * HD) * HD
    first = project(place, *pieces, chunks, 0, cols - last, 8)
    first_more = swap(first[2], "heads")
    beside.append(swap(after(beside[0], there[1]), "groups"))
    chunks[1] = (here[1], after(there[1], first[2]))
    second = project(place, *pieces, chunks, cols - last, last, 1)
    second_more = swap(second[2], "heads")
    attended = attend_all(place, members, counts, *first[:2], first_more)
    same, diff = attend_all(place, members, counts, *second[:2], second_more, attended)
    attended = [same] + [swap(same if s % 2 == 0 else diff, "rows", s) for s in range(1, rows_n)]
    beside_across = [swap(part, "heads") for part in (beside[0], after(beside[1], same))]
    near_keep, near_send, far_keep, far_send = mix(place, attended, w_out, across, beside, beside_across)
    far_more = swap(far_send, "frames")
    far = swap((far_keep + far_more.astype(jnp.float32)).astype(jnp.bfloat16), "rows", 2)
    near_more = swap(after(near_send, far_more), "frames")
    return finish(place, near_keep, near_more, far)[None]


def local(latents, w_qkv, w_out, win_blocks, win_counts, block_window):
    rows_n = lax.axis_size("rows")
    pairs = all(lax.axis_size(axis) == 2 for axis in ("groups", "frames", "heads"))
    heads_here = w_qkv.shape[2] // HD
    if pairs and rows_n == 4 and heads_here == 6 and latents.shape[:2] == (1, 2 * BS):
        plan = by_heads
    else:
        plan = by_tokens
    return plan(latents, w_qkv, w_out, win_blocks, win_counts, block_window)


def solution(mesh):
    in_specs = (
        P(("groups", "frames"), "rows", None),
        P("rows", None, ("frames", "heads")),
        P(("frames", "heads"), "rows"),
        P(("groups", "rows"), None),
        P(("groups", "rows")),
        P(("groups", "rows")),
    )
    out_specs = P(("groups", "frames"), ("rows", "heads"), None)
    return jax.shard_map(local, mesh=mesh, in_specs=in_specs, out_specs=out_specs, check_vma=False)
```

```python
import math

import jax
import jax.numpy as jnp
from jax import lax
from jax.experimental import pallas as pl
from jax.experimental.pallas import tpu as pltpu
from jax.sharding import PartitionSpec as P

HD = 128
BS = 64
MAXB = 4
VMEM_BYTES = 24 * 1024 * 1024
WHOLE_VMEM_BYTES = 56 * 1024 * 1024
EXP2_SCALE = math.log2(math.e) / math.sqrt(HD)


def with_halo(value, sides, width):
    for axis, dim in sides:
        peers, length = (lax.axis_size(axis), value.shape[dim])
        up = [(i, (i + 1) % peers) for i in range(peers)]
        down = [(j, i) for i, j in up]
        last = lax.slice_in_dim(value, length - width, length, axis=dim)
        first = lax.slice_in_dim(value, 0, width, axis=dim)
        before = lax.ppermute(last, axis, up)
        after = lax.ppermute(first, axis, down)
        value = jnp.concatenate([before, value, after], axis=dim)
    return value


def by_tokens(latents, w_qkv, w_out, win_blocks, win_counts, block_window):
    rows_n = lax.axis_size("rows")
    shard_idx = lax.axis_index("rows")
    frames = latents.shape[0] * lax.axis_size("frames")
    tok_frame = latents.shape[1]
    model_width = latents.shape[2]
    local_cols = w_qkv.shape[2]
    per_shard = tok_frame // BS
    block_total = per_shard * rows_n
    heads_here = local_cols // HD
    block_len = frames * BS
    score_scale = 1.0 / math.sqrt(HD)
    gathered = lax.all_gather(latents, "frames", axis=0, tiled=True)
    flat_tokens = gathered.reshape(frames * tok_frame, model_width)
    weight_rows = lax.all_gather(w_qkv, "rows", axis=0, tiled=True)
    projected = jnp.dot(
        flat_tokens,
        weight_rows.reshape(weight_rows.shape[0], 3 * local_cols),
        preferred_element_type=jnp.float32,
    ).astype(jnp.bfloat16)
    blocked = projected.reshape(frames, per_shard, BS, 3, local_cols).transpose(1, 0, 2, 3, 4)
    blocked = blocked.reshape(per_shard, block_len, 3, local_cols)
    queries = blocked[:, :, 0]
    keyvals = blocked[:, :, 1:]
    nearby = with_halo(keyvals, (("rows", 0),), per_shard)
    first_block = shard_idx * per_shard
    owners = block_window - first_block
    members = win_blocks[owners]
    lengths = win_counts[owners]
    positions = (members - first_block + per_shard + block_total) % block_total

    def attend(query_rows, picked, live_mask):
        key_count = picked.shape[0]
        key_blocks = nearby[picked]
        key_part = key_blocks[:, :, 0].reshape(key_count * block_len, heads_here, HD)
        value_part = key_blocks[:, :, 1].reshape(key_count * block_len, heads_here, HD)
        scores = (
            jnp.einsum(
                "qhd,khd->hqk",
                query_rows.reshape(block_len, heads_here, HD),
                key_part,
                preferred_element_type=jnp.float32,
            )
            * score_scale
        )
        scores = jnp.where(live_mask[None, None, :], scores, -jnp.inf)
        row_max = jnp.max(scores, axis=-1, keepdims=True)
        raised = jnp.exp(scores - row_max)
        weights = (raised / jnp.sum(raised, axis=-1, keepdims=True)).astype(jnp.bfloat16)
        blended = jnp.einsum(
            "hqk,khd->qhd", weights, value_part, preferred_element_type=jnp.float32
        )
        return blended.reshape(block_len, local_cols).astype(jnp.bfloat16)

    def one_block(block_item):
        query_rows, picked, length = block_item
        live_mask = jnp.repeat(jnp.arange(MAXB) < length, block_len)
        return attend(query_rows, picked, live_mask)

    attended = lax.map(one_block, (queries, positions, lengths))
    ordered = attended.reshape(per_shard, frames, BS, local_cols).transpose(1, 0, 2, 3)
    ordered = ordered.reshape(frames * tok_frame, local_cols)
    w_full = lax.all_gather(w_out, "rows", axis=1, tiled=True)
    group_count = lax.axis_size(("frames", "heads"))
    out_rows = frames * tok_frame // group_count
    summed = lax.psum_scatter(
        jnp.dot(ordered, w_full, preferred_element_type=jnp.float32).astype(jnp.bfloat16),
        ("frames", "heads"),
        scatter_dimension=0,
        tiled=True,
    )
    return summed.reshape(1, out_rows, model_width)


def swap(value, axis, step=1):
    peers = lax.axis_size(axis)
    return lax.ppermute(value, axis, [(i, i ^ step) for i in range(peers)])


def after(value, *others):
    return lax.optimization_barrier((value, *others))[0]


def call(kernel, out_shape, prefetch, operands, scratch=(), flops=0, read=0, limit=VMEM_BYTES):
    return pl.pallas_call(
        kernel,
        out_shape=out_shape,
        grid_spec=pltpu.PrefetchScalarGridSpec(
            num_scalar_prefetch=len(prefetch),
            grid=(),
            in_specs=[pl.BlockSpec(memory_space=pltpu.VMEM)] * len(operands),
            out_specs=jax.tree.map(lambda _: pl.BlockSpec(memory_space=pltpu.VMEM), out_shape),
            scratch_shapes=scratch,
        ),
        compiler_params=pltpu.CompilerParams(vmem_limit_bytes=limit),
        cost_estimate=pl.CostEstimate(flops=flops, bytes_accessed=read, transcendentals=0),
    )(*prefetch, *operands)


def project(place, mine, theirs, chunks, first, cols):
    rows, (count, width) = len(mine), theirs[0].shape
    half = chunks[0][0].shape[1]
    slices = len(chunks)
    flat = [w for of_round in chunks for w in of_round]
    fetched = 2 * rows + len(flat)

    def kernel(place_ref, *refs):
        row, group, frame, core = (place_ref[i] for i in range(4))
        w_refs = refs[2 * rows : fetched]
        q_keep, kv_keep, send, x_all, w_all, total, sems = refs[fetched:]
        copies = []
        for k in range(slices):
            for g in range(2):
                at = pl.multiple_of((row + slices - k) % slices * (2 * half) + (group + g) % 2 * half, half)
                for part in range(3):
                    source = w_refs[2 * k + g].at[part, :, first : first + cols]
                    into = w_all.at[pl.ds(at, half), part * cols : (part + 1) * cols]
                    copies.append(pltpu.make_async_copy(source, into, sems.at[len(copies)]))
        for i in range(2 * rows):
            to = x_all.at[row ^ (i % rows), (frame + i // rows) % 2]
            copies.append(pltpu.make_async_copy(refs[i].at[pl.ds(0, count)], to, sems.at[len(copies)]))
        for copy in copies:
            copy.start()
        for copy in copies:
            copy.wait()
        acc = jnp.dot(x_all[...].reshape(-1, width), w_all[...], preferred_element_type=jnp.float32)
        kv_part = acc[:, cols:].reshape(rows, 2 * count, 2 * cols)
        kv_keep[...] = kv_part
        send[:, : 2 * count, :] = kv_part.astype(jnp.bfloat16)
        total[...] = acc[:, :cols].reshape(rows, 2, count, cols)
        own = pl.multiple_of(core * BS, BS)
        other = pl.multiple_of((1 - core) * BS, BS)
        q_keep[...] = total[:, :, pl.ds(own, BS), :].reshape(q_keep.shape)
        for f in range(2):
            at = slice(f * cols, (f + 1) * cols)
            send[:, 2 * count :, at] = total[:, f, pl.ds(other, BS), :].astype(jnp.bfloat16)

    vmem, hbm = pl.BlockSpec(memory_space=pltpu.VMEM), pl.BlockSpec(memory_space=pltpu.HBM)
    flops = 2 * rows * 2 * count * width * 3 * cols
    return pl.pallas_call(
        kernel,
        out_shape=(
            jax.ShapeDtypeStruct((rows, 2 * BS, cols), jnp.float32),
            jax.ShapeDtypeStruct((rows, 2 * count, 2 * cols), jnp.float32),
            jax.ShapeDtypeStruct((rows, 2 * count + BS, 2 * cols), jnp.bfloat16),
        ),
        grid_spec=pltpu.PrefetchScalarGridSpec(
            num_scalar_prefetch=1,
            grid=(),
            in_specs=[hbm] * fetched,
            out_specs=(vmem, vmem, vmem),
            scratch_shapes=[
                pltpu.VMEM((rows, 2, count, width), jnp.bfloat16),
                pltpu.VMEM((width, 3 * cols), jnp.bfloat16),
                pltpu.VMEM((rows, 2, count, cols), jnp.float32),
                pltpu.SemaphoreType.DMA((2 * rows + 3 * len(flat),)),
            ],
        ),
        compiler_params=pltpu.CompilerParams(vmem_limit_bytes=VMEM_BYTES),
        cost_estimate=pl.CostEstimate(flops=8 * flops, bytes_accessed=flops // 300, transcendentals=0),
    )(place, *mine, *theirs, *flat)


def attend_all(place, members, counts, queries, keyvals, more, earlier=()):
    blocks, block_len, cols = queries.shape
    first = earlier[0].shape[2] if earlier else 0
    rows = keyvals.shape[1]
    per_row = rows // block_len

    def kernel(place_ref, members_ref, counts_ref, q_ref, kv_ref, more_ref, *refs):
        same_ref, diff_ref, q_sum, kv_sum, out = refs[len(earlier) :]
        for r in range(blocks):
            added = more_ref[r, rows:, :].astype(jnp.float32)
            added = jnp.concatenate([added[:, :cols], added[:, cols:]], axis=0)
            q_sum[r] = (q_ref[r] + added).astype(jnp.bfloat16)
            both = (kv_ref[r] + more_ref[r, :rows, :].astype(jnp.float32)).astype(jnp.bfloat16)
            both = both.reshape(2, rows // 2, 2 * cols)
            for j in range(per_row):
                part = both[:, j * BS : (j + 1) * BS, :]
                kv_sum[r * per_row + j] = part.reshape(block_len, 2 * cols)
        column = lax.broadcasted_iota(jnp.int32, (block_len, MAXB * block_len), 1)
        for b in range(blocks):
            live = column < counts_ref[b] * block_len
            listed = [kv_sum.at[members_ref[b * MAXB + j]] for j in range(MAXB)]
            for h in range(cols // HD):
                at = slice(h * HD, (h + 1) * HD)
                at_v = slice(cols + h * HD, cols + (h + 1) * HD)
                keys = jnp.concatenate([block[:, at] for block in listed], axis=0)
                values = jnp.concatenate([block[:, at_v] for block in listed], axis=0)
                scores = lax.dot_general(
                    q_sum[b, :, at], keys, (((1,), (1,)), ((), ())), preferred_element_type=jnp.float32
                )
                scores = jnp.where(live, scores, -jnp.inf)
                raised = jnp.exp2((scores - jnp.max(scores, axis=-1, keepdims=True)) * EXP2_SCALE)
                weights = raised * (1.0 / jnp.sum(raised, axis=-1, keepdims=True))
                blended = jnp.dot(
                    weights.astype(jnp.bfloat16), values, preferred_element_type=jnp.float32
                )
                out[(b + place_ref[0]) % 2, b // 2, :, at] = blended.astype(jnp.bfloat16)
        for i, out_ref in enumerate((same_ref, diff_ref)):
            if earlier:
                out_ref[:, :, :first] = refs[i][...]
            out_ref[:, :, first:] = out[i]

    half = jax.ShapeDtypeStruct((blocks // 2, block_len, first + cols), jnp.bfloat16)
    return call(
        kernel,
        (half, half),
        [place, members, counts],
        [queries, keyvals, more, *earlier],
        scratch=[
            pltpu.VMEM((blocks, block_len, cols), jnp.bfloat16),
            pltpu.VMEM((blocks * per_row, block_len, 2 * cols), jnp.bfloat16),
            pltpu.VMEM((2, blocks // 2, block_len, cols), jnp.bfloat16),
        ],
        flops=4 * blocks * block_len * MAXB * block_len * cols,
        read=16 * blocks * block_len * cols,
    )


def mix(place, attended, w_own, w_across, beside, beside_across):
    blocks, block_len, cols = attended[0].shape
    width = w_own.shape[1]

    def kernel(place_ref, *refs):
        row, group, frame, core = (place_ref[i] for i in range(4))
        w_refs = refs[4:10]
        near_keep, near_send, far_keep, far_send, a_all, sums = refs[10:]
        for s in range(4):
            a_all[s] = refs[s][...].reshape(blocks * block_len, cols)

        def term(c, other):
            side = 1 - core if other else core
            acc = None
            for i in range(2):
                if c == 0:
                    weight, half = w_refs[other][i * cols : (i + 1) * cols, :], i
                else:
                    weight, half = w_refs[2 + 2 * other + i][...], (i + group) % 2
                part = jnp.dot(a_all[(2 * side + half) ^ row], weight, preferred_element_type=jnp.float32)
                acc = part if acc is None else acc + part
            return acc.astype(jnp.bfloat16).astype(jnp.float32)

        for c in range(2):
            sums[...] = (term(c, 0) + term(c, 1)).reshape(blocks, 2, BS, width)
            at = (row + c) % 2
            near_keep[at] = sums[row // 2, frame]
            near_send[at] = sums[row // 2, 1 - frame].astype(jnp.bfloat16)
            far_keep[at] = sums[1 - row // 2, frame]
            far_send[at] = sums[1 - row // 2, 1 - frame].astype(jnp.bfloat16)

    kept = jax.ShapeDtypeStruct((2, BS, width), jnp.float32)
    sent = jax.ShapeDtypeStruct((2, BS, width), jnp.bfloat16)
    return call(
        kernel,
        (kept, sent, kept, sent),
        [place],
        [*attended, w_own, w_across, *beside, *beside_across],
        scratch=[
            pltpu.VMEM((4, blocks * block_len, cols), jnp.bfloat16),
            pltpu.VMEM((blocks, 2, BS, width), jnp.float32),
        ],
        flops=2 * blocks * block_len * 4 * cols * 2 * width,
        read=16 * cols * width,
    )


def finish(place, near_keep, near_more, far):
    halves, rows, width = near_keep.shape

    def kernel(place_ref, keep_ref, more_ref, far_ref, out_ref):
        pair = place_ref[0] // 2
        for c in range(halves):
            here = pl.multiple_of((pair * halves + c) * width, width)
            there = pl.multiple_of(((1 - pair) * halves + c) * width, width)
            out_ref[:, pl.ds(here, width)] = (keep_ref[c] + more_ref[c].astype(jnp.float32)).astype(jnp.bfloat16)
            out_ref[:, pl.ds(there, width)] = far_ref[c]

    return call(
        kernel,
        jax.ShapeDtypeStruct((rows, 2 * halves * width), jnp.bfloat16),
        [place],
        [near_keep, near_more, far],
        read=12 * rows * halves * width,
    )


def by_heads(latents, w_qkv, w_out, win_blocks, win_counts, block_window):
    rows_n, heads_n = lax.axis_size("rows"), lax.axis_size("heads")
    group, row = lax.axis_index("groups"), lax.axis_index("rows")
    frame, core = lax.axis_index("frames"), lax.axis_index("heads")
    count = latents.shape[1]
    depth, _, local_cols = w_qkv.shape
    span = rows_n // heads_n
    cols = local_cols // span
    half = depth // 2
    place = jnp.stack([row, group, frame, core]).astype(jnp.int32)

    def reshard(k, *others):
        value = lax.dynamic_slice(
            w_qkv.transpose(1, 0, 2), (0, group * half, (k + row) % span * cols), (3, half, cols)
        )
        pairs = [
            (r * heads_n + h, (h * span + (k + r) % span) * heads_n + r // span)
            for r in range(rows_n)
            for h in range(heads_n)
        ]
        return lax.ppermute(after(value, *others) if others else value, ("rows", "heads"), pairs)

    mine = lax.dynamic_slice_in_dim(latents[0], core * span * depth, span * depth, axis=1)
    mine_x = swap(mine, "frames")
    here, there = [reshard(0)], []
    tables = jnp.concatenate([win_blocks, win_counts[:, None], block_window[:, None]], axis=1)
    tables = jnp.pad(tables, ((0, 8 - heads_n), (0, span * depth - MAXB - 2))).astype(mine.dtype)
    joined = jnp.concatenate([mine, tables], axis=0)
    near = swap(joined, "rows")
    near_x = swap(near, "frames")
    across = swap(after(w_out, near), "heads")
    there.append(swap(here[0], "groups"))
    here.append(reshard(1, near))
    far_2 = swap(after(joined, here[0], mine_x), "rows", 2)
    out_half = lax.dynamic_slice_in_dim(w_out, group * cols, cols, axis=0)
    beside = [swap(after(out_half, near), "rows")]
    beside.append(swap(beside[0], "groups"))
    there.append(swap(after(here[1], there[0], beside[1]), "groups"))
    far_2x = swap(far_2, "frames")
    far_3 = swap(after(joined, far_2, across, near_x, beside[0]), "rows", 3)
    far_3x = swap(far_3, "frames")

    found = jnp.stack([x[count : count + heads_n, : MAXB + 2] for x in (joined, near, far_2, far_3)])
    tables = found.astype(jnp.int32)[row ^ jnp.arange(rows_n)].reshape(rows_n * heads_n, MAXB + 2)
    windows = lax.dynamic_index_in_dim(
        tables[:, MAXB + 1].reshape(rows_n, heads_n), core, axis=1, keepdims=False
    )
    picked = tables[windows]
    members, counts = picked[:, :MAXB].reshape(-1), picked[:, MAXB]

    pieces = [joined, near, far_2, far_3], [mine_x, near_x, far_2x, far_3x]
    chunks = [(here[0], there[0]), (here[1], after(there[1], members, counts))]
    last = cols // (3 * HD) * HD
    first = project(place, *pieces, chunks, 0, cols - last)
    first_more = swap(first[2], "heads")
    chunks[1] = (here[1], after(there[1], first[2]))
    second = project(place, *pieces, chunks, cols - last, last)
    second_more = swap(second[2], "heads")
    attended = attend_all(place, members, counts, *first[:2], first_more)
    beside_across = [swap(part, "heads") for part in beside]
    same, diff = attend_all(place, members, counts, *second[:2], second_more, attended)
    attended = [same] + [swap(same if s % 2 == 0 else diff, "rows", s) for s in range(1, rows_n)]
    near_keep, near_send, far_keep, far_send = mix(place, attended, w_out, across, beside, beside_across)
    far_more = swap(far_send, "frames")
    far = swap((far_keep + far_more.astype(jnp.float32)).astype(jnp.bfloat16), "rows", 2)
    near_more = swap(after(near_send, far_more), "frames")
    return finish(place, near_keep, near_more, far)[None]


def local(latents, w_qkv, w_out, win_blocks, win_counts, block_window):
    rows_n = lax.axis_size("rows")
    pairs = all(lax.axis_size(axis) == 2 for axis in ("groups", "frames", "heads"))
    heads_here = w_qkv.shape[2] // HD
    if pairs and rows_n == 4 and heads_here == 6 and latents.shape[:2] == (1, 2 * BS):
        plan = by_heads
    else:
        plan = by_tokens
    return plan(latents, w_qkv, w_out, win_blocks, win_counts, block_window)


def solution(mesh):
    in_specs = (
        P(("groups", "frames"), "rows", None),
        P("rows", None, ("frames", "heads")),
        P(("frames", "heads"), "rows"),
        P(("groups", "rows"), None),
        P(("groups", "rows")),
        P(("groups", "rows")),
    )
    out_specs = P(("groups", "frames"), ("rows", "heads"), None)
    return jax.shard_map(local, mesh=mesh, in_specs=in_specs, out_specs=out_specs, check_vma=False)
```

```python
import math

import jax
import jax.numpy as jnp
from jax import lax
from jax.experimental import pallas as pl
from jax.experimental.pallas import tpu as pltpu
from jax.sharding import PartitionSpec as P

HD = 128
BS = 64
MAXB = 4
VMEM_BYTES = 24 * 1024 * 1024
WHOLE_VMEM_BYTES = 56 * 1024 * 1024
EXP2_SCALE = math.log2(math.e) / math.sqrt(HD)


def with_halo(value, sides, width):
    for axis, dim in sides:
        peers, length = (lax.axis_size(axis), value.shape[dim])
        up = [(i, (i + 1) % peers) for i in range(peers)]
        down = [(j, i) for i, j in up]
        last = lax.slice_in_dim(value, length - width, length, axis=dim)
        first = lax.slice_in_dim(value, 0, width, axis=dim)
        before = lax.ppermute(last, axis, up)
        after = lax.ppermute(first, axis, down)
        value = jnp.concatenate([before, value, after], axis=dim)
    return value


def by_tokens(latents, w_qkv, w_out, win_blocks, win_counts, block_window):
    rows_n = lax.axis_size("rows")
    shard_idx = lax.axis_index("rows")
    frames = latents.shape[0] * lax.axis_size("frames")
    tok_frame = latents.shape[1]
    model_width = latents.shape[2]
    local_cols = w_qkv.shape[2]
    per_shard = tok_frame // BS
    block_total = per_shard * rows_n
    heads_here = local_cols // HD
    block_len = frames * BS
    score_scale = 1.0 / math.sqrt(HD)
    gathered = lax.all_gather(latents, "frames", axis=0, tiled=True)
    flat_tokens = gathered.reshape(frames * tok_frame, model_width)
    weight_rows = lax.all_gather(w_qkv, "rows", axis=0, tiled=True)
    projected = jnp.dot(
        flat_tokens,
        weight_rows.reshape(weight_rows.shape[0], 3 * local_cols),
        preferred_element_type=jnp.float32,
    ).astype(jnp.bfloat16)
    blocked = projected.reshape(frames, per_shard, BS, 3, local_cols).transpose(1, 0, 2, 3, 4)
    blocked = blocked.reshape(per_shard, block_len, 3, local_cols)
    queries = blocked[:, :, 0]
    keyvals = blocked[:, :, 1:]
    nearby = with_halo(keyvals, (("rows", 0),), per_shard)
    first_block = shard_idx * per_shard
    owners = block_window - first_block
    members = win_blocks[owners]
    lengths = win_counts[owners]
    positions = (members - first_block + per_shard + block_total) % block_total

    def attend(query_rows, picked, live_mask):
        key_count = picked.shape[0]
        key_blocks = nearby[picked]
        key_part = key_blocks[:, :, 0].reshape(key_count * block_len, heads_here, HD)
        value_part = key_blocks[:, :, 1].reshape(key_count * block_len, heads_here, HD)
        scores = (
            jnp.einsum(
                "qhd,khd->hqk",
                query_rows.reshape(block_len, heads_here, HD),
                key_part,
                preferred_element_type=jnp.float32,
            )
            * score_scale
        )
        scores = jnp.where(live_mask[None, None, :], scores, -jnp.inf)
        row_max = jnp.max(scores, axis=-1, keepdims=True)
        raised = jnp.exp(scores - row_max)
        weights = (raised / jnp.sum(raised, axis=-1, keepdims=True)).astype(jnp.bfloat16)
        blended = jnp.einsum(
            "hqk,khd->qhd", weights, value_part, preferred_element_type=jnp.float32
        )
        return blended.reshape(block_len, local_cols).astype(jnp.bfloat16)

    def one_block(block_item):
        query_rows, picked, length = block_item
        live_mask = jnp.repeat(jnp.arange(MAXB) < length, block_len)
        return attend(query_rows, picked, live_mask)

    attended = lax.map(one_block, (queries, positions, lengths))
    ordered = attended.reshape(per_shard, frames, BS, local_cols).transpose(1, 0, 2, 3)
    ordered = ordered.reshape(frames * tok_frame, local_cols)
    w_full = lax.all_gather(w_out, "rows", axis=1, tiled=True)
    group_count = lax.axis_size(("frames", "heads"))
    out_rows = frames * tok_frame // group_count
    summed = lax.psum_scatter(
        jnp.dot(ordered, w_full, preferred_element_type=jnp.float32).astype(jnp.bfloat16),
        ("frames", "heads"),
        scatter_dimension=0,
        tiled=True,
    )
    return summed.reshape(1, out_rows, model_width)


def swap(value, axis, step=1):
    peers = lax.axis_size(axis)
    return lax.ppermute(value, axis, [(i, i ^ step) for i in range(peers)])


def after(value, *others):
    return lax.optimization_barrier((value, *others))[0]


def call(kernel, out_shape, prefetch, operands, scratch=(), flops=0, read=0, limit=VMEM_BYTES):
    return pl.pallas_call(
        kernel,
        out_shape=out_shape,
        grid_spec=pltpu.PrefetchScalarGridSpec(
            num_scalar_prefetch=len(prefetch),
            grid=(),
            in_specs=[pl.BlockSpec(memory_space=pltpu.VMEM)] * len(operands),
            out_specs=jax.tree.map(lambda _: pl.BlockSpec(memory_space=pltpu.VMEM), out_shape),
            scratch_shapes=scratch,
        ),
        compiler_params=pltpu.CompilerParams(vmem_limit_bytes=limit),
        cost_estimate=pl.CostEstimate(flops=flops, bytes_accessed=read, transcendentals=0),
    )(*prefetch, *operands)


def project(place, mine, theirs, chunks, first, cols):
    rows, (count, width) = len(mine), theirs[0].shape
    half = chunks[0][0].shape[1]
    slices = len(chunks)
    flat = [w for of_round in chunks for w in of_round]
    fetched = 2 * rows + len(flat)

    def kernel(place_ref, *refs):
        row, group, frame, core = (place_ref[i] for i in range(4))
        w_refs = refs[2 * rows : fetched]
        q_keep, kv_keep, send, x_all, w_all, total, sems = refs[fetched:]
        copies = []
        for k in range(slices):
            for g in range(2):
                at = pl.multiple_of((row + slices - k) % slices * (2 * half) + (group + g) % 2 * half, half)
                for part in range(3):
                    source = w_refs[2 * k + g].at[part, :, first : first + cols]
                    into = w_all.at[pl.ds(at, half), part * cols : (part + 1) * cols]
                    copies.append(pltpu.make_async_copy(source, into, sems.at[len(copies)]))
        for i in range(2 * rows):
            to = x_all.at[row ^ (i % rows), (frame + i // rows) % 2]
            copies.append(pltpu.make_async_copy(refs[i].at[pl.ds(0, count)], to, sems.at[len(copies)]))
        for copy in copies:
            copy.start()
        for copy in copies:
            copy.wait()
        acc = jnp.dot(x_all[...].reshape(-1, width), w_all[...], preferred_element_type=jnp.float32)
        kv_part = acc[:, cols:].reshape(rows, 2 * count, 2 * cols)
        kv_keep[...] = kv_part
        send[:, : 2 * count, :] = kv_part.astype(jnp.bfloat16)
        total[...] = acc[:, :cols].reshape(rows, 2, count, cols)
        own = pl.multiple_of(core * BS, BS)
        other = pl.multiple_of((1 - core) * BS, BS)
        q_keep[...] = total[:, :, pl.ds(own, BS), :].reshape(q_keep.shape)
        for f in range(2):
            at = slice(f * cols, (f + 1) * cols)
            send[:, 2 * count :, at] = total[:, f, pl.ds(other, BS), :].astype(jnp.bfloat16)

    vmem, hbm = pl.BlockSpec(memory_space=pltpu.VMEM), pl.BlockSpec(memory_space=pltpu.HBM)
    flops = 2 * rows * 2 * count * width * 3 * cols
    return pl.pallas_call(
        kernel,
        out_shape=(
            jax.ShapeDtypeStruct((rows, 2 * BS, cols), jnp.float32),
            jax.ShapeDtypeStruct((rows, 2 * count, 2 * cols), jnp.float32),
            jax.ShapeDtypeStruct((rows, 2 * count + BS, 2 * cols), jnp.bfloat16),
        ),
        grid_spec=pltpu.PrefetchScalarGridSpec(
            num_scalar_prefetch=1,
            grid=(),
            in_specs=[hbm] * fetched,
            out_specs=(vmem, vmem, vmem),
            scratch_shapes=[
                pltpu.VMEM((rows, 2, count, width), jnp.bfloat16),
                pltpu.VMEM((width, 3 * cols), jnp.bfloat16),
                pltpu.VMEM((rows, 2, count, cols), jnp.float32),
                pltpu.SemaphoreType.DMA((2 * rows + 3 * len(flat),)),
            ],
        ),
        compiler_params=pltpu.CompilerParams(vmem_limit_bytes=VMEM_BYTES),
        cost_estimate=pl.CostEstimate(flops=8 * flops, bytes_accessed=flops // 300, transcendentals=0),
    )(place, *mine, *theirs, *flat)


def attend_all(place, members, counts, queries, keyvals, more, earlier=()):
    blocks, block_len, cols = queries.shape
    first = earlier[0].shape[2] if earlier else 0
    rows = keyvals.shape[1]
    per_row = rows // block_len

    def kernel(place_ref, members_ref, counts_ref, q_ref, kv_ref, more_ref, *refs):
        same_ref, diff_ref, q_sum, kv_sum, out = refs[len(earlier) :]
        for r in range(blocks):
            added = more_ref[r, rows:, :].astype(jnp.float32)
            added = jnp.concatenate([added[:, :cols], added[:, cols:]], axis=0)
            q_sum[r] = (q_ref[r] + added).astype(jnp.bfloat16)
            both = (kv_ref[r] + more_ref[r, :rows, :].astype(jnp.float32)).astype(jnp.bfloat16)
            both = both.reshape(2, rows // 2, 2 * cols)
            for j in range(per_row):
                part = both[:, j * BS : (j + 1) * BS, :]
                kv_sum[r * per_row + j] = part.reshape(block_len, 2 * cols)
        column = lax.broadcasted_iota(jnp.int32, (block_len, MAXB * block_len), 1)
        for b in range(blocks):
            live = column < counts_ref[b] * block_len
            listed = [kv_sum.at[members_ref[b * MAXB + j]] for j in range(MAXB)]
            for h in range(cols // HD):
                at = slice(h * HD, (h + 1) * HD)
                at_v = slice(cols + h * HD, cols + (h + 1) * HD)
                keys = jnp.concatenate([block[:, at] for block in listed], axis=0)
                values = jnp.concatenate([block[:, at_v] for block in listed], axis=0)
                scores = lax.dot_general(
                    q_sum[b, :, at], keys, (((1,), (1,)), ((), ())), preferred_element_type=jnp.float32
                )
                scores = jnp.where(live, scores, -jnp.inf)
                raised = jnp.exp2((scores - jnp.max(scores, axis=-1, keepdims=True)) * EXP2_SCALE)
                weights = raised * (1.0 / jnp.sum(raised, axis=-1, keepdims=True))
                blended = jnp.dot(
                    weights.astype(jnp.bfloat16), values, preferred_element_type=jnp.float32
                )
                out[(b + place_ref[0]) % 2, b // 2, :, at] = blended.astype(jnp.bfloat16)
        for i, out_ref in enumerate((same_ref, diff_ref)):
            if earlier:
                out_ref[:, :, :first] = refs[i][...]
            out_ref[:, :, first:] = out[i]

    half = jax.ShapeDtypeStruct((blocks // 2, block_len, first + cols), jnp.bfloat16)
    return call(
        kernel,
        (half, half),
        [place, members, counts],
        [queries, keyvals, more, *earlier],
        scratch=[
            pltpu.VMEM((blocks, block_len, cols), jnp.bfloat16),
            pltpu.VMEM((blocks * per_row, block_len, 2 * cols), jnp.bfloat16),
            pltpu.VMEM((2, blocks // 2, block_len, cols), jnp.bfloat16),
        ],
        flops=4 * blocks * block_len * MAXB * block_len * cols,
        read=16 * blocks * block_len * cols,
    )


def mix(place, attended, w_own, w_across, beside, beside_across):
    blocks, block_len, cols = attended[0].shape
    width = w_own.shape[1]

    def kernel(place_ref, *refs):
        row, group, frame, core = (place_ref[i] for i in range(4))
        w_refs = refs[4:10]
        near_keep, near_send, far_keep, far_send, a_all, sums = refs[10:]
        for s in range(4):
            a_all[s] = refs[s][...].reshape(blocks * block_len, cols)

        def term(c, other):
            side = 1 - core if other else core
            acc = None
            for i in range(2):
                if c == 0:
                    weight, half = w_refs[other][i * cols : (i + 1) * cols, :], i
                else:
                    weight, half = w_refs[2 + 2 * other + i][...], (i + group) % 2
                part = jnp.dot(a_all[(2 * side + half) ^ row], weight, preferred_element_type=jnp.float32)
                acc = part if acc is None else acc + part
            return acc.astype(jnp.bfloat16).astype(jnp.float32)

        for c in range(2):
            sums[...] = (term(c, 0) + term(c, 1)).reshape(blocks, 2, BS, width)
            at = (row + c) % 2
            near_keep[at] = sums[row // 2, frame]
            near_send[at] = sums[row // 2, 1 - frame].astype(jnp.bfloat16)
            far_keep[at] = sums[1 - row // 2, frame]
            far_send[at] = sums[1 - row // 2, 1 - frame].astype(jnp.bfloat16)

    kept = jax.ShapeDtypeStruct((2, BS, width), jnp.float32)
    sent = jax.ShapeDtypeStruct((2, BS, width), jnp.bfloat16)
    return call(
        kernel,
        (kept, sent, kept, sent),
        [place],
        [*attended, w_own, w_across, *beside, *beside_across],
        scratch=[
            pltpu.VMEM((4, blocks * block_len, cols), jnp.bfloat16),
            pltpu.VMEM((blocks, 2, BS, width), jnp.float32),
        ],
        flops=2 * blocks * block_len * 4 * cols * 2 * width,
        read=16 * cols * width,
    )


def finish(place, near_keep, near_more, far):
    halves, rows, width = near_keep.shape

    def kernel(place_ref, keep_ref, more_ref, far_ref, out_ref):
        pair = place_ref[0] // 2
        for c in range(halves):
            here = pl.multiple_of((pair * halves + c) * width, width)
            there = pl.multiple_of(((1 - pair) * halves + c) * width, width)
            out_ref[:, pl.ds(here, width)] = (keep_ref[c] + more_ref[c].astype(jnp.float32)).astype(jnp.bfloat16)
            out_ref[:, pl.ds(there, width)] = far_ref[c]

    return call(
        kernel,
        jax.ShapeDtypeStruct((rows, 2 * halves * width), jnp.bfloat16),
        [place],
        [near_keep, near_more, far],
        read=12 * rows * halves * width,
    )


def by_heads(latents, w_qkv, w_out, win_blocks, win_counts, block_window):
    rows_n, heads_n = lax.axis_size("rows"), lax.axis_size("heads")
    group, row = lax.axis_index("groups"), lax.axis_index("rows")
    frame, core = lax.axis_index("frames"), lax.axis_index("heads")
    count = latents.shape[1]
    depth, _, local_cols = w_qkv.shape
    span = rows_n // heads_n
    cols = local_cols // span
    half = depth // 2
    place = jnp.stack([row, group, frame, core]).astype(jnp.int32)

    def reshard(k, *others):
        value = lax.dynamic_slice(
            w_qkv.transpose(1, 0, 2), (0, group * half, (k + row) % span * cols), (3, half, cols)
        )
        pairs = [
            (r * heads_n + h, (h * span + (k + r) % span) * heads_n + r // span)
            for r in range(rows_n)
            for h in range(heads_n)
        ]
        return lax.ppermute(after(value, *others) if others else value, ("rows", "heads"), pairs)

    mine = lax.dynamic_slice_in_dim(latents[0], core * span * depth, span * depth, axis=1)
    here, there = [reshard(0)], []
    tables = jnp.concatenate([win_blocks, win_counts[:, None], block_window[:, None]], axis=1)
    tables = jnp.pad(tables, ((0, 8 - heads_n), (0, span * depth - MAXB - 2))).astype(mine.dtype)
    joined = jnp.concatenate([mine, tables], axis=0)
    near = swap(joined, "rows")
    near_x = swap(near, "frames")
    mine_x = swap(mine, "frames")
    across = swap(after(w_out, near), "heads")
    there.append(swap(here[0], "groups"))
    here.append(reshard(1, near))
    far_2 = swap(after(joined, here[0]), "rows", 2)
    out_half = lax.dynamic_slice_in_dim(w_out, group * cols, cols, axis=0)
    beside = [swap(after(out_half, near), "rows")]
    beside.append(swap(beside[0], "groups"))
    there.append(swap(after(here[1], there[0], beside[1]), "groups"))
    far_2x = swap(far_2, "frames")
    far_3 = swap(after(joined, far_2, across, near_x, beside[0]), "rows", 3)
    far_3x = swap(far_3, "frames")

    found = jnp.stack([x[count : count + heads_n, : MAXB + 2] for x in (joined, near, far_2, far_3)])
    tables = found.astype(jnp.int32)[row ^ jnp.arange(rows_n)].reshape(rows_n * heads_n, MAXB + 2)
    windows = lax.dynamic_index_in_dim(
        tables[:, MAXB + 1].reshape(rows_n, heads_n), core, axis=1, keepdims=False
    )
    picked = tables[windows]
    members, counts = picked[:, :MAXB].reshape(-1), picked[:, MAXB]

    pieces = [joined, near, far_2, far_3], [mine_x, near_x, far_2x, far_3x]
    chunks = [(here[0], there[0]), (here[1], after(there[1], members, counts))]
    last = cols // (3 * HD) * HD
    first = project(place, *pieces, chunks, 0, cols - last)
    first_more = swap(first[2], "heads")
    chunks[1] = (here[1], after(there[1], first[2]))
    second = project(place, *pieces, chunks, cols - last, last)
    second_more = swap(second[2], "heads")
    attended = attend_all(place, members, counts, *first[:2], first_more)
    beside_across = [swap(part, "heads") for part in beside]
    same, diff = attend_all(place, members, counts, *second[:2], second_more, attended)
    attended = [same] + [swap(same if s % 2 == 0 else diff, "rows", s) for s in range(1, rows_n)]
    near_keep, near_send, far_keep, far_send = mix(place, attended, w_out, across, beside, beside_across)
    far_more = swap(far_send, "frames")
    far = swap((far_keep + far_more.astype(jnp.float32)).astype(jnp.bfloat16), "rows", 2)
    near_more = swap(after(near_send, far_more), "frames")
    return finish(place, near_keep, near_more, far)[None]


def local(latents, w_qkv, w_out, win_blocks, win_counts, block_window):
    rows_n = lax.axis_size("rows")
    pairs = all(lax.axis_size(axis) == 2 for axis in ("groups", "frames", "heads"))
    heads_here = w_qkv.shape[2] // HD
    if pairs and rows_n == 4 and heads_here == 6 and latents.shape[:2] == (1, 2 * BS):
        plan = by_heads
    else:
        plan = by_tokens
    return plan(latents, w_qkv, w_out, win_blocks, win_counts, block_window)


def solution(mesh):
    in_specs = (
        P(("groups", "frames"), "rows", None),
        P("rows", None, ("frames", "heads")),
        P(("frames", "heads"), "rows"),
        P(("groups", "rows"), None),
        P(("groups", "rows")),
        P(("groups", "rows")),
    )
    out_specs = P(("groups", "frames"), ("rows", "heads"), None)
    return jax.shard_map(local, mesh=mesh, in_specs=in_specs, out_specs=out_specs, check_vma=False)
```

```python
import math

import jax
import jax.numpy as jnp
from jax import lax
from jax.experimental import pallas as pl
from jax.experimental.pallas import tpu as pltpu
from jax.sharding import PartitionSpec as P

HD = 128
BS = 64
MAXB = 4
VMEM_BYTES = 24 * 1024 * 1024
WHOLE_VMEM_BYTES = 56 * 1024 * 1024
EXP2_SCALE = math.log2(math.e) / math.sqrt(HD)


def with_halo(value, sides, width):
    for axis, dim in sides:
        peers, length = (lax.axis_size(axis), value.shape[dim])
        up = [(i, (i + 1) % peers) for i in range(peers)]
        down = [(j, i) for i, j in up]
        last = lax.slice_in_dim(value, length - width, length, axis=dim)
        first = lax.slice_in_dim(value, 0, width, axis=dim)
        before = lax.ppermute(last, axis, up)
        after = lax.ppermute(first, axis, down)
        value = jnp.concatenate([before, value, after], axis=dim)
    return value


def by_tokens(latents, w_qkv, w_out, win_blocks, win_counts, block_window):
    rows_n = lax.axis_size("rows")
    shard_idx = lax.axis_index("rows")
    frames = latents.shape[0] * lax.axis_size("frames")
    tok_frame = latents.shape[1]
    model_width = latents.shape[2]
    local_cols = w_qkv.shape[2]
    per_shard = tok_frame // BS
    block_total = per_shard * rows_n
    heads_here = local_cols // HD
    block_len = frames * BS
    score_scale = 1.0 / math.sqrt(HD)
    gathered = lax.all_gather(latents, "frames", axis=0, tiled=True)
    flat_tokens = gathered.reshape(frames * tok_frame, model_width)
    weight_rows = lax.all_gather(w_qkv, "rows", axis=0, tiled=True)
    projected = jnp.dot(
        flat_tokens,
        weight_rows.reshape(weight_rows.shape[0], 3 * local_cols),
        preferred_element_type=jnp.float32,
    ).astype(jnp.bfloat16)
    blocked = projected.reshape(frames, per_shard, BS, 3, local_cols).transpose(1, 0, 2, 3, 4)
    blocked = blocked.reshape(per_shard, block_len, 3, local_cols)
    queries = blocked[:, :, 0]
    keyvals = blocked[:, :, 1:]
    nearby = with_halo(keyvals, (("rows", 0),), per_shard)
    first_block = shard_idx * per_shard
    owners = block_window - first_block
    members = win_blocks[owners]
    lengths = win_counts[owners]
    positions = (members - first_block + per_shard + block_total) % block_total

    def attend(query_rows, picked, live_mask):
        key_count = picked.shape[0]
        key_blocks = nearby[picked]
        key_part = key_blocks[:, :, 0].reshape(key_count * block_len, heads_here, HD)
        value_part = key_blocks[:, :, 1].reshape(key_count * block_len, heads_here, HD)
        scores = (
            jnp.einsum(
                "qhd,khd->hqk",
                query_rows.reshape(block_len, heads_here, HD),
                key_part,
                preferred_element_type=jnp.float32,
            )
            * score_scale
        )
        scores = jnp.where(live_mask[None, None, :], scores, -jnp.inf)
        row_max = jnp.max(scores, axis=-1, keepdims=True)
        raised = jnp.exp(scores - row_max)
        weights = (raised / jnp.sum(raised, axis=-1, keepdims=True)).astype(jnp.bfloat16)
        blended = jnp.einsum(
            "hqk,khd->qhd", weights, value_part, preferred_element_type=jnp.float32
        )
        return blended.reshape(block_len, local_cols).astype(jnp.bfloat16)

    def one_block(block_item):
        query_rows, picked, length = block_item
        live_mask = jnp.repeat(jnp.arange(MAXB) < length, block_len)
        return attend(query_rows, picked, live_mask)

    attended = lax.map(one_block, (queries, positions, lengths))
    ordered = attended.reshape(per_shard, frames, BS, local_cols).transpose(1, 0, 2, 3)
    ordered = ordered.reshape(frames * tok_frame, local_cols)
    w_full = lax.all_gather(w_out, "rows", axis=1, tiled=True)
    group_count = lax.axis_size(("frames", "heads"))
    out_rows = frames * tok_frame // group_count
    summed = lax.psum_scatter(
        jnp.dot(ordered, w_full, preferred_element_type=jnp.float32).astype(jnp.bfloat16),
        ("frames", "heads"),
        scatter_dimension=0,
        tiled=True,
    )
    return summed.reshape(1, out_rows, model_width)


def swap(value, axis, step=1):
    peers = lax.axis_size(axis)
    return lax.ppermute(value, axis, [(i, i ^ step) for i in range(peers)])


def after(value, *others):
    return lax.optimization_barrier((value, *others))[0]


def call(kernel, out_shape, prefetch, operands, scratch=(), flops=0, read=0, limit=VMEM_BYTES):
    return pl.pallas_call(
        kernel,
        out_shape=out_shape,
        grid_spec=pltpu.PrefetchScalarGridSpec(
            num_scalar_prefetch=len(prefetch),
            grid=(),
            in_specs=[pl.BlockSpec(memory_space=pltpu.VMEM)] * len(operands),
            out_specs=jax.tree.map(lambda _: pl.BlockSpec(memory_space=pltpu.VMEM), out_shape),
            scratch_shapes=scratch,
        ),
        compiler_params=pltpu.CompilerParams(vmem_limit_bytes=limit),
        cost_estimate=pl.CostEstimate(flops=flops, bytes_accessed=read, transcendentals=0),
    )(*prefetch, *operands)


def project(place, mine, theirs, chunks, first, cols):
    rows, (count, width) = len(mine), theirs[0].shape
    half = chunks[0][0].shape[1]
    slices = len(chunks)
    flat = [w for of_round in chunks for w in of_round]
    fetched = 2 * rows + len(flat)

    def kernel(place_ref, *refs):
        row, group, frame, core = (place_ref[i] for i in range(4))
        w_refs = refs[2 * rows : fetched]
        q_keep, kv_keep, send, x_all, w_all, total, sems = refs[fetched:]
        copies = []
        for k in range(slices):
            for g in range(2):
                at = pl.multiple_of((row + slices - k) % slices * (2 * half) + (group + g) % 2 * half, half)
                for part in range(3):
                    source = w_refs[2 * k + g].at[part, :, first : first + cols]
                    into = w_all.at[pl.ds(at, half), part * cols : (part + 1) * cols]
                    copies.append(pltpu.make_async_copy(source, into, sems.at[len(copies)]))
        for i in range(2 * rows):
            to = x_all.at[row ^ (i % rows), (frame + i // rows) % 2]
            copies.append(pltpu.make_async_copy(refs[i].at[pl.ds(0, count)], to, sems.at[len(copies)]))
        for copy in copies:
            copy.start()
        for copy in copies:
            copy.wait()
        acc = jnp.dot(x_all[...].reshape(-1, width), w_all[...], preferred_element_type=jnp.float32)
        kv_part = acc[:, cols:].reshape(rows, 2 * count, 2 * cols)
        kv_keep[...] = kv_part
        send[:, : 2 * count, :] = kv_part.astype(jnp.bfloat16)
        total[...] = acc[:, :cols].reshape(rows, 2, count, cols)
        own = pl.multiple_of(core * BS, BS)
        other = pl.multiple_of((1 - core) * BS, BS)
        q_keep[...] = total[:, :, pl.ds(own, BS), :].reshape(q_keep.shape)
        for f in range(2):
            at = slice(f * cols, (f + 1) * cols)
            send[:, 2 * count :, at] = total[:, f, pl.ds(other, BS), :].astype(jnp.bfloat16)

    vmem, hbm = pl.BlockSpec(memory_space=pltpu.VMEM), pl.BlockSpec(memory_space=pltpu.HBM)
    flops = 2 * rows * 2 * count * width * 3 * cols
    return pl.pallas_call(
        kernel,
        out_shape=(
            jax.ShapeDtypeStruct((rows, 2 * BS, cols), jnp.float32),
            jax.ShapeDtypeStruct((rows, 2 * count, 2 * cols), jnp.float32),
            jax.ShapeDtypeStruct((rows, 2 * count + BS, 2 * cols), jnp.bfloat16),
        ),
        grid_spec=pltpu.PrefetchScalarGridSpec(
            num_scalar_prefetch=1,
            grid=(),
            in_specs=[hbm] * fetched,
            out_specs=(vmem, vmem, vmem),
            scratch_shapes=[
                pltpu.VMEM((rows, 2, count, width), jnp.bfloat16),
                pltpu.VMEM((width, 3 * cols), jnp.bfloat16),
                pltpu.VMEM((rows, 2, count, cols), jnp.float32),
                pltpu.SemaphoreType.DMA((2 * rows + 3 * len(flat),)),
            ],
        ),
        compiler_params=pltpu.CompilerParams(vmem_limit_bytes=VMEM_BYTES),
        cost_estimate=pl.CostEstimate(flops=8 * flops, bytes_accessed=flops // 300, transcendentals=0),
    )(place, *mine, *theirs, *flat)


def attend_all(place, members, counts, queries, keyvals, more, earlier=()):
    blocks, block_len, cols = queries.shape
    first = earlier[0].shape[2] if earlier else 0
    rows = keyvals.shape[1]
    per_row = rows // block_len

    def kernel(place_ref, members_ref, counts_ref, q_ref, kv_ref, more_ref, *refs):
        same_ref, diff_ref, q_sum, kv_sum, out = refs[len(earlier) :]
        for r in range(blocks):
            added = more_ref[r, rows:, :].astype(jnp.float32)
            added = jnp.concatenate([added[:, :cols], added[:, cols:]], axis=0)
            q_sum[r] = (q_ref[r] + added).astype(jnp.bfloat16)
            both = (kv_ref[r] + more_ref[r, :rows, :].astype(jnp.float32)).astype(jnp.bfloat16)
            both = both.reshape(2, rows // 2, 2 * cols)
            for j in range(per_row):
                part = both[:, j * BS : (j + 1) * BS, :]
                kv_sum[r * per_row + j] = part.reshape(block_len, 2 * cols)
        column = lax.broadcasted_iota(jnp.int32, (block_len, MAXB * block_len), 1)
        for b in range(blocks):
            live = column < counts_ref[b] * block_len
            listed = [kv_sum.at[members_ref[b * MAXB + j]] for j in range(MAXB)]
            for h in range(cols // HD):
                at = slice(h * HD, (h + 1) * HD)
                at_v = slice(cols + h * HD, cols + (h + 1) * HD)
                keys = jnp.concatenate([block[:, at] for block in listed], axis=0)
                values = jnp.concatenate([block[:, at_v] for block in listed], axis=0)
                scores = lax.dot_general(
                    q_sum[b, :, at], keys, (((1,), (1,)), ((), ())), preferred_element_type=jnp.float32
                )
                scores = jnp.where(live, scores, -jnp.inf)
                raised = jnp.exp2((scores - jnp.max(scores, axis=-1, keepdims=True)) * EXP2_SCALE)
                weights = raised * (1.0 / jnp.sum(raised, axis=-1, keepdims=True))
                blended = jnp.dot(
                    weights.astype(jnp.bfloat16), values, preferred_element_type=jnp.float32
                )
                out[(b + place_ref[0]) % 2, b // 2, :, at] = blended.astype(jnp.bfloat16)
        for i, out_ref in enumerate((same_ref, diff_ref)):
            if earlier:
                out_ref[:, :, :first] = refs[i][...]
            out_ref[:, :, first:] = out[i]

    half = jax.ShapeDtypeStruct((blocks // 2, block_len, first + cols), jnp.bfloat16)
    return call(
        kernel,
        (half, half),
        [place, members, counts],
        [queries, keyvals, more, *earlier],
        scratch=[
            pltpu.VMEM((blocks, block_len, cols), jnp.bfloat16),
            pltpu.VMEM((blocks * per_row, block_len, 2 * cols), jnp.bfloat16),
            pltpu.VMEM((2, blocks // 2, block_len, cols), jnp.bfloat16),
        ],
        flops=4 * blocks * block_len * MAXB * block_len * cols,
        read=16 * blocks * block_len * cols,
    )


def mix(place, attended, w_own, w_across, beside, beside_across):
    blocks, block_len, cols = attended[0].shape
    width = w_own.shape[1]

    def kernel(place_ref, *refs):
        row, group, frame, core = (place_ref[i] for i in range(4))
        w_refs = refs[4:10]
        near_keep, near_send, far_keep, far_send, a_all, sums = refs[10:]
        for s in range(4):
            a_all[s] = refs[s][...].reshape(blocks * block_len, cols)

        def term(c, other):
            side = 1 - core if other else core
            acc = None
            for i in range(2):
                if c == 0:
                    weight, half = w_refs[other][i * cols : (i + 1) * cols, :], i
                else:
                    weight, half = w_refs[2 + 2 * other + i][...], (i + group) % 2
                part = jnp.dot(a_all[(2 * side + half) ^ row], weight, preferred_element_type=jnp.float32)
                acc = part if acc is None else acc + part
            return acc.astype(jnp.bfloat16).astype(jnp.float32)

        for c in range(2):
            sums[...] = (term(c, 0) + term(c, 1)).reshape(blocks, 2, BS, width)
            at = (row + c) % 2
            near_keep[at] = sums[row // 2, frame]
            near_send[at] = sums[row // 2, 1 - frame].astype(jnp.bfloat16)
            far_keep[at] = sums[1 - row // 2, frame]
            far_send[at] = sums[1 - row // 2, 1 - frame].astype(jnp.bfloat16)

    kept = jax.ShapeDtypeStruct((2, BS, width), jnp.float32)
    sent = jax.ShapeDtypeStruct((2, BS, width), jnp.bfloat16)
    return call(
        kernel,
        (kept, sent, kept, sent),
        [place],
        [*attended, w_own, w_across, *beside, *beside_across],
        scratch=[
            pltpu.VMEM((4, blocks * block_len, cols), jnp.bfloat16),
            pltpu.VMEM((blocks, 2, BS, width), jnp.float32),
        ],
        flops=2 * blocks * block_len * 4 * cols * 2 * width,
        read=16 * cols * width,
    )


def finish(place, near_keep, near_more, far):
    halves, rows, width = near_keep.shape

    def kernel(place_ref, keep_ref, more_ref, far_ref, out_ref):
        pair = place_ref[0] // 2
        for c in range(halves):
            here = pl.multiple_of((pair * halves + c) * width, width)
            there = pl.multiple_of(((1 - pair) * halves + c) * width, width)
            out_ref[:, pl.ds(here, width)] = (keep_ref[c] + more_ref[c].astype(jnp.float32)).astype(jnp.bfloat16)
            out_ref[:, pl.ds(there, width)] = far_ref[c]

    return call(
        kernel,
        jax.ShapeDtypeStruct((rows, 2 * halves * width), jnp.bfloat16),
        [place],
        [near_keep, near_more, far],
        read=12 * rows * halves * width,
    )


def by_heads(latents, w_qkv, w_out, win_blocks, win_counts, block_window):
    rows_n, heads_n = lax.axis_size("rows"), lax.axis_size("heads")
    group, row = lax.axis_index("groups"), lax.axis_index("rows")
    frame, core = lax.axis_index("frames"), lax.axis_index("heads")
    count = latents.shape[1]
    depth, _, local_cols = w_qkv.shape
    span = rows_n // heads_n
    cols = local_cols // span
    half = depth // 2
    place = jnp.stack([row, group, frame, core]).astype(jnp.int32)

    def reshard(k, *others):
        value = lax.dynamic_slice(
            w_qkv.transpose(1, 0, 2), (0, group * half, (k + row) % span * cols), (3, half, cols)
        )
        pairs = [
            (r * heads_n + h, (h * span + (k + r) % span) * heads_n + r // span)
            for r in range(rows_n)
            for h in range(heads_n)
        ]
        return lax.ppermute(after(value, *others) if others else value, ("rows", "heads"), pairs)

    mine = lax.dynamic_slice_in_dim(latents[0], core * span * depth, span * depth, axis=1)
    here, there = [reshard(0)], []
    tables = jnp.concatenate([win_blocks, win_counts[:, None], block_window[:, None]], axis=1)
    tables = jnp.pad(tables, ((0, 8 - heads_n), (0, span * depth - MAXB - 2))).astype(mine.dtype)
    joined = jnp.concatenate([mine, tables], axis=0)
    near = swap(joined, "rows")
    near_x = swap(near, "frames")
    mine_x = swap(mine, "frames")
    across = swap(after(w_out, near), "heads")
    there.append(swap(here[0], "groups"))
    here.append(reshard(1, near))
    far_2 = swap(after(joined, here[0]), "rows", 2)
    out_half = lax.dynamic_slice_in_dim(w_out, group * cols, cols, axis=0)
    beside = [swap(after(out_half, far_2), "rows")]
    beside.append(swap(beside[0], "groups"))
    there.append(swap(after(here[1], there[0]), "groups"))
    far_2x = swap(far_2, "frames")
    far_3 = swap(after(joined, far_2, across, near_x), "rows", 3)
    far_3x = swap(far_3, "frames")

    found = jnp.stack([x[count : count + heads_n, : MAXB + 2] for x in (joined, near, far_2, far_3)])
    tables = found.astype(jnp.int32)[row ^ jnp.arange(rows_n)].reshape(rows_n * heads_n, MAXB + 2)
    windows = lax.dynamic_index_in_dim(
        tables[:, MAXB + 1].reshape(rows_n, heads_n), core, axis=1, keepdims=False
    )
    picked = tables[windows]
    members, counts = picked[:, :MAXB].reshape(-1), picked[:, MAXB]

    pieces = [joined, near, far_2, far_3], [mine_x, near_x, far_2x, far_3x]
    chunks = [(here[0], there[0]), (here[1], after(there[1], members, counts, beside[0]))]
    last = cols // (3 * HD) * HD
    first = project(place, *pieces, chunks, 0, cols - last)
    first_more = swap(first[2], "heads")
    chunks[1] = (here[1], after(there[1], first[2], beside[1]))
    second = project(place, *pieces, chunks, cols - last, last)
    second_more = swap(second[2], "heads")
    attended = attend_all(place, members, counts, *first[:2], first_more)
    beside_across = [swap(part, "heads") for part in beside]
    same, diff = attend_all(place, members, counts, *second[:2], second_more, attended)
    attended = [same] + [swap(same if s % 2 == 0 else diff, "rows", s) for s in range(1, rows_n)]
    near_keep, near_send, far_keep, far_send = mix(place, attended, w_out, across, beside, beside_across)
    far_more = swap(far_send, "frames")
    far = swap((far_keep + far_more.astype(jnp.float32)).astype(jnp.bfloat16), "rows", 2)
    near_more = swap(after(near_send, far_more), "frames")
    return finish(place, near_keep, near_more, far)[None]


def local(latents, w_qkv, w_out, win_blocks, win_counts, block_window):
    rows_n = lax.axis_size("rows")
    pairs = all(lax.axis_size(axis) == 2 for axis in ("groups", "frames", "heads"))
    heads_here = w_qkv.shape[2] // HD
    if pairs and rows_n == 4 and heads_here == 6 and latents.shape[:2] == (1, 2 * BS):
        plan = by_heads
    else:
        plan = by_tokens
    return plan(latents, w_qkv, w_out, win_blocks, win_counts, block_window)


def solution(mesh):
    in_specs = (
        P(("groups", "frames"), "rows", None),
        P("rows", None, ("frames", "heads")),
        P(("frames", "heads"), "rows"),
        P(("groups", "rows"), None),
        P(("groups", "rows")),
        P(("groups", "rows")),
    )
    out_specs = P(("groups", "frames"), ("rows", "heads"), None)
    return jax.shard_map(local, mesh=mesh, in_specs=in_specs, out_specs=out_specs, check_vma=False)
```

```python
import math

import jax
import jax.numpy as jnp
from jax import lax
from jax.experimental import pallas as pl
from jax.experimental.pallas import tpu as pltpu
from jax.sharding import PartitionSpec as P

HD = 128
BS = 64
MAXB = 4
VMEM_BYTES = 24 * 1024 * 1024
WHOLE_VMEM_BYTES = 56 * 1024 * 1024
EXP2_SCALE = math.log2(math.e) / math.sqrt(HD)


def with_halo(value, sides, width):
    for axis, dim in sides:
        peers, length = (lax.axis_size(axis), value.shape[dim])
        up = [(i, (i + 1) % peers) for i in range(peers)]
        down = [(j, i) for i, j in up]
        last = lax.slice_in_dim(value, length - width, length, axis=dim)
        first = lax.slice_in_dim(value, 0, width, axis=dim)
        before = lax.ppermute(last, axis, up)
        after = lax.ppermute(first, axis, down)
        value = jnp.concatenate([before, value, after], axis=dim)
    return value


def by_tokens(latents, w_qkv, w_out, win_blocks, win_counts, block_window):
    rows_n = lax.axis_size("rows")
    shard_idx = lax.axis_index("rows")
    frames = latents.shape[0] * lax.axis_size("frames")
    tok_frame = latents.shape[1]
    model_width = latents.shape[2]
    local_cols = w_qkv.shape[2]
    per_shard = tok_frame // BS
    block_total = per_shard * rows_n
    heads_here = local_cols // HD
    block_len = frames * BS
    score_scale = 1.0 / math.sqrt(HD)
    gathered = lax.all_gather(latents, "frames", axis=0, tiled=True)
    flat_tokens = gathered.reshape(frames * tok_frame, model_width)
    weight_rows = lax.all_gather(w_qkv, "rows", axis=0, tiled=True)
    projected = jnp.dot(
        flat_tokens,
        weight_rows.reshape(weight_rows.shape[0], 3 * local_cols),
        preferred_element_type=jnp.float32,
    ).astype(jnp.bfloat16)
    blocked = projected.reshape(frames, per_shard, BS, 3, local_cols).transpose(1, 0, 2, 3, 4)
    blocked = blocked.reshape(per_shard, block_len, 3, local_cols)
    queries = blocked[:, :, 0]
    keyvals = blocked[:, :, 1:]
    nearby = with_halo(keyvals, (("rows", 0),), per_shard)
    first_block = shard_idx * per_shard
    owners = block_window - first_block
    members = win_blocks[owners]
    lengths = win_counts[owners]
    positions = (members - first_block + per_shard + block_total) % block_total

    def attend(query_rows, picked, live_mask):
        key_count = picked.shape[0]
        key_blocks = nearby[picked]
        key_part = key_blocks[:, :, 0].reshape(key_count * block_len, heads_here, HD)
        value_part = key_blocks[:, :, 1].reshape(key_count * block_len, heads_here, HD)
        scores = (
            jnp.einsum(
                "qhd,khd->hqk",
                query_rows.reshape(block_len, heads_here, HD),
                key_part,
                preferred_element_type=jnp.float32,
            )
            * score_scale
        )
        scores = jnp.where(live_mask[None, None, :], scores, -jnp.inf)
        row_max = jnp.max(scores, axis=-1, keepdims=True)
        raised = jnp.exp(scores - row_max)
        weights = (raised / jnp.sum(raised, axis=-1, keepdims=True)).astype(jnp.bfloat16)
        blended = jnp.einsum(
            "hqk,khd->qhd", weights, value_part, preferred_element_type=jnp.float32
        )
        return blended.reshape(block_len, local_cols).astype(jnp.bfloat16)

    def one_block(block_item):
        query_rows, picked, length = block_item
        live_mask = jnp.repeat(jnp.arange(MAXB) < length, block_len)
        return attend(query_rows, picked, live_mask)

    attended = lax.map(one_block, (queries, positions, lengths))
    ordered = attended.reshape(per_shard, frames, BS, local_cols).transpose(1, 0, 2, 3)
    ordered = ordered.reshape(frames * tok_frame, local_cols)
    w_full = lax.all_gather(w_out, "rows", axis=1, tiled=True)
    group_count = lax.axis_size(("frames", "heads"))
    out_rows = frames * tok_frame // group_count
    summed = lax.psum_scatter(
        jnp.dot(ordered, w_full, preferred_element_type=jnp.float32).astype(jnp.bfloat16),
        ("frames", "heads"),
        scatter_dimension=0,
        tiled=True,
    )
    return summed.reshape(1, out_rows, model_width)


def swap(value, axis, step=1):
    peers = lax.axis_size(axis)
    return lax.ppermute(value, axis, [(i, i ^ step) for i in range(peers)])


def after(value, *others):
    return lax.optimization_barrier((value, *others))[0]


def call(kernel, out_shape, prefetch, operands, scratch=(), flops=0, read=0, limit=VMEM_BYTES):
    return pl.pallas_call(
        kernel,
        out_shape=out_shape,
        grid_spec=pltpu.PrefetchScalarGridSpec(
            num_scalar_prefetch=len(prefetch),
            grid=(),
            in_specs=[pl.BlockSpec(memory_space=pltpu.VMEM)] * len(operands),
            out_specs=jax.tree.map(lambda _: pl.BlockSpec(memory_space=pltpu.VMEM), out_shape),
            scratch_shapes=scratch,
        ),
        compiler_params=pltpu.CompilerParams(vmem_limit_bytes=limit),
        cost_estimate=pl.CostEstimate(flops=flops, bytes_accessed=read, transcendentals=0),
    )(*prefetch, *operands)


def project(place, mine, theirs, chunks, first, cols):
    rows, (count, width) = len(mine), theirs[0].shape
    half = chunks[0][0].shape[1]
    slices = len(chunks)
    flat = [w for of_round in chunks for w in of_round]
    fetched = 2 * rows + len(flat)

    def kernel(place_ref, *refs):
        row, group, frame, core = (place_ref[i] for i in range(4))
        w_refs = refs[2 * rows : fetched]
        q_keep, kv_keep, send, x_all, w_all, total, sems = refs[fetched:]
        copies = []
        for k in range(slices):
            for g in range(2):
                at = pl.multiple_of((row + slices - k) % slices * (2 * half) + (group + g) % 2 * half, half)
                for part in range(3):
                    source = w_refs[2 * k + g].at[part, :, first : first + cols]
                    into = w_all.at[pl.ds(at, half), part * cols : (part + 1) * cols]
                    copies.append(pltpu.make_async_copy(source, into, sems.at[len(copies)]))
        fetch_x = []
        for i in range(2 * rows):
            to = x_all.at[row ^ (i % rows), (frame + i // rows) % 2]
            fetch_x.append(pltpu.make_async_copy(refs[i].at[pl.ds(0, count)], to, sems.at[len(copies) + i]))
        for copy in copies + fetch_x:
            copy.start()
        for copy in copies:
            copy.wait()
        for s in range(rows):
            fetch_x[s].wait()
            fetch_x[rows + s].wait()
            at = row ^ s
            acc = jnp.dot(x_all[at].reshape(-1, width), w_all[...], preferred_element_type=jnp.float32)
            kv_part = acc[:, cols:]
            kv_keep[at] = kv_part
            send[at, : 2 * count, :] = kv_part.astype(jnp.bfloat16)
            total[s] = acc[:, :cols].reshape(2, count, cols)
            own = pl.multiple_of(core * BS, BS)
            other = pl.multiple_of((1 - core) * BS, BS)
            q_keep[at] = total[s, :, pl.ds(own, BS), :].reshape(2 * BS, cols)
            for f in range(2):
                where = slice(f * cols, (f + 1) * cols)
                send[at, 2 * count :, where] = total[s, f, pl.ds(other, BS), :].astype(jnp.bfloat16)

    vmem, hbm = pl.BlockSpec(memory_space=pltpu.VMEM), pl.BlockSpec(memory_space=pltpu.HBM)
    flops = 2 * rows * 2 * count * width * 3 * cols
    return pl.pallas_call(
        kernel,
        out_shape=(
            jax.ShapeDtypeStruct((rows, 2 * BS, cols), jnp.float32),
            jax.ShapeDtypeStruct((rows, 2 * count, 2 * cols), jnp.float32),
            jax.ShapeDtypeStruct((rows, 2 * count + BS, 2 * cols), jnp.bfloat16),
        ),
        grid_spec=pltpu.PrefetchScalarGridSpec(
            num_scalar_prefetch=1,
            grid=(),
            in_specs=[hbm] * fetched,
            out_specs=(vmem, vmem, vmem),
            scratch_shapes=[
                pltpu.VMEM((rows, 2, count, width), jnp.bfloat16),
                pltpu.VMEM((width, 3 * cols), jnp.bfloat16),
                pltpu.VMEM((rows, 2, count, cols), jnp.float32),
                pltpu.SemaphoreType.DMA((2 * rows + 3 * len(flat),)),
            ],
        ),
        compiler_params=pltpu.CompilerParams(vmem_limit_bytes=VMEM_BYTES),
        cost_estimate=pl.CostEstimate(flops=8 * flops, bytes_accessed=flops // 300, transcendentals=0),
    )(place, *mine, *theirs, *flat)


def attend_all(place, members, counts, queries, keyvals, more, earlier=()):
    blocks, block_len, cols = queries.shape
    first = earlier[0].shape[2] if earlier else 0
    rows = keyvals.shape[1]
    per_row = rows // block_len

    def kernel(place_ref, members_ref, counts_ref, q_ref, kv_ref, more_ref, *refs):
        same_ref, diff_ref, q_sum, kv_sum, out = refs[len(earlier) :]
        for r in range(blocks):
            added = more_ref[r, rows:, :].astype(jnp.float32)
            added = jnp.concatenate([added[:, :cols], added[:, cols:]], axis=0)
            q_sum[r] = (q_ref[r] + added).astype(jnp.bfloat16)
            both = (kv_ref[r] + more_ref[r, :rows, :].astype(jnp.float32)).astype(jnp.bfloat16)
            both = both.reshape(2, rows // 2, 2 * cols)
            for j in range(per_row):
                part = both[:, j * BS : (j + 1) * BS, :]
                kv_sum[r * per_row + j] = part.reshape(block_len, 2 * cols)
        column = lax.broadcasted_iota(jnp.int32, (block_len, MAXB * block_len), 1)
        for b in range(blocks):
            live = column < counts_ref[b] * block_len
            listed = [kv_sum.at[members_ref[b * MAXB + j]] for j in range(MAXB)]
            for h in range(cols // HD):
                at = slice(h * HD, (h + 1) * HD)
                at_v = slice(cols + h * HD, cols + (h + 1) * HD)
                keys = jnp.concatenate([block[:, at] for block in listed], axis=0)
                values = jnp.concatenate([block[:, at_v] for block in listed], axis=0)
                scores = lax.dot_general(
                    q_sum[b, :, at], keys, (((1,), (1,)), ((), ())), preferred_element_type=jnp.float32
                )
                scores = jnp.where(live, scores, -jnp.inf)
                raised = jnp.exp2((scores - jnp.max(scores, axis=-1, keepdims=True)) * EXP2_SCALE)
                weights = raised * (1.0 / jnp.sum(raised, axis=-1, keepdims=True))
                blended = jnp.dot(
                    weights.astype(jnp.bfloat16), values, preferred_element_type=jnp.float32
                )
                out[(b + place_ref[0]) % 2, b // 2, :, at] = blended.astype(jnp.bfloat16)
        for i, out_ref in enumerate((same_ref, diff_ref)):
            if earlier:
                out_ref[:, :, :first] = refs[i][...]
            out_ref[:, :, first:] = out[i]

    half = jax.ShapeDtypeStruct((blocks // 2, block_len, first + cols), jnp.bfloat16)
    return call(
        kernel,
        (half, half),
        [place, members, counts],
        [queries, keyvals, more, *earlier],
        scratch=[
            pltpu.VMEM((blocks, block_len, cols), jnp.bfloat16),
            pltpu.VMEM((blocks * per_row, block_len, 2 * cols), jnp.bfloat16),
            pltpu.VMEM((2, blocks // 2, block_len, cols), jnp.bfloat16),
        ],
        flops=4 * blocks * block_len * MAXB * block_len * cols,
        read=16 * blocks * block_len * cols,
    )


def mix(place, attended, w_own, w_across, beside, beside_across, far):
    _, block_len, cols = attended[0].shape
    width = w_own.shape[1]

    def kernel(place_ref, *refs):
        row, group, frame, core = (place_ref[i] for i in range(4))
        w_refs = refs[4:10]
        keep, send, a_all, sums = refs[10:]
        block = 1 - row // 2 if far else row // 2
        for s in range(4):
            a_all[s] = refs[s][block]

        def term(c, other):
            side = 1 - core if other else core
            acc = None
            for i in range(2):
                if c == 0:
                    weight, half = w_refs[other][i * cols : (i + 1) * cols, :], i
                else:
                    weight, half = w_refs[2 + 2 * other + i][...], (i + group) % 2
                part = jnp.dot(a_all[(2 * side + half) ^ row], weight, preferred_element_type=jnp.float32)
                acc = part if acc is None else acc + part
            return acc.astype(jnp.bfloat16).astype(jnp.float32)

        for c in range(2):
            sums[...] = (term(c, 0) + term(c, 1)).reshape(2, BS, width)
            at = (row + c) % 2
            keep[at] = sums[frame]
            send[at] = sums[1 - frame].astype(jnp.bfloat16)

    return call(
        kernel,
        (
            jax.ShapeDtypeStruct((2, BS, width), jnp.float32),
            jax.ShapeDtypeStruct((2, BS, width), jnp.bfloat16),
        ),
        [place],
        [*attended, w_own, w_across, *beside, *beside_across],
        scratch=[pltpu.VMEM((4, block_len, cols), jnp.bfloat16), pltpu.VMEM((2, BS, width), jnp.float32)],
        flops=2 * block_len * 4 * cols * 2 * width,
        read=16 * cols * width,
    )


def finish(place, near_keep, near_more, far):
    halves, rows, width = near_keep.shape

    def kernel(place_ref, keep_ref, more_ref, far_ref, out_ref):
        pair = place_ref[0] // 2
        for c in range(halves):
            here = pl.multiple_of((pair * halves + c) * width, width)
            there = pl.multiple_of(((1 - pair) * halves + c) * width, width)
            out_ref[:, pl.ds(here, width)] = (keep_ref[c] + more_ref[c].astype(jnp.float32)).astype(jnp.bfloat16)
            out_ref[:, pl.ds(there, width)] = far_ref[c]

    return call(
        kernel,
        jax.ShapeDtypeStruct((rows, 2 * halves * width), jnp.bfloat16),
        [place],
        [near_keep, near_more, far],
        read=12 * rows * halves * width,
    )


def by_heads(latents, w_qkv, w_out, win_blocks, win_counts, block_window):
    rows_n, heads_n = lax.axis_size("rows"), lax.axis_size("heads")
    group, row = lax.axis_index("groups"), lax.axis_index("rows")
    frame, core = lax.axis_index("frames"), lax.axis_index("heads")
    count = latents.shape[1]
    depth, _, local_cols = w_qkv.shape
    span = rows_n // heads_n
    cols = local_cols // span
    half = depth // 2
    place = jnp.stack([row, group, frame, core]).astype(jnp.int32)

    def reshard(k, *others):
        value = lax.dynamic_slice(
            w_qkv.transpose(1, 0, 2), (0, group * half, (k + row) % span * cols), (3, half, cols)
        )
        pairs = [
            (r * heads_n + h, (h * span + (k + r) % span) * heads_n + r // span)
            for r in range(rows_n)
            for h in range(heads_n)
        ]
        return lax.ppermute(after(value, *others) if others else value, ("rows", "heads"), pairs)

    mine = lax.dynamic_slice_in_dim(latents[0], core * span * depth, span * depth, axis=1)
    mine_x = swap(mine, "frames")
    here, there = [reshard(0)], []
    tables = jnp.concatenate([win_blocks, win_counts[:, None], block_window[:, None]], axis=1)
    tables = jnp.pad(tables, ((0, 8 - heads_n), (0, span * depth - MAXB - 2))).astype(mine.dtype)
    joined = jnp.concatenate([mine, tables], axis=0)
    near = swap(joined, "rows")
    near_x = swap(near, "frames")
    across = swap(after(w_out, near), "heads")
    there.append(swap(here[0], "groups"))
    here.append(reshard(1, near))
    far_2 = swap(after(joined, here[0], mine_x), "rows", 2)
    out_half = lax.dynamic_slice_in_dim(w_out, group * cols, cols, axis=0)
    beside = [swap(after(out_half, near), "rows")]
    beside.append(swap(beside[0], "groups"))
    there.append(swap(after(here[1], there[0], beside[1]), "groups"))
    far_2x = swap(far_2, "frames")
    far_3 = swap(after(joined, far_2, across, near_x, beside[0]), "rows", 3)
    far_3x = swap(far_3, "frames")

    found = jnp.stack([x[count : count + heads_n, : MAXB + 2] for x in (joined, near, far_2, far_3)])
    tables = found.astype(jnp.int32)[row ^ jnp.arange(rows_n)].reshape(rows_n * heads_n, MAXB + 2)
    windows = lax.dynamic_index_in_dim(
        tables[:, MAXB + 1].reshape(rows_n, heads_n), core, axis=1, keepdims=False
    )
    picked = tables[windows]
    members, counts = picked[:, :MAXB].reshape(-1), picked[:, MAXB]

    pieces = [joined, near, far_2, far_3], [mine_x, near_x, far_2x, far_3x]
    chunks = [(here[0], there[0]), (here[1], after(there[1], members, counts))]
    last = cols // (3 * HD) * HD
    first = project(place, *pieces, chunks, 0, cols - last)
    first_more = swap(first[2], "heads")
    chunks[1] = (here[1], after(there[1], first[2]))
    second = project(place, *pieces, chunks, cols - last, last)
    second_more = swap(second[2], "heads")
    attended = attend_all(place, members, counts, *first[:2], first_more)
    beside_across = [swap(part, "heads") for part in beside]
    same, diff = attend_all(place, members, counts, *second[:2], second_more, attended)
    attended = [same] + [swap(same if s % 2 == 0 else diff, "rows", s) for s in range(1, rows_n)]
    weights = w_out, across, beside, beside_across
    far_keep, far_send = mix(place, attended, *weights, True)
    near_keep, near_send = mix(place, attended, *weights, False)
    far_more = swap(far_send, "frames")
    far = swap((far_keep + far_more.astype(jnp.float32)).astype(jnp.bfloat16), "rows", 2)
    near_more = swap(after(near_send, far_more), "frames")
    return finish(place, near_keep, near_more, far)[None]


def local(latents, w_qkv, w_out, win_blocks, win_counts, block_window):
    rows_n = lax.axis_size("rows")
    pairs = all(lax.axis_size(axis) == 2 for axis in ("groups", "frames", "heads"))
    heads_here = w_qkv.shape[2] // HD
    if pairs and rows_n == 4 and heads_here == 6 and latents.shape[:2] == (1, 2 * BS):
        plan = by_heads
    else:
        plan = by_tokens
    return plan(latents, w_qkv, w_out, win_blocks, win_counts, block_window)


def solution(mesh):
    in_specs = (
        P(("groups", "frames"), "rows", None),
        P("rows", None, ("frames", "heads")),
        P(("frames", "heads"), "rows"),
        P(("groups", "rows"), None),
        P(("groups", "rows")),
        P(("groups", "rows")),
    )
    out_specs = P(("groups", "frames"), ("rows", "heads"), None)
    return jax.shard_map(local, mesh=mesh, in_specs=in_specs, out_specs=out_specs, check_vma=False)
```

```python
import math

import jax
import jax.numpy as jnp
from jax import lax
from jax.experimental import pallas as pl
from jax.experimental.pallas import tpu as pltpu
from jax.sharding import PartitionSpec as P

HD = 128
BS = 64
MAXB = 4
VMEM_BYTES = 24 * 1024 * 1024
WHOLE_VMEM_BYTES = 56 * 1024 * 1024
EXP2_SCALE = math.log2(math.e) / math.sqrt(HD)


def with_halo(value, sides, width):
    for axis, dim in sides:
        peers, length = (lax.axis_size(axis), value.shape[dim])
        up = [(i, (i + 1) % peers) for i in range(peers)]
        down = [(j, i) for i, j in up]
        last = lax.slice_in_dim(value, length - width, length, axis=dim)
        first = lax.slice_in_dim(value, 0, width, axis=dim)
        before = lax.ppermute(last, axis, up)
        after = lax.ppermute(first, axis, down)
        value = jnp.concatenate([before, value, after], axis=dim)
    return value


def by_tokens(latents, w_qkv, w_out, win_blocks, win_counts, block_window):
    rows_n = lax.axis_size("rows")
    shard_idx = lax.axis_index("rows")
    frames = latents.shape[0] * lax.axis_size("frames")
    tok_frame = latents.shape[1]
    model_width = latents.shape[2]
    local_cols = w_qkv.shape[2]
    per_shard = tok_frame // BS
    block_total = per_shard * rows_n
    heads_here = local_cols // HD
    block_len = frames * BS
    score_scale = 1.0 / math.sqrt(HD)
    gathered = lax.all_gather(latents, "frames", axis=0, tiled=True)
    flat_tokens = gathered.reshape(frames * tok_frame, model_width)
    weight_rows = lax.all_gather(w_qkv, "rows", axis=0, tiled=True)
    projected = jnp.dot(
        flat_tokens,
        weight_rows.reshape(weight_rows.shape[0], 3 * local_cols),
        preferred_element_type=jnp.float32,
    ).astype(jnp.bfloat16)
    blocked = projected.reshape(frames, per_shard, BS, 3, local_cols).transpose(1, 0, 2, 3, 4)
    blocked = blocked.reshape(per_shard, block_len, 3, local_cols)
    queries = blocked[:, :, 0]
    keyvals = blocked[:, :, 1:]
    nearby = with_halo(keyvals, (("rows", 0),), per_shard)
    first_block = shard_idx * per_shard
    owners = block_window - first_block
    members = win_blocks[owners]
    lengths = win_counts[owners]
    positions = (members - first_block + per_shard + block_total) % block_total

    def attend(query_rows, picked, live_mask):
        key_count = picked.shape[0]
        key_blocks = nearby[picked]
        key_part = key_blocks[:, :, 0].reshape(key_count * block_len, heads_here, HD)
        value_part = key_blocks[:, :, 1].reshape(key_count * block_len, heads_here, HD)
        scores = (
            jnp.einsum(
                "qhd,khd->hqk",
                query_rows.reshape(block_len, heads_here, HD),
                key_part,
                preferred_element_type=jnp.float32,
            )
            * score_scale
        )
        scores = jnp.where(live_mask[None, None, :], scores, -jnp.inf)
        row_max = jnp.max(scores, axis=-1, keepdims=True)
        raised = jnp.exp(scores - row_max)
        weights = (raised / jnp.sum(raised, axis=-1, keepdims=True)).astype(jnp.bfloat16)
        blended = jnp.einsum(
            "hqk,khd->qhd", weights, value_part, preferred_element_type=jnp.float32
        )
        return blended.reshape(block_len, local_cols).astype(jnp.bfloat16)

    def one_block(block_item):
        query_rows, picked, length = block_item
        live_mask = jnp.repeat(jnp.arange(MAXB) < length, block_len)
        return attend(query_rows, picked, live_mask)

    attended = lax.map(one_block, (queries, positions, lengths))
    ordered = attended.reshape(per_shard, frames, BS, local_cols).transpose(1, 0, 2, 3)
    ordered = ordered.reshape(frames * tok_frame, local_cols)
    w_full = lax.all_gather(w_out, "rows", axis=1, tiled=True)
    group_count = lax.axis_size(("frames", "heads"))
    out_rows = frames * tok_frame // group_count
    summed = lax.psum_scatter(
        jnp.dot(ordered, w_full, preferred_element_type=jnp.float32).astype(jnp.bfloat16),
        ("frames", "heads"),
        scatter_dimension=0,
        tiled=True,
    )
    return summed.reshape(1, out_rows, model_width)


def swap(value, axis, step=1):
    peers = lax.axis_size(axis)
    return lax.ppermute(value, axis, [(i, i ^ step) for i in range(peers)])


def after(value, *others):
    return lax.optimization_barrier((value, *others))[0]


def call(kernel, out_shape, prefetch, operands, scratch=(), flops=0, read=0, limit=VMEM_BYTES):
    return pl.pallas_call(
        kernel,
        out_shape=out_shape,
        grid_spec=pltpu.PrefetchScalarGridSpec(
            num_scalar_prefetch=len(prefetch),
            grid=(),
            in_specs=[pl.BlockSpec(memory_space=pltpu.VMEM)] * len(operands),
            out_specs=jax.tree.map(lambda _: pl.BlockSpec(memory_space=pltpu.VMEM), out_shape),
            scratch_shapes=scratch,
        ),
        compiler_params=pltpu.CompilerParams(vmem_limit_bytes=limit),
        cost_estimate=pl.CostEstimate(flops=flops, bytes_accessed=read, transcendentals=0),
    )(*prefetch, *operands)


def project(place, mine, theirs, chunks, first, cols):
    rows, (count, width) = len(mine), theirs[0].shape
    half = chunks[0][0].shape[1]
    slices = len(chunks)
    flat = [w for of_round in chunks for w in of_round]
    fetched = 2 * rows + len(flat)

    def kernel(place_ref, *refs):
        row, group, frame, core = (place_ref[i] for i in range(4))
        w_refs = refs[2 * rows : fetched]
        q_keep, kv_keep, send, x_all, w_all, total, sems = refs[fetched:]
        copies = []
        for k in range(slices):
            for g in range(2):
                at = pl.multiple_of((row + slices - k) % slices * (2 * half) + (group + g) % 2 * half, half)
                for part in range(3):
                    source = w_refs[2 * k + g].at[part, :, first : first + cols]
                    into = w_all.at[pl.ds(at, half), part * cols : (part + 1) * cols]
                    copies.append(pltpu.make_async_copy(source, into, sems.at[len(copies)]))
        fetch_x = []
        for i in range(2 * rows):
            to = x_all.at[row ^ (i % rows), (frame + i // rows) % 2]
            fetch_x.append(pltpu.make_async_copy(refs[i].at[pl.ds(0, count)], to, sems.at[len(copies) + i]))
        for copy in copies + fetch_x:
            copy.start()
        for copy in copies:
            copy.wait()
        for s in range(rows):
            fetch_x[s].wait()
            fetch_x[rows + s].wait()
            at = row ^ s
            acc = jnp.dot(x_all[at].reshape(-1, width), w_all[...], preferred_element_type=jnp.float32)
            kv_part = acc[:, cols:]
            kv_keep[at] = kv_part
            send[at, : 2 * count, :] = kv_part.astype(jnp.bfloat16)
            total[s] = acc[:, :cols].reshape(2, count, cols)
            own = pl.multiple_of(core * BS, BS)
            other = pl.multiple_of((1 - core) * BS, BS)
            q_keep[at] = total[s, :, pl.ds(own, BS), :].reshape(2 * BS, cols)
            for f in range(2):
                where = slice(f * cols, (f + 1) * cols)
                send[at, 2 * count :, where] = total[s, f, pl.ds(other, BS), :].astype(jnp.bfloat16)

    vmem, hbm = pl.BlockSpec(memory_space=pltpu.VMEM), pl.BlockSpec(memory_space=pltpu.HBM)
    flops = 2 * rows * 2 * count * width * 3 * cols
    return pl.pallas_call(
        kernel,
        out_shape=(
            jax.ShapeDtypeStruct((rows, 2 * BS, cols), jnp.float32),
            jax.ShapeDtypeStruct((rows, 2 * count, 2 * cols), jnp.float32),
            jax.ShapeDtypeStruct((rows, 2 * count + BS, 2 * cols), jnp.bfloat16),
        ),
        grid_spec=pltpu.PrefetchScalarGridSpec(
            num_scalar_prefetch=1,
            grid=(),
            in_specs=[hbm] * fetched,
            out_specs=(vmem, vmem, vmem),
            scratch_shapes=[
                pltpu.VMEM((rows, 2, count, width), jnp.bfloat16),
                pltpu.VMEM((width, 3 * cols), jnp.bfloat16),
                pltpu.VMEM((rows, 2, count, cols), jnp.float32),
                pltpu.SemaphoreType.DMA((2 * rows + 3 * len(flat),)),
            ],
        ),
        compiler_params=pltpu.CompilerParams(vmem_limit_bytes=VMEM_BYTES),
        cost_estimate=pl.CostEstimate(flops=8 * flops, bytes_accessed=flops // 300, transcendentals=0),
    )(place, *mine, *theirs, *flat)


def attend_all(place, members, counts, queries, keyvals, more, earlier=()):
    blocks, block_len, cols = queries.shape
    first = earlier[0].shape[2] if earlier else 0
    rows = keyvals.shape[1]
    per_row = rows // block_len

    def kernel(place_ref, members_ref, counts_ref, q_ref, kv_ref, more_ref, *refs):
        same_ref, diff_ref, q_sum, kv_sum, out = refs[len(earlier) :]
        for r in range(blocks):
            added = more_ref[r, rows:, :].astype(jnp.float32)
            added = jnp.concatenate([added[:, :cols], added[:, cols:]], axis=0)
            q_sum[r] = (q_ref[r] + added).astype(jnp.bfloat16)
            both = (kv_ref[r] + more_ref[r, :rows, :].astype(jnp.float32)).astype(jnp.bfloat16)
            both = both.reshape(2, rows // 2, 2 * cols)
            for j in range(per_row):
                part = both[:, j * BS : (j + 1) * BS, :]
                kv_sum[r * per_row + j] = part.reshape(block_len, 2 * cols)
        column = lax.broadcasted_iota(jnp.int32, (block_len, MAXB * block_len), 1)
        for b in range(blocks):
            live = column < counts_ref[b] * block_len
            listed = [kv_sum.at[members_ref[b * MAXB + j]] for j in range(MAXB)]
            for h in range(cols // HD):
                at = slice(h * HD, (h + 1) * HD)
                at_v = slice(cols + h * HD, cols + (h + 1) * HD)
                keys = jnp.concatenate([block[:, at] for block in listed], axis=0)
                values = jnp.concatenate([block[:, at_v] for block in listed], axis=0)
                scores = lax.dot_general(
                    q_sum[b, :, at], keys, (((1,), (1,)), ((), ())), preferred_element_type=jnp.float32
                )
                scores = jnp.where(live, scores, -jnp.inf)
                raised = jnp.exp2((scores - jnp.max(scores, axis=-1, keepdims=True)) * EXP2_SCALE)
                weights = raised * (1.0 / jnp.sum(raised, axis=-1, keepdims=True))
                blended = jnp.dot(
                    weights.astype(jnp.bfloat16), values, preferred_element_type=jnp.float32
                )
                out[(b + place_ref[0]) % 2, b // 2, :, at] = blended.astype(jnp.bfloat16)
        for i, out_ref in enumerate((same_ref, diff_ref)):
            if earlier:
                out_ref[:, :, :first] = refs[i][...]
            out_ref[:, :, first:] = out[i]

    half = jax.ShapeDtypeStruct((blocks // 2, block_len, first + cols), jnp.bfloat16)
    return call(
        kernel,
        (half, half),
        [place, members, counts],
        [queries, keyvals, more, *earlier],
        scratch=[
            pltpu.VMEM((blocks, block_len, cols), jnp.bfloat16),
            pltpu.VMEM((blocks * per_row, block_len, 2 * cols), jnp.bfloat16),
            pltpu.VMEM((2, blocks // 2, block_len, cols), jnp.bfloat16),
        ],
        flops=4 * blocks * block_len * MAXB * block_len * cols,
        read=16 * blocks * block_len * cols,
    )


def mix(place, attended, w_own, w_across, beside, beside_across, far):
    _, block_len, cols = attended[0].shape
    width = w_own.shape[1]

    def kernel(place_ref, *refs):
        row, group, frame, core = (place_ref[i] for i in range(4))
        w_refs = refs[4:10]
        keep, send, a_all, sums = refs[10:]
        block = 1 - row // 2 if far else row // 2
        for s in range(4):
            a_all[s] = refs[s][block]

        def term(c, other):
            side = 1 - core if other else core
            acc = None
            for i in range(2):
                if c == 0:
                    weight, half = w_refs[other][i * cols : (i + 1) * cols, :], i
                else:
                    weight, half = w_refs[2 + 2 * other + i][...], (i + group) % 2
                part = jnp.dot(a_all[(2 * side + half) ^ row], weight, preferred_element_type=jnp.float32)
                acc = part if acc is None else acc + part
            return acc.astype(jnp.bfloat16).astype(jnp.float32)

        for c in range(2):
            sums[...] = (term(c, 0) + term(c, 1)).reshape(2, BS, width)
            at = (row + c) % 2
            keep[at] = sums[frame]
            send[at] = sums[1 - frame].astype(jnp.bfloat16)

    return call(
        kernel,
        (
            jax.ShapeDtypeStruct((2, BS, width), jnp.float32),
            jax.ShapeDtypeStruct((2, BS, width), jnp.bfloat16),
        ),
        [place],
        [*attended, w_own, w_across, *beside, *beside_across],
        scratch=[pltpu.VMEM((4, block_len, cols), jnp.bfloat16), pltpu.VMEM((2, BS, width), jnp.float32)],
        flops=2 * block_len * 4 * cols * 2 * width,
        read=16 * cols * width,
    )


def finish(place, near_keep, near_more, far):
    halves, rows, width = near_keep.shape

    def kernel(place_ref, keep_ref, more_ref, far_ref, out_ref):
        pair = place_ref[0] // 2
        for c in range(halves):
            here = pl.multiple_of((pair * halves + c) * width, width)
            there = pl.multiple_of(((1 - pair) * halves + c) * width, width)
            out_ref[:, pl.ds(here, width)] = (keep_ref[c] + more_ref[c].astype(jnp.float32)).astype(jnp.bfloat16)
            out_ref[:, pl.ds(there, width)] = far_ref[c]

    return call(
        kernel,
        jax.ShapeDtypeStruct((rows, 2 * halves * width), jnp.bfloat16),
        [place],
        [near_keep, near_more, far],
        read=12 * rows * halves * width,
    )


def by_heads(latents, w_qkv, w_out, win_blocks, win_counts, block_window):
    rows_n, heads_n = lax.axis_size("rows"), lax.axis_size("heads")
    group, row = lax.axis_index("groups"), lax.axis_index("rows")
    frame, core = lax.axis_index("frames"), lax.axis_index("heads")
    count = latents.shape[1]
    depth, _, local_cols = w_qkv.shape
    span = rows_n // heads_n
    cols = local_cols // span
    half = depth // 2
    place = jnp.stack([row, group, frame, core]).astype(jnp.int32)

    def reshard(k, *others):
        value = lax.dynamic_slice(
            w_qkv.transpose(1, 0, 2), (0, group * half, (k + row) % span * cols), (3, half, cols)
        )
        pairs = [
            (r * heads_n + h, (h * span + (k + r) % span) * heads_n + r // span)
            for r in range(rows_n)
            for h in range(heads_n)
        ]
        return lax.ppermute(after(value, *others) if others else value, ("rows", "heads"), pairs)

    mine = lax.dynamic_slice_in_dim(latents[0], core * span * depth, span * depth, axis=1)
    mine_x = swap(mine, "frames")
    here, there = [reshard(0)], []
    tables = jnp.concatenate([win_blocks, win_counts[:, None], block_window[:, None]], axis=1)
    tables = jnp.pad(tables, ((0, 8 - heads_n), (0, span * depth - MAXB - 2))).astype(mine.dtype)
    joined = jnp.concatenate([mine, tables], axis=0)
    near = swap(joined, "rows")
    near_x = swap(near, "frames")
    across = swap(after(w_out, near), "heads")
    there.append(swap(here[0], "groups"))
    here.append(reshard(1, near))
    far_2 = swap(after(joined, here[0], mine_x), "rows", 2)
    out_half = lax.dynamic_slice_in_dim(w_out, group * cols, cols, axis=0)
    beside = [swap(after(out_half, near), "rows")]
    beside.append(swap(beside[0], "groups"))
    there.append(swap(after(here[1], there[0], beside[1]), "groups"))
    far_2x = swap(far_2, "frames")
    far_3 = swap(after(joined, here[0], across, near_x), "rows", 3)
    far_3x = swap(far_3, "frames")

    found = jnp.stack([x[count : count + heads_n, : MAXB + 2] for x in (joined, near, far_2, far_3)])
    tables = found.astype(jnp.int32)[row ^ jnp.arange(rows_n)].reshape(rows_n * heads_n, MAXB + 2)
    windows = lax.dynamic_index_in_dim(
        tables[:, MAXB + 1].reshape(rows_n, heads_n), core, axis=1, keepdims=False
    )
    picked = tables[windows]
    members, counts = picked[:, :MAXB].reshape(-1), picked[:, MAXB]

    pieces = [joined, near, far_2, far_3], [mine_x, near_x, far_2x, far_3x]
    chunks = [(here[0], there[0]), (here[1], after(there[1], members, counts))]
    last = cols // (3 * HD) * HD
    first = project(place, *pieces, chunks, 0, cols - last)
    first_more = swap(first[2], "heads")
    chunks[1] = (here[1], after(there[1], first[2]))
    second = project(place, *pieces, chunks, cols - last, last)
    second_more = swap(second[2], "heads")
    attended = attend_all(place, members, counts, *first[:2], first_more)
    beside_across = [swap(part, "heads") for part in beside]
    same, diff = attend_all(place, members, counts, *second[:2], second_more, attended)
    attended = [same] + [swap(same if s % 2 == 0 else diff, "rows", s) for s in range(1, rows_n)]
    weights = w_out, across, beside, beside_across
    far_keep, far_send = mix(place, attended, *weights, True)
    near_keep, near_send = mix(place, attended, *weights, False)
    far_more = swap(far_send, "frames")
    far = swap((far_keep + far_more.astype(jnp.float32)).astype(jnp.bfloat16), "rows", 2)
    near_more = swap(after(near_send, far_more), "frames")
    return finish(place, near_keep, near_more, far)[None]


def local(latents, w_qkv, w_out, win_blocks, win_counts, block_window):
    rows_n = lax.axis_size("rows")
    pairs = all(lax.axis_size(axis) == 2 for axis in ("groups", "frames", "heads"))
    heads_here = w_qkv.shape[2] // HD
    if pairs and rows_n == 4 and heads_here == 6 and latents.shape[:2] == (1, 2 * BS):
        plan = by_heads
    else:
        plan = by_tokens
    return plan(latents, w_qkv, w_out, win_blocks, win_counts, block_window)


def solution(mesh):
    in_specs = (
        P(("groups", "frames"), "rows", None),
        P("rows", None, ("frames", "heads")),
        P(("frames", "heads"), "rows"),
        P(("groups", "rows"), None),
        P(("groups", "rows")),
        P(("groups", "rows")),
    )
    out_specs = P(("groups", "frames"), ("rows", "heads"), None)
    return jax.shard_map(local, mesh=mesh, in_specs=in_specs, out_specs=out_specs, check_vma=False)
```

```python
import math

import jax
import jax.numpy as jnp
from jax import lax
from jax.experimental import pallas as pl
from jax.experimental.pallas import tpu as pltpu
from jax.sharding import PartitionSpec as P

HD = 128
BS = 64
MAXB = 4
VMEM_BYTES = 24 * 1024 * 1024
WHOLE_VMEM_BYTES = 56 * 1024 * 1024
EXP2_SCALE = math.log2(math.e) / math.sqrt(HD)


def with_halo(value, sides, width):
    for axis, dim in sides:
        peers, length = (lax.axis_size(axis), value.shape[dim])
        up = [(i, (i + 1) % peers) for i in range(peers)]
        down = [(j, i) for i, j in up]
        last = lax.slice_in_dim(value, length - width, length, axis=dim)
        first = lax.slice_in_dim(value, 0, width, axis=dim)
        before = lax.ppermute(last, axis, up)
        after = lax.ppermute(first, axis, down)
        value = jnp.concatenate([before, value, after], axis=dim)
    return value


def by_tokens(latents, w_qkv, w_out, win_blocks, win_counts, block_window):
    rows_n = lax.axis_size("rows")
    shard_idx = lax.axis_index("rows")
    frames = latents.shape[0] * lax.axis_size("frames")
    tok_frame = latents.shape[1]
    model_width = latents.shape[2]
    local_cols = w_qkv.shape[2]
    per_shard = tok_frame // BS
    block_total = per_shard * rows_n
    heads_here = local_cols // HD
    block_len = frames * BS
    score_scale = 1.0 / math.sqrt(HD)
    gathered = lax.all_gather(latents, "frames", axis=0, tiled=True)
    flat_tokens = gathered.reshape(frames * tok_frame, model_width)
    weight_rows = lax.all_gather(w_qkv, "rows", axis=0, tiled=True)
    projected = jnp.dot(
        flat_tokens,
        weight_rows.reshape(weight_rows.shape[0], 3 * local_cols),
        preferred_element_type=jnp.float32,
    ).astype(jnp.bfloat16)
    blocked = projected.reshape(frames, per_shard, BS, 3, local_cols).transpose(1, 0, 2, 3, 4)
    blocked = blocked.reshape(per_shard, block_len, 3, local_cols)
    queries = blocked[:, :, 0]
    keyvals = blocked[:, :, 1:]
    nearby = with_halo(keyvals, (("rows", 0),), per_shard)
    first_block = shard_idx * per_shard
    owners = block_window - first_block
    members = win_blocks[owners]
    lengths = win_counts[owners]
    positions = (members - first_block + per_shard + block_total) % block_total

    def attend(query_rows, picked, live_mask):
        key_count = picked.shape[0]
        key_blocks = nearby[picked]
        key_part = key_blocks[:, :, 0].reshape(key_count * block_len, heads_here, HD)
        value_part = key_blocks[:, :, 1].reshape(key_count * block_len, heads_here, HD)
        scores = (
            jnp.einsum(
                "qhd,khd->hqk",
                query_rows.reshape(block_len, heads_here, HD),
                key_part,
                preferred_element_type=jnp.float32,
            )
            * score_scale
        )
        scores = jnp.where(live_mask[None, None, :], scores, -jnp.inf)
        row_max = jnp.max(scores, axis=-1, keepdims=True)
        raised = jnp.exp(scores - row_max)
        weights = (raised / jnp.sum(raised, axis=-1, keepdims=True)).astype(jnp.bfloat16)
        blended = jnp.einsum(
            "hqk,khd->qhd", weights, value_part, preferred_element_type=jnp.float32
        )
        return blended.reshape(block_len, local_cols).astype(jnp.bfloat16)

    def one_block(block_item):
        query_rows, picked, length = block_item
        live_mask = jnp.repeat(jnp.arange(MAXB) < length, block_len)
        return attend(query_rows, picked, live_mask)

    attended = lax.map(one_block, (queries, positions, lengths))
    ordered = attended.reshape(per_shard, frames, BS, local_cols).transpose(1, 0, 2, 3)
    ordered = ordered.reshape(frames * tok_frame, local_cols)
    w_full = lax.all_gather(w_out, "rows", axis=1, tiled=True)
    group_count = lax.axis_size(("frames", "heads"))
    out_rows = frames * tok_frame // group_count
    summed = lax.psum_scatter(
        jnp.dot(ordered, w_full, preferred_element_type=jnp.float32).astype(jnp.bfloat16),
        ("frames", "heads"),
        scatter_dimension=0,
        tiled=True,
    )
    return summed.reshape(1, out_rows, model_width)


def swap(value, axis, step=1):
    peers = lax.axis_size(axis)
    return lax.ppermute(value, axis, [(i, i ^ step) for i in range(peers)])


def after(value, *others):
    return lax.optimization_barrier((value, *others))[0]


def call(kernel, out_shape, prefetch, operands, scratch=(), flops=0, read=0, limit=VMEM_BYTES):
    return pl.pallas_call(
        kernel,
        out_shape=out_shape,
        grid_spec=pltpu.PrefetchScalarGridSpec(
            num_scalar_prefetch=len(prefetch),
            grid=(),
            in_specs=[pl.BlockSpec(memory_space=pltpu.VMEM)] * len(operands),
            out_specs=jax.tree.map(lambda _: pl.BlockSpec(memory_space=pltpu.VMEM), out_shape),
            scratch_shapes=scratch,
        ),
        compiler_params=pltpu.CompilerParams(vmem_limit_bytes=limit),
        cost_estimate=pl.CostEstimate(flops=flops, bytes_accessed=read, transcendentals=0),
    )(*prefetch, *operands)


def project(place, mine, theirs, chunks, first, cols):
    rows, (count, width) = len(mine), theirs[0].shape
    half = chunks[0][0].shape[1]
    slices = len(chunks)
    flat = [w for of_round in chunks for w in of_round]
    fetched = 2 * rows + len(flat)

    def kernel(place_ref, *refs):
        row, group, frame, core = (place_ref[i] for i in range(4))
        w_refs = refs[2 * rows : fetched]
        q_keep, kv_keep, send, x_all, w_all, total, sems = refs[fetched:]
        copies = []
        for k in range(slices):
            for g in range(2):
                at = pl.multiple_of((row + slices - k) % slices * (2 * half) + (group + g) % 2 * half, half)
                for part in range(3):
                    source = w_refs[2 * k + g].at[part, :, first : first + cols]
                    into = w_all.at[pl.ds(at, half), part * cols : (part + 1) * cols]
                    copies.append(pltpu.make_async_copy(source, into, sems.at[len(copies)]))
        fetch_x = []
        for i in range(2 * rows):
            to = x_all.at[row ^ (i % rows), (frame + i // rows) % 2]
            fetch_x.append(pltpu.make_async_copy(refs[i].at[pl.ds(0, count)], to, sems.at[len(copies) + i]))
        for copy in copies + fetch_x:
            copy.start()
        for copy in copies:
            copy.wait()
        for s in range(rows):
            fetch_x[s].wait()
            fetch_x[rows + s].wait()
            at = row ^ s
            acc = jnp.dot(x_all[at].reshape(-1, width), w_all[...], preferred_element_type=jnp.float32)
            kv_part = acc[:, cols:]
            kv_keep[at] = kv_part
            send[at, : 2 * count, :] = kv_part.astype(jnp.bfloat16)
            total[s] = acc[:, :cols].reshape(2, count, cols)
            own = pl.multiple_of(core * BS, BS)
            other = pl.multiple_of((1 - core) * BS, BS)
            q_keep[at] = total[s, :, pl.ds(own, BS), :].reshape(2 * BS, cols)
            for f in range(2):
                where = slice(f * cols, (f + 1) * cols)
                send[at, 2 * count :, where] = total[s, f, pl.ds(other, BS), :].astype(jnp.bfloat16)

    vmem, hbm = pl.BlockSpec(memory_space=pltpu.VMEM), pl.BlockSpec(memory_space=pltpu.HBM)
    flops = 2 * rows * 2 * count * width * 3 * cols
    return pl.pallas_call(
        kernel,
        out_shape=(
            jax.ShapeDtypeStruct((rows, 2 * BS, cols), jnp.float32),
            jax.ShapeDtypeStruct((rows, 2 * count, 2 * cols), jnp.float32),
            jax.ShapeDtypeStruct((rows, 2 * count + BS, 2 * cols), jnp.bfloat16),
        ),
        grid_spec=pltpu.PrefetchScalarGridSpec(
            num_scalar_prefetch=1,
            grid=(),
            in_specs=[hbm] * fetched,
            out_specs=(vmem, vmem, vmem),
            scratch_shapes=[
                pltpu.VMEM((rows, 2, count, width), jnp.bfloat16),
                pltpu.VMEM((width, 3 * cols), jnp.bfloat16),
                pltpu.VMEM((rows, 2, count, cols), jnp.float32),
                pltpu.SemaphoreType.DMA((2 * rows + 3 * len(flat),)),
            ],
        ),
        compiler_params=pltpu.CompilerParams(vmem_limit_bytes=VMEM_BYTES),
        cost_estimate=pl.CostEstimate(flops=8 * flops, bytes_accessed=flops // 300, transcendentals=0),
    )(place, *mine, *theirs, *flat)


def attend_all(place, members, counts, queries, keyvals, more, earlier=()):
    blocks, block_len, cols = queries.shape
    first = earlier[0].shape[2] if earlier else 0
    rows = keyvals.shape[1]
    per_row = rows // block_len

    def kernel(place_ref, members_ref, counts_ref, q_ref, kv_ref, more_ref, *refs):
        same_ref, diff_ref, q_sum, kv_sum, out = refs[len(earlier) :]
        for r in range(blocks):
            added = more_ref[r, rows:, :].astype(jnp.float32)
            added = jnp.concatenate([added[:, :cols], added[:, cols:]], axis=0)
            q_sum[r] = (q_ref[r] + added).astype(jnp.bfloat16)
            both = (kv_ref[r] + more_ref[r, :rows, :].astype(jnp.float32)).astype(jnp.bfloat16)
            both = both.reshape(2, rows // 2, 2 * cols)
            for j in range(per_row):
                part = both[:, j * BS : (j + 1) * BS, :]
                kv_sum[r * per_row + j] = part.reshape(block_len, 2 * cols)
        column = lax.broadcasted_iota(jnp.int32, (block_len, MAXB * block_len), 1)
        for b in range(blocks):
            live = column < counts_ref[b] * block_len
            listed = [kv_sum.at[members_ref[b * MAXB + j]] for j in range(MAXB)]
            for h in range(cols // HD):
                at = slice(h * HD, (h + 1) * HD)
                at_v = slice(cols + h * HD, cols + (h + 1) * HD)
                keys = jnp.concatenate([block[:, at] for block in listed], axis=0)
                values = jnp.concatenate([block[:, at_v] for block in listed], axis=0)
                scores = lax.dot_general(
                    q_sum[b, :, at], keys, (((1,), (1,)), ((), ())), preferred_element_type=jnp.float32
                )
                scores = jnp.where(live, scores, -jnp.inf)
                raised = jnp.exp2((scores - jnp.max(scores, axis=-1, keepdims=True)) * EXP2_SCALE)
                weights = raised * (1.0 / jnp.sum(raised, axis=-1, keepdims=True))
                blended = jnp.dot(
                    weights.astype(jnp.bfloat16), values, preferred_element_type=jnp.float32
                )
                out[(b + place_ref[0]) % 2, b // 2, :, at] = blended.astype(jnp.bfloat16)
        for i, out_ref in enumerate((same_ref, diff_ref)):
            if earlier:
                out_ref[:, :, :first] = refs[i][...]
            out_ref[:, :, first:] = out[i]

    half = jax.ShapeDtypeStruct((blocks // 2, block_len, first + cols), jnp.bfloat16)
    return call(
        kernel,
        (half, half),
        [place, members, counts],
        [queries, keyvals, more, *earlier],
        scratch=[
            pltpu.VMEM((blocks, block_len, cols), jnp.bfloat16),
            pltpu.VMEM((blocks * per_row, block_len, 2 * cols), jnp.bfloat16),
            pltpu.VMEM((2, blocks // 2, block_len, cols), jnp.bfloat16),
        ],
        flops=4 * blocks * block_len * MAXB * block_len * cols,
        read=16 * blocks * block_len * cols,
    )


def mix(place, attended, w_own, w_across, beside, beside_across, far):
    _, block_len, cols = attended[0].shape
    width = w_own.shape[1]

    def kernel(place_ref, *refs):
        row, group, frame, core = (place_ref[i] for i in range(4))
        w_refs = refs[4:10]
        keep, send, a_all, sums = refs[10:]
        block = 1 - row // 2 if far else row // 2
        for s in range(4):
            a_all[s] = refs[s][block]

        def term(c, other):
            side = 1 - core if other else core
            acc = None
            for i in range(2):
                if c == 0:
                    weight, half = w_refs[other][i * cols : (i + 1) * cols, :], i
                else:
                    weight, half = w_refs[2 + 2 * other + i][:cols], (i + group) % 2
                part = jnp.dot(a_all[(2 * side + half) ^ row], weight, preferred_element_type=jnp.float32)
                acc = part if acc is None else acc + part
            return acc.astype(jnp.bfloat16).astype(jnp.float32)

        for c in range(2):
            sums[...] = (term(c, 0) + term(c, 1)).reshape(2, BS, width)
            at = (row + c) % 2
            keep[at] = sums[frame]
            send[at] = sums[1 - frame].astype(jnp.bfloat16)

    return call(
        kernel,
        (
            jax.ShapeDtypeStruct((2, BS, width), jnp.float32),
            jax.ShapeDtypeStruct((2, BS, width), jnp.bfloat16),
        ),
        [place],
        [*attended, w_own, w_across, *beside, *beside_across],
        scratch=[pltpu.VMEM((4, block_len, cols), jnp.bfloat16), pltpu.VMEM((2, BS, width), jnp.float32)],
        flops=2 * block_len * 4 * cols * 2 * width,
        read=16 * cols * width,
    )


def finish(place, near_keep, near_more, far):
    halves, rows, width = near_keep.shape

    def kernel(place_ref, keep_ref, more_ref, far_ref, out_ref):
        pair = place_ref[0] // 2
        for c in range(halves):
            here = pl.multiple_of((pair * halves + c) * width, width)
            there = pl.multiple_of(((1 - pair) * halves + c) * width, width)
            out_ref[:, pl.ds(here, width)] = (keep_ref[c] + more_ref[c].astype(jnp.float32)).astype(jnp.bfloat16)
            out_ref[:, pl.ds(there, width)] = far_ref[c]

    return call(
        kernel,
        jax.ShapeDtypeStruct((rows, 2 * halves * width), jnp.bfloat16),
        [place],
        [near_keep, near_more, far],
        read=12 * rows * halves * width,
    )


def by_heads(latents, w_qkv, w_out, win_blocks, win_counts, block_window):
    rows_n, heads_n = lax.axis_size("rows"), lax.axis_size("heads")
    group, row = lax.axis_index("groups"), lax.axis_index("rows")
    frame, core = lax.axis_index("frames"), lax.axis_index("heads")
    count = latents.shape[1]
    depth, _, local_cols = w_qkv.shape
    span = rows_n // heads_n
    cols = local_cols // span
    half = depth // 2
    place = jnp.stack([row, group, frame, core]).astype(jnp.int32)

    def reshard(k, *others):
        value = lax.dynamic_slice(
            w_qkv.transpose(1, 0, 2), (0, group * half, (k + row) % span * cols), (3, half, cols)
        )
        pairs = [
            (r * heads_n + h, (h * span + (k + r) % span) * heads_n + r // span)
            for r in range(rows_n)
            for h in range(heads_n)
        ]
        return lax.ppermute(after(value, *others) if others else value, ("rows", "heads"), pairs)

    mine = lax.dynamic_slice_in_dim(latents[0], core * span * depth, span * depth, axis=1)
    mine_x = swap(mine, "frames")
    here, there = [reshard(0)], []
    near = swap(mine, "rows")
    near_x = swap(near, "frames")
    across = swap(after(w_out, near), "heads")
    there.append(swap(here[0], "groups"))
    here.append(reshard(1, near))
    tables = jnp.concatenate([win_blocks, win_counts[:, None], block_window[:, None]], axis=1)
    tables = after(tables, near)
    tables = jnp.pad(tables, ((0, 8 - heads_n), (0, span * depth - MAXB - 2))).astype(mine.dtype)
    joined = jnp.concatenate([mine, tables], axis=0)
    far_2 = swap(after(joined, here[0], mine_x), "rows", 2)
    out_half = lax.dynamic_slice_in_dim(w_out, group * cols, cols, axis=0)
    out_half = jnp.concatenate([out_half, tables[:, : out_half.shape[1]]], axis=0)
    beside = [swap(after(out_half, near), "rows")]
    beside.append(swap(beside[0], "groups"))
    there.append(swap(after(here[1], there[0], beside[1]), "groups"))
    far_2x = swap(far_2, "frames")
    far_3 = swap(after(joined, far_2, across, near_x, beside[0]), "rows", 3)
    far_3x = swap(far_3, "frames")

    found = [tables, beside[0][cols:], far_2[count:], far_3[count:]]
    found = jnp.stack([x[:heads_n, : MAXB + 2] for x in found])
    tables = found.astype(jnp.int32)[row ^ jnp.arange(rows_n)].reshape(rows_n * heads_n, MAXB + 2)
    windows = lax.dynamic_index_in_dim(
        tables[:, MAXB + 1].reshape(rows_n, heads_n), core, axis=1, keepdims=False
    )
    picked = tables[windows]
    members, counts = picked[:, :MAXB].reshape(-1), picked[:, MAXB]

    pieces = [mine, near, far_2, far_3], [mine_x, near_x, far_2x, far_3x]
    chunks = [(here[0], there[0]), (here[1], after(there[1], members, counts))]
    last = cols // (3 * HD) * HD
    first = project(place, *pieces, chunks, 0, cols - last)
    first_more = swap(first[2], "heads")
    chunks[1] = (here[1], after(there[1], first[2]))
    second = project(place, *pieces, chunks, cols - last, last)
    second_more = swap(second[2], "heads")
    attended = attend_all(place, members, counts, *first[:2], first_more)
    beside_across = [swap(part, "heads") for part in beside]
    same, diff = attend_all(place, members, counts, *second[:2], second_more, attended)
    attended = [same] + [swap(same if s % 2 == 0 else diff, "rows", s) for s in range(1, rows_n)]
    weights = w_out, across, beside, beside_across
    far_keep, far_send = mix(place, attended, *weights, True)
    near_keep, near_send = mix(place, attended, *weights, False)
    far_more = swap(far_send, "frames")
    far = swap((far_keep + far_more.astype(jnp.float32)).astype(jnp.bfloat16), "rows", 2)
    near_more = swap(after(near_send, far_more), "frames")
    return finish(place, near_keep, near_more, far)[None]


def local(latents, w_qkv, w_out, win_blocks, win_counts, block_window):
    rows_n = lax.axis_size("rows")
    pairs = all(lax.axis_size(axis) == 2 for axis in ("groups", "frames", "heads"))
    heads_here = w_qkv.shape[2] // HD
    if pairs and rows_n == 4 and heads_here == 6 and latents.shape[:2] == (1, 2 * BS):
        plan = by_heads
    else:
        plan = by_tokens
    return plan(latents, w_qkv, w_out, win_blocks, win_counts, block_window)


def solution(mesh):
    in_specs = (
        P(("groups", "frames"), "rows", None),
        P("rows", None, ("frames", "heads")),
        P(("frames", "heads"), "rows"),
        P(("groups", "rows"), None),
        P(("groups", "rows")),
        P(("groups", "rows")),
    )
    out_specs = P(("groups", "frames"), ("rows", "heads"), None)
    return jax.shard_map(local, mesh=mesh, in_specs=in_specs, out_specs=out_specs, check_vma=False)
```

```python
import math

import jax
import jax.numpy as jnp
from jax import lax
from jax.experimental import pallas as pl
from jax.experimental.pallas import tpu as pltpu
from jax.sharding import PartitionSpec as P

HD = 128
BS = 64
MAXB = 4
VMEM_BYTES = 24 * 1024 * 1024
WHOLE_VMEM_BYTES = 56 * 1024 * 1024
EXP2_SCALE = math.log2(math.e) / math.sqrt(HD)


def with_halo(value, sides, width):
    for axis, dim in sides:
        peers, length = (lax.axis_size(axis), value.shape[dim])
        up = [(i, (i + 1) % peers) for i in range(peers)]
        down = [(j, i) for i, j in up]
        last = lax.slice_in_dim(value, length - width, length, axis=dim)
        first = lax.slice_in_dim(value, 0, width, axis=dim)
        before = lax.ppermute(last, axis, up)
        after = lax.ppermute(first, axis, down)
        value = jnp.concatenate([before, value, after], axis=dim)
    return value


def by_tokens(latents, w_qkv, w_out, win_blocks, win_counts, block_window):
    rows_n = lax.axis_size("rows")
    shard_idx = lax.axis_index("rows")
    frames = latents.shape[0] * lax.axis_size("frames")
    tok_frame = latents.shape[1]
    model_width = latents.shape[2]
    local_cols = w_qkv.shape[2]
    per_shard = tok_frame // BS
    block_total = per_shard * rows_n
    heads_here = local_cols // HD
    block_len = frames * BS
    score_scale = 1.0 / math.sqrt(HD)
    gathered = lax.all_gather(latents, "frames", axis=0, tiled=True)
    flat_tokens = gathered.reshape(frames * tok_frame, model_width)
    weight_rows = lax.all_gather(w_qkv, "rows", axis=0, tiled=True)
    projected = jnp.dot(
        flat_tokens,
        weight_rows.reshape(weight_rows.shape[0], 3 * local_cols),
        preferred_element_type=jnp.float32,
    ).astype(jnp.bfloat16)
    blocked = projected.reshape(frames, per_shard, BS, 3, local_cols).transpose(1, 0, 2, 3, 4)
    blocked = blocked.reshape(per_shard, block_len, 3, local_cols)
    queries = blocked[:, :, 0]
    keyvals = blocked[:, :, 1:]
    nearby = with_halo(keyvals, (("rows", 0),), per_shard)
    first_block = shard_idx * per_shard
    owners = block_window - first_block
    members = win_blocks[owners]
    lengths = win_counts[owners]
    positions = (members - first_block + per_shard + block_total) % block_total

    def attend(query_rows, picked, live_mask):
        key_count = picked.shape[0]
        key_blocks = nearby[picked]
        key_part = key_blocks[:, :, 0].reshape(key_count * block_len, heads_here, HD)
        value_part = key_blocks[:, :, 1].reshape(key_count * block_len, heads_here, HD)
        scores = (
            jnp.einsum(
                "qhd,khd->hqk",
                query_rows.reshape(block_len, heads_here, HD),
                key_part,
                preferred_element_type=jnp.float32,
            )
            * score_scale
        )
        scores = jnp.where(live_mask[None, None, :], scores, -jnp.inf)
        row_max = jnp.max(scores, axis=-1, keepdims=True)
        raised = jnp.exp(scores - row_max)
        weights = (raised / jnp.sum(raised, axis=-1, keepdims=True)).astype(jnp.bfloat16)
        blended = jnp.einsum(
            "hqk,khd->qhd", weights, value_part, preferred_element_type=jnp.float32
        )
        return blended.reshape(block_len, local_cols).astype(jnp.bfloat16)

    def one_block(block_item):
        query_rows, picked, length = block_item
        live_mask = jnp.repeat(jnp.arange(MAXB) < length, block_len)
        return attend(query_rows, picked, live_mask)

    attended = lax.map(one_block, (queries, positions, lengths))
    ordered = attended.reshape(per_shard, frames, BS, local_cols).transpose(1, 0, 2, 3)
    ordered = ordered.reshape(frames * tok_frame, local_cols)
    w_full = lax.all_gather(w_out, "rows", axis=1, tiled=True)
    group_count = lax.axis_size(("frames", "heads"))
    out_rows = frames * tok_frame // group_count
    summed = lax.psum_scatter(
        jnp.dot(ordered, w_full, preferred_element_type=jnp.float32).astype(jnp.bfloat16),
        ("frames", "heads"),
        scatter_dimension=0,
        tiled=True,
    )
    return summed.reshape(1, out_rows, model_width)


def swap(value, axis, step=1):
    peers = lax.axis_size(axis)
    return lax.ppermute(value, axis, [(i, i ^ step) for i in range(peers)])


def after(value, *others):
    return lax.optimization_barrier((value, *others))[0]


def call(kernel, out_shape, prefetch, operands, scratch=(), flops=0, read=0, limit=VMEM_BYTES):
    return pl.pallas_call(
        kernel,
        out_shape=out_shape,
        grid_spec=pltpu.PrefetchScalarGridSpec(
            num_scalar_prefetch=len(prefetch),
            grid=(),
            in_specs=[pl.BlockSpec(memory_space=pltpu.VMEM)] * len(operands),
            out_specs=jax.tree.map(lambda _: pl.BlockSpec(memory_space=pltpu.VMEM), out_shape),
            scratch_shapes=scratch,
        ),
        compiler_params=pltpu.CompilerParams(vmem_limit_bytes=limit),
        cost_estimate=pl.CostEstimate(flops=flops, bytes_accessed=read, transcendentals=0),
    )(*prefetch, *operands)


def project(place, mine, theirs, chunks, first, cols):
    rows, (count, width) = len(mine), theirs[0].shape
    half = chunks[0][0].shape[1]
    slices = len(chunks)
    flat = [w for of_round in chunks for w in of_round]
    fetched = 2 * rows + len(flat)

    def kernel(place_ref, *refs):
        row, group, frame, core = (place_ref[i] for i in range(4))
        w_refs = refs[2 * rows : fetched]
        q_keep, kv_keep, send, x_all, w_all, total, sems = refs[fetched:]
        copies = []
        for k in range(slices):
            for g in range(2):
                at = pl.multiple_of((row + slices - k) % slices * (2 * half) + (group + g) % 2 * half, half)
                for part in range(3):
                    source = w_refs[2 * k + g].at[part, :, first : first + cols]
                    into = w_all.at[pl.ds(at, half), part * cols : (part + 1) * cols]
                    copies.append(pltpu.make_async_copy(source, into, sems.at[len(copies)]))
        fetch_x = []
        for i in range(2 * rows):
            to = x_all.at[row ^ (i % rows), (frame + i // rows) % 2]
            fetch_x.append(pltpu.make_async_copy(refs[i].at[pl.ds(0, count)], to, sems.at[len(copies) + i]))
        for copy in copies + fetch_x:
            copy.start()
        for copy in copies:
            copy.wait()
        for s in range(rows):
            fetch_x[s].wait()
            fetch_x[rows + s].wait()
            at = row ^ s
            acc = jnp.dot(x_all[at].reshape(-1, width), w_all[...], preferred_element_type=jnp.float32)
            kv_part = acc[:, cols:]
            kv_keep[at] = kv_part
            send[at, : 2 * count, :] = kv_part.astype(jnp.bfloat16)
            total[s] = acc[:, :cols].reshape(2, count, cols)
            own = pl.multiple_of(core * BS, BS)
            other = pl.multiple_of((1 - core) * BS, BS)
            q_keep[at] = total[s, :, pl.ds(own, BS), :].reshape(2 * BS, cols)
            for f in range(2):
                where = slice(f * cols, (f + 1) * cols)
                send[at, 2 * count :, where] = total[s, f, pl.ds(other, BS), :].astype(jnp.bfloat16)

    vmem, hbm = pl.BlockSpec(memory_space=pltpu.VMEM), pl.BlockSpec(memory_space=pltpu.HBM)
    flops = 2 * rows * 2 * count * width * 3 * cols
    return pl.pallas_call(
        kernel,
        out_shape=(
            jax.ShapeDtypeStruct((rows, 2 * BS, cols), jnp.float32),
            jax.ShapeDtypeStruct((rows, 2 * count, 2 * cols), jnp.float32),
            jax.ShapeDtypeStruct((rows, 2 * count + BS, 2 * cols), jnp.bfloat16),
        ),
        grid_spec=pltpu.PrefetchScalarGridSpec(
            num_scalar_prefetch=1,
            grid=(),
            in_specs=[hbm] * fetched,
            out_specs=(vmem, vmem, vmem),
            scratch_shapes=[
                pltpu.VMEM((rows, 2, count, width), jnp.bfloat16),
                pltpu.VMEM((width, 3 * cols), jnp.bfloat16),
                pltpu.VMEM((rows, 2, count, cols), jnp.float32),
                pltpu.SemaphoreType.DMA((2 * rows + 3 * len(flat),)),
            ],
        ),
        compiler_params=pltpu.CompilerParams(vmem_limit_bytes=VMEM_BYTES),
        cost_estimate=pl.CostEstimate(flops=8 * flops, bytes_accessed=flops // 300, transcendentals=0),
    )(place, *mine, *theirs, *flat)


def attend_all(place, members, counts, queries, keyvals, more, earlier=()):
    blocks, block_len, cols = queries.shape
    first = earlier[0].shape[2] if earlier else 0
    rows = keyvals.shape[1]
    per_row = rows // block_len

    def kernel(place_ref, members_ref, counts_ref, q_ref, kv_ref, more_ref, *refs):
        same_ref, diff_ref, q_sum, kv_sum, out = refs[len(earlier) :]
        for r in range(blocks):
            added = more_ref[r, rows:, :].astype(jnp.float32)
            added = jnp.concatenate([added[:, :cols], added[:, cols:]], axis=0)
            q_sum[r] = (q_ref[r] + added).astype(jnp.bfloat16)
            both = (kv_ref[r] + more_ref[r, :rows, :].astype(jnp.float32)).astype(jnp.bfloat16)
            both = both.reshape(2, rows // 2, 2 * cols)
            for j in range(per_row):
                part = both[:, j * BS : (j + 1) * BS, :]
                kv_sum[r * per_row + j] = part.reshape(block_len, 2 * cols)
        column = lax.broadcasted_iota(jnp.int32, (block_len, MAXB * block_len), 1)
        for b in range(blocks):
            live = column < counts_ref[b] * block_len
            listed = [kv_sum.at[members_ref[b * MAXB + j]] for j in range(MAXB)]
            for h in range(cols // HD):
                at = slice(h * HD, (h + 1) * HD)
                at_v = slice(cols + h * HD, cols + (h + 1) * HD)
                keys = jnp.concatenate([block[:, at] for block in listed], axis=0)
                values = jnp.concatenate([block[:, at_v] for block in listed], axis=0)
                scores = lax.dot_general(
                    q_sum[b, :, at], keys, (((1,), (1,)), ((), ())), preferred_element_type=jnp.float32
                )
                scores = jnp.where(live, scores, -jnp.inf)
                raised = jnp.exp2((scores - jnp.max(scores, axis=-1, keepdims=True)) * EXP2_SCALE)
                weights = raised * (1.0 / jnp.sum(raised, axis=-1, keepdims=True))
                blended = jnp.dot(
                    weights.astype(jnp.bfloat16), values, preferred_element_type=jnp.float32
                )
                out[(b + place_ref[0]) % 2, b // 2, :, at] = blended.astype(jnp.bfloat16)
        for i, out_ref in enumerate((same_ref, diff_ref)):
            if earlier:
                out_ref[:, :, :first] = refs[i][...]
            out_ref[:, :, first:] = out[i]

    half = jax.ShapeDtypeStruct((blocks // 2, block_len, first + cols), jnp.bfloat16)
    return call(
        kernel,
        (half, half),
        [place, members, counts],
        [queries, keyvals, more, *earlier],
        scratch=[
            pltpu.VMEM((blocks, block_len, cols), jnp.bfloat16),
            pltpu.VMEM((blocks * per_row, block_len, 2 * cols), jnp.bfloat16),
            pltpu.VMEM((2, blocks // 2, block_len, cols), jnp.bfloat16),
        ],
        flops=4 * blocks * block_len * MAXB * block_len * cols,
        read=16 * blocks * block_len * cols,
    )


def mix(place, attended, w_own, w_across, beside, beside_across, far):
    _, block_len, cols = attended[0].shape
    width = w_own.shape[1]

    def kernel(place_ref, *refs):
        row, group, frame, core = (place_ref[i] for i in range(4))
        w_refs = refs[4:10]
        keep, send, a_all, sums = refs[10:]
        block = 1 - row // 2 if far else row // 2
        for s in range(4):
            a_all[s] = refs[s][block]

        def term(c, other):
            side = 1 - core if other else core
            acc = None
            for i in range(2):
                if c == 0:
                    weight, half = w_refs[other][i * cols : (i + 1) * cols, :], i
                else:
                    weight, half = w_refs[2 + 2 * other + i][...], (i + group) % 2
                part = jnp.dot(a_all[(2 * side + half) ^ row], weight, preferred_element_type=jnp.float32)
                acc = part if acc is None else acc + part
            return acc.astype(jnp.bfloat16).astype(jnp.float32)

        for c in range(2):
            sums[...] = (term(c, 0) + term(c, 1)).reshape(2, BS, width)
            at = (row + c) % 2
            keep[at] = sums[frame]
            send[at] = sums[1 - frame].astype(jnp.bfloat16)

    return call(
        kernel,
        (
            jax.ShapeDtypeStruct((2, BS, width), jnp.float32),
            jax.ShapeDtypeStruct((2, BS, width), jnp.bfloat16),
        ),
        [place],
        [*attended, w_own, w_across, *beside, *beside_across],
        scratch=[pltpu.VMEM((4, block_len, cols), jnp.bfloat16), pltpu.VMEM((2, BS, width), jnp.float32)],
        flops=2 * block_len * 4 * cols * 2 * width,
        read=16 * cols * width,
    )


def finish(place, near_keep, near_more, far):
    halves, rows, width = near_keep.shape

    def kernel(place_ref, keep_ref, more_ref, far_ref, out_ref):
        pair = place_ref[0] // 2
        for c in range(halves):
            here = pl.multiple_of((pair * halves + c) * width, width)
            there = pl.multiple_of(((1 - pair) * halves + c) * width, width)
            out_ref[:, pl.ds(here, width)] = (keep_ref[c] + more_ref[c].astype(jnp.float32)).astype(jnp.bfloat16)
            out_ref[:, pl.ds(there, width)] = far_ref[c]

    return call(
        kernel,
        jax.ShapeDtypeStruct((rows, 2 * halves * width), jnp.bfloat16),
        [place],
        [near_keep, near_more, far],
        read=12 * rows * halves * width,
    )


def by_heads(latents, w_qkv, w_out, win_blocks, win_counts, block_window):
    rows_n, heads_n = lax.axis_size("rows"), lax.axis_size("heads")
    group, row = lax.axis_index("groups"), lax.axis_index("rows")
    frame, core = lax.axis_index("frames"), lax.axis_index("heads")
    count = latents.shape[1]
    depth, _, local_cols = w_qkv.shape
    span = rows_n // heads_n
    cols = local_cols // span
    half = depth // 2
    place = jnp.stack([row, group, frame, core]).astype(jnp.int32)

    def reshard(k, *others):
        value = lax.dynamic_slice(
            w_qkv.transpose(1, 0, 2), (0, group * half, (k + row) % span * cols), (3, half, cols)
        )
        pairs = [
            (r * heads_n + h, (h * span + (k + r) % span) * heads_n + r // span)
            for r in range(rows_n)
            for h in range(heads_n)
        ]
        return lax.ppermute(after(value, *others) if others else value, ("rows", "heads"), pairs)

    mine = lax.dynamic_slice_in_dim(latents[0], core * span * depth, span * depth, axis=1)
    mine_x = swap(mine, "frames")
    here, there = [reshard(0)], []
    tables = jnp.concatenate([win_blocks, win_counts[:, None], block_window[:, None]], axis=1)
    tables = jnp.pad(tables, ((0, 8 - heads_n), (0, span * depth - MAXB - 2))).astype(mine.dtype)
    joined = jnp.concatenate([mine, tables], axis=0)
    near = swap(joined, "rows")
    near_x = swap(near, "frames")
    across = swap(after(w_out, near), "heads")
    there.append(swap(here[0], "groups"))
    here.append(reshard(1, near))
    far_2 = swap(after(joined, here[0], mine_x), "rows", 2)
    there.append(swap(after(here[1], there[0]), "groups"))
    far_2x = swap(far_2, "frames")
    far_3 = swap(after(joined, far_2, across, near_x), "rows", 3)
    far_3x = swap(far_3, "frames")
    out_half = lax.dynamic_slice_in_dim(w_out, group * cols, cols, axis=0)
    beside = [swap(after(out_half, far_3), "rows")]
    beside.append(swap(beside[0], "groups"))

    found = jnp.stack([x[count : count + heads_n, : MAXB + 2] for x in (joined, near, far_2, far_3)])
    tables = found.astype(jnp.int32)[row ^ jnp.arange(rows_n)].reshape(rows_n * heads_n, MAXB + 2)
    windows = lax.dynamic_index_in_dim(
        tables[:, MAXB + 1].reshape(rows_n, heads_n), core, axis=1, keepdims=False
    )
    picked = tables[windows]
    members, counts = picked[:, :MAXB].reshape(-1), picked[:, MAXB]

    pieces = [joined, near, far_2, far_3], [mine_x, near_x, far_2x, far_3x]
    chunks = [(here[0], there[0]), (here[1], after(there[1], members, counts))]
    last = cols // (3 * HD) * HD
    first = project(place, *pieces, chunks, 0, cols - last)
    first_more = swap(first[2], "heads")
    chunks[1] = (here[1], after(there[1], first[2]))
    second = project(place, *pieces, chunks, cols - last, last)
    second_more = swap(second[2], "heads")
    attended = attend_all(place, members, counts, *first[:2], first_more)
    beside_across = [swap(part, "heads") for part in beside]
    same, diff = attend_all(place, members, counts, *second[:2], second_more, attended)
    attended = [same] + [swap(same if s % 2 == 0 else diff, "rows", s) for s in range(1, rows_n)]
    weights = w_out, across, beside, beside_across
    far_keep, far_send = mix(place, attended, *weights, True)
    near_keep, near_send = mix(place, attended, *weights, False)
    far_more = swap(far_send, "frames")
    far = swap((far_keep + far_more.astype(jnp.float32)).astype(jnp.bfloat16), "rows", 2)
    near_more = swap(after(near_send, far_more), "frames")
    return finish(place, near_keep, near_more, far)[None]


def local(latents, w_qkv, w_out, win_blocks, win_counts, block_window):
    rows_n = lax.axis_size("rows")
    pairs = all(lax.axis_size(axis) == 2 for axis in ("groups", "frames", "heads"))
    heads_here = w_qkv.shape[2] // HD
    if pairs and rows_n == 4 and heads_here == 6 and latents.shape[:2] == (1, 2 * BS):
        plan = by_heads
    else:
        plan = by_tokens
    return plan(latents, w_qkv, w_out, win_blocks, win_counts, block_window)


def solution(mesh):
    in_specs = (
        P(("groups", "frames"), "rows", None),
        P("rows", None, ("frames", "heads")),
        P(("frames", "heads"), "rows"),
        P(("groups", "rows"), None),
        P(("groups", "rows")),
        P(("groups", "rows")),
    )
    out_specs = P(("groups", "frames"), ("rows", "heads"), None)
    return jax.shard_map(local, mesh=mesh, in_specs=in_specs, out_specs=out_specs, check_vma=False)
```

```python
import math

import jax
import jax.numpy as jnp
from jax import lax
from jax.experimental import pallas as pl
from jax.experimental.pallas import tpu as pltpu
from jax.sharding import PartitionSpec as P

HD = 128
BS = 64
MAXB = 4
VMEM_BYTES = 24 * 1024 * 1024
WHOLE_VMEM_BYTES = 56 * 1024 * 1024
EXP2_SCALE = math.log2(math.e) / math.sqrt(HD)


def with_halo(value, sides, width):
    for axis, dim in sides:
        peers, length = (lax.axis_size(axis), value.shape[dim])
        up = [(i, (i + 1) % peers) for i in range(peers)]
        down = [(j, i) for i, j in up]
        last = lax.slice_in_dim(value, length - width, length, axis=dim)
        first = lax.slice_in_dim(value, 0, width, axis=dim)
        before = lax.ppermute(last, axis, up)
        after = lax.ppermute(first, axis, down)
        value = jnp.concatenate([before, value, after], axis=dim)
    return value


def by_tokens(latents, w_qkv, w_out, win_blocks, win_counts, block_window):
    rows_n = lax.axis_size("rows")
    shard_idx = lax.axis_index("rows")
    frames = latents.shape[0] * lax.axis_size("frames")
    tok_frame = latents.shape[1]
    model_width = latents.shape[2]
    local_cols = w_qkv.shape[2]
    per_shard = tok_frame // BS
    block_total = per_shard * rows_n
    heads_here = local_cols // HD
    block_len = frames * BS
    score_scale = 1.0 / math.sqrt(HD)
    gathered = lax.all_gather(latents, "frames", axis=0, tiled=True)
    flat_tokens = gathered.reshape(frames * tok_frame, model_width)
    weight_rows = lax.all_gather(w_qkv, "rows", axis=0, tiled=True)
    projected = jnp.dot(
        flat_tokens,
        weight_rows.reshape(weight_rows.shape[0], 3 * local_cols),
        preferred_element_type=jnp.float32,
    ).astype(jnp.bfloat16)
    blocked = projected.reshape(frames, per_shard, BS, 3, local_cols).transpose(1, 0, 2, 3, 4)
    blocked = blocked.reshape(per_shard, block_len, 3, local_cols)
    queries = blocked[:, :, 0]
    keyvals = blocked[:, :, 1:]
    nearby = with_halo(keyvals, (("rows", 0),), per_shard)
    first_block = shard_idx * per_shard
    owners = block_window - first_block
    members = win_blocks[owners]
    lengths = win_counts[owners]
    positions = (members - first_block + per_shard + block_total) % block_total

    def attend(query_rows, picked, live_mask):
        key_count = picked.shape[0]
        key_blocks = nearby[picked]
        key_part = key_blocks[:, :, 0].reshape(key_count * block_len, heads_here, HD)
        value_part = key_blocks[:, :, 1].reshape(key_count * block_len, heads_here, HD)
        scores = (
            jnp.einsum(
                "qhd,khd->hqk",
                query_rows.reshape(block_len, heads_here, HD),
                key_part,
                preferred_element_type=jnp.float32,
            )
            * score_scale
        )
        scores = jnp.where(live_mask[None, None, :], scores, -jnp.inf)
        row_max = jnp.max(scores, axis=-1, keepdims=True)
        raised = jnp.exp(scores - row_max)
        weights = (raised / jnp.sum(raised, axis=-1, keepdims=True)).astype(jnp.bfloat16)
        blended = jnp.einsum(
            "hqk,khd->qhd", weights, value_part, preferred_element_type=jnp.float32
        )
        return blended.reshape(block_len, local_cols).astype(jnp.bfloat16)

    def one_block(block_item):
        query_rows, picked, length = block_item
        live_mask = jnp.repeat(jnp.arange(MAXB) < length, block_len)
        return attend(query_rows, picked, live_mask)

    attended = lax.map(one_block, (queries, positions, lengths))
    ordered = attended.reshape(per_shard, frames, BS, local_cols).transpose(1, 0, 2, 3)
    ordered = ordered.reshape(frames * tok_frame, local_cols)
    w_full = lax.all_gather(w_out, "rows", axis=1, tiled=True)
    group_count = lax.axis_size(("frames", "heads"))
    out_rows = frames * tok_frame // group_count
    summed = lax.psum_scatter(
        jnp.dot(ordered, w_full, preferred_element_type=jnp.float32).astype(jnp.bfloat16),
        ("frames", "heads"),
        scatter_dimension=0,
        tiled=True,
    )
    return summed.reshape(1, out_rows, model_width)


def swap(value, axis, step=1):
    peers = lax.axis_size(axis)
    return lax.ppermute(value, axis, [(i, i ^ step) for i in range(peers)])


def after(value, *others):
    return lax.optimization_barrier((value, *others))[0]


def call(kernel, out_shape, prefetch, operands, scratch=(), flops=0, read=0, limit=VMEM_BYTES):
    return pl.pallas_call(
        kernel,
        out_shape=out_shape,
        grid_spec=pltpu.PrefetchScalarGridSpec(
            num_scalar_prefetch=len(prefetch),
            grid=(),
            in_specs=[pl.BlockSpec(memory_space=pltpu.VMEM)] * len(operands),
            out_specs=jax.tree.map(lambda _: pl.BlockSpec(memory_space=pltpu.VMEM), out_shape),
            scratch_shapes=scratch,
        ),
        compiler_params=pltpu.CompilerParams(vmem_limit_bytes=limit),
        cost_estimate=pl.CostEstimate(flops=flops, bytes_accessed=read, transcendentals=0),
    )(*prefetch, *operands)


def project(place, mine, theirs, chunks, first, cols):
    rows, (count, width) = len(mine) - 1, theirs[0].shape
    half = chunks[0][0].shape[1]
    slices = len(chunks)
    flat = [w for of_round in chunks for w in of_round]
    fetched = 2 * len(mine) + len(flat)

    def kernel(place_ref, *refs):
        row, group, frame, core = (place_ref[i] for i in range(4))
        w_refs = refs[2 * len(mine) : fetched]
        q_keep, kv_keep, send, x_all, w_all, total, sems = refs[fetched:]
        copies = []
        for k in range(slices):
            for g in range(2):
                at = pl.multiple_of((row + slices - k) % slices * (2 * half) + (group + g) % 2 * half, half)
                for part in range(3):
                    source = w_refs[2 * k + g].at[part, :, first : first + cols]
                    into = w_all.at[pl.ds(at, half), part * cols : (part + 1) * cols]
                    copies.append(pltpu.make_async_copy(source, into, sems.at[len(copies)]))
        for copy in copies:
            copy.start()
        middle = (row == 1) | (row == 2)
        fetch_x = []
        for i in range(2 * rows):
            f, s = divmod(i, rows)
            to, sem = x_all.at[row ^ s, (frame + f) % 2], sems.at[len(copies) + i]
            x_refs = refs[f * len(mine) : (f + 1) * len(mine)]
            fetch_x.append(pltpu.make_async_copy(x_refs[s].at[pl.ds(0, count)], to, sem))
            if s < rows - 1:
                fetch_x[-1].start()
            else:
                other = pltpu.make_async_copy(x_refs[rows].at[pl.ds(0, count)], to, sem)
                pl.when(middle)(fetch_x[-1].start)
                pl.when(jnp.logical_not(middle))(other.start)
        for copy in copies:
            copy.wait()
        for s in range(rows):
            fetch_x[s].wait()
            fetch_x[rows + s].wait()
            at = row ^ s
            acc = jnp.dot(x_all[at].reshape(-1, width), w_all[...], preferred_element_type=jnp.float32)
            kv_part = acc[:, cols:]
            kv_keep[at] = kv_part
            send[at, : 2 * count, :] = kv_part.astype(jnp.bfloat16)
            total[s] = acc[:, :cols].reshape(2, count, cols)
            own = pl.multiple_of(core * BS, BS)
            other = pl.multiple_of((1 - core) * BS, BS)
            q_keep[at] = total[s, :, pl.ds(own, BS), :].reshape(2 * BS, cols)
            for f in range(2):
                where = slice(f * cols, (f + 1) * cols)
                send[at, 2 * count :, where] = total[s, f, pl.ds(other, BS), :].astype(jnp.bfloat16)

    vmem, hbm = pl.BlockSpec(memory_space=pltpu.VMEM), pl.BlockSpec(memory_space=pltpu.HBM)
    flops = 2 * rows * 2 * count * width * 3 * cols
    return pl.pallas_call(
        kernel,
        out_shape=(
            jax.ShapeDtypeStruct((rows, 2 * BS, cols), jnp.float32),
            jax.ShapeDtypeStruct((rows, 2 * count, 2 * cols), jnp.float32),
            jax.ShapeDtypeStruct((rows, 2 * count + BS, 2 * cols), jnp.bfloat16),
        ),
        grid_spec=pltpu.PrefetchScalarGridSpec(
            num_scalar_prefetch=1,
            grid=(),
            in_specs=[hbm] * fetched,
            out_specs=(vmem, vmem, vmem),
            scratch_shapes=[
                pltpu.VMEM((rows, 2, count, width), jnp.bfloat16),
                pltpu.VMEM((width, 3 * cols), jnp.bfloat16),
                pltpu.VMEM((rows, 2, count, cols), jnp.float32),
                pltpu.SemaphoreType.DMA((2 * rows + 3 * len(flat),)),
            ],
        ),
        compiler_params=pltpu.CompilerParams(vmem_limit_bytes=VMEM_BYTES),
        cost_estimate=pl.CostEstimate(flops=8 * flops, bytes_accessed=flops // 300, transcendentals=0),
    )(place, *mine, *theirs, *flat)


def attend_all(place, members, counts, queries, keyvals, more, earlier=()):
    blocks, block_len, cols = queries.shape
    first = earlier[0].shape[2] if earlier else 0
    rows = keyvals.shape[1]
    per_row = rows // block_len

    def kernel(place_ref, members_ref, counts_ref, q_ref, kv_ref, more_ref, *refs):
        same_ref, diff_ref, q_sum, kv_sum, out = refs[len(earlier) :]
        for r in range(blocks):
            added = more_ref[r, rows:, :].astype(jnp.float32)
            added = jnp.concatenate([added[:, :cols], added[:, cols:]], axis=0)
            q_sum[r] = (q_ref[r] + added).astype(jnp.bfloat16)
            both = (kv_ref[r] + more_ref[r, :rows, :].astype(jnp.float32)).astype(jnp.bfloat16)
            both = both.reshape(2, rows // 2, 2 * cols)
            for j in range(per_row):
                part = both[:, j * BS : (j + 1) * BS, :]
                kv_sum[r * per_row + j] = part.reshape(block_len, 2 * cols)
        column = lax.broadcasted_iota(jnp.int32, (block_len, MAXB * block_len), 1)
        for b in range(blocks):
            live = column < counts_ref[b] * block_len
            listed = [kv_sum.at[members_ref[b * MAXB + j]] for j in range(MAXB)]
            for h in range(cols // HD):
                at = slice(h * HD, (h + 1) * HD)
                at_v = slice(cols + h * HD, cols + (h + 1) * HD)
                keys = jnp.concatenate([block[:, at] for block in listed], axis=0)
                values = jnp.concatenate([block[:, at_v] for block in listed], axis=0)
                scores = lax.dot_general(
                    q_sum[b, :, at], keys, (((1,), (1,)), ((), ())), preferred_element_type=jnp.float32
                )
                scores = jnp.where(live, scores, -jnp.inf)
                raised = jnp.exp2((scores - jnp.max(scores, axis=-1, keepdims=True)) * EXP2_SCALE)
                weights = raised * (1.0 / jnp.sum(raised, axis=-1, keepdims=True))
                blended = jnp.dot(
                    weights.astype(jnp.bfloat16), values, preferred_element_type=jnp.float32
                )
                out[(b + place_ref[0]) % 2, b // 2, :, at] = blended.astype(jnp.bfloat16)
        for i, out_ref in enumerate((same_ref, diff_ref)):
            if earlier:
                out_ref[:, :, :first] = refs[i][...]
            out_ref[:, :, first:] = out[i]

    half = jax.ShapeDtypeStruct((blocks // 2, block_len, first + cols), jnp.bfloat16)
    return call(
        kernel,
        (half, half),
        [place, members, counts],
        [queries, keyvals, more, *earlier],
        scratch=[
            pltpu.VMEM((blocks, block_len, cols), jnp.bfloat16),
            pltpu.VMEM((blocks * per_row, block_len, 2 * cols), jnp.bfloat16),
            pltpu.VMEM((2, blocks // 2, block_len, cols), jnp.bfloat16),
        ],
        flops=4 * blocks * block_len * MAXB * block_len * cols,
        read=16 * blocks * block_len * cols,
    )


def mix(place, attended, w_own, w_across, beside, beside_across, far):
    _, block_len, cols = attended[0].shape
    width = w_own.shape[1]

    def kernel(place_ref, *refs):
        row, group, frame, core = (place_ref[i] for i in range(4))
        w_refs = refs[4:10]
        keep, send, a_all, sums = refs[10:]
        block = 1 - row // 2 if far else row // 2
        for s in range(4):
            a_all[s] = refs[s][block]

        def term(c, other):
            side = 1 - core if other else core
            acc = None
            for i in range(2):
                if c == 0:
                    weight, half = w_refs[other][i * cols : (i + 1) * cols, :], i
                else:
                    weight, half = w_refs[2 + 2 * other + i][:cols], (i + group) % 2
                part = jnp.dot(a_all[(2 * side + half) ^ row], weight, preferred_element_type=jnp.float32)
                acc = part if acc is None else acc + part
            return acc.astype(jnp.bfloat16).astype(jnp.float32)

        for c in range(2):
            sums[...] = (term(c, 0) + term(c, 1)).reshape(2, BS, width)
            at = (row + c) % 2
            keep[at] = sums[frame]
            send[at] = sums[1 - frame].astype(jnp.bfloat16)

    return call(
        kernel,
        (
            jax.ShapeDtypeStruct((2, BS, width), jnp.float32),
            jax.ShapeDtypeStruct((2, BS, width), jnp.bfloat16),
        ),
        [place],
        [*attended, w_own, w_across, *beside, *beside_across],
        scratch=[pltpu.VMEM((4, block_len, cols), jnp.bfloat16), pltpu.VMEM((2, BS, width), jnp.float32)],
        flops=2 * block_len * 4 * cols * 2 * width,
        read=16 * cols * width,
    )


def finish(place, near_keep, near_more, far):
    halves, rows, width = near_keep.shape

    def kernel(place_ref, keep_ref, more_ref, far_ref, out_ref):
        pair = place_ref[0] // 2
        for c in range(halves):
            here = pl.multiple_of((pair * halves + c) * width, width)
            there = pl.multiple_of(((1 - pair) * halves + c) * width, width)
            out_ref[:, pl.ds(here, width)] = (keep_ref[c] + more_ref[c].astype(jnp.float32)).astype(jnp.bfloat16)
            out_ref[:, pl.ds(there, width)] = far_ref[c]

    return call(
        kernel,
        jax.ShapeDtypeStruct((rows, 2 * halves * width), jnp.bfloat16),
        [place],
        [near_keep, near_more, far],
        read=12 * rows * halves * width,
    )


def by_heads(latents, w_qkv, w_out, win_blocks, win_counts, block_window):
    rows_n, heads_n = lax.axis_size("rows"), lax.axis_size("heads")
    group, row = lax.axis_index("groups"), lax.axis_index("rows")
    frame, core = lax.axis_index("frames"), lax.axis_index("heads")
    count = latents.shape[1]
    depth, _, local_cols = w_qkv.shape
    span = rows_n // heads_n
    cols = local_cols // span
    half = depth // 2
    place = jnp.stack([row, group, frame, core]).astype(jnp.int32)

    def over_frames(value, rows):
        pairs = [(2 * r + f, 2 * r + 1 - f) for r in rows for f in range(2)]
        return lax.ppermute(value, ("rows", "frames"), pairs)

    def reshard(k, *others):
        value = lax.dynamic_slice(
            w_qkv.transpose(1, 0, 2), (0, group * half, (k + row) % span * cols), (3, half, cols)
        )
        pairs = [
            (r * heads_n + h, (h * span + (k + r) % span) * heads_n + r // span)
            for r in range(rows_n)
            for h in range(heads_n)
        ]
        return lax.ppermute(after(value, *others) if others else value, ("rows", "heads"), pairs)

    mine = lax.dynamic_slice_in_dim(latents[0], core * span * depth, span * depth, axis=1)
    mine_x = swap(mine, "frames")
    here, there = [reshard(0)], []
    near = swap(mine, "rows")
    near_x = swap(near, "frames")
    across = swap(after(w_out, near), "heads")
    there.append(swap(here[0], "groups"))
    here.append(reshard(1, near))
    tables = jnp.concatenate([win_blocks, win_counts[:, None], block_window[:, None]], axis=1)
    tables = after(tables, near)
    tables = jnp.pad(tables, ((0, 8 - heads_n), (0, span * depth - MAXB - 2))).astype(mine.dtype)
    joined = jnp.concatenate([mine, tables], axis=0)
    in_3 = lax.ppermute(joined, "rows", [(1, 2), (2, 1)])
    far_2 = swap(after(joined, here[0], mine_x, in_3), "rows", 2)
    out_half = lax.dynamic_slice_in_dim(w_out, group * cols, cols, axis=0)
    out_half = jnp.concatenate([out_half, tables[:, : out_half.shape[1]]], axis=0)
    beside = [swap(after(out_half, near), "rows")]
    beside.append(swap(beside[0], "groups"))
    there.append(swap(after(here[1], there[0], beside[1]), "groups"))
    far_2x = swap(far_2, "frames")
    in_3x = over_frames(in_3, (1, 2))
    out_3 = after(far_2, across, near_x, beside[0], in_3x)
    out_3 = lax.ppermute(out_3, "rows", [(1, 0), (2, 3)])
    out_3x = over_frames(out_3, (0, 3))

    extra = jnp.where((row == 1) | (row == 2), in_3[count:], out_3[count:])
    found = [tables, beside[0][cols:], far_2[count:], extra]
    found = jnp.stack([x[:heads_n, : MAXB + 2] for x in found])
    tables = found.astype(jnp.int32)[row ^ jnp.arange(rows_n)].reshape(rows_n * heads_n, MAXB + 2)
    windows = lax.dynamic_index_in_dim(
        tables[:, MAXB + 1].reshape(rows_n, heads_n), core, axis=1, keepdims=False
    )
    picked = tables[windows]
    members, counts = picked[:, :MAXB].reshape(-1), picked[:, MAXB]

    pieces = [mine, near, far_2, in_3, out_3], [mine_x, near_x, far_2x, in_3x, out_3x]
    chunks = [(here[0], there[0]), (here[1], after(there[1], members, counts))]
    last = cols // (3 * HD) * HD
    first = project(place, *pieces, chunks, 0, cols - last)
    first_more = swap(first[2], "heads")
    chunks[1] = (here[1], after(there[1], first[2]))
    second = project(place, *pieces, chunks, cols - last, last)
    second_more = swap(second[2], "heads")
    attended = attend_all(place, members, counts, *first[:2], first_more)
    beside_across = [swap(part, "heads") for part in beside]
    same, diff = attend_all(place, members, counts, *second[:2], second_more, attended)
    attended = [same] + [swap(same if s % 2 == 0 else diff, "rows", s) for s in range(1, rows_n)]
    weights = w_out, across, beside, beside_across
    far_keep, far_send = mix(place, attended, *weights, True)
    near_keep, near_send = mix(place, attended, *weights, False)
    far_more = swap(far_send, "frames")
    far = swap((far_keep + far_more.astype(jnp.float32)).astype(jnp.bfloat16), "rows", 2)
    near_more = swap(after(near_send, far_more), "frames")
    return finish(place, near_keep, near_more, far)[None]


def local(latents, w_qkv, w_out, win_blocks, win_counts, block_window):
    rows_n = lax.axis_size("rows")
    pairs = all(lax.axis_size(axis) == 2 for axis in ("groups", "frames", "heads"))
    heads_here = w_qkv.shape[2] // HD
    if pairs and rows_n == 4 and heads_here == 6 and latents.shape[:2] == (1, 2 * BS):
        plan = by_heads
    else:
        plan = by_tokens
    return plan(latents, w_qkv, w_out, win_blocks, win_counts, block_window)


def solution(mesh):
    in_specs = (
        P(("groups", "frames"), "rows", None),
        P("rows", None, ("frames", "heads")),
        P(("frames", "heads"), "rows"),
        P(("groups", "rows"), None),
        P(("groups", "rows")),
        P(("groups", "rows")),
    )
    out_specs = P(("groups", "frames"), ("rows", "heads"), None)
    return jax.shard_map(local, mesh=mesh, in_specs=in_specs, out_specs=out_specs, check_vma=False)
```

```python
import math

import jax
import jax.numpy as jnp
from jax import lax
from jax.experimental import pallas as pl
from jax.experimental.pallas import tpu as pltpu
from jax.sharding import PartitionSpec as P

HD = 128
BS = 64
MAXB = 4
VMEM_BYTES = 24 * 1024 * 1024
WHOLE_VMEM_BYTES = 56 * 1024 * 1024
EXP2_SCALE = math.log2(math.e) / math.sqrt(HD)


def with_halo(value, sides, width):
    for axis, dim in sides:
        peers, length = (lax.axis_size(axis), value.shape[dim])
        up = [(i, (i + 1) % peers) for i in range(peers)]
        down = [(j, i) for i, j in up]
        last = lax.slice_in_dim(value, length - width, length, axis=dim)
        first = lax.slice_in_dim(value, 0, width, axis=dim)
        before = lax.ppermute(last, axis, up)
        after = lax.ppermute(first, axis, down)
        value = jnp.concatenate([before, value, after], axis=dim)
    return value


def by_tokens(latents, w_qkv, w_out, win_blocks, win_counts, block_window):
    rows_n = lax.axis_size("rows")
    shard_idx = lax.axis_index("rows")
    frames = latents.shape[0] * lax.axis_size("frames")
    tok_frame = latents.shape[1]
    model_width = latents.shape[2]
    local_cols = w_qkv.shape[2]
    per_shard = tok_frame // BS
    block_total = per_shard * rows_n
    heads_here = local_cols // HD
    block_len = frames * BS
    score_scale = 1.0 / math.sqrt(HD)
    gathered = lax.all_gather(latents, "frames", axis=0, tiled=True)
    flat_tokens = gathered.reshape(frames * tok_frame, model_width)
    weight_rows = lax.all_gather(w_qkv, "rows", axis=0, tiled=True)
    projected = jnp.dot(
        flat_tokens,
        weight_rows.reshape(weight_rows.shape[0], 3 * local_cols),
        preferred_element_type=jnp.float32,
    ).astype(jnp.bfloat16)
    blocked = projected.reshape(frames, per_shard, BS, 3, local_cols).transpose(1, 0, 2, 3, 4)
    blocked = blocked.reshape(per_shard, block_len, 3, local_cols)
    queries = blocked[:, :, 0]
    keyvals = blocked[:, :, 1:]
    nearby = with_halo(keyvals, (("rows", 0),), per_shard)
    first_block = shard_idx * per_shard
    owners = block_window - first_block
    members = win_blocks[owners]
    lengths = win_counts[owners]
    positions = (members - first_block + per_shard + block_total) % block_total

    def attend(query_rows, picked, live_mask):
        key_count = picked.shape[0]
        key_blocks = nearby[picked]
        key_part = key_blocks[:, :, 0].reshape(key_count * block_len, heads_here, HD)
        value_part = key_blocks[:, :, 1].reshape(key_count * block_len, heads_here, HD)
        scores = (
            jnp.einsum(
                "qhd,khd->hqk",
                query_rows.reshape(block_len, heads_here, HD),
                key_part,
                preferred_element_type=jnp.float32,
            )
            * score_scale
        )
        scores = jnp.where(live_mask[None, None, :], scores, -jnp.inf)
        row_max = jnp.max(scores, axis=-1, keepdims=True)
        raised = jnp.exp(scores - row_max)
        weights = (raised / jnp.sum(raised, axis=-1, keepdims=True)).astype(jnp.bfloat16)
        blended = jnp.einsum(
            "hqk,khd->qhd", weights, value_part, preferred_element_type=jnp.float32
        )
        return blended.reshape(block_len, local_cols).astype(jnp.bfloat16)

    def one_block(block_item):
        query_rows, picked, length = block_item
        live_mask = jnp.repeat(jnp.arange(MAXB) < length, block_len)
        return attend(query_rows, picked, live_mask)

    attended = lax.map(one_block, (queries, positions, lengths))
    ordered = attended.reshape(per_shard, frames, BS, local_cols).transpose(1, 0, 2, 3)
    ordered = ordered.reshape(frames * tok_frame, local_cols)
    w_full = lax.all_gather(w_out, "rows", axis=1, tiled=True)
    group_count = lax.axis_size(("frames", "heads"))
    out_rows = frames * tok_frame // group_count
    summed = lax.psum_scatter(
        jnp.dot(ordered, w_full, preferred_element_type=jnp.float32).astype(jnp.bfloat16),
        ("frames", "heads"),
        scatter_dimension=0,
        tiled=True,
    )
    return summed.reshape(1, out_rows, model_width)


def swap(value, axis, step=1):
    peers = lax.axis_size(axis)
    return lax.ppermute(value, axis, [(i, i ^ step) for i in range(peers)])


def after(value, *others):
    return lax.optimization_barrier((value, *others))[0]


def call(kernel, out_shape, prefetch, operands, scratch=(), flops=0, read=0, limit=VMEM_BYTES):
    return pl.pallas_call(
        kernel,
        out_shape=out_shape,
        grid_spec=pltpu.PrefetchScalarGridSpec(
            num_scalar_prefetch=len(prefetch),
            grid=(),
            in_specs=[pl.BlockSpec(memory_space=pltpu.VMEM)] * len(operands),
            out_specs=jax.tree.map(lambda _: pl.BlockSpec(memory_space=pltpu.VMEM), out_shape),
            scratch_shapes=scratch,
        ),
        compiler_params=pltpu.CompilerParams(vmem_limit_bytes=limit),
        cost_estimate=pl.CostEstimate(flops=flops, bytes_accessed=read, transcendentals=0),
    )(*prefetch, *operands)


def project(place, mine, theirs, chunks, firsts, cols):
    rows, (count, width) = len(mine), theirs[0].shape
    half = chunks[0][0].shape[1]
    slices = len(chunks)
    flat = [w for of_round in chunks for w in of_round]
    fetched = 2 * rows + len(flat)

    def kernel(place_ref, *refs):
        row, group, frame, core = (place_ref[i] for i in range(4))
        w_refs = refs[2 * rows : fetched]
        q_keep, kv_keep, send, x_all, w_all, total, sems = refs[fetched:]
        copies = []
        for k in range(slices):
            for g in range(2):
                at = pl.multiple_of((row + slices - k) % slices * (2 * half) + (group + g) % 2 * half, half)
                for part in range(3):
                    source = w_refs[2 * k + g].at[part, :, firsts[k] : firsts[k] + cols]
                    into = w_all.at[pl.ds(at, half), part * cols : (part + 1) * cols]
                    copies.append(pltpu.make_async_copy(source, into, sems.at[len(copies)]))
        fetch_x = []
        for i in range(2 * rows):
            to = x_all.at[row ^ (i % rows), (frame + i // rows) % 2]
            fetch_x.append(pltpu.make_async_copy(refs[i].at[pl.ds(0, count)], to, sems.at[len(copies) + i]))
        for copy in copies + fetch_x:
            copy.start()
        for copy in copies:
            copy.wait()
        for s in range(rows):
            fetch_x[s].wait()
            fetch_x[rows + s].wait()
            at = row ^ s
            acc = jnp.dot(x_all[at].reshape(-1, width), w_all[...], preferred_element_type=jnp.float32)
            kv_part = acc[:, cols:]
            kv_keep[at] = kv_part
            send[at, : 2 * count, :] = kv_part.astype(jnp.bfloat16)
            total[s] = acc[:, :cols].reshape(2, count, cols)
            own = pl.multiple_of(core * BS, BS)
            other = pl.multiple_of((1 - core) * BS, BS)
            q_keep[at] = total[s, :, pl.ds(own, BS), :].reshape(2 * BS, cols)
            for f in range(2):
                where = slice(f * cols, (f + 1) * cols)
                send[at, 2 * count :, where] = total[s, f, pl.ds(other, BS), :].astype(jnp.bfloat16)

    vmem, hbm = pl.BlockSpec(memory_space=pltpu.VMEM), pl.BlockSpec(memory_space=pltpu.HBM)
    flops = 2 * rows * 2 * count * width * 3 * cols
    return pl.pallas_call(
        kernel,
        out_shape=(
            jax.ShapeDtypeStruct((rows, 2 * BS, cols), jnp.float32),
            jax.ShapeDtypeStruct((rows, 2 * count, 2 * cols), jnp.float32),
            jax.ShapeDtypeStruct((rows, 2 * count + BS, 2 * cols), jnp.bfloat16),
        ),
        grid_spec=pltpu.PrefetchScalarGridSpec(
            num_scalar_prefetch=1,
            grid=(),
            in_specs=[hbm] * fetched,
            out_specs=(vmem, vmem, vmem),
            scratch_shapes=[
                pltpu.VMEM((rows, 2, count, width), jnp.bfloat16),
                pltpu.VMEM((width, 3 * cols), jnp.bfloat16),
                pltpu.VMEM((rows, 2, count, cols), jnp.float32),
                pltpu.SemaphoreType.DMA((2 * rows + 3 * len(flat),)),
            ],
        ),
        compiler_params=pltpu.CompilerParams(vmem_limit_bytes=VMEM_BYTES),
        cost_estimate=pl.CostEstimate(flops=8 * flops, bytes_accessed=flops // 300, transcendentals=0),
    )(place, *mine, *theirs, *flat)


def attend_all(place, members, counts, queries, keyvals, more, earlier=()):
    blocks, block_len, cols = queries.shape
    first = earlier[0].shape[2] if earlier else 0
    rows = keyvals.shape[1]
    per_row = rows // block_len

    def kernel(place_ref, members_ref, counts_ref, q_ref, kv_ref, more_ref, *refs):
        same_ref, diff_ref, q_sum, kv_sum, out = refs[len(earlier) :]
        for r in range(blocks):
            added = more_ref[r, rows:, :].astype(jnp.float32)
            added = jnp.concatenate([added[:, :cols], added[:, cols:]], axis=0)
            q_sum[r] = (q_ref[r] + added).astype(jnp.bfloat16)
            both = (kv_ref[r] + more_ref[r, :rows, :].astype(jnp.float32)).astype(jnp.bfloat16)
            both = both.reshape(2, rows // 2, 2 * cols)
            for j in range(per_row):
                part = both[:, j * BS : (j + 1) * BS, :]
                kv_sum[r * per_row + j] = part.reshape(block_len, 2 * cols)
        column = lax.broadcasted_iota(jnp.int32, (block_len, MAXB * block_len), 1)
        for b in range(blocks):
            live = column < counts_ref[b] * block_len
            listed = [kv_sum.at[members_ref[b * MAXB + j]] for j in range(MAXB)]
            for h in range(cols // HD):
                at = slice(h * HD, (h + 1) * HD)
                at_v = slice(cols + h * HD, cols + (h + 1) * HD)
                keys = jnp.concatenate([block[:, at] for block in listed], axis=0)
                values = jnp.concatenate([block[:, at_v] for block in listed], axis=0)
                scores = lax.dot_general(
                    q_sum[b, :, at], keys, (((1,), (1,)), ((), ())), preferred_element_type=jnp.float32
                )
                scores = jnp.where(live, scores, -jnp.inf)
                raised = jnp.exp2((scores - jnp.max(scores, axis=-1, keepdims=True)) * EXP2_SCALE)
                weights = raised * (1.0 / jnp.sum(raised, axis=-1, keepdims=True))
                blended = jnp.dot(
                    weights.astype(jnp.bfloat16), values, preferred_element_type=jnp.float32
                )
                out[(b + place_ref[0]) % 2, b // 2, :, at] = blended.astype(jnp.bfloat16)
        for i, out_ref in enumerate((same_ref, diff_ref)):
            if earlier:
                out_ref[:, :, :first] = refs[i][...]
            out_ref[:, :, first:] = out[i]

    half = jax.ShapeDtypeStruct((blocks // 2, block_len, first + cols), jnp.bfloat16)
    return call(
        kernel,
        (half, half),
        [place, members, counts],
        [queries, keyvals, more, *earlier],
        scratch=[
            pltpu.VMEM((blocks, block_len, cols), jnp.bfloat16),
            pltpu.VMEM((blocks * per_row, block_len, 2 * cols), jnp.bfloat16),
            pltpu.VMEM((2, blocks // 2, block_len, cols), jnp.bfloat16),
        ],
        flops=4 * blocks * block_len * MAXB * block_len * cols,
        read=16 * blocks * block_len * cols,
    )


def mix(place, attended, w_own, w_across, beside, beside_across, far):
    _, block_len, cols = attended[0].shape
    width = w_own.shape[1]

    def kernel(place_ref, *refs):
        row, group, frame, core = (place_ref[i] for i in range(4))
        w_refs = refs[4:10]
        keep, send, a_all, sums = refs[10:]
        block = 1 - row // 2 if far else row // 2
        for s in range(4):
            a_all[s] = refs[s][block]

        def term(c, other):
            side = 1 - core if other else core
            acc = None
            for i in range(2):
                if c == 0:
                    weight, half = w_refs[other][i * cols : (i + 1) * cols, :], i
                else:
                    weight, half = w_refs[2 + 2 * other + i][:cols], (i + group) % 2
                part = jnp.dot(a_all[(2 * side + half) ^ row], weight, preferred_element_type=jnp.float32)
                acc = part if acc is None else acc + part
            return acc.astype(jnp.bfloat16).astype(jnp.float32)

        for c in range(2):
            sums[...] = (term(c, 0) + term(c, 1)).reshape(2, BS, width)
            at = (row + c) % 2
            keep[at] = sums[frame]
            send[at] = sums[1 - frame].astype(jnp.bfloat16)

    return call(
        kernel,
        (
            jax.ShapeDtypeStruct((2, BS, width), jnp.float32),
            jax.ShapeDtypeStruct((2, BS, width), jnp.bfloat16),
        ),
        [place],
        [*attended, w_own, w_across, *beside, *beside_across],
        scratch=[pltpu.VMEM((4, block_len, cols), jnp.bfloat16), pltpu.VMEM((2, BS, width), jnp.float32)],
        flops=2 * block_len * 4 * cols * 2 * width,
        read=16 * cols * width,
    )


def finish(place, near_keep, near_more, far):
    halves, rows, width = near_keep.shape

    def kernel(place_ref, keep_ref, more_ref, far_ref, out_ref):
        pair = place_ref[0] // 2
        for c in range(halves):
            here = pl.multiple_of((pair * halves + c) * width, width)
            there = pl.multiple_of(((1 - pair) * halves + c) * width, width)
            out_ref[:, pl.ds(here, width)] = (keep_ref[c] + more_ref[c].astype(jnp.float32)).astype(jnp.bfloat16)
            out_ref[:, pl.ds(there, width)] = far_ref[c]

    return call(
        kernel,
        jax.ShapeDtypeStruct((rows, 2 * halves * width), jnp.bfloat16),
        [place],
        [near_keep, near_more, far],
        read=12 * rows * halves * width,
    )


def by_heads(latents, w_qkv, w_out, win_blocks, win_counts, block_window):
    rows_n, heads_n = lax.axis_size("rows"), lax.axis_size("heads")
    group, row = lax.axis_index("groups"), lax.axis_index("rows")
    frame, core = lax.axis_index("frames"), lax.axis_index("heads")
    count = latents.shape[1]
    depth, _, local_cols = w_qkv.shape
    span = rows_n // heads_n
    cols = local_cols // span
    half = depth // 2
    place = jnp.stack([row, group, frame, core]).astype(jnp.int32)

    last = cols // (3 * HD) * HD

    def reshard(k, at, wide, *others):
        start = (0, group * half, (k + row) % span * cols + at)
        value = lax.dynamic_slice(w_qkv.transpose(1, 0, 2), start, (3, half, wide))
        pairs = [
            (r * heads_n + h, (h * span + (k + r) % span) * heads_n + r // span)
            for r in range(rows_n)
            for h in range(heads_n)
        ]
        return lax.ppermute(after(value, *others) if others else value, ("rows", "heads"), pairs)

    mine = lax.dynamic_slice_in_dim(latents[0], core * span * depth, span * depth, axis=1)
    mine_x = swap(mine, "frames")
    here, there = [reshard(0, 0, cols)], []
    near = swap(mine, "rows")
    near_x = swap(near, "frames")
    across = swap(after(w_out, near), "heads")
    there.append(swap(here[0], "groups"))
    here.append(reshard(1, 0, cols - last, near))
    tables = jnp.concatenate([win_blocks, win_counts[:, None], block_window[:, None]], axis=1)
    tables = after(tables, near)
    tables = jnp.pad(tables, ((0, 8 - heads_n), (0, span * depth - MAXB - 2))).astype(mine.dtype)
    joined = jnp.concatenate([mine, tables], axis=0)
    far_2 = swap(after(joined, here[0], mine_x), "rows", 2)
    out_half = lax.dynamic_slice_in_dim(w_out, group * cols, cols, axis=0)
    out_half = jnp.concatenate([out_half, tables[:, : out_half.shape[1]]], axis=0)
    beside = [swap(after(out_half, near), "rows")]
    beside.append(swap(beside[0], "groups"))
    there.append(swap(after(here[1], there[0], beside[1]), "groups"))
    far_2x = swap(far_2, "frames")
    far_3 = swap(after(joined, far_2, across, near_x, beside[0]), "rows", 3)
    far_3x = swap(far_3, "frames")
    here.append(reshard(1, cols - last, last, far_3))
    there.append(swap(here[2], "groups"))

    found = [tables, beside[0][cols:], far_2[count:], far_3[count:]]
    found = jnp.stack([x[:heads_n, : MAXB + 2] for x in found])
    tables = found.astype(jnp.int32)[row ^ jnp.arange(rows_n)].reshape(rows_n * heads_n, MAXB + 2)
    windows = lax.dynamic_index_in_dim(
        tables[:, MAXB + 1].reshape(rows_n, heads_n), core, axis=1, keepdims=False
    )
    picked = tables[windows]
    members, counts = picked[:, :MAXB].reshape(-1), picked[:, MAXB]

    pieces = [mine, near, far_2, far_3], [mine_x, near_x, far_2x, far_3x]
    chunks = [(here[0], there[0]), (here[1], after(there[1], members, counts))]
    first = project(place, *pieces, chunks, (0, 0), cols - last)
    first_more = swap(first[2], "heads")
    chunks[1] = (here[2], after(there[2], first[2]))
    second = project(place, *pieces, chunks, (cols - last, 0), last)
    second_more = swap(second[2], "heads")
    attended = attend_all(place, members, counts, *first[:2], first_more)
    beside_across = [swap(part, "heads") for part in beside]
    same, diff = attend_all(place, members, counts, *second[:2], second_more, attended)
    attended = [same] + [swap(same if s % 2 == 0 else diff, "rows", s) for s in range(1, rows_n)]
    weights = w_out, across, beside, beside_across
    far_keep, far_send = mix(place, attended, *weights, True)
    near_keep, near_send = mix(place, attended, *weights, False)
    far_more = swap(far_send, "frames")
    far = swap((far_keep + far_more.astype(jnp.float32)).astype(jnp.bfloat16), "rows", 2)
    near_more = swap(after(near_send, far_more), "frames")
    return finish(place, near_keep, near_more, far)[None]


def local(latents, w_qkv, w_out, win_blocks, win_counts, block_window):
    rows_n = lax.axis_size("rows")
    pairs = all(lax.axis_size(axis) == 2 for axis in ("groups", "frames", "heads"))
    heads_here = w_qkv.shape[2] // HD
    if pairs and rows_n == 4 and heads_here == 6 and latents.shape[:2] == (1, 2 * BS):
        plan = by_heads
    else:
        plan = by_tokens
    return plan(latents, w_qkv, w_out, win_blocks, win_counts, block_window)


def solution(mesh):
    in_specs = (
        P(("groups", "frames"), "rows", None),
        P("rows", None, ("frames", "heads")),
        P(("frames", "heads"), "rows"),
        P(("groups", "rows"), None),
        P(("groups", "rows")),
        P(("groups", "rows")),
    )
    out_specs = P(("groups", "frames"), ("rows", "heads"), None)
    return jax.shard_map(local, mesh=mesh, in_specs=in_specs, out_specs=out_specs, check_vma=False)
```

```python
import math

import jax
import jax.numpy as jnp
from jax import lax
from jax.experimental import pallas as pl
from jax.experimental.pallas import tpu as pltpu
from jax.sharding import PartitionSpec as P

HD = 128
BS = 64
MAXB = 4
VMEM_BYTES = 24 * 1024 * 1024
WHOLE_VMEM_BYTES = 56 * 1024 * 1024
EXP2_SCALE = math.log2(math.e) / math.sqrt(HD)


def with_halo(value, sides, width):
    for axis, dim in sides:
        peers, length = (lax.axis_size(axis), value.shape[dim])
        up = [(i, (i + 1) % peers) for i in range(peers)]
        down = [(j, i) for i, j in up]
        last = lax.slice_in_dim(value, length - width, length, axis=dim)
        first = lax.slice_in_dim(value, 0, width, axis=dim)
        before = lax.ppermute(last, axis, up)
        after = lax.ppermute(first, axis, down)
        value = jnp.concatenate([before, value, after], axis=dim)
    return value


def by_tokens(latents, w_qkv, w_out, win_blocks, win_counts, block_window):
    rows_n = lax.axis_size("rows")
    shard_idx = lax.axis_index("rows")
    frames = latents.shape[0] * lax.axis_size("frames")
    tok_frame = latents.shape[1]
    model_width = latents.shape[2]
    local_cols = w_qkv.shape[2]
    per_shard = tok_frame // BS
    block_total = per_shard * rows_n
    heads_here = local_cols // HD
    block_len = frames * BS
    score_scale = 1.0 / math.sqrt(HD)
    gathered = lax.all_gather(latents, "frames", axis=0, tiled=True)
    flat_tokens = gathered.reshape(frames * tok_frame, model_width)
    weight_rows = lax.all_gather(w_qkv, "rows", axis=0, tiled=True)
    projected = jnp.dot(
        flat_tokens,
        weight_rows.reshape(weight_rows.shape[0], 3 * local_cols),
        preferred_element_type=jnp.float32,
    ).astype(jnp.bfloat16)
    blocked = projected.reshape(frames, per_shard, BS, 3, local_cols).transpose(1, 0, 2, 3, 4)
    blocked = blocked.reshape(per_shard, block_len, 3, local_cols)
    queries = blocked[:, :, 0]
    keyvals = blocked[:, :, 1:]
    nearby = with_halo(keyvals, (("rows", 0),), per_shard)
    first_block = shard_idx * per_shard
    owners = block_window - first_block
    members = win_blocks[owners]
    lengths = win_counts[owners]
    positions = (members - first_block + per_shard + block_total) % block_total

    def attend(query_rows, picked, live_mask):
        key_count = picked.shape[0]
        key_blocks = nearby[picked]
        key_part = key_blocks[:, :, 0].reshape(key_count * block_len, heads_here, HD)
        value_part = key_blocks[:, :, 1].reshape(key_count * block_len, heads_here, HD)
        scores = (
            jnp.einsum(
                "qhd,khd->hqk",
                query_rows.reshape(block_len, heads_here, HD),
                key_part,
                preferred_element_type=jnp.float32,
            )
            * score_scale
        )
        scores = jnp.where(live_mask[None, None, :], scores, -jnp.inf)
        row_max = jnp.max(scores, axis=-1, keepdims=True)
        raised = jnp.exp(scores - row_max)
        weights = (raised / jnp.sum(raised, axis=-1, keepdims=True)).astype(jnp.bfloat16)
        blended = jnp.einsum(
            "hqk,khd->qhd", weights, value_part, preferred_element_type=jnp.float32
        )
        return blended.reshape(block_len, local_cols).astype(jnp.bfloat16)

    def one_block(block_item):
        query_rows, picked, length = block_item
        live_mask = jnp.repeat(jnp.arange(MAXB) < length, block_len)
        return attend(query_rows, picked, live_mask)

    attended = lax.map(one_block, (queries, positions, lengths))
    ordered = attended.reshape(per_shard, frames, BS, local_cols).transpose(1, 0, 2, 3)
    ordered = ordered.reshape(frames * tok_frame, local_cols)
    w_full = lax.all_gather(w_out, "rows", axis=1, tiled=True)
    group_count = lax.axis_size(("frames", "heads"))
    out_rows = frames * tok_frame // group_count
    summed = lax.psum_scatter(
        jnp.dot(ordered, w_full, preferred_element_type=jnp.float32).astype(jnp.bfloat16),
        ("frames", "heads"),
        scatter_dimension=0,
        tiled=True,
    )
    return summed.reshape(1, out_rows, model_width)


def swap(value, axis, step=1):
    peers = lax.axis_size(axis)
    return lax.ppermute(value, axis, [(i, i ^ step) for i in range(peers)])


def after(value, *others):
    return lax.optimization_barrier((value, *others))[0]


def call(kernel, out_shape, prefetch, operands, scratch=(), flops=0, read=0, limit=VMEM_BYTES):
    return pl.pallas_call(
        kernel,
        out_shape=out_shape,
        grid_spec=pltpu.PrefetchScalarGridSpec(
            num_scalar_prefetch=len(prefetch),
            grid=(),
            in_specs=[pl.BlockSpec(memory_space=pltpu.VMEM)] * len(operands),
            out_specs=jax.tree.map(lambda _: pl.BlockSpec(memory_space=pltpu.VMEM), out_shape),
            scratch_shapes=scratch,
        ),
        compiler_params=pltpu.CompilerParams(vmem_limit_bytes=limit),
        cost_estimate=pl.CostEstimate(flops=flops, bytes_accessed=read, transcendentals=0),
    )(*prefetch, *operands)


def project(place, mine, theirs, chunks, firsts, cols):
    rows, (count, width) = len(mine), theirs[0].shape
    half = chunks[0][0].shape[1]
    slices = len(chunks)
    flat = [w for of_round in chunks for w in of_round]
    fetched = 2 * rows + len(flat)

    def kernel(place_ref, *refs):
        row, group, frame, core = (place_ref[i] for i in range(4))
        w_refs = refs[2 * rows : fetched]
        q_keep, kv_keep, send, x_all, w_all, total, sems = refs[fetched:]
        copies = []
        for k in range(slices):
            for g in range(2):
                at = pl.multiple_of((row + slices - k) % slices * (2 * half) + (group + g) % 2 * half, half)
                for part in range(3):
                    source = w_refs[2 * k + g].at[part, :, firsts[k] : firsts[k] + cols]
                    into = w_all.at[pl.ds(at, half), part * cols : (part + 1) * cols]
                    copies.append(pltpu.make_async_copy(source, into, sems.at[len(copies)]))
        fetch_x = []
        for i in range(2 * rows):
            to = x_all.at[row ^ (i % rows), (frame + i // rows) % 2]
            fetch_x.append(pltpu.make_async_copy(refs[i].at[pl.ds(0, count)], to, sems.at[len(copies) + i]))
        for copy in copies + fetch_x:
            copy.start()
        for copy in copies:
            copy.wait()
        for s in range(rows):
            fetch_x[s].wait()
            fetch_x[rows + s].wait()
            at = row ^ s
            acc = jnp.dot(x_all[at].reshape(-1, width), w_all[...], preferred_element_type=jnp.float32)
            kv_part = acc[:, cols:]
            kv_keep[at] = kv_part
            send[at, : 2 * count, :] = kv_part.astype(jnp.bfloat16)
            total[s] = acc[:, :cols].reshape(2, count, cols)
            own = pl.multiple_of(core * BS, BS)
            other = pl.multiple_of((1 - core) * BS, BS)
            q_keep[at] = total[s, :, pl.ds(own, BS), :].reshape(2 * BS, cols)
            for f in range(2):
                where = slice(f * cols, (f + 1) * cols)
                send[at, 2 * count :, where] = total[s, f, pl.ds(other, BS), :].astype(jnp.bfloat16)

    vmem, hbm = pl.BlockSpec(memory_space=pltpu.VMEM), pl.BlockSpec(memory_space=pltpu.HBM)
    flops = 2 * rows * 2 * count * width * 3 * cols
    return pl.pallas_call(
        kernel,
        out_shape=(
            jax.ShapeDtypeStruct((rows, 2 * BS, cols), jnp.float32),
            jax.ShapeDtypeStruct((rows, 2 * count, 2 * cols), jnp.float32),
            jax.ShapeDtypeStruct((rows, 2 * count + BS, 2 * cols), jnp.bfloat16),
        ),
        grid_spec=pltpu.PrefetchScalarGridSpec(
            num_scalar_prefetch=1,
            grid=(),
            in_specs=[hbm] * fetched,
            out_specs=(vmem, vmem, vmem),
            scratch_shapes=[
                pltpu.VMEM((rows, 2, count, width), jnp.bfloat16),
                pltpu.VMEM((width, 3 * cols), jnp.bfloat16),
                pltpu.VMEM((rows, 2, count, cols), jnp.float32),
                pltpu.SemaphoreType.DMA((2 * rows + 3 * len(flat),)),
            ],
        ),
        compiler_params=pltpu.CompilerParams(vmem_limit_bytes=VMEM_BYTES),
        cost_estimate=pl.CostEstimate(flops=8 * flops, bytes_accessed=flops // 300, transcendentals=0),
    )(place, *mine, *theirs, *flat)


def attend_all(place, members, counts, queries, keyvals, more, earlier=()):
    blocks, block_len, cols = queries.shape
    first = earlier[0].shape[2] if earlier else 0
    rows = keyvals.shape[1]
    per_row = rows // block_len

    def kernel(place_ref, members_ref, counts_ref, q_ref, kv_ref, more_ref, *refs):
        same_ref, diff_ref, q_sum, kv_sum, out = refs[len(earlier) :]
        for r in range(blocks):
            added = more_ref[r, rows:, :].astype(jnp.float32)
            added = jnp.concatenate([added[:, :cols], added[:, cols:]], axis=0)
            q_sum[r] = (q_ref[r] + added).astype(jnp.bfloat16)
            both = (kv_ref[r] + more_ref[r, :rows, :].astype(jnp.float32)).astype(jnp.bfloat16)
            both = both.reshape(2, rows // 2, 2 * cols)
            for j in range(per_row):
                part = both[:, j * BS : (j + 1) * BS, :]
                kv_sum[r * per_row + j] = part.reshape(block_len, 2 * cols)
        column = lax.broadcasted_iota(jnp.int32, (block_len, MAXB * block_len), 1)
        for b in range(blocks):
            live = column < counts_ref[b] * block_len
            listed = [kv_sum.at[members_ref[b * MAXB + j]] for j in range(MAXB)]
            for h in range(cols // HD):
                at = slice(h * HD, (h + 1) * HD)
                at_v = slice(cols + h * HD, cols + (h + 1) * HD)
                keys = jnp.concatenate([block[:, at] for block in listed], axis=0)
                values = jnp.concatenate([block[:, at_v] for block in listed], axis=0)
                scores = lax.dot_general(
                    q_sum[b, :, at], keys, (((1,), (1,)), ((), ())), preferred_element_type=jnp.float32
                )
                scores = jnp.where(live, scores, -jnp.inf)
                raised = jnp.exp2((scores - jnp.max(scores, axis=-1, keepdims=True)) * EXP2_SCALE)
                weights = raised * (1.0 / jnp.sum(raised, axis=-1, keepdims=True))
                blended = jnp.dot(
                    weights.astype(jnp.bfloat16), values, preferred_element_type=jnp.float32
                )
                out[(b + place_ref[0]) % 2, b // 2, :, at] = blended.astype(jnp.bfloat16)
        for i, out_ref in enumerate((same_ref, diff_ref)):
            if earlier:
                out_ref[:, :, :first] = refs[i][...]
            out_ref[:, :, first:] = out[i]

    half = jax.ShapeDtypeStruct((blocks // 2, block_len, first + cols), jnp.bfloat16)
    return call(
        kernel,
        (half, half),
        [place, members, counts],
        [queries, keyvals, more, *earlier],
        scratch=[
            pltpu.VMEM((blocks, block_len, cols), jnp.bfloat16),
            pltpu.VMEM((blocks * per_row, block_len, 2 * cols), jnp.bfloat16),
            pltpu.VMEM((2, blocks // 2, block_len, cols), jnp.bfloat16),
        ],
        flops=4 * blocks * block_len * MAXB * block_len * cols,
        read=16 * blocks * block_len * cols,
    )


def mix(place, attended, w_own, w_across, beside, beside_across, far):
    _, block_len, cols = attended[0].shape
    width = w_own.shape[1]

    def kernel(place_ref, *refs):
        row, group, frame, core = (place_ref[i] for i in range(4))
        w_refs = refs[4:10]
        keep, send, a_all, sums = refs[10:]
        block = 1 - row // 2 if far else row // 2
        for s in range(4):
            a_all[s] = refs[s][block]

        def term(c, other):
            side = 1 - core if other else core
            acc = None
            for i in range(2):
                if c == 0:
                    weight, half = w_refs[other][i * cols : (i + 1) * cols, :], i
                else:
                    weight, half = w_refs[2 + 2 * other + i][:cols], (i + group) % 2
                part = jnp.dot(a_all[(2 * side + half) ^ row], weight, preferred_element_type=jnp.float32)
                acc = part if acc is None else acc + part
            return acc.astype(jnp.bfloat16).astype(jnp.float32)

        for c in range(2):
            sums[...] = (term(c, 0) + term(c, 1)).reshape(2, BS, width)
            at = (row + c) % 2
            keep[at] = sums[frame]
            send[at] = sums[1 - frame].astype(jnp.bfloat16)

    return call(
        kernel,
        (
            jax.ShapeDtypeStruct((2, BS, width), jnp.float32),
            jax.ShapeDtypeStruct((2, BS, width), jnp.bfloat16),
        ),
        [place],
        [*attended, w_own, w_across, *beside, *beside_across],
        scratch=[pltpu.VMEM((4, block_len, cols), jnp.bfloat16), pltpu.VMEM((2, BS, width), jnp.float32)],
        flops=2 * block_len * 4 * cols * 2 * width,
        read=16 * cols * width,
    )


def finish(place, near_keep, near_more, far):
    halves, rows, width = near_keep.shape

    def kernel(place_ref, keep_ref, more_ref, far_ref, out_ref):
        pair = place_ref[0] // 2
        for c in range(halves):
            here = pl.multiple_of((pair * halves + c) * width, width)
            there = pl.multiple_of(((1 - pair) * halves + c) * width, width)
            out_ref[:, pl.ds(here, width)] = (keep_ref[c] + more_ref[c].astype(jnp.float32)).astype(jnp.bfloat16)
            out_ref[:, pl.ds(there, width)] = far_ref[c]

    return call(
        kernel,
        jax.ShapeDtypeStruct((rows, 2 * halves * width), jnp.bfloat16),
        [place],
        [near_keep, near_more, far],
        read=12 * rows * halves * width,
    )


def by_heads(latents, w_qkv, w_out, win_blocks, win_counts, block_window):
    rows_n, heads_n = lax.axis_size("rows"), lax.axis_size("heads")
    group, row = lax.axis_index("groups"), lax.axis_index("rows")
    frame, core = lax.axis_index("frames"), lax.axis_index("heads")
    count = latents.shape[1]
    depth, _, local_cols = w_qkv.shape
    span = rows_n // heads_n
    cols = local_cols // span
    half = depth // 2
    place = jnp.stack([row, group, frame, core]).astype(jnp.int32)

    last = cols // (3 * HD) * HD

    def reshard(k, at, wide, *others):
        start = (0, group * half, (k + row) % span * cols + at)
        value = lax.dynamic_slice(w_qkv.transpose(1, 0, 2), start, (3, half, wide))
        pairs = [
            (r * heads_n + h, (h * span + (k + r) % span) * heads_n + r // span)
            for r in range(rows_n)
            for h in range(heads_n)
        ]
        return lax.ppermute(after(value, *others) if others else value, ("rows", "heads"), pairs)

    mine = lax.dynamic_slice_in_dim(latents[0], core * span * depth, span * depth, axis=1)
    mine_x = swap(mine, "frames")
    here, there = [reshard(0, 0, cols)], []
    near = swap(mine, "rows")
    near_x = swap(near, "frames")
    across = swap(after(w_out, near), "heads")
    there.append(swap(here[0], "groups"))
    here.append(reshard(1, 0, cols - last, near))
    tables = jnp.concatenate([win_blocks, win_counts[:, None], block_window[:, None]], axis=1)
    tables = after(tables, near)
    tables = jnp.pad(tables, ((0, 8 - heads_n), (0, span * depth - MAXB - 2))).astype(mine.dtype)
    joined = jnp.concatenate([mine, tables], axis=0)
    far_2 = swap(after(joined, here[0], mine_x), "rows", 2)
    out_half = lax.dynamic_slice_in_dim(w_out, group * cols, cols, axis=0)
    out_half = jnp.concatenate([out_half, tables[:, : out_half.shape[1]]], axis=0)
    beside = [swap(after(out_half, near), "rows")]
    beside.append(swap(beside[0], "groups"))
    there.append(swap(after(here[1], there[0], beside[1]), "groups"))
    far_2x = swap(far_2, "frames")
    far_3 = swap(after(joined, far_2, across, near_x, beside[0]), "rows", 3)
    far_3x = swap(far_3, "frames")
    here.append(reshard(1, cols - last, last, far_3, there[1]))
    there.append(swap(here[2], "groups"))

    found = [tables, beside[0][cols:], far_2[count:], far_3[count:]]
    found = jnp.stack([x[:heads_n, : MAXB + 2] for x in found])
    tables = found.astype(jnp.int32)[row ^ jnp.arange(rows_n)].reshape(rows_n * heads_n, MAXB + 2)
    windows = lax.dynamic_index_in_dim(
        tables[:, MAXB + 1].reshape(rows_n, heads_n), core, axis=1, keepdims=False
    )
    picked = tables[windows]
    members, counts = picked[:, :MAXB].reshape(-1), picked[:, MAXB]

    pieces = [mine, near, far_2, far_3], [mine_x, near_x, far_2x, far_3x]
    chunks = [(here[0], there[0]), (here[1], after(there[1], members, counts))]
    first = project(place, *pieces, chunks, (0, 0), cols - last)
    first_more = swap(first[2], "heads")
    chunks[1] = (here[2], after(there[2], first[2]))
    second = project(place, *pieces, chunks, (cols - last, 0), last)
    second_more = swap(second[2], "heads")
    attended = attend_all(place, members, counts, *first[:2], first_more)
    beside_across = [swap(part, "heads") for part in beside]
    same, diff = attend_all(place, members, counts, *second[:2], second_more, attended)
    attended = [same] + [swap(same if s % 2 == 0 else diff, "rows", s) for s in range(1, rows_n)]
    weights = w_out, across, beside, beside_across
    far_keep, far_send = mix(place, attended, *weights, True)
    near_keep, near_send = mix(place, attended, *weights, False)
    far_more = swap(far_send, "frames")
    far = swap((far_keep + far_more.astype(jnp.float32)).astype(jnp.bfloat16), "rows", 2)
    near_more = swap(after(near_send, far_more), "frames")
    return finish(place, near_keep, near_more, far)[None]


def local(latents, w_qkv, w_out, win_blocks, win_counts, block_window):
    rows_n = lax.axis_size("rows")
    pairs = all(lax.axis_size(axis) == 2 for axis in ("groups", "frames", "heads"))
    heads_here = w_qkv.shape[2] // HD
    if pairs and rows_n == 4 and heads_here == 6 and latents.shape[:2] == (1, 2 * BS):
        plan = by_heads
    else:
        plan = by_tokens
    return plan(latents, w_qkv, w_out, win_blocks, win_counts, block_window)


def solution(mesh):
    in_specs = (
        P(("groups", "frames"), "rows", None),
        P("rows", None, ("frames", "heads")),
        P(("frames", "heads"), "rows"),
        P(("groups", "rows"), None),
        P(("groups", "rows")),
        P(("groups", "rows")),
    )
    out_specs = P(("groups", "frames"), ("rows", "heads"), None)
    return jax.shard_map(local, mesh=mesh, in_specs=in_specs, out_specs=out_specs, check_vma=False)
```

```python
import math

import jax
import jax.numpy as jnp
from jax import lax
from jax.experimental import pallas as pl
from jax.experimental.pallas import tpu as pltpu
from jax.sharding import PartitionSpec as P

HD = 128
BS = 64
MAXB = 4
VMEM_BYTES = 24 * 1024 * 1024
WHOLE_VMEM_BYTES = 56 * 1024 * 1024
EXP2_SCALE = math.log2(math.e) / math.sqrt(HD)


def with_halo(value, sides, width):
    for axis, dim in sides:
        peers, length = (lax.axis_size(axis), value.shape[dim])
        up = [(i, (i + 1) % peers) for i in range(peers)]
        down = [(j, i) for i, j in up]
        last = lax.slice_in_dim(value, length - width, length, axis=dim)
        first = lax.slice_in_dim(value, 0, width, axis=dim)
        before = lax.ppermute(last, axis, up)
        after = lax.ppermute(first, axis, down)
        value = jnp.concatenate([before, value, after], axis=dim)
    return value


def by_tokens(latents, w_qkv, w_out, win_blocks, win_counts, block_window):
    rows_n = lax.axis_size("rows")
    shard_idx = lax.axis_index("rows")
    frames = latents.shape[0] * lax.axis_size("frames")
    tok_frame = latents.shape[1]
    model_width = latents.shape[2]
    local_cols = w_qkv.shape[2]
    per_shard = tok_frame // BS
    block_total = per_shard * rows_n
    heads_here = local_cols // HD
    block_len = frames * BS
    score_scale = 1.0 / math.sqrt(HD)
    gathered = lax.all_gather(latents, "frames", axis=0, tiled=True)
    flat_tokens = gathered.reshape(frames * tok_frame, model_width)
    weight_rows = lax.all_gather(w_qkv, "rows", axis=0, tiled=True)
    projected = jnp.dot(
        flat_tokens,
        weight_rows.reshape(weight_rows.shape[0], 3 * local_cols),
        preferred_element_type=jnp.float32,
    ).astype(jnp.bfloat16)
    blocked = projected.reshape(frames, per_shard, BS, 3, local_cols).transpose(1, 0, 2, 3, 4)
    blocked = blocked.reshape(per_shard, block_len, 3, local_cols)
    queries = blocked[:, :, 0]
    keyvals = blocked[:, :, 1:]
    nearby = with_halo(keyvals, (("rows", 0),), per_shard)
    first_block = shard_idx * per_shard
    owners = block_window - first_block
    members = win_blocks[owners]
    lengths = win_counts[owners]
    positions = (members - first_block + per_shard + block_total) % block_total

    def attend(query_rows, picked, live_mask):
        key_count = picked.shape[0]
        key_blocks = nearby[picked]
        key_part = key_blocks[:, :, 0].reshape(key_count * block_len, heads_here, HD)
        value_part = key_blocks[:, :, 1].reshape(key_count * block_len, heads_here, HD)
        scores = (
            jnp.einsum(
                "qhd,khd->hqk",
                query_rows.reshape(block_len, heads_here, HD),
                key_part,
                preferred_element_type=jnp.float32,
            )
            * score_scale
        )
        scores = jnp.where(live_mask[None, None, :], scores, -jnp.inf)
        row_max = jnp.max(scores, axis=-1, keepdims=True)
        raised = jnp.exp(scores - row_max)
        weights = (raised / jnp.sum(raised, axis=-1, keepdims=True)).astype(jnp.bfloat16)
        blended = jnp.einsum(
            "hqk,khd->qhd", weights, value_part, preferred_element_type=jnp.float32
        )
        return blended.reshape(block_len, local_cols).astype(jnp.bfloat16)

    def one_block(block_item):
        query_rows, picked, length = block_item
        live_mask = jnp.repeat(jnp.arange(MAXB) < length, block_len)
        return attend(query_rows, picked, live_mask)

    attended = lax.map(one_block, (queries, positions, lengths))
    ordered = attended.reshape(per_shard, frames, BS, local_cols).transpose(1, 0, 2, 3)
    ordered = ordered.reshape(frames * tok_frame, local_cols)
    w_full = lax.all_gather(w_out, "rows", axis=1, tiled=True)
    group_count = lax.axis_size(("frames", "heads"))
    out_rows = frames * tok_frame // group_count
    summed = lax.psum_scatter(
        jnp.dot(ordered, w_full, preferred_element_type=jnp.float32).astype(jnp.bfloat16),
        ("frames", "heads"),
        scatter_dimension=0,
        tiled=True,
    )
    return summed.reshape(1, out_rows, model_width)


def swap(value, axis, step=1):
    peers = lax.axis_size(axis)
    return lax.ppermute(value, axis, [(i, i ^ step) for i in range(peers)])


def after(value, *others):
    return lax.optimization_barrier((value, *others))[0]


def call(kernel, out_shape, prefetch, operands, scratch=(), flops=0, read=0, limit=VMEM_BYTES):
    return pl.pallas_call(
        kernel,
        out_shape=out_shape,
        grid_spec=pltpu.PrefetchScalarGridSpec(
            num_scalar_prefetch=len(prefetch),
            grid=(),
            in_specs=[pl.BlockSpec(memory_space=pltpu.VMEM)] * len(operands),
            out_specs=jax.tree.map(lambda _: pl.BlockSpec(memory_space=pltpu.VMEM), out_shape),
            scratch_shapes=scratch,
        ),
        compiler_params=pltpu.CompilerParams(vmem_limit_bytes=limit),
        cost_estimate=pl.CostEstimate(flops=flops, bytes_accessed=read, transcendentals=0),
    )(*prefetch, *operands)


def project(place, mine, theirs, chunks, firsts, cols, tokens=None):
    rows, (count, width) = len(mine), theirs[0].shape
    pieces = [] if tokens is not None else [*mine, *theirs]
    half = chunks[0][0].shape[1]
    slices = len(chunks)
    flat = [w for of_round in chunks for w in of_round]
    fetched = len(pieces) + len(flat)

    def kernel(place_ref, *refs):
        row, group, frame, core = (place_ref[i] for i in range(4))
        w_refs = refs[len(pieces) : fetched]
        if pieces:
            q_keep, kv_keep, send, x_all, w_all, total, sems = refs[fetched:]
        else:
            x_all, q_keep, kv_keep, send, w_all, total, sems = refs[fetched:]
        copies = []
        for k in range(slices):
            for g in range(2):
                at = pl.multiple_of((row + slices - k) % slices * (2 * half) + (group + g) % 2 * half, half)
                for part in range(3):
                    source = w_refs[2 * k + g].at[part, :, firsts[k] : firsts[k] + cols]
                    into = w_all.at[pl.ds(at, half), part * cols : (part + 1) * cols]
                    copies.append(pltpu.make_async_copy(source, into, sems.at[len(copies)]))
        fetch_x = []
        for i in range(len(pieces)):
            to = x_all.at[row ^ (i % rows), (frame + i // rows) % 2]
            fetch_x.append(pltpu.make_async_copy(refs[i].at[pl.ds(0, count)], to, sems.at[len(copies) + i]))
        for copy in copies + fetch_x:
            copy.start()
        for copy in copies:
            copy.wait()
        for s in range(rows):
            if pieces:
                fetch_x[s].wait()
                fetch_x[rows + s].wait()
            at = row ^ s
            acc = jnp.dot(x_all[at].reshape(-1, width), w_all[...], preferred_element_type=jnp.float32)
            kv_part = acc[:, cols:]
            kv_keep[at] = kv_part
            send[at, : 2 * count, :] = kv_part.astype(jnp.bfloat16)
            total[s] = acc[:, :cols].reshape(2, count, cols)
            own = pl.multiple_of(core * BS, BS)
            other = pl.multiple_of((1 - core) * BS, BS)
            q_keep[at] = total[s, :, pl.ds(own, BS), :].reshape(2 * BS, cols)
            for f in range(2):
                where = slice(f * cols, (f + 1) * cols)
                send[at, 2 * count :, where] = total[s, f, pl.ds(other, BS), :].astype(jnp.bfloat16)

    vmem, hbm = pl.BlockSpec(memory_space=pltpu.VMEM), pl.BlockSpec(memory_space=pltpu.HBM)
    flops = 2 * rows * 2 * count * width * 3 * cols
    return pl.pallas_call(
        kernel,
        out_shape=(
            jax.ShapeDtypeStruct((rows, 2 * BS, cols), jnp.float32),
            jax.ShapeDtypeStruct((rows, 2 * count, 2 * cols), jnp.float32),
            jax.ShapeDtypeStruct((rows, 2 * count + BS, 2 * cols), jnp.bfloat16),
        )
        + ((jax.ShapeDtypeStruct((rows, 2, count, width), jnp.bfloat16),) if pieces else ()),
        grid_spec=pltpu.PrefetchScalarGridSpec(
            num_scalar_prefetch=1,
            grid=(),
            in_specs=[hbm] * fetched + [vmem] * (not pieces),
            out_specs=(vmem,) * (4 if pieces else 3),
            scratch_shapes=[
                pltpu.VMEM((width, 3 * cols), jnp.bfloat16),
                pltpu.VMEM((rows, 2, count, cols), jnp.float32),
                pltpu.SemaphoreType.DMA((2 * rows + 3 * len(flat),)),
            ],
        ),
        compiler_params=pltpu.CompilerParams(vmem_limit_bytes=VMEM_BYTES),
        cost_estimate=pl.CostEstimate(flops=8 * flops, bytes_accessed=flops // 300, transcendentals=0),
    )(place, *pieces, *flat, *([] if pieces else [tokens]))


def attend_all(place, members, counts, queries, keyvals, more, earlier=()):
    blocks, block_len, cols = queries.shape
    first = earlier[0].shape[2] if earlier else 0
    rows = keyvals.shape[1]
    per_row = rows // block_len

    def kernel(place_ref, members_ref, counts_ref, q_ref, kv_ref, more_ref, *refs):
        same_ref, diff_ref, q_sum, kv_sum, out = refs[len(earlier) :]
        for r in range(blocks):
            added = more_ref[r, rows:, :].astype(jnp.float32)
            added = jnp.concatenate([added[:, :cols], added[:, cols:]], axis=0)
            q_sum[r] = (q_ref[r] + added).astype(jnp.bfloat16)
            both = (kv_ref[r] + more_ref[r, :rows, :].astype(jnp.float32)).astype(jnp.bfloat16)
            both = both.reshape(2, rows // 2, 2 * cols)
            for j in range(per_row):
                part = both[:, j * BS : (j + 1) * BS, :]
                kv_sum[r * per_row + j] = part.reshape(block_len, 2 * cols)
        column = lax.broadcasted_iota(jnp.int32, (block_len, MAXB * block_len), 1)
        for b in range(blocks):
            live = column < counts_ref[b] * block_len
            listed = [kv_sum.at[members_ref[b * MAXB + j]] for j in range(MAXB)]
            for h in range(cols // HD):
                at = slice(h * HD, (h + 1) * HD)
                at_v = slice(cols + h * HD, cols + (h + 1) * HD)
                keys = jnp.concatenate([block[:, at] for block in listed], axis=0)
                values = jnp.concatenate([block[:, at_v] for block in listed], axis=0)
                scores = lax.dot_general(
                    q_sum[b, :, at], keys, (((1,), (1,)), ((), ())), preferred_element_type=jnp.float32
                )
                scores = jnp.where(live, scores, -jnp.inf)
                raised = jnp.exp2((scores - jnp.max(scores, axis=-1, keepdims=True)) * EXP2_SCALE)
                weights = raised * (1.0 / jnp.sum(raised, axis=-1, keepdims=True))
                blended = jnp.dot(
                    weights.astype(jnp.bfloat16), values, preferred_element_type=jnp.float32
                )
                out[(b + place_ref[0]) % 2, b // 2, :, at] = blended.astype(jnp.bfloat16)
        for i, out_ref in enumerate((same_ref, diff_ref)):
            if earlier:
                out_ref[:, :, :first] = refs[i][...]
            out_ref[:, :, first:] = out[i]

    half = jax.ShapeDtypeStruct((blocks // 2, block_len, first + cols), jnp.bfloat16)
    return call(
        kernel,
        (half, half),
        [place, members, counts],
        [queries, keyvals, more, *earlier],
        scratch=[
            pltpu.VMEM((blocks, block_len, cols), jnp.bfloat16),
            pltpu.VMEM((blocks * per_row, block_len, 2 * cols), jnp.bfloat16),
            pltpu.VMEM((2, blocks // 2, block_len, cols), jnp.bfloat16),
        ],
        flops=4 * blocks * block_len * MAXB * block_len * cols,
        read=16 * blocks * block_len * cols,
    )


def mix(place, attended, w_own, w_across, beside, beside_across, far):
    _, block_len, cols = attended[0].shape
    width = w_own.shape[1]

    def kernel(place_ref, *refs):
        row, group, frame, core = (place_ref[i] for i in range(4))
        w_refs = refs[4:10]
        keep, send, a_all, sums = refs[10:]
        block = 1 - row // 2 if far else row // 2
        for s in range(4):
            a_all[s] = refs[s][block]

        def term(c, other):
            side = 1 - core if other else core
            if c == 0:
                both = jnp.concatenate([a_all[(2 * side) ^ row], a_all[(2 * side + 1) ^ row]], axis=1)
                acc = jnp.dot(both, w_refs[other][...], preferred_element_type=jnp.float32)
                return acc.astype(jnp.bfloat16).astype(jnp.float32)
            acc = None
            for i in range(2):
                weight, half = w_refs[2 + 2 * other + i][:cols], (i + group) % 2
                part = jnp.dot(a_all[(2 * side + half) ^ row], weight, preferred_element_type=jnp.float32)
                acc = part if acc is None else acc + part
            return acc.astype(jnp.bfloat16).astype(jnp.float32)

        for c in range(2):
            sums[...] = (term(c, 0) + term(c, 1)).reshape(2, BS, width)
            at = (row + c) % 2
            keep[at] = sums[frame]
            send[at] = sums[1 - frame].astype(jnp.bfloat16)

    return call(
        kernel,
        (
            jax.ShapeDtypeStruct((2, BS, width), jnp.float32),
            jax.ShapeDtypeStruct((2, BS, width), jnp.bfloat16),
        ),
        [place],
        [*attended, w_own, w_across, *beside, *beside_across],
        scratch=[pltpu.VMEM((4, block_len, cols), jnp.bfloat16), pltpu.VMEM((2, BS, width), jnp.float32)],
        flops=2 * block_len * 4 * cols * 2 * width,
        read=16 * cols * width,
    )


def finish(place, near_keep, near_more, far):
    halves, rows, width = near_keep.shape

    def kernel(place_ref, keep_ref, more_ref, far_ref, out_ref):
        pair = place_ref[0] // 2
        for c in range(halves):
            here = pl.multiple_of((pair * halves + c) * width, width)
            there = pl.multiple_of(((1 - pair) * halves + c) * width, width)
            out_ref[:, pl.ds(here, width)] = (keep_ref[c] + more_ref[c].astype(jnp.float32)).astype(jnp.bfloat16)
            out_ref[:, pl.ds(there, width)] = far_ref[c]

    return call(
        kernel,
        jax.ShapeDtypeStruct((rows, 2 * halves * width), jnp.bfloat16),
        [place],
        [near_keep, near_more, far],
        read=12 * rows * halves * width,
    )


def by_heads(latents, w_qkv, w_out, win_blocks, win_counts, block_window):
    rows_n, heads_n = lax.axis_size("rows"), lax.axis_size("heads")
    group, row = lax.axis_index("groups"), lax.axis_index("rows")
    frame, core = lax.axis_index("frames"), lax.axis_index("heads")
    count = latents.shape[1]
    depth, _, local_cols = w_qkv.shape
    span = rows_n // heads_n
    cols = local_cols // span
    half = depth // 2
    place = jnp.stack([row, group, frame, core]).astype(jnp.int32)

    last = cols // (3 * HD) * HD

    def reshard(k, at, wide, *others):
        start = (0, group * half, (k + row) % span * cols + at)
        value = lax.dynamic_slice(w_qkv.transpose(1, 0, 2), start, (3, half, wide))
        pairs = [
            (r * heads_n + h, (h * span + (k + r) % span) * heads_n + r // span)
            for r in range(rows_n)
            for h in range(heads_n)
        ]
        return lax.ppermute(after(value, *others) if others else value, ("rows", "heads"), pairs)

    mine = lax.dynamic_slice_in_dim(latents[0], core * span * depth, span * depth, axis=1)
    mine_x = swap(mine, "frames")
    here, there = [reshard(0, 0, cols)], []
    near = swap(mine, "rows")
    near_x = swap(near, "frames")
    across = swap(after(w_out, near), "heads")
    there.append(swap(here[0], "groups"))
    here.append(reshard(1, 0, cols - last, near))
    tables = jnp.concatenate([win_blocks, win_counts[:, None], block_window[:, None]], axis=1)
    tables = after(tables, near)
    tables = jnp.pad(tables, ((0, 8 - heads_n), (0, span * depth - MAXB - 2))).astype(mine.dtype)
    joined = jnp.concatenate([mine, tables], axis=0)
    far_2 = swap(after(joined, here[0], mine_x), "rows", 2)
    out_half = lax.dynamic_slice_in_dim(w_out, group * cols, cols, axis=0)
    out_half = jnp.concatenate([out_half, tables[:, : out_half.shape[1]]], axis=0)
    beside = [swap(after(out_half, near), "rows")]
    beside.append(swap(beside[0], "groups"))
    there.append(swap(after(here[1], there[0], beside[1]), "groups"))
    far_2x = swap(far_2, "frames")
    far_3 = swap(after(joined, far_2, across, near_x, beside[0]), "rows", 3)
    far_3x = swap(far_3, "frames")
    here.append(reshard(1, cols - last, last, far_3, there[1]))
    there.append(swap(here[2], "groups"))

    found = [tables, beside[0][cols:], far_2[count:], far_3[count:]]
    found = jnp.stack([x[:heads_n, : MAXB + 2] for x in found])
    tables = found.astype(jnp.int32)[row ^ jnp.arange(rows_n)].reshape(rows_n * heads_n, MAXB + 2)
    windows = lax.dynamic_index_in_dim(
        tables[:, MAXB + 1].reshape(rows_n, heads_n), core, axis=1, keepdims=False
    )
    picked = tables[windows]
    members, counts = picked[:, :MAXB].reshape(-1), picked[:, MAXB]

    pieces = [mine, near, far_2, far_3], [mine_x, near_x, far_2x, far_3x]
    chunks = [(here[0], there[0]), (here[1], after(there[1], members, counts))]
    *first, tokens = project(place, *pieces, chunks, (0, 0), cols - last)
    first_more = swap(first[2], "heads")
    chunks[1] = (here[2], after(there[2], first[2]))
    second = project(place, *pieces, chunks, (cols - last, 0), last, tokens)
    second_more = swap(second[2], "heads")
    attended = attend_all(place, members, counts, *first[:2], first_more)
    beside_across = [swap(part, "heads") for part in beside]
    same, diff = attend_all(place, members, counts, *second[:2], second_more, attended)
    attended = [same] + [swap(same if s % 2 == 0 else diff, "rows", s) for s in range(1, rows_n)]
    weights = w_out, across, beside, beside_across
    far_keep, far_send = mix(place, attended, *weights, True)
    near_keep, near_send = mix(place, attended, *weights, False)
    far_more = swap(far_send, "frames")
    far = swap((far_keep + far_more.astype(jnp.float32)).astype(jnp.bfloat16), "rows", 2)
    near_more = swap(after(near_send, far_more), "frames")
    return finish(place, near_keep, near_more, far)[None]


def local(latents, w_qkv, w_out, win_blocks, win_counts, block_window):
    rows_n = lax.axis_size("rows")
    pairs = all(lax.axis_size(axis) == 2 for axis in ("groups", "frames", "heads"))
    heads_here = w_qkv.shape[2] // HD
    if pairs and rows_n == 4 and heads_here == 6 and latents.shape[:2] == (1, 2 * BS):
        plan = by_heads
    else:
        plan = by_tokens
    return plan(latents, w_qkv, w_out, win_blocks, win_counts, block_window)


def solution(mesh):
    in_specs = (
        P(("groups", "frames"), "rows", None),
        P("rows", None, ("frames", "heads")),
        P(("frames", "heads"), "rows"),
        P(("groups", "rows"), None),
        P(("groups", "rows")),
        P(("groups", "rows")),
    )
    out_specs = P(("groups", "frames"), ("rows", "heads"), None)
    return jax.shard_map(local, mesh=mesh, in_specs=in_specs, out_specs=out_specs, check_vma=False)
```
